32 devices in a mesh: section: 2 (over core), dp: 4 (over y, x), tensor: 4 (over z).
Axes of the slice: x: 2, y: 2, z: 4, core: 2. Of those that a mesh axis runs over, the one named last changes fastest.
Arguments:
- inputs: bfloat16 [4, 6, 192, 1024], P('dp', None, 'tensor'), may hold values from -6 to 6
- starts: int32 [4, 6, 192], P('dp'), may hold values from 0 to 1, as said below
- cotangent: bfloat16 [4, 6, 192, 1024], P('dp', None, 'tensor'), may hold values from -6 to 6
- qkv_master: float32 [2, 1024, 3, 1024], P('section', 'dp', None, 'tensor'), may hold values from -0.1875 to 0.1875
- out_master: float32 [2, 1024, 1024], P('section', 'tensor', 'dp'), may hold values from -0.25 to 0.25
- gateup_master: float32 [2, 1024, 2, 2816], P('section', 'dp', None, 'tensor'), may hold values from -0.1875 to 0.1875
- down_master: float32 [2, 2816, 1024], P('section', 'tensor', 'dp'), may hold values from -0.109375 to 0.109375
- gain_master: float32 [2, 2, 1024], P('section', None, ('dp', 'tensor')), may hold values from 0.25 to 1.75
Outputs:
- layer_outputs: bfloat16 [2, 4, 6, 192, 1024], P('section', 'dp', None, 'tensor')
- input_grads: bfloat16 [2, 4, 6, 192, 1024], P('section', 'dp', None, 'tensor')
- qkv_grad: float32 [2, 1024, 3, 1024], P('section', 'dp', None, 'tensor')
- out_grad: float32 [2, 1024, 1024], P('section', 'tensor', 'dp')
- gateup_grad: float32 [2, 1024, 2, 2816], P('section', 'dp', None, 'tensor')
- down_grad: float32 [2, 2816, 1024], P('section', 'tensor', 'dp')
- gain_grad: float32 [2, 2, 1024], P('section', None, ('dp', 'tensor'))
The draws below stay inside these ranges and needn't reach their ends.
Inputs may be any that keep to these rules, and one draw needn't show every extreme that they name: `starts`: 1 marks the first token of a document and 0 a token that continues the document of the token before it; the first token of every sequence is 1.
All inputs are finite; a program needn't handle non-finite values.
Results may differ from the reference program's by a relative error of at most 0.024.
Values may be sent and summed in bfloat16 or wider, within the bound.
A program may use at most 256 MiB of HBM per device.

```python
import jax
import jax.numpy as jnp
from jax import lax

D = 1024
HEADS = 16
FF = 2816
DH = 64
BLOCK = 64
LAYERS = 2
MICRO = 6
MB_TOK = 192
SEQS = 4
N_TENSOR = 4


def draw_starts(key, part):
    key = jax.random.fold_in(key, 7)
    key_flags, key_anchor = jax.random.split(key)
    seq_length = MICRO * MB_TOK
    start_flags = (jax.random.randint(key_flags, (SEQS, seq_length), 0, MB_TOK // 4 + 1) == 0).astype(jnp.int32)
    anchor = jax.random.randint(key_anchor, (SEQS, 1), 1, MB_TOK)
    position = jnp.arange(seq_length)[None, :]
    inside = (position > anchor) & (position <= anchor + 2 * MB_TOK)
    start_flags = jnp.where(inside, 0, start_flags)
    start_flags = jnp.where((position == anchor) | (position == 0), 1, start_flags)
    return start_flags.reshape(SEQS, MICRO, MB_TOK).astype(jnp.int32)


def spiked(values, own_key, source, target, blocks, factor):
    def block_of(dim):
        return (jnp.arange(values.shape[dim]) // (values.shape[dim] // blocks)).reshape((-1,) + (1,) * (values.ndim - 1 - dim))

    first = jax.random.permutation(own_key, blocks)[block_of(target)]
    other_side = (block_of(target) + blocks // 2) % blocks
    return jnp.where((block_of(source) == first) | (block_of(source) == other_side), factor * values, values)


def shard_levels(key, extent, pieces, low, high):
    loudness, own = 1.0, jax.random.fold_in(key, 6)
    for axis_at, blocks in pieces:
        heights = jnp.exp(jax.random.uniform(jax.random.fold_in(own, axis_at), (blocks,), jnp.float32, low / len(pieces), high / len(pieces)))
        loudness = loudness * jnp.repeat(heights, extent[axis_at] // blocks).reshape([-1 if axis == axis_at else 1 for axis in range(len(extent))])
    return loudness


def gaussian(own_key, dims, deviation, bound, cuts=(), held_as=jnp.bfloat16):
    result = deviation * jax.random.normal(own_key, dims, jnp.float32)
    if cuts:
        result = result * shard_levels(own_key, dims, cuts, -0.22, 0.18)
    return jnp.clip(result, -bound, bound).astype(held_as)


def gaussian_with(own_key, extent, spread, bound, shards, heavy, held_as=jnp.bfloat16):
    drawn = spread * jax.random.normal(own_key, extent, jnp.float32)
    if shards:
        drawn = drawn * shard_levels(own_key, extent, shards, -0.22, 0.18)
    return jnp.clip(spiked(drawn, jax.random.fold_in(own_key, 3), *heavy), -bound, bound).astype(held_as)


def setup_inputs(seed: int = 0) -> dict:
    arg_keys = jax.random.split(jax.random.key(seed), 9)
    inputs = gaussian_with(arg_keys[0], (SEQS, MICRO, MB_TOK, D), 1.0, 6.0, ((0, 4), (2, 4)), (0, 3, 4, 2.0))
    starts = draw_starts(jax.random.fold_in(arg_keys[8], 71), 0)
    cotangent = gaussian_with(arg_keys[2], (SEQS, MICRO, MB_TOK, D), 1.0, 6.0, ((0, 4), (2, 4)), (0, 3, 4, 2.0))
    qkv_master = gaussian(arg_keys[3], (LAYERS, D, 3, D), D ** -0.5, 0.1875, ((0, 2), (1, 4), (3, 4)), jnp.float32)
    out_master = gaussian(arg_keys[4], (LAYERS, D, D), (D // 2) ** -0.5, 0.25, ((0, 2), (1, 4), (2, 4)), jnp.float32)
    gateup_master = gaussian(arg_keys[5], (LAYERS, D, 2, FF), D ** -0.5, 0.1875, ((0, 2), (1, 4), (3, 4)), jnp.float32)
    down_master = gaussian(arg_keys[6], (LAYERS, FF, D), FF ** -0.5, 0.109375, ((0, 2), (1, 4), (2, 4)), jnp.float32)
    gain_master = jnp.clip(1.0 + 0.15 * jax.random.normal(arg_keys[7], (LAYERS, 2, D), jnp.float32), 0.25, 1.75)
    return dict(inputs=inputs, starts=starts, cotangent=cotangent, qkv_master=qkv_master, out_master=out_master, gateup_master=gateup_master, down_master=down_master, gain_master=gain_master)


EPSILON = 1e-06

@jax.custom_vjp
def low(v):
    return lax.optimization_barrier(v.astype(jnp.bfloat16)).astype(jnp.float32)

@jax.custom_vjp
def low_back(v):
    return v

def low_keep(v):
    return (low(v), None)

def low_pass(kept, grad):
    return (grad,)

def back_keep(v):
    return (v, None)

def back_low(kept, grad):
    return (low(grad),)
low.defvjp(low_keep, low_pass)
low_back.defvjp(back_keep, back_low)

def exact(form, first, second):
    return jnp.einsum(form, first, second, precision=lax.Precision.HIGHEST)

def rms_scale(flat_rows, gain_row):
    return flat_rows * lax.rsqrt(lax.optimization_barrier(jnp.mean(flat_rows * flat_rows, axis=-1, keepdims=True)) + EPSILON) * gain_row

def block_masks(doc_ids):
    blocked = doc_ids.reshape(-1, BLOCK)
    position = jnp.arange(BLOCK)
    causal = position[:, None] >= position[None, :]
    inside = causal[None] & (blocked[:, :, None] == blocked[:, None, :])
    return (blocked, inside)

def head_blocks(flat_rows):
    return flat_rows.reshape(-1, BLOCK, HEADS, DH)

def diag_mix(query_rows, key_rows, value_rows, doc_ids):
    blocked, inside = block_masks(doc_ids)
    raw_scores = low_back(exact('bqhd,bkhd->bhqk', head_blocks(query_rows), head_blocks(key_rows)))
    scores = jnp.where(inside[:, None], raw_scores * DH ** (-0.5), -1000000000.0)
    weights_soft = jax.nn.softmax(scores, axis=-1)
    attended = exact('bhqk,bkhd->bqhd', low(weights_soft), head_blocks(value_rows))
    return low(low_back(attended)).reshape(-1, HEADS * DH)

def norm_mix(query_rows, key_rows, value_rows, doc_ids):
    blocked, inside = block_masks(doc_ids)
    query_feat = low(jax.nn.softplus(head_blocks(query_rows)))
    key_feat = low(jax.nn.softplus(head_blocks(key_rows)))
    value_blocks = head_blocks(value_rows)
    last_doc = blocked[:, -1]
    state_doc = jnp.concatenate([jnp.zeros((1,), jnp.int32), last_doc[:-1].astype(jnp.int32)])
    keep_mask = (last_doc == state_doc).astype(jnp.float32)
    carry_mask = (blocked == state_doc[:, None]).astype(jnp.float32)
    tail_mask = (blocked == last_doc[:, None]).astype(jnp.float32)
    raw_scores = low_back(exact('bqhd,bkhd->bhqk', query_feat, key_feat))
    local_scores = low(jnp.where(inside[:, None], raw_scores, 0.0))
    kv_terms = exact('bkhd,bkhe->bhde', key_feat, tail_mask[:, :, None, None] * value_blocks)

    def advance(kv_state, seq_item):
        keep_value, kv_term = seq_item
        return (keep_value * kv_state + kv_term, kv_state)
    zero_state = jnp.zeros((HEADS, DH, DH), jnp.float32)
    _, state_starts = lax.scan(advance, zero_state, (keep_mask, kv_terms))
    mixed_rows = exact('bhqk,bkhd->bqhd', local_scores, value_blocks)
    mixed_rows = mixed_rows + carry_mask[:, :, None, None] * exact('bqhd,bhde->bqhe', query_feat, state_starts)
    mixed_rows = low_back(mixed_rows)
    normed = mixed_rows * lax.rsqrt(lax.optimization_barrier(jnp.mean(mixed_rows * mixed_rows, axis=-1, keepdims=True)) + EPSILON)
    return low(normed).reshape(-1, HEADS * DH)

def partial_sum(flat_rows, weight_rows):
    groups = flat_rows.reshape(flat_rows.shape[0], N_TENSOR, -1)
    split_weight = weight_rows.reshape(N_TENSOR, -1, weight_rows.shape[1])
    parts = exact('lgc,gcd->lgd', groups, split_weight)
    return low_back(lax.optimization_barrier(jnp.sum(low(parts), axis=1)))

def layer(x_rows, qkv_w, out_w, gateup_w, down_w, gain_w, doc_ids, mixer):
    qkv_low = low(qkv_w)
    out_low = low(out_w)
    gateup_low = low(gateup_w)
    down_low = low(down_w)
    gain_low = low(gain_w)
    normed_first = low(rms_scale(x_rows, gain_low[0]))
    projected = low(low_back(exact('ld,dkc->lkc', normed_first, qkv_low)))
    attended = mixer(projected[:, 0], projected[:, 1], projected[:, 2], doc_ids)
    hidden_in = x_rows + partial_sum(attended, out_low)
    normed_second = low(rms_scale(hidden_in, gain_low[1]))
    gate_up = low_back(exact('ld,dkf->lkf', normed_second, gateup_low))
    product = low(gate_up[:, 0] * gate_up[:, 1])
    return hidden_in + partial_sum(product, down_low)

def reference(inputs, starts, cotangent, qkv_master, out_master, gateup_master, down_master, gain_master):
    seq_length = MICRO * MB_TOK
    seq_inputs = inputs.astype(jnp.float32).reshape(SEQS, seq_length, D)
    seq_cot = cotangent.astype(jnp.float32).reshape(SEQS, seq_length, D)
    doc_all = jnp.cumsum(starts.reshape(SEQS, seq_length), axis=1).astype(jnp.int32)
    masters = (qkv_master, out_master, gateup_master, down_master, gain_master)

    def one_sequence(totals, seq_item):
        x_rows, doc_ids, cot_rows = seq_item

        def first_layer(rows_in, qkv_w, out_w, gateup_w, down_w, gain_w):
            return layer(rows_in, qkv_w, out_w, gateup_w, down_w, gain_w, doc_ids, diag_mix)

        def second_layer(rows_in, qkv_w, out_w, gateup_w, down_w, gain_w):
            return layer(rows_in, qkv_w, out_w, gateup_w, down_w, gain_w, doc_ids, norm_mix)
        first_out, first_back = jax.vjp(first_layer, x_rows, qkv_master[0], out_master[0], gateup_master[0], down_master[0], gain_master[0])
        middle = low(first_out)
        second_out, second_back = jax.vjp(second_layer, middle, qkv_master[1], out_master[1], gateup_master[1], down_master[1], gain_master[1])
        second_grads = second_back(cot_rows)
        middle_grad = low(second_grads[0])
        first_grads = first_back(middle_grad)
        totals = tuple((running + jnp.stack([first_grads[slot_number + 1], second_grads[slot_number + 1]]) for slot_number, running in enumerate(totals)))
        return (totals, (middle, low(second_out), first_grads[0], middle_grad))
    zero_totals = tuple((jnp.zeros_like(master) for master in masters))
    totals, kept_rows = lax.scan(one_sequence, zero_totals, (seq_inputs, doc_all, seq_cot))
    middles, finals, input_grad, middle_grads = kept_rows
    shape_out = (SEQS, MICRO, MB_TOK, D)
    layer_outputs = jnp.stack([middles.reshape(shape_out), finals.reshape(shape_out)]).astype(jnp.bfloat16)
    input_grads = jnp.stack([input_grad.reshape(shape_out), middle_grads.reshape(shape_out)]).astype(jnp.bfloat16)
    return (layer_outputs, input_grads, totals[0], totals[1], totals[2], totals[3], totals[4])
```

```python
import math

import jax
import jax.numpy as jnp
from jax import lax
from jax.sharding import PartitionSpec as P

DH = 64
BLOCK = 64


EPSILON = 1e-06


def passed_along(value, axis, steps):
    count = lax.axis_size(axis)
    first, last = (max(0, -steps), min(count, count - steps))
    return lax.ppermute(value, axis, [(source, source + steps) for source in range(first, last)])


def running_sum(marks):
    position = jnp.arange(marks.shape[0])
    return jnp.sum(jnp.where(position[:, None] >= position[None, :], marks[None, :], 0), axis=1)


def blocks_of(flat_rows):
    return flat_rows.reshape(-1, BLOCK, flat_rows.shape[1] // DH, DH)


def rows_of(block_rows):
    return block_rows.reshape(-1, block_rows.shape[2] * DH)


def block_masks(doc_local):
    blocked = doc_local.reshape(-1, BLOCK)
    position = jnp.arange(BLOCK)
    causal = position[:, None] >= position[None, :]
    inside = causal[None] & (blocked[:, :, None] == blocked[:, None, :])
    return (blocked, inside)


def rms_forward(flat_rows, gain_row):
    inverse = lax.rsqrt(jnp.mean(flat_rows * flat_rows, axis=-1, keepdims=True) + EPSILON)
    return (flat_rows * inverse * gain_row, inverse)


def rms_backward(flat_rows, gain_row, inverse, grad_rows):
    scaled = grad_rows * gain_row
    back_rows = inverse * scaled - flat_rows * inverse**3 * jnp.mean(
        scaled * flat_rows, axis=-1, keepdims=True
    )
    return (back_rows, jnp.sum(grad_rows * flat_rows * inverse, axis=0))


def diag_weights(query_rows, key_rows, doc_local):
    blocked, inside = block_masks(doc_local)
    raw_scores = jnp.einsum(
        "bqhd,bkhd->bhqk",
        blocks_of(query_rows),
        blocks_of(key_rows),
        preferred_element_type=jnp.float32,
    )
    scores = jnp.where(inside[:, None], raw_scores * (1.0 / math.sqrt(DH)), -1000000000.0)
    return (jax.nn.softmax(scores, axis=-1), inside)


def diag_forward(query_rows, key_rows, value_rows, doc_local, kv_state):
    weights_soft, inside = diag_weights(query_rows, key_rows, doc_local)
    attended = jnp.einsum(
        "bhqk,bkhd->bqhd",
        weights_soft.astype(jnp.bfloat16),
        blocks_of(value_rows),
        preferred_element_type=jnp.float32,
    )
    return (rows_of(attended).astype(jnp.bfloat16), kv_state)


def diag_backward(query_rows, key_rows, value_rows, doc_local, kv_state, grad_attended, grad_state):
    weights_soft, inside = diag_weights(query_rows, key_rows, doc_local)
    grad_low = blocks_of(grad_attended).astype(jnp.bfloat16)
    grad_value = jnp.einsum(
        "bhqk,bqhd->bkhd",
        weights_soft.astype(jnp.bfloat16),
        grad_low,
        preferred_element_type=jnp.float32,
    )
    grad_weights = jnp.einsum(
        "bqhd,bkhd->bhqk", grad_low, blocks_of(value_rows), preferred_element_type=jnp.float32
    )
    grad_scores = weights_soft * (
        grad_weights - jnp.sum(grad_weights * weights_soft, axis=-1, keepdims=True)
    )
    grad_raw = jnp.where(inside[:, None], grad_scores * (1.0 / math.sqrt(DH)), 0.0).astype(
        jnp.bfloat16
    )
    grad_query = jnp.einsum(
        "bhqk,bkhd->bqhd", grad_raw, blocks_of(key_rows), preferred_element_type=jnp.float32
    )
    grad_key = jnp.einsum(
        "bhqk,bqhd->bkhd", grad_raw, blocks_of(query_rows), preferred_element_type=jnp.float32
    )
    return (rows_of(grad_query), rows_of(grad_key), rows_of(grad_value), grad_state)


def norm_pieces(query_feat, key_feat, value_blocks, doc_local, kv_state):
    blocked, inside = block_masks(doc_local)
    last_doc = blocked[:, -1]
    state_doc = jnp.concatenate([jnp.zeros((1,), jnp.int32), last_doc[:-1]])
    keep_mask = (last_doc == state_doc).astype(jnp.float32)
    carry_mask = (blocked == state_doc[:, None]).astype(jnp.float32)
    tail_mask = (blocked == last_doc[:, None]).astype(jnp.bfloat16)
    raw_scores = jnp.einsum(
        "bqhd,bkhd->bhqk", query_feat, key_feat, preferred_element_type=jnp.float32
    )
    local_scores = jnp.where(inside[:, None], raw_scores, 0.0).astype(jnp.bfloat16)
    kv_terms = jnp.einsum(
        "bkhd,bkhe->bhde",
        key_feat,
        value_blocks * tail_mask[:, :, None, None],
        preferred_element_type=jnp.float32,
    )

    def advance(state_now, block_item):
        keep_value, kv_term = block_item
        return (keep_value * state_now + kv_term, state_now)

    state_end, state_starts = lax.scan(advance, kv_state, (keep_mask, kv_terms))
    mixed_rows = jnp.einsum(
        "bhqk,bkhd->bqhd", local_scores, value_blocks, preferred_element_type=jnp.float32
    )
    carried = jnp.einsum(
        "bqhd,bhde->bqhe",
        query_feat.astype(jnp.float32),
        state_starts,
        precision=lax.Precision.HIGHEST,
    )
    mixed_rows = mixed_rows + carry_mask[:, :, None, None] * carried
    return (
        mixed_rows,
        local_scores,
        state_starts,
        state_end,
        keep_mask,
        carry_mask,
        tail_mask,
        inside,
    )


def norm_forward(query_rows, key_rows, value_rows, doc_local, kv_state):
    query_feat = jax.nn.softplus(blocks_of(query_rows).astype(jnp.float32)).astype(jnp.bfloat16)
    key_feat = jax.nn.softplus(blocks_of(key_rows).astype(jnp.float32)).astype(jnp.bfloat16)
    pieces = norm_pieces(query_feat, key_feat, blocks_of(value_rows), doc_local, kv_state)
    mixed_rows = pieces[0]
    normed = mixed_rows * lax.rsqrt(
        jnp.mean(mixed_rows * mixed_rows, axis=-1, keepdims=True) + EPSILON
    )
    return (rows_of(normed).astype(jnp.bfloat16), pieces[3])


def norm_backward(query_rows, key_rows, value_rows, doc_local, kv_state, grad_attended, grad_state):
    query_float = blocks_of(query_rows).astype(jnp.float32)
    key_float = blocks_of(key_rows).astype(jnp.float32)
    query_feat = jax.nn.softplus(query_float).astype(jnp.bfloat16)
    key_feat = jax.nn.softplus(key_float).astype(jnp.bfloat16)
    value_blocks = blocks_of(value_rows)
    pieces = norm_pieces(query_feat, key_feat, value_blocks, doc_local, kv_state)
    mixed_rows, local_scores, state_starts, _, keep_mask, carry_mask, tail_mask, inside = pieces
    scale_rows = lax.rsqrt(jnp.mean(mixed_rows * mixed_rows, axis=-1, keepdims=True) + EPSILON)
    grad_normed = blocks_of(grad_attended)
    grad_mixed = scale_rows * grad_normed - mixed_rows * scale_rows**3 * jnp.mean(
        grad_normed * mixed_rows, axis=-1, keepdims=True
    )
    grad_low = grad_mixed.astype(jnp.bfloat16)
    carry_wide = carry_mask[:, :, None, None]
    grad_carried = grad_low * carry_wide.astype(jnp.bfloat16)
    use_terms = jnp.einsum(
        "bqhd,bqhe->bhde", query_feat, grad_carried, preferred_element_type=jnp.float32
    )

    def retreat(grad_now, block_item):
        keep_value, use_term = block_item
        return (keep_value * grad_now + use_term, grad_now)

    grad_start, grad_after = lax.scan(retreat, grad_state, (keep_mask, use_terms), reverse=True)
    tail_wide = tail_mask.astype(jnp.float32)[:, :, None, None]
    key_state = tail_wide * jnp.einsum(
        "bkhe,bhde->bkhd",
        value_blocks.astype(jnp.float32),
        grad_after,
        precision=lax.Precision.HIGHEST,
    )
    value_state = tail_wide * jnp.einsum(
        "bkhd,bhde->bkhe", key_feat.astype(jnp.float32), grad_after, precision=lax.Precision.HIGHEST
    )
    query_state = carry_wide * jnp.einsum(
        "bqhe,bhde->bqhd",
        grad_low.astype(jnp.float32),
        state_starts,
        precision=lax.Precision.HIGHEST,
    )
    value_local = jnp.einsum(
        "bhqk,bqhd->bkhd", local_scores, grad_low, preferred_element_type=jnp.float32
    )
    grad_products = jnp.einsum(
        "bqhd,bkhd->bhqk", grad_low, value_blocks, preferred_element_type=jnp.float32
    )
    grad_scores = jnp.where(inside[:, None], grad_products, 0.0).astype(jnp.bfloat16)
    query_local = jnp.einsum(
        "bhqk,bkhd->bqhd", grad_scores, key_feat, preferred_element_type=jnp.float32
    )
    key_local = jnp.einsum(
        "bhqk,bqhd->bkhd", grad_scores, query_feat, preferred_element_type=jnp.float32
    )
    grad_query = (query_local + query_state) * jax.nn.sigmoid(query_float)
    grad_key = (key_local + key_state) * jax.nn.sigmoid(key_float)
    grad_value = value_local + value_state
    return (rows_of(grad_query), rows_of(grad_key), rows_of(grad_value), grad_start)


def on_device(
    inputs, starts, cotangent, qkv_master, out_master, gateup_master, down_master, gain_master
):
    section_index = lax.axis_index("section")
    micro_count = inputs.shape[1]
    row_count = inputs.shape[2]
    model_width = inputs.shape[3]
    local_cols = qkv_master.shape[3]
    local_hidden = gateup_master.shape[3]
    head_count = local_cols // DH
    norm_gains = lax.all_gather(
        gain_master[0].astype(jnp.bfloat16), ("dp", "tensor"), axis=1, tiled=True
    ).astype(jnp.float32)

    def fetch_weights():
        pieces = (
            lax.all_gather(qkv_master[0].astype(jnp.bfloat16), "dp", axis=0, tiled=True),
            lax.all_gather(out_master[0].astype(jnp.bfloat16), "dp", axis=1, tiled=True),
            lax.all_gather(gateup_master[0].astype(jnp.bfloat16), "dp", axis=0, tiled=True),
            lax.all_gather(down_master[0].astype(jnp.bfloat16), "dp", axis=1, tiled=True),
        )
        return (
            pieces[0].reshape(model_width, 3 * local_cols),
            pieces[1],
            pieces[2].reshape(model_width, 2 * local_hidden),
            pieces[3],
        )

    def spread(row_block):
        return lax.all_gather(row_block, "tensor", axis=0, tiled=True)

    def collect(full_rows, weight_rows):

        def term_rows(start_row, row_total):
            return jnp.dot(full_rows, weight_rows, preferred_element_type=jnp.float32)

        return lax.psum_scatter(
            term_rows(jnp.int32(0), lax.axis_size("tensor") * row_count).astype(jnp.bfloat16),
            "tensor",
            scatter_dimension=0,
            tiled=True,
        ).astype(jnp.float32)

    def spread_grad(row_block):
        return lax.all_gather(row_block, "tensor", axis=0, tiled=True)

    def collect_grad(full_rows, weight_rows):

        def term_rows(start_row, row_total):
            return lax.dot_general(
                full_rows, weight_rows, (((1,), (1,)), ((), ())), preferred_element_type=jnp.float32
            )

        return lax.psum_scatter(
            term_rows(jnp.int32(0), lax.axis_size("tensor") * row_count).astype(jnp.bfloat16),
            "tensor",
            scatter_dimension=0,
            tiled=True,
        ).astype(jnp.float32)

    def layer_forward(x_in, weights, doc_local, kv_state):
        wqkv_rows, wout_rows, wgu_rows, wdown_rows = weights
        normed_first, scale_first = rms_forward(x_in, norm_gains[0])
        full_first = spread(normed_first.astype(jnp.bfloat16))
        projected = jnp.dot(full_first, wqkv_rows, preferred_element_type=jnp.float32).astype(
            jnp.bfloat16
        )
        query_rows = projected[:, :local_cols]
        key_rows = projected[:, local_cols : 2 * local_cols]
        value_rows = projected[:, 2 * local_cols :]
        attended, new_state = lax.cond(
            section_index == 0,
            diag_forward,
            norm_forward,
            query_rows,
            key_rows,
            value_rows,
            doc_local,
            kv_state,
        )
        hidden_in = x_in + collect(attended, wout_rows)
        normed_second, scale_second = rms_forward(hidden_in, norm_gains[1])
        full_second = spread(normed_second.astype(jnp.bfloat16))
        gate_up = jnp.dot(full_second, wgu_rows, preferred_element_type=jnp.float32)
        gate_rows = gate_up[:, :local_hidden]
        upward = gate_up[:, local_hidden:]
        product = (gate_rows * upward).astype(jnp.bfloat16)
        output = hidden_in + collect(product, wdown_rows)
        record = (
            full_first,
            projected,
            attended,
            hidden_in,
            scale_first,
            full_second,
            gate_rows,
            upward,
            product,
            scale_second,
        )
        return (output, new_state, record)

    def layer_backward(x_in, grad_out, doc_local, kv_state, grad_state, weights):
        wqkv_rows, wout_rows, wgu_rows, wdown_rows = weights
        _, _, record = layer_forward(x_in, weights, doc_local, kv_state)
        (
            full_first,
            projected,
            attended,
            hidden_in,
            scale_first,
            full_second,
            gate_rows,
            upward,
            product,
            scale_second,
        ) = record
        grad_full = spread_grad(grad_out.astype(jnp.bfloat16))
        down_terms = jnp.einsum("tf,td->fd", product, grad_full, preferred_element_type=jnp.float32)
        grad_product = lax.dot_general(
            grad_full, wdown_rows, (((1,), (1,)), ((), ())), preferred_element_type=jnp.float32
        )
        grad_gate_up = jnp.concatenate(
            [grad_product * upward, grad_product * gate_rows], axis=1
        ).astype(jnp.bfloat16)
        gateup_terms = jnp.einsum(
            "td,tf->df", full_second, grad_gate_up, preferred_element_type=jnp.float32
        )
        grad_second, gain_second = rms_backward(
            hidden_in, norm_gains[1], scale_second, collect_grad(grad_gate_up, wgu_rows)
        )
        grad_hidden = grad_out + grad_second
        grad_branch = spread_grad(grad_hidden.astype(jnp.bfloat16))
        out_terms = jnp.einsum(
            "tc,td->cd", attended, grad_branch, preferred_element_type=jnp.float32
        )
        grad_attended = lax.dot_general(
            grad_branch, wout_rows, (((1,), (1,)), ((), ())), preferred_element_type=jnp.float32
        )
        query_rows = projected[:, :local_cols]
        key_rows = projected[:, local_cols : 2 * local_cols]
        value_rows = projected[:, 2 * local_cols :]
        grad_query, grad_key, grad_value, grad_start = lax.cond(
            section_index == 0,
            diag_backward,
            norm_backward,
            query_rows,
            key_rows,
            value_rows,
            doc_local,
            kv_state,
            grad_attended,
            grad_state,
        )
        grad_projected = jnp.concatenate([grad_query, grad_key, grad_value], axis=1).astype(
            jnp.bfloat16
        )
        qkv_terms = jnp.einsum(
            "td,tc->dc", full_first, grad_projected, preferred_element_type=jnp.float32
        )
        grad_first, gain_first = rms_backward(
            x_in, norm_gains[0], scale_first, collect_grad(grad_projected, wqkv_rows)
        )
        grad_in = grad_hidden + grad_first
        weight_terms = (
            qkv_terms.reshape(model_width, 3, local_cols),
            out_terms,
            gateup_terms.reshape(model_width, 2, local_hidden),
            down_terms,
        )
        return (grad_in, grad_start, weight_terms, jnp.stack([gain_first, gain_second]))

    own_inputs = inputs[0]
    own_starts = starts[0]
    own_cot = cotangent[0]
    kv_state = jnp.zeros((head_count, DH, DH), jnp.float32)
    state_log = jnp.zeros((micro_count, head_count, DH, DH), jnp.float32)
    held_inputs = jnp.zeros((micro_count, row_count, model_width), jnp.bfloat16)
    results = jnp.zeros((micro_count, row_count, model_width), jnp.bfloat16)
    sent_rows = jnp.zeros((row_count, model_width), jnp.bfloat16)
    weights = fetch_weights()
    for tick_number in range(micro_count + 1):
        if tick_number > 0:
            arrived = passed_along(sent_rows, "section", 1)
        else:
            arrived = sent_rows
        tick_order = tick_number - section_index
        is_valid = (tick_order >= 0) & (tick_order < micro_count)
        mb_index = jnp.clip(tick_order, 0, micro_count - 1)
        fresh_rows = lax.dynamic_index_in_dim(own_inputs, mb_index, 0, keepdims=False)
        layer_input = jnp.where(section_index == 0, fresh_rows, arrived)
        doc_local = running_sum(lax.dynamic_index_in_dim(own_starts, mb_index, 0, keepdims=False))
        output, new_state, _ = layer_forward(
            layer_input.astype(jnp.float32), weights, doc_local, kv_state
        )
        sent_rows = output.astype(jnp.bfloat16)
        held_inputs = jnp.where(
            is_valid,
            lax.dynamic_update_index_in_dim(held_inputs, layer_input, mb_index, 0),
            held_inputs,
        )
        results = jnp.where(
            is_valid, lax.dynamic_update_index_in_dim(results, sent_rows, mb_index, 0), results
        )
        state_log = jnp.where(
            is_valid, lax.dynamic_update_index_in_dim(state_log, kv_state, mb_index, 0), state_log
        )
        kv_state = jnp.where(is_valid, new_state, kv_state)
    grad_state = jnp.zeros((head_count, DH, DH), jnp.float32)
    grad_log = jnp.zeros((micro_count, row_count, model_width), jnp.bfloat16)
    back_sent = jnp.zeros((row_count, model_width), jnp.bfloat16)
    gain_total = jnp.zeros((2, model_width), jnp.float32)
    totals = (
        jnp.zeros((model_width, 3, local_cols), jnp.float32),
        jnp.zeros((local_cols, model_width), jnp.float32),
        jnp.zeros((model_width, 2, local_hidden), jnp.float32),
        jnp.zeros((local_hidden, model_width), jnp.float32),
    )
    for tick_number in range(micro_count + 1):
        if tick_number > 0:
            arrived = passed_along(back_sent, "section", -1)
        else:
            arrived = back_sent
        tick_order = tick_number - (1 - section_index)
        is_valid = (tick_order >= 0) & (tick_order < micro_count)
        mb_index = jnp.clip(micro_count - 1 - tick_order, 0, micro_count - 1)
        layer_input = lax.dynamic_index_in_dim(held_inputs, mb_index, 0, keepdims=False)
        upstream = jnp.where(
            section_index == 1,
            lax.dynamic_index_in_dim(own_cot, mb_index, 0, keepdims=False),
            arrived,
        )
        doc_local = running_sum(lax.dynamic_index_in_dim(own_starts, mb_index, 0, keepdims=False))
        start_state = lax.dynamic_index_in_dim(state_log, mb_index, 0, keepdims=False)
        grad_in, grad_start, weight_terms, gain_terms = layer_backward(
            layer_input.astype(jnp.float32),
            upstream.astype(jnp.float32),
            doc_local,
            start_state,
            grad_state,
            weights,
        )
        grad_state = jnp.where(is_valid, grad_start, grad_state)
        back_sent = grad_in.astype(jnp.bfloat16)
        grad_log = jnp.where(
            is_valid, lax.dynamic_update_index_in_dim(grad_log, back_sent, mb_index, 0), grad_log
        )
        weight_terms = tuple((jnp.where(is_valid, term_value, 0.0) for term_value in weight_terms))
        gain_total = gain_total + jnp.where(is_valid, gain_terms, 0.0)
        totals = tuple((running + term for running, term in zip(totals, weight_terms)))
    totals = (
        lax.psum_scatter(totals[0].astype(jnp.bfloat16), "dp", scatter_dimension=0, tiled=True).astype(jnp.float32),
        lax.psum_scatter(totals[1].astype(jnp.bfloat16), "dp", scatter_dimension=1, tiled=True).astype(jnp.float32),
        lax.psum_scatter(totals[2].astype(jnp.bfloat16), "dp", scatter_dimension=0, tiled=True).astype(jnp.float32),
        lax.psum_scatter(totals[3].astype(jnp.bfloat16), "dp", scatter_dimension=1, tiled=True).astype(jnp.float32),
    )
    gain_share = lax.psum_scatter(gain_total, ("dp", "tensor"), scatter_dimension=1, tiled=True)
    return (
        results[None, None],
        grad_log[None, None],
        totals[0][None],
        totals[1][None],
        totals[2][None],
        totals[3][None],
        gain_share[None],
    )


def solution(mesh):
    return jax.shard_map(
        on_device,
        mesh=mesh,
        in_specs=(
            P("dp", None, "tensor", None),
            P("dp", None, None),
            P("dp", None, "tensor", None),
            P("section", "dp", None, "tensor"),
            P("section", "tensor", "dp"),
            P("section", "dp", None, "tensor"),
            P("section", "tensor", "dp"),
            P("section", None, ("dp", "tensor")),
        ),
        out_specs=(
            P("section", "dp", None, "tensor", None),
            P("section", "dp", None, "tensor", None),
            P("section", "dp", None, "tensor"),
            P("section", "tensor", "dp"),
            P("section", "dp", None, "tensor"),
            P("section", "tensor", "dp"),
            P("section", None, ("dp", "tensor")),
        ),
        check_vma=False,
    )
```

```python
import functools
import math

import jax
import jax.numpy as jnp
from jax import lax
from jax.experimental import pallas as pl
from jax.experimental.pallas import tpu as pltpu
from jax.sharding import PartitionSpec as P

DH = 64
BLOCK = 64
EPS = 1e-6
BF = jnp.bfloat16
F32 = jnp.float32
MESH = pl.DeviceIdType.MESH
NN = (((1,), (0,)), ((), ()))
NT = (((1,), (1,)), ((), ()))
TN = (((0,), (0,)), ((), ()))


def mm(a, b, dims=NN):
    return lax.dot_general(a, b, dims, preferred_element_type=F32)


def ceil_to(value, unit):
    return (value + unit - 1) // unit * unit


class Sizes:
    def __init__(self, mesh, model, micro, rows, cols, hidden):
        self.nd, self.nt = mesh.shape["dp"], mesh.shape["tensor"]
        self.D, self.M, self.R, self.C, self.F = model, micro, rows, cols, hidden
        self.FP = ceil_to(hidden, 128)
        self.Dr = model // self.nd
        self.MH, self.Hn = micro // 2, self.nt // 2
        self.MB = rows * self.nt
        self.T = self.MH * self.MB
        self.NH = cols // DH
        self.NB = self.MB // BLOCK
        self.NBH = self.MH * self.NB
        self.oO, self.oG = 3 * cols, 4 * cols
        self.oU, self.oD = self.oG + self.FP, self.oG + 2 * self.FP
        self.N = self.oG + 3 * self.FP
        self.pieces = (
            (0, 3 * cols),
            (self.oO, cols),
            (self.oG, self.FP),
            (self.oU, self.FP),
            (self.oD, self.FP),
        )


def body(
    z_,
    wsh,
    xin,
    cot,
    marks,
    gain_in,
    out_y,
    out_g,
    out_w,
    out_gain,
    W,
    LW,
    L2,
    XF,
    GF,
    N1,
    N2,
    QKV,
    O,
    GATE,
    UP,
    HID,
    H,
    Y,
    GA,
    GGU,
    GQKV,
    GH,
    GX,
    PT,
    RL1,
    RL2,
    RSB,
    AP,
    UU,
    DU,
    ST,
    SIN,
    SEND_STATE,
    MSK,
    CAR,
    TAIL,
    KEEP,
    GL1,
    GL2,
    GV,
    GOWN,
    DG,
    DL0,
    DL1,
    DL2,
    in_sem,
    x_ss,
    x_rs,
    x_fs,
    w1_ss,
    w1_rs,
    w2_ss,
    w2_rs,
    ag_ss,
    ag_fs,
    ag_rs,
    r1_ss,
    r1_rs,
    r2_ss,
    r2_rs,
    st_ss,
    st_rs,
    o_ss,
    o_rs,
    d1_ss,
    d1_rs,
    d2_ss,
    d2_rs,
    g_ss,
    g_rs,
):
    D, R, C, FP, Dr, MH, Hn, MB, T, NH, NB, NBH = (
        z_.D,
        z_.R,
        z_.C,
        z_.FP,
        z_.Dr,
        z_.MH,
        z_.Hn,
        z_.MB,
        z_.T,
        z_.NH,
        z_.NB,
        z_.NBH,
    )
    nd, nt = z_.nd, z_.nt
    pieces = z_.pieces
    s, d, z = lax.axis_index("section"), lax.axis_index("dp"), lax.axis_index("tensor")
    zh, zl = z // Hn, z % Hn
    own = s * Hn + zl
    core_dev = (1 - s, d, z)

    def remote(src, dst, ssem, rsem, dev):
        return pltpu.make_async_remote_copy(
            src_ref=src, dst_ref=dst, send_sem=ssem, recv_sem=rsem, device_id=dev, device_id_type=MESH
        )

    def got(dst, sem):
        pltpu.make_async_copy(dst, dst, sem).wait()

    def dp_dev(step):
        return (s, (d + step) % nd, z)

    def z_dev(step):
        return (s, d, (z + step) % nt)

    def peer_zl(step):
        return (zl + step) % Hn

    barrier = pltpu.get_barrier_semaphore()
    for step in range(1, nt):
        pl.semaphore_signal(barrier, inc=1, device_id=z_dev(step), device_id_type=MESH)
    for step in range(1, nd):
        pl.semaphore_signal(barrier, inc=1, device_id=dp_dev(step), device_id_type=MESH)
    pl.semaphore_signal(barrier, inc=1, device_id=core_dev, device_id_type=MESH)
    far_dev = (1 - s, d, (z + Hn) % nt)
    pl.semaphore_signal(barrier, inc=1, device_id=far_dev, device_id_type=MESH)
    pl.semaphore_wait(barrier, nt - 1 + nd - 1 + 2)

    def spread_tokens(src, dst):
        for m in range(MH):
            mine = dst.at[pl.ds(m * MB + z * R, R)]
            pltpu.make_async_copy(src.at[zh * MH + m], mine, in_sem.at[s, m]).start()
            for step in range(1, nt):
                other = (z + step) % nt
                remote(
                    src.at[(other // Hn) * MH + m],
                    mine,
                    x_ss.at[m, step - 1],
                    x_rs.at[s, m, step - 1],
                    z_dev(step),
                ).start()

    def forward_tokens(dst, array):
        for m in range(MH):
            got(dst.at[pl.ds(m * MB + z * R, R)], in_sem.at[array, m])
            for step in range(1, nt):
                rows = dst.at[pl.ds(m * MB + (z + nt - step) % nt * R, R)]
                got(rows, x_rs.at[array, m, step - 1])
                remote(
                    rows, rows, x_fs.at[m, step - 1], x_rs.at[array, m, step - 1], core_dev
                ).start()

    def await_tokens(src, dst, array):
        for m in range(MH):
            got(dst.at[pl.ds(m * MB + z * R, R)], in_sem.at[array, m])
            for step in range(1, nt):
                rows = dst.at[pl.ds(m * MB + (z + nt - step) % nt * R, R)]
                got(rows, x_rs.at[array, m, step - 1])

    def own_tokens(src, dst, array):
        for m in range(MH):
            mine = dst.at[pl.ds(m * MB + z * R, R)]
            pltpu.make_async_copy(src.at[zh * MH + m], mine, in_sem.at[array, m]).start()

    def w_rows(l, block, p):
        col, width = pieces[p]
        return W.at[l, pl.ds(block * Dr, Dr), pl.ds(col, width)]

    def shard_cols(p):
        col, width = pieces[p]
        return wsh.at[:, pl.ds(col, width)]

    def w_hand_out(l, p):
        for half in range(2):
            dest_z = half * Hn + zl
            to_self = (zh == s) & (half == zh)

            @pl.when(to_self)
            def _():
                pltpu.make_async_copy(shard_cols(p), w_rows(l, d, p), w1_rs.at[l, p]).start()

            @pl.when(jnp.logical_not(to_self))
            def _():
                remote(
                    shard_cols(p),
                    w_rows(l, d, p),
                    w1_ss.at[p, half],
                    w1_rs.at[l, p],
                    (zh, d, dest_z),
                ).start()

    def w_handed_out(l, p):
        for half in range(2):
            to_self = (zh == s) & (half == zh)

            @pl.when(jnp.logical_not(to_self))
            def _():
                remote(
                    shard_cols(p), w_rows(l, d, p), w1_ss.at[p, half], w1_rs.at[l, p], core_dev
                ).wait_send()

    def w_share(l, p):
        got(w_rows(l, d, p), w1_rs.at[l, p])

        def one(step, carry):
            remote(
                w_rows(l, d, p),
                w_rows(l, d, p),
                w2_ss.at[l, p, step - 1],
                w2_rs.at[l, p, step - 1],
                dp_dev(step),
            ).start()
            return carry

        lax.fori_loop(1, nd, one, 0)

    def w_ready(l, p):
        def one(step, carry):
            got(w_rows(l, (d + nd - step) % nd, p), w2_rs.at[l, p, step - 1])
            return carry

        lax.fori_loop(1, nd, one, 0)

    def w_shared(l, p):
        def one(step, carry):
            remote(
                w_rows(l, d, p),
                w_rows(l, d, p),
                w2_ss.at[l, p, step - 1],
                w2_rs.at[l, p, step - 1],
                dp_dev(step),
            ).wait_send()
            return carry

        lax.fori_loop(1, nd, one, 0)

    def d_send(l, p):
        col, width = pieces[p]

        def one(step, carry):
            remote(
                w_rows(l, (d + step) % nd, p),
                LW.at[l, step - 1, :, pl.ds(col, width)],
                d1_ss.at[l, p, step - 1],
                d1_rs.at[l, p, step - 1],
                dp_dev(step),
            ).start()
            return carry

        lax.fori_loop(1, nd, one, 0)

    def d_sum(l, p):
        col, width = pieces[p]

        def one(step, carry):
            got(LW.at[l, step - 1, :, pl.ds(col, width)], d1_rs.at[l, p, step - 1])
            return carry

        lax.fori_loop(1, nd, one, 0)
        rows = pl.ds(d * Dr, Dr)
        total = W[l, rows, pl.ds(col, width)].astype(F32)
        for step in range(1, nd):
            total = total + LW[l, step - 1, :, pl.ds(col, width)].astype(F32)
        W[l, rows, pl.ds(col, width)] = total.astype(BF)
        dest = L2.at[zh, :, pl.ds(col, width)]
        to_self = (s == l) & (zh == s)

        @pl.when(to_self)
        def _():
            pltpu.make_async_copy(w_rows(l, d, p), dest, d2_rs.at[p, zh]).start()

        @pl.when(jnp.logical_not(to_self))
        def _():
            remote(
                w_rows(l, d, p), dest, d2_ss.at[l, p], d2_rs.at[p, zh], (l, d, s * Hn + zl)
            ).start()

    def d_sent(l, p):
        col, width = pieces[p]

        def one(step, carry):
            remote(
                w_rows(l, (d + step) % nd, p),
                LW.at[l, step - 1, :, pl.ds(col, width)],
                d1_ss.at[l, p, step - 1],
                d1_rs.at[l, p, step - 1],
                dp_dev(step),
            ).wait_send()
            return carry

        lax.fori_loop(1, nd, one, 0)
        to_self = (s == l) & (zh == s)

        @pl.when(jnp.logical_not(to_self))
        def _():
            remote(
                w_rows(l, d, p),
                L2.at[zh, :, pl.ds(col, width)],
                d2_ss.at[l, p],
                d2_rs.at[p, zh],
                core_dev,
            ).wait_send()

    def d_final(p):
        col, width = pieces[p]
        for half in range(2):
            got(L2.at[half, :, pl.ds(col, width)], d2_rs.at[p, half])
        cols = pl.ds(col, width)
        out_w[:, cols] = L2[0, :, cols].astype(F32) + L2[1, :, cols].astype(F32)

    def chunk_rows(m, c):
        return pl.ds(m * MB + c * R, R)

    def ag_send(k, buf, m):
        rows = buf.at[chunk_rows(m, own)]
        for step in range(1, Hn):
            remote(
                rows,
                rows,
                ag_ss.at[k, m, step],
                ag_rs.at[k, m, own],
                (s, d, zh * Hn + peer_zl(step)),
            ).start()
        remote(rows, rows, ag_ss.at[k, m, 0], ag_rs.at[k, m, own], core_dev).start()

    def ag_forward(k, buf, m):
        for step in range(1, Hn):
            c = s * Hn + peer_zl(step)
            rows = buf.at[chunk_rows(m, c)]
            got(rows, ag_rs.at[k, m, c])
            remote(rows, rows, ag_fs.at[k, m, step - 1], ag_rs.at[k, m, c], core_dev).start()

    def ag_wait(k, buf, m):
        for step in range(Hn):
            c = (1 - s) * Hn + step
            got(buf.at[chunk_rows(m, c)], ag_rs.at[k, m, c])

    def ag_sent(k, buf, m):
        rows = buf.at[chunk_rows(m, own)]
        for step in range(Hn):
            remote(rows, rows, ag_ss.at[k, m, step], ag_rs.at[k, m, own], core_dev).wait_send()
        for step in range(1, Hn):
            rows = buf.at[chunk_rows(m, s * Hn + peer_zl(step))]
            remote(rows, rows, ag_fs.at[k, m, step - 1], ag_rs.at[k, m, own], core_dev).wait_send()

    def rs_copy1(k, m):
        par = k % 2
        return remote(
            PT.at[par, pl.ds(m * MB + (1 - s) * Hn * R, Hn * R)],
            RL1.at[par, m],
            r1_ss.at[k, m],
            r1_rs.at[k, m],
            core_dev,
        )

    def rs_copy2(k, m, step):
        par = k % 2
        return remote(
            RSB.at[par, m, step - 1],
            RL2.at[par, m, step - 1],
            r2_ss.at[k, m, step - 1],
            r2_rs.at[k, m, step - 1],
            (s, d, zh * Hn + peer_zl(step)),
        )

    def rs_first(k, m, value):
        PT[k % 2, pl.ds(m * MB, MB), :] = value.astype(BF)
        rs_copy1(k, m).start()

    def rs_second(k, m):
        par = k % 2
        copy = rs_copy1(k, m)
        copy.wait_send()
        copy.wait_recv()
        for step in range(1, Hn):
            there = peer_zl(step)
            part = PT[par, chunk_rows(m, s * Hn + there), :].astype(F32) + RL1[
                par, m, pl.ds(there * R, R), :
            ].astype(F32)
            RSB[par, m, step - 1] = part.astype(BF)
            rs_copy2(k, m, step).start()

    def rs_third(k, m):
        par = k % 2
        total = PT[par, chunk_rows(m, own), :].astype(F32) + RL1[
            par, m, pl.ds(zl * R, R), :
        ].astype(F32)
        for step in range(1, Hn):
            copy = rs_copy2(k, m, step)
            copy.wait_send()
            copy.wait_recv()
            total = total + RL2[par, m, step - 1].astype(F32)
        return total

    def own_rows(m):
        return pl.ds(m * R, R)

    def rms(rows):
        return lax.rsqrt(jnp.mean(rows * rows, axis=-1, keepdims=True) + EPS)

    def gain(l, which):
        return GV[l, which : which + 1, :]

    def rms_back(l, which, rows, grad):
        inverse = rms(rows)
        scaled = grad * gain(l, which)
        back = inverse * scaled - rows * (inverse * inverse * inverse) * jnp.mean(
            scaled * rows, axis=-1, keepdims=True
        )
        DG[l, which : which + 1, :] += jnp.sum(grad * rows * inverse, axis=0, keepdims=True)
        return back

    def send_out(buf, l, out, which, m):
        src = buf.at[l, own_rows(m)]
        dst = out.at[zh * MH + m]
        to_self = (s == l) & (zh == s)

        @pl.when(to_self)
        def _():
            pltpu.make_async_copy(src, dst, o_rs.at[which, zh, m]).start()

        @pl.when(jnp.logical_not(to_self))
        def _():
            remote(
                src, dst, o_ss.at[which, l, m], o_rs.at[which, zh, m], (l, d, s * Hn + zl)
            ).start()

    def sent_out(buf, l, out, which, m):
        to_self = (s == l) & (zh == s)

        @pl.when(jnp.logical_not(to_self))
        def _():
            remote(
                buf.at[l, own_rows(m)],
                out.at[zh * MH + m],
                o_ss.at[which, l, m],
                o_rs.at[which, zh, m],
                core_dev,
            ).wait_send()

    lane_head = lax.broadcasted_iota(jnp.int32, (1, C), 1) // DH
    head_bf = [(lane_head == h).astype(F32).astype(BF) for h in range(NH)]
    head_f = [(lane_head == h).astype(F32) for h in range(NH)]

    def stack(rows):
        return jnp.concatenate([rows * head_bf[h] for h in range(NH)], axis=0)

    def unstack(wide):
        out = wide[0:DH] * head_f[0]
        for h in range(1, NH):
            out = out + wide[h * DH : (h + 1) * DH] * head_f[h]
        return out

    def tall(mask):
        return jnp.concatenate([mask] * NH, axis=0)

    def head_mean(values):
        row = lax.broadcasted_iota(jnp.int32, (C, C), 0) // DH
        col = lax.broadcasted_iota(jnp.int32, (C, C), 1) // DH
        same = jnp.where(row == col, 1.0 / DH, 0.0).astype(BF)
        high = values.astype(BF)
        low = (values - high.astype(F32)).astype(BF)
        return mm(high, same) + mm(low, same)

    def block_rows(b):
        return pl.ds(pl.multiple_of(b * BLOCK, BLOCK), BLOCK)

    def qkv_block(l, b):
        rows = block_rows(b)
        return (QKV[l, rows, 0:C], QKV[l, rows, C : 2 * C], QKV[l, rows, 2 * C : 3 * C])

    def softplus(values):
        return jnp.maximum(values, 0.0) + jnp.log(1.0 + jnp.exp(-jnp.abs(values)))

    def features(values):
        return softplus(values.astype(F32)).astype(BF)

    def diag_forward(b):
        q, k, v = qkv_block(0, b)
        scores = mm(stack(q), k, NT) * (1.0 / math.sqrt(DH))
        scores = jnp.where(tall(MSK[b]) > 0.5, scores, -1e9)
        top = jnp.max(scores, axis=-1, keepdims=True)
        weights = jnp.exp(scores - top)
        weights = (weights / jnp.sum(weights, axis=-1, keepdims=True)).astype(BF)
        AP[0, b] = weights
        O[0, block_rows(b), :] = unstack(mm(weights, v)).astype(BF)

    def diag_backward(b, grad_o):
        q, k, v = qkv_block(0, b)
        low = stack(grad_o.astype(BF))
        weights = AP[0, b]
        wide = weights.astype(F32)
        grad_v = mm(weights, low, TN)
        grad_w = mm(low, v, NT)
        grad_s = wide * (grad_w - jnp.sum(grad_w * wide, axis=-1, keepdims=True))
        grad_s = (grad_s * (1.0 / math.sqrt(DH))).astype(BF)
        grad_q = unstack(mm(grad_s, k))
        grad_k = mm(grad_s, stack(q), TN)
        rows = block_rows(b)
        GQKV[rows, 0:C] = grad_q.astype(BF)
        GQKV[rows, C : 2 * C] = grad_k.astype(BF)
        GQKV[rows, 2 * C : 3 * C] = grad_v.astype(BF)

    def fold(square):
        out = square[0:DH] * head_f[0]
        for h in range(1, NH):
            out = out + square[h * DH : (h + 1) * DH] * head_f[h]
        return out

    def unfold(flat):
        return stack(flat.astype(BF))

    def wide_lanes(column):
        return jnp.concatenate([column] * (C // 128), axis=1)

    def norm_state(b, state):
        q, k, v = qkv_block(1, b)
        ST[b] = state
        key = features(k)
        term = mm(key, (v.astype(F32) * wide_lanes(TAIL[b])).astype(BF), TN)
        return wide_lanes(KEEP[b, 0:1, :]) * state + fold(term)

    def norm_forward(b, passed):
        q, k, v = qkv_block(1, b)
        query, key = features(q), features(k)
        local = jnp.where(tall(MSK[b]) > 0.5, mm(stack(query), key, NT), 0.0).astype(BF)
        AP[1, b] = local
        state = ST[b] + passed * SIN[0]
        ST[b] = state
        mixed = unstack(mm(local, v)) + wide_lanes(CAR[b]) * mm(query, unfold(state))
        rows = block_rows(b)
        UU[rows, :] = mixed
        O[1, rows, :] = (mixed * lax.rsqrt(head_mean(mixed * mixed) + EPS)).astype(BF)
        return passed * wide_lanes(KEEP[b, 0:1, :])

    def norm_back_first(b, grad_o, state):
        rows = block_rows(b)
        mixed = UU[rows, :]
        scale = lax.rsqrt(head_mean(mixed * mixed) + EPS)
        grad = scale * grad_o - mixed * (scale * scale * scale) * head_mean(grad_o * mixed)
        low = grad.astype(BF)
        DU[rows, :] = low
        ST2_store(b, state)
        query = features(QKV[1, rows, 0:C])
        term = mm(query, (low.astype(F32) * wide_lanes(CAR[b])).astype(BF), TN)
        return wide_lanes(KEEP[b, 0:1, :]) * state + fold(term)

    def ST2_store(b, state):
        ST[NBH + b] = state

    def norm_back_second(b, passed):
        rows = block_rows(b)
        q, k, v = qkv_block(1, b)
        query, key = features(q), features(k)
        low = DU[rows, :]
        stacked = stack(low)
        grad_state = ST[NBH + b] + passed * SIN[1]
        grad_wide = unfold(grad_state)
        grad_a = jnp.where(tall(MSK[b]) > 0.5, mm(stacked, v, NT), 0.0).astype(BF)
        tail, carry = wide_lanes(TAIL[b]), wide_lanes(CAR[b])
        grad_q = unstack(mm(grad_a, key)) + carry * mm(low, unfold(ST[b]), NT)
        grad_k = mm(grad_a, stack(query), TN) + tail * mm(v, grad_wide, NT)
        grad_v = mm(AP[1, b], stacked, TN) + tail * mm(key, grad_wide)
        sig_q = 1.0 / (1.0 + jnp.exp(-q.astype(F32)))
        sig_k = 1.0 / (1.0 + jnp.exp(-k.astype(F32)))
        GQKV[rows, 0:C] = (grad_q * sig_q).astype(BF)
        GQKV[rows, C : 2 * C] = (grad_k * sig_k).astype(BF)
        GQKV[rows, 2 * C : 3 * C] = grad_v.astype(BF)
        return passed * wide_lanes(KEEP[b, 0:1, :])

    def masks():
        row = lax.broadcasted_iota(jnp.int32, (BLOCK, BLOCK), 0)
        col = lax.broadcasted_iota(jnp.int32, (BLOCK, BLOCK), 1)
        upper = (row <= col).astype(F32).astype(BF)
        start = marks[...].astype(BF)
        count_row = mm(start, upper)
        count_col = mm(upper, start, (((0,), (1,)), ((), ())))
        lane = lax.broadcasted_iota(jnp.int32, count_col.shape, 1)
        for b in range(NBH):
            c_row = count_row[b : b + 1, :]
            c_col = jnp.sum(jnp.where(lane == b, count_col, 0.0), axis=1, keepdims=True)
            last = jnp.sum(
                jnp.where(col[0:1] == BLOCK - 1, c_row, 0.0), axis=1, keepdims=True
            )
            MSK[b] = jnp.where((c_row == c_col) & (row >= col), 1.0, 0.0)
            CAR[b] = jnp.broadcast_to(jnp.where(c_col == 0.0, 1.0, 0.0), (BLOCK, 128))
            TAIL[b] = jnp.broadcast_to(jnp.where(c_col == last, 1.0, 0.0), (BLOCK, 128))
            KEEP[b] = jnp.broadcast_to(jnp.where(last == 0.0, 1.0, 0.0), (8, 128))

    def gains():
        GOWN[...] = gain_in[...]

        def copy(stage, src, dst, step, dev):
            return remote(src, dst, g_ss.at[stage, step - 1], g_rs.at[stage, step - 1], dev)

        for step in range(1, nd):
            copy(0, GOWN, GL1.at[step - 1], step, dp_dev(step)).start()
        total = GOWN[...]
        for step in range(1, nd):
            copy(0, GOWN, GL1.at[step - 1], step, dp_dev(step)).wait()
            total = total + GL1[step - 1]
        GOWN[...] = total
        for step in range(1, nt):
            copy(1, GOWN, GL2.at[step - 1], step, z_dev(step)).start()
        for step in range(1, nt):
            copy(1, GOWN, GL2.at[step - 1], step, z_dev(step)).wait()
            total = total + GL2[step - 1]
        GV[s] = total
        last = remote(GV.at[s], GV.at[s], g_ss.at[2, 0], g_rs.at[2, 0], core_dev)
        last.start()
        last.wait_send()
        got(GV.at[1 - s], g_rs.at[2, 0])

    def gain_grads():
        first = remote(DG.at[1 - s], DL0, g_ss.at[3, 0], g_rs.at[3, 0], core_dev)
        first.start()
        first.wait()
        total = DG[s] + DL0[...]
        DG[s] = total
        for step in range(1, nt):
            remote(
                DG.at[s], DL1.at[step - 1], g_ss.at[4, step - 1], g_rs.at[4, step - 1], z_dev(step)
            ).start()
        for step in range(1, nt):
            remote(
                DG.at[s], DL1.at[step - 1], g_ss.at[4, step - 1], g_rs.at[4, step - 1], z_dev(step)
            ).wait()
            total = total + DL1[step - 1]
        GOWN[...] = total
        for step in range(1, nd):
            remote(
                GOWN, DL2.at[step - 1], g_ss.at[5, step - 1], g_rs.at[5, step - 1], dp_dev(step)
            ).start()
        for step in range(1, nd):
            remote(
                GOWN, DL2.at[step - 1], g_ss.at[5, step - 1], g_rs.at[5, step - 1], dp_dev(step)
            ).wait()
            total = total + DL2[step - 1]
        out_gain[...] = total

    def loop(count, fn):
        def step(i, carry):
            fn(i)
            return carry

        lax.fori_loop(0, count, step, 0)

    def chunk(m):
        return pl.ds(pl.multiple_of(m * MB, BLOCK), MB)

    def w_cols(l, p):
        col, width = pieces[p]
        return W[l, :, col : col + width]

    def pass_state(slot, value, sender):
        near = sender
        SEND_STATE[slot] = value

        def copy():
            return remote(
                SEND_STATE.at[slot],
                SIN.at[slot],
                st_ss.at[slot],
                st_rs.at[slot],
                (s, d, (z + Hn) % nt),
            )

        @pl.when(zh == near)
        def _():
            SIN[slot] = jnp.zeros((DH, C), F32)
            copy().start()
            copy().wait_send()

        @pl.when(zh != near)
        def _():
            copy().wait_recv()

    @pl.when(s == 0)
    def _():
        spread_tokens(xin, XF)

    @pl.when(s == 1)
    def _():
        own_tokens(xin, XF, 0)

    for p in range(5):

        @pl.when(s == 0)
        def _():
            w_hand_out(0, p)

    masks()
    gains()
    for l in range(2):
        DG[l] = jnp.zeros((2, D), F32)

    @pl.when(s == 0)
    def _():
        forward_tokens(XF, 0)
        own_tokens(cot, GF.at[1], 1)

    @pl.when(s == 1)
    def _():
        await_tokens(xin, XF, 0)
        spread_tokens(cot, GF.at[1])

    for p in range(5):
        w_share(0, p)
    for p in range(5):

        @pl.when(s == 1)
        def _():
            w_hand_out(1, p)

    def input_rows(l, m):
        if l == 0:
            return XF[chunk_rows(m, own), :].astype(F32)
        return Y[0, own_rows(m), :].astype(F32)

    def forward(l, ag1, rs1, ag2, rs2, ag3):
        w_ready(l, 0)

        def qkv_chunk(m):
            if l == 0:
                rows = XF[chunk(m), :].astype(F32)
                N1[0, chunk(m), :] = (rows * rms(rows) * gain(0, 0)).astype(BF)
            else:
                ag_forward(ag1, N1.at[1], m)
                ag_wait(ag1, N1.at[1], m)
            QKV[l, chunk(m), :] = mm(N1[l, chunk(m), :], w_cols(l, 0)).astype(BF)

        def out_chunk(m):
            rs_first(rs1, m, mm(O[l, chunk(m), :], w_cols(l, 1), NT))

        if l == 0:

            def attend(m):
                qkv_chunk(m)
                for i in range(NB):
                    diag_forward(m * NB + i)

            loop(MH, attend)
            w_ready(l, 1)
            loop(MH, out_chunk)
        else:

            def states(m, state):
                qkv_chunk(m)
                for i in range(NB):
                    state = norm_state(m * NB + i, state)
                return state

            last = lax.fori_loop(0, MH, states, jnp.zeros((DH, C), F32))
            pass_state(0, last, 0)
            w_ready(l, 1)

            def attend(m, passed):
                for i in range(NB):
                    passed = norm_forward(m * NB + i, passed)
                out_chunk(m)
                return passed

            lax.fori_loop(0, MH, attend, jnp.ones((1, C), F32))

        def second(m):
            rs_second(rs1, m)

        loop(MH, second)

        def hidden_rows(m):
            rows = input_rows(l, m) + rs_third(rs1, m)
            H[l, own_rows(m), :] = rows
            N2[l, chunk_rows(m, own), :] = (rows * rms(rows) * gain(l, 1)).astype(BF)
            ag_send(ag2, N2.at[l], m)

        loop(MH, hidden_rows)
        w_ready(l, 2)
        w_ready(l, 3)
        w_ready(l, 4)

        def feed(m):
            ag_forward(ag2, N2.at[l], m)
            ag_wait(ag2, N2.at[l], m)
            rows = N2[l, chunk(m), :]
            gate = mm(rows, w_cols(l, 2))
            up = mm(rows, w_cols(l, 3))
            GATE[l, chunk(m), :] = gate.astype(BF)
            UP[l, chunk(m), :] = up.astype(BF)
            hidden = (gate * up).astype(BF)
            HID[l, chunk(m), :] = hidden
            rs_first(rs2, m, mm(hidden, w_cols(l, 4), NT))

        loop(MH, feed)

        def feed_second(m):
            rs_second(rs2, m)

        loop(MH, feed_second)

        def result(m):
            rows = (H[l, own_rows(m), :] + rs_third(rs2, m)).astype(BF)
            Y[l, own_rows(m), :] = rows
            send_out(Y, l, out_y, 0, m)
            if l == 0:
                wide = rows.astype(F32)
                N1[1, chunk_rows(m, own), :] = (wide * rms(wide) * gain(1, 0)).astype(BF)
                ag_send(ag3, N1.at[1], m)

        loop(MH, result)

    forward(0, None, 0, 0, 1, 1)
    for p in range(5):
        w_share(1, p)

    @pl.when(s == 1)
    def _():
        forward_tokens(GF.at[1], 1)

    @pl.when(s == 0)
    def _():
        await_tokens(cot, GF.at[1], 1)

    forward(1, 1, 2, 2, 3, None)

    RB = min(D, 256)

    def grad_weight(l, p, left, right):
        col, width = pieces[p]
        for r in range(D // RB):
            W[l, r * RB : (r + 1) * RB, col : col + width] = mm(
                left[:, r * RB : (r + 1) * RB], right, TN
            ).astype(BF)
        d_send(l, p)

    def backward(l, ag_in, rs1, ag2, rs2, ag_out):
        for p in range(5):
            w_shared(l, p)

        def feed_back(m):
            if l == 0:
                ag_forward(ag_in, GF.at[0], m)
                ag_wait(ag_in, GF.at[0], m)
            grad = mm(GF[l, chunk(m), :], w_cols(l, 4))
            GGU[chunk(m), 0:FP] = (grad * UP[l, chunk(m), :].astype(F32)).astype(BF)
            GGU[chunk(m), FP : 2 * FP] = (grad * GATE[l, chunk(m), :].astype(F32)).astype(BF)
            rs_first(
                rs1,
                m,
                mm(GGU[chunk(m), :], W[l, :, z_.oG : z_.oG + 2 * FP], NT),
            )

        loop(MH, feed_back)

        def second(m):
            rs_second(rs1, m)

        loop(MH, second)
        grad_weight(l, 4, GF[l], HID[l])

        def middle(m):
            rows = H[l, own_rows(m), :]
            grad = GF[l, chunk_rows(m, own), :].astype(F32) + rms_back(
                l, 1, rows, rs_third(rs1, m)
            )
            GH[own_rows(m), :] = grad
            GA[l, chunk_rows(m, own), :] = grad.astype(BF)
            ag_send(ag2, GA.at[l], m)

        loop(MH, middle)
        grad_weight(l, 2, N2[l], GGU[:, 0:FP])
        grad_weight(l, 3, N2[l], GGU[:, FP : 2 * FP])

        def grad_o(m):
            ag_forward(ag2, GA.at[l], m)
            ag_wait(ag2, GA.at[l], m)
            return mm(GA[l, chunk(m), :], w_cols(l, 1))

        def qkv_back(m):
            rs_first(rs2, m, mm(GQKV[chunk(m), :], w_cols(l, 0), NT))

        if l == 0:

            def attend(m):
                grad = grad_o(m)
                for i in range(NB):
                    diag_backward(m * NB + i, grad[i * BLOCK : (i + 1) * BLOCK])
                qkv_back(m)

            loop(MH, attend)
        else:

            def states(i, state):
                m = MH - 1 - i
                grad = grad_o(m)
                for j in reversed(range(NB)):
                    state = norm_back_first(m * NB + j, grad[j * BLOCK : (j + 1) * BLOCK], state)
                return state

            last = lax.fori_loop(0, MH, states, jnp.zeros((DH, C), F32))
            pass_state(1, last, 1)

            def attend(i, passed):
                m = MH - 1 - i
                for j in reversed(range(NB)):
                    passed = norm_back_second(m * NB + j, passed)
                qkv_back(m)
                return passed

            lax.fori_loop(0, MH, attend, jnp.ones((1, C), F32))

        def third(m):
            rs_second(rs2, m)

        loop(MH, third)
        grad_weight(l, 1, GA[l], O[l])
        grad_weight(l, 0, N1[l], GQKV[...])

        def result(m):
            grad = GH[own_rows(m), :] + rms_back(l, 0, input_rows(l, m), rs_third(rs2, m))
            low = grad.astype(BF)
            GX[l, own_rows(m), :] = low
            send_out(GX, l, out_g, 1, m)
            if l == 1:
                GF[0, chunk_rows(m, own), :] = low
                ag_send(ag_out, GF.at[0], m)

        loop(MH, result)

    backward(1, None, 4, 3, 5, 4)
    for p in (4, 2, 3, 1, 0):
        d_sum(1, p)
    backward(0, 4, 6, 5, 7, None)
    for p in (4, 2, 3, 1, 0):
        d_sum(0, p)
    gain_grads()

    for p in (4, 2, 3, 1, 0):
        d_final(p)
    for l in range(2):
        for p in range(5):
            d_sent(l, p)

            @pl.when(s == l)
            def _():
                w_handed_out(l, p)

    ags = ((0, N2.at[0]), (1, N1.at[1]), (2, N2.at[1]), (3, GA.at[1]), (4, GF.at[0]), (5, GA.at[0]))

    def finish(m):
        for k, buf in ags:
            ag_sent(k, buf, m)
        for l in range(2):
            sent_out(Y, l, out_y, 0, m)
            sent_out(GX, l, out_g, 1, m)
        for half in range(2):
            got(out_y.at[half * MH + m], o_rs.at[0, half, m])
            got(out_g.at[half * MH + m], o_rs.at[1, half, m])

    loop(MH, finish)
    for array, src, dst in ((0, xin, XF), (1, cot, GF.at[1])):

        @pl.when(s == array)
        def _():
            for m in range(MH):
                mine = dst.at[pl.ds(m * MB + z * R, R)]
                for step in range(1, nt):
                    copy = remote(
                        src.at[m], mine, x_ss.at[m, step - 1], x_rs.at[array, m, step - 1], core_dev
                    )
                    copy.wait_send()
                    remote(
                        mine, mine, x_fs.at[m, step - 1], x_rs.at[array, m, step - 1], core_dev
                    ).wait_send()


def solution(mesh):
    nd, nt = mesh.shape["dp"], mesh.shape["tensor"]

    def on_device(inputs, starts, cotangent, qkv_m, out_m, gateup_m, down_m, gain_m):
        z_ = Sizes(
            mesh,
            inputs.shape[3],
            inputs.shape[1],
            inputs.shape[2],
            qkv_m.shape[3],
            gateup_m.shape[3],
        )
        D, R, C, F, FP, Dr, M, MH, Hn, MB, T, NBH, N, NH = (
            z_.D,
            z_.R,
            z_.C,
            z_.F,
            z_.FP,
            z_.Dr,
            z_.M,
            z_.MH,
            z_.Hn,
            z_.MB,
            z_.T,
            z_.NBH,
            z_.N,
            z_.NH,
        )
        pad = ((0, 0), (0, FP - F))
        shard = jnp.concatenate(
            [
                qkv_m[0].reshape(Dr, 3 * C).astype(BF),
                out_m[0].T.astype(BF),
                jnp.pad(gateup_m[0, :, 0].astype(BF), pad),
                jnp.pad(gateup_m[0, :, 1].astype(BF), pad),
                jnp.pad(down_m[0].T.astype(BF), pad),
            ],
            axis=1,
        )
        half = lax.axis_index("tensor") // Hn
        marks = (
            lax.dynamic_slice_in_dim(starts[0], half * MH, MH, 0)
            .reshape(NBH, BLOCK)
            .astype(F32)
        )
        width = gain_m.shape[2]
        place = lax.axis_index("dp") * nt + lax.axis_index("tensor")
        low = gain_m[0].astype(BF).astype(F32)
        gain_in = jnp.where(
            jnp.arange(D)[None] // width == place, jnp.tile(low, (1, D // width)), 0.0
        )
        anywhere = pl.BlockSpec(memory_space=pl.ANY)
        vmem = pl.BlockSpec(memory_space=pltpu.VMEM)
        DMA = pltpu.SemaphoreType.DMA
        V = pltpu.VMEM
        scratch = [
            V((2, D, N), BF),
            V((2, nd - 1, Dr, N), BF),
            V((2, Dr, N), BF),
            V((T, D), BF),
            V((2, T, D), BF),
            V((2, T, D), BF),
            V((2, T, D), BF),
            V((2, T, 3 * C), BF),
            V((2, T, C), BF),
            V((2, T, FP), BF),
            V((2, T, FP), BF),
            V((2, T, FP), BF),
            V((2, MH * R, D), F32),
            V((2, MH * R, D), BF),
            V((2, T, D), BF),
            V((T, 2 * FP), BF),
            V((T, 3 * C), BF),
            V((MH * R, D), F32),
            V((2, MH * R, D), BF),
            V((2, T, D), BF),
            V((2, MH, Hn * R, D), BF),
            V((2, MH, Hn - 1, R, D), BF),
            V((2, MH, Hn - 1, R, D), BF),
            V((2, NBH, NH * BLOCK, BLOCK), BF),
            V((T, C), F32),
            V((T, C), BF),
            V((2 * NBH, DH, C), F32),
            V((2, DH, C), F32),
            V((2, DH, C), F32),
            V((NBH, BLOCK, BLOCK), F32),
            V((NBH, BLOCK, 128), F32),
            V((NBH, BLOCK, 128), F32),
            V((NBH, 8, 128), F32),
            V((nd - 1, 2, D), F32),
            V((nt - 1, 2, D), F32),
            V((2, 2, D), F32),
            V((2, D), F32),
            V((2, 2, D), F32),
            V((2, D), F32),
            V((nt - 1, 2, D), F32),
            V((nd - 1, 2, D), F32),
            DMA((2, MH)),
            DMA((MH, nt - 1)),
            DMA((2, MH, nt - 1)),
            DMA((MH, nt - 1)),
            DMA((5, 2)),
            DMA((2, 5)),
            DMA((2, 5, nd - 1)),
            DMA((2, 5, nd - 1)),
            DMA((6, MH, Hn)),
            DMA((6, MH, Hn - 1)),
            DMA((6, MH, nt)),
            DMA((8, MH)),
            DMA((8, MH)),
            DMA((8, MH, Hn - 1)),
            DMA((8, MH, Hn - 1)),
            DMA((2,)),
            DMA((2,)),
            DMA((2, 2, MH)),
            DMA((2, 2, MH)),
            DMA((2, 5, nd - 1)),
            DMA((2, 5, nd - 1)),
            DMA((2, 5)),
            DMA((5, 2)),
            DMA((6, max(nd, nt) - 1)),
            DMA((6, max(nd, nt) - 1)),
        ]
        out_y, out_g, out_w, out_gain = pl.pallas_call(
            functools.partial(body, z_),
            out_shape=(
                jax.ShapeDtypeStruct((M, R, D), BF),
                jax.ShapeDtypeStruct((M, R, D), BF),
                jax.ShapeDtypeStruct((Dr, N), F32),
                jax.ShapeDtypeStruct((2, D), F32),
            ),
            in_specs=[anywhere, anywhere, anywhere, vmem, vmem],
            out_specs=(anywhere, anywhere, vmem, vmem),
            scratch_shapes=scratch,
            compiler_params=pltpu.CompilerParams(
                collective_id=0, has_side_effects=True, vmem_limit_bytes=63 * 1024 * 1024
            ),
        )(shard, inputs[0], cotangent[0], marks, gain_in)
        gateup = jnp.stack(
            [out_w[:, z_.oG : z_.oG + F], out_w[:, z_.oU : z_.oU + F]], axis=1
        )
        gain_share = lax.dynamic_slice_in_dim(out_gain, place * width, width, 1)
        return (
            out_y[None, None],
            out_g[None, None],
            out_w[:, : 3 * C].reshape(1, Dr, 3, C),
            out_w[:, z_.oO : z_.oO + C].T[None],
            gateup[None],
            out_w[:, z_.oD : z_.oD + F].T[None],
            gain_share[None],
        )

    return jax.shard_map(
        on_device,
        mesh=mesh,
        in_specs=(
            P("dp", None, "tensor", None),
            P("dp", None, None),
            P("dp", None, "tensor", None),
            P("section", "dp", None, "tensor"),
            P("section", "tensor", "dp"),
            P("section", "dp", None, "tensor"),
            P("section", "tensor", "dp"),
            P("section", None, ("dp", "tensor")),
        ),
        out_specs=(
            P("section", "dp", None, "tensor", None),
            P("section", "dp", None, "tensor", None),
            P("section", "dp", None, "tensor"),
            P("section", "tensor", "dp"),
            P("section", "dp", None, "tensor"),
            P("section", "tensor", "dp"),
            P("section", None, ("dp", "tensor")),
        ),
        check_vma=False,
    )
```

```python
import functools
import math

import jax
import jax.numpy as jnp
from jax import lax
from jax.experimental import pallas as pl
from jax.experimental.pallas import tpu as pltpu
from jax.sharding import PartitionSpec as P

DH = 64
BLOCK = 64
EPS = 1e-6
BF = jnp.bfloat16
F32 = jnp.float32
MESH = pl.DeviceIdType.MESH
NN = (((1,), (0,)), ((), ()))
NT = (((1,), (1,)), ((), ()))
TN = (((0,), (0,)), ((), ()))


def mm(a, b, dims=NN):
    return lax.dot_general(a, b, dims, preferred_element_type=F32)


def ceil_to(value, unit):
    return (value + unit - 1) // unit * unit


def scoped(fn):
    @functools.wraps(fn)
    def inner(*args):
        with jax.named_scope(fn.__name__):
            return fn(*args)

    return inner


class Sizes:
    def __init__(self, mesh, model, micro, rows, cols, hidden):
        self.nd, self.nt = mesh.shape["dp"], mesh.shape["tensor"]
        self.D, self.M, self.R, self.C, self.F = model, micro, rows, cols, hidden
        self.FP = ceil_to(hidden, 128)
        self.Dr = model // self.nd
        self.MH, self.Hn = micro // 2, self.nt // 2
        self.MB = rows * self.nt
        self.T = self.MH * self.MB
        self.NH = cols // DH
        self.NB = self.MB // BLOCK
        self.NBH = self.MH * self.NB
        self.oO, self.oG = 3 * cols, 4 * cols
        self.oU, self.oD = self.oG + self.FP, self.oG + 2 * self.FP
        self.N = self.oG + 3 * self.FP
        self.pieces = (
            (0, 3 * cols),
            (self.oO, cols),
            (self.oG, self.FP),
            (self.oU, self.FP),
            (self.oD, self.FP),
            (0, 4 * cols),
        )


def body(
    z_,
    wsh,
    xin,
    cot,
    marks,
    gain_in,
    out_y,
    out_g,
    out_w,
    out_gain,
    W,
    LW,
    L2,
    XF,
    GF,
    N1,
    N2,
    QKV,
    O,
    GATE,
    UP,
    HID,
    H,
    Y,
    GA,
    GGU,
    GQKV,
    GH,
    GX,
    PT,
    RL1,
    RL2,
    RSB,
    AP,
    UU,
    DU,
    ST,
    SIN,
    SEND_STATE,
    MSK,
    CAR,
    TAIL,
    KEEP,
    GL,
    GV,
    GOWN,
    DG,
    DL0,
    DL1,
    DL2,
    in_sem,
    x_ss,
    x_rs,
    x_fs,
    w1_ss,
    w1_rs,
    w2_ss,
    w2_rs,
    ag_ss,
    ag_fs,
    ag_rs,
    r1_ss,
    r1_rs,
    r2_ss,
    r2_rs,
    st_ss,
    st_rs,
    o_ss,
    o_rs,
    d1_ss,
    d1_rs,
    d2_ss,
    d2_rs,
    g_ss,
    g_rs,
    gl_ss,
    gl_rs,
):
    D, R, C, FP, Dr, MH, Hn, MB, T, NH, NB, NBH = (
        z_.D,
        z_.R,
        z_.C,
        z_.FP,
        z_.Dr,
        z_.MH,
        z_.Hn,
        z_.MB,
        z_.T,
        z_.NH,
        z_.NB,
        z_.NBH,
    )
    nd, nt = z_.nd, z_.nt
    pieces = z_.pieces
    s, d, z = lax.axis_index("section"), lax.axis_index("dp"), lax.axis_index("tensor")
    zh, zl = z // Hn, z % Hn
    own = s * Hn + zl
    core_dev = (1 - s, d, z)

    def remote(src, dst, ssem, rsem, dev):
        return pltpu.make_async_remote_copy(
            src_ref=src, dst_ref=dst, send_sem=ssem, recv_sem=rsem, device_id=dev, device_id_type=MESH
        )

    def got(dst, sem):
        pltpu.make_async_copy(dst, dst, sem).wait()

    def dp_dev(step):
        return (s, (d + step) % nd, z)

    def z_dev(step):
        return (s, d, (z + step) % nt)

    def peer_zl(step):
        return (zl + step) % Hn

    barrier = pltpu.get_barrier_semaphore()

    def section_dev(i):
        return (s, (d + i // nt) % nd, (z + i % nt) % nt)

    def greet(i, carry):
        pl.semaphore_signal(barrier, inc=1, device_id=section_dev(i), device_id_type=MESH)
        return carry

    lax.fori_loop(1, nd * nt, greet, 0)
    pl.semaphore_signal(barrier, inc=1, device_id=core_dev, device_id_type=MESH)
    far_dev = (1 - s, d, (z + Hn) % nt)
    pl.semaphore_signal(barrier, inc=1, device_id=far_dev, device_id_type=MESH)
    pl.semaphore_wait(barrier, nd * nt + 1)

    def own_tokens(src, dst, array):
        for m in range(MH):
            mine = dst.at[pl.ds(m * MB + z * R, R)]
            pltpu.make_async_copy(src.at[zh * MH + m], mine, in_sem.at[array, m]).start()

    def spread_tokens(src, dst, array):
        for m in range(MH):
            mine = dst.at[pl.ds(m * MB + z * R, R)]
            for step in range(1, nt):
                other = (z + step) % nt
                remote(
                    src.at[(other // Hn) * MH + m],
                    mine,
                    x_ss.at[m, step - 1],
                    x_rs.at[array, m, step - 1],
                    z_dev(step),
                ).start()

    def await_tokens(dst, array, m):
        got(dst.at[pl.ds(m * MB + z * R, R)], in_sem.at[array, m])
        for step in range(1, nt):
            rows = dst.at[pl.ds(m * MB + (z + nt - step) % nt * R, R)]
            got(rows, x_rs.at[array, m, step - 1])

            @pl.when(s == array)
            def _():
                remote(
                    rows, rows, x_fs.at[m, step - 1], x_rs.at[array, m, step - 1], core_dev
                ).start()

    def w_rows(l, block, p):
        col, width = pieces[p]
        return W.at[l, pl.ds(block * Dr, Dr), pl.ds(col, width)]

    def shard_cols(p):
        col, width = pieces[p]
        return wsh.at[:, pl.ds(col, width)]

    def w_hand_near(l, p):
        @pl.when(zh == s)
        def _():
            pltpu.make_async_copy(shard_cols(p), w_rows(l, d, p), w1_rs.at[l, p]).start()

        @pl.when(zh != s)
        def _():
            w_hand(l, p, 0, core_dev).start()

    def w_hand(l, p, which, dev):
        return remote(
            shard_cols(p), w_rows(l, d, p), w1_ss.at[p, which], w1_rs.at[l, p], dev
        )

    def w_hand_far(l, p):
        w_hand(l, p, 1, (zh, d, (z + Hn) % nt)).start()

    def w_handed_out(l, p):
        @pl.when(zh != s)
        def _():
            w_hand(l, p, 0, core_dev).wait_send()

        w_hand(l, p, 1, core_dev).wait_send()

    square = nd == 4
    half_rows = Dr // 2
    dp_x, dp_y = d + 1 - 2 * (d % 2), (d + 2) % nd

    def w_half(l, block, half, p):
        col, width = pieces[p]
        return W.at[l, pl.ds(block * Dr + half * half_rows, half_rows), pl.ds(col, width)]

    def w_copy(l, p, k):
        if not square:
            rows, dev = w_rows(l, d, p), dp_dev(k + 1)
        elif k < 2:
            rows, dev = w_rows(l, d, p), (s, (dp_x, dp_y)[k], z)
        elif k == 2:
            rows, dev = w_half(l, dp_x, 0, p), (s, dp_y, z)
        else:
            rows, dev = w_half(l, dp_y, 1, p), (s, dp_x, z)
        return remote(rows, rows, w2_ss.at[l, p, k], w2_rs.at[l, p, k], dev)

    def w_share(l, p):
        got(w_rows(l, d, p), w1_rs.at[l, p])
        for k in range(2 if square else nd - 1):
            w_copy(l, p, k).start()

    def w_forward(l, p):
        if square:
            got(w_rows(l, dp_x, p), w2_rs.at[l, p, 0])
            w_copy(l, p, 2).start()
            got(w_rows(l, dp_y, p), w2_rs.at[l, p, 1])
            w_copy(l, p, 3).start()

    def w_ready(l, p):
        if square:
            got(w_half(l, 3 - d, 0, p), w2_rs.at[l, p, 2])
            got(w_half(l, 3 - d, 1, p), w2_rs.at[l, p, 3])
        else:
            for step in range(1, nd):
                got(w_rows(l, (d + nd - step) % nd, p), w2_rs.at[l, p, step - 1])

    def w_shared(l, p):
        for k in range(4 if square else nd - 1):
            w_copy(l, p, k).wait_send()

    def pump(ops):
        for what, l, p in ops:
            with jax.named_scope(what + str(l) + str(p)):
                {"s": w_share, "f": w_forward}[what](l, p)

    near = s == zh
    gathered = (5, 2, 3, 4)

    def pump_near(ops):
        pl.when(near)(lambda: pump(ops))

    def pump_far(ops):
        pl.when(jnp.logical_not(near))(lambda: pump(ops))

    def d_copy(l, p, k):
        col, width = pieces[p]
        cols = pl.ds(col, width)
        if not square:
            src, dst, dev = w_rows(l, (d + k + 1) % nd, p), LW.at[l, k, :, cols], dp_dev(k + 1)
        else:
            first, second = pl.ds(0, half_rows), pl.ds(half_rows, half_rows)
            block, half, slot, rows, to = (
                (3 - d, 0, 2, first, dp_x),
                (3 - d, 1, 2, second, dp_y),
                (dp_x, 0, 0, first, dp_x),
                (dp_y, 1, 1, second, dp_y),
                (dp_y, 0, 1, first, dp_y),
                (dp_x, 1, 0, second, dp_x),
            )[k]
            src, dst, dev = w_half(l, block, half, p), LW.at[l, slot, rows, cols], (s, to, z)
        return remote(src, dst, d1_ss.at[l, p, k], d1_rs.at[l, p, k], dev)

    def d_send(l, p):
        for k in range(4 if square else nd - 1):
            d_copy(l, p, k).start()

    @scoped
    def d_mid(l, p):
        if square:
            col, width = pieces[p]
            cols = pl.ds(col, width)
            for k, block, half in ((0, dp_y, 0), (1, dp_x, 1)):
                copy = d_copy(l, p, k)
                copy.wait_recv()
                rows = pl.ds(block * Dr + half * half_rows, half_rows)
                arrived = LW[l, 2, half * half_rows : (half + 1) * half_rows, cols]
                W[l, rows, cols] = (W[l, rows, cols].astype(F32) + arrived.astype(F32)).astype(BF)
                d_copy(l, p, 4 + k).start()

    def d_hop(l, p):
        col, width = pieces[p]
        return remote(
            w_rows(l, d, p),
            L2.at[zh, :, pl.ds(col, width)],
            d2_ss.at[l, p],
            d2_rs.at[p, zh],
            (l, d, s * Hn + zl),
        )

    @scoped
    def d_sum(l, p):
        col, width = pieces[p]
        for k in (2, 3, 4, 5) if square else range(nd - 1):
            d_copy(l, p, k).wait_recv()
        rows = pl.ds(d * Dr, Dr)
        cols = pl.ds(col, width)
        total = W[l, rows, cols].astype(F32)
        for slot in range(2 if square else nd - 1):
            total = total + LW[l, slot, :, cols].astype(F32)
        W[l, rows, cols] = total.astype(BF)
        to_self = (s == l) & (zh == s)

        @pl.when(to_self)
        def _():
            pltpu.make_async_copy(
                w_rows(l, d, p), L2.at[zh, :, cols], d2_rs.at[p, zh]
            ).start()

        @pl.when(jnp.logical_not(to_self))
        def _():
            d_hop(l, p).start()

    def d_sent(l, p):
        for k in range(6 if square else nd - 1):
            d_copy(l, p, k).wait_send()
        to_self = (s == l) & (zh == s)

        @pl.when(jnp.logical_not(to_self))
        def _():
            d_hop(l, p).wait_send()

    @scoped
    def d_final(p):
        col, width = pieces[p]
        for half in range(2):
            got(L2.at[half, :, pl.ds(col, width)], d2_rs.at[p, half])
        cols = pl.ds(col, width)
        out_w[:, cols] = L2[0, :, cols].astype(F32) + L2[1, :, cols].astype(F32)

    def chunk_rows(m, c):
        return pl.ds(m * MB + c * R, R)

    def ag_send(k, buf, m):
        rows = buf.at[chunk_rows(m, own)]
        for step in range(1, Hn):
            remote(
                rows,
                rows,
                ag_ss.at[k, m, step],
                ag_rs.at[k, m, own],
                (s, d, zh * Hn + peer_zl(step)),
            ).start()
        remote(rows, rows, ag_ss.at[k, m, 0], ag_rs.at[k, m, own], core_dev).start()

    def ag_forward(k, buf, m):
        for step in range(1, Hn):
            c = s * Hn + peer_zl(step)
            rows = buf.at[chunk_rows(m, c)]
            got(rows, ag_rs.at[k, m, c])
            remote(rows, rows, ag_fs.at[k, m, step - 1], ag_rs.at[k, m, c], core_dev).start()

    def ag_wait(k, buf, m):
        for step in range(Hn):
            c = (1 - s) * Hn + step
            got(buf.at[chunk_rows(m, c)], ag_rs.at[k, m, c])

    def ag_sent(k, buf, m):
        rows = buf.at[chunk_rows(m, own)]
        for step in range(Hn):
            remote(rows, rows, ag_ss.at[k, m, step], ag_rs.at[k, m, own], core_dev).wait_send()
        for step in range(1, Hn):
            rows = buf.at[chunk_rows(m, s * Hn + peer_zl(step))]
            remote(rows, rows, ag_fs.at[k, m, step - 1], ag_rs.at[k, m, own], core_dev).wait_send()

    def rs_copy1(k, m):
        par = k % 2
        return remote(
            PT.at[par, pl.ds(m * MB + (1 - s) * Hn * R, Hn * R)],
            RL1.at[par, m],
            r1_ss.at[k, m],
            r1_rs.at[k, m],
            core_dev,
        )

    def rs_copy2(k, m, step):
        par = k % 2
        return remote(
            RSB.at[par, m, step - 1],
            RL2.at[par, m, step - 1],
            r2_ss.at[k, m, step - 1],
            r2_rs.at[k, m, step - 1],
            (s, d, zh * Hn + peer_zl(step)),
        )

    def rs_first(k, m, value):
        PT[k % 2, pl.ds(m * MB, MB), :] = value.astype(BF)
        rs_copy1(k, m).start()

    def rs_second(k, m):
        par = k % 2
        copy = rs_copy1(k, m)
        copy.wait_send()
        copy.wait_recv()
        for step in range(1, Hn):
            there = peer_zl(step)
            part = PT[par, chunk_rows(m, s * Hn + there), :].astype(F32) + RL1[
                par, m, pl.ds(there * R, R), :
            ].astype(F32)
            RSB[par, m, step - 1] = part.astype(BF)
            rs_copy2(k, m, step).start()

    def after(k, i, m):
        @pl.when(i > 0)
        def _():
            rs_second(k, m)

    def rs_third(k, m):
        par = k % 2
        total = PT[par, chunk_rows(m, own), :].astype(F32) + RL1[
            par, m, pl.ds(zl * R, R), :
        ].astype(F32)
        for step in range(1, Hn):
            copy = rs_copy2(k, m, step)
            copy.wait_send()
            copy.wait_recv()
            total = total + RL2[par, m, step - 1].astype(F32)
        return total

    def own_rows(m):
        return pl.ds(m * R, R)

    def rms(rows):
        return lax.rsqrt(jnp.mean(rows * rows, axis=-1, keepdims=True) + EPS)

    def gain(l, which):
        return GV[l, which : which + 1, :]

    def rms_back(l, which, rows, grad):
        inverse = rms(rows)
        scaled = grad * gain(l, which)
        back = inverse * scaled - rows * (inverse * inverse * inverse) * jnp.mean(
            scaled * rows, axis=-1, keepdims=True
        )
        DG[l, which : which + 1, :] += jnp.sum(grad * rows * inverse, axis=0, keepdims=True)
        return back

    def send_out(buf, l, out, which, m):
        src = buf.at[l, own_rows(m)]
        dst = out.at[zh * MH + m]
        to_self = (s == l) & (zh == s)

        @pl.when(to_self)
        def _():
            pltpu.make_async_copy(src, dst, o_rs.at[which, zh, m]).start()

        @pl.when(jnp.logical_not(to_self))
        def _():
            remote(
                src, dst, o_ss.at[which, l, m], o_rs.at[which, zh, m], (l, d, s * Hn + zl)
            ).start()

    def sent_out(buf, l, out, which, m):
        to_self = (s == l) & (zh == s)

        @pl.when(jnp.logical_not(to_self))
        def _():
            remote(
                buf.at[l, own_rows(m)],
                out.at[zh * MH + m],
                o_ss.at[which, l, m],
                o_rs.at[which, zh, m],
                core_dev,
            ).wait_send()

    lane_head = lax.broadcasted_iota(jnp.int32, (1, C), 1) // DH
    head_bf = [(lane_head == h).astype(F32).astype(BF) for h in range(NH)]
    head_f = [(lane_head == h).astype(F32) for h in range(NH)]

    def stack(rows):
        return jnp.concatenate([rows * head_bf[h] for h in range(NH)], axis=0)

    def unstack(wide):
        out = wide[0:DH] * head_f[0]
        for h in range(1, NH):
            out = out + wide[h * DH : (h + 1) * DH] * head_f[h]
        return out

    def tall(mask):
        return jnp.concatenate([mask] * NH, axis=0)

    def head_mean(values):
        row = lax.broadcasted_iota(jnp.int32, (C, C), 0) // DH
        col = lax.broadcasted_iota(jnp.int32, (C, C), 1) // DH
        same = jnp.where(row == col, 1.0 / DH, 0.0).astype(BF)
        high = values.astype(BF)
        low = (values - high.astype(F32)).astype(BF)
        return mm(high, same) + mm(low, same)

    def block_rows(b):
        return pl.ds(pl.multiple_of(b * BLOCK, BLOCK), BLOCK)

    def qkv_block(l, b):
        rows = block_rows(b)
        return (QKV[l, rows, 0:C], QKV[l, rows, C : 2 * C], QKV[l, rows, 2 * C : 3 * C])

    def softplus(values):
        return jnp.maximum(values, 0.0) + jnp.log(1.0 + jnp.exp(-jnp.abs(values)))

    def features(values):
        return softplus(values.astype(F32)).astype(BF)

    def diag_forward(b):
        q, k, v = qkv_block(0, b)
        scores = mm(stack(q), k, NT) * (1.0 / math.sqrt(DH))
        scores = jnp.where(tall(MSK[b]) > 0.5, scores, -1e9)
        top = jnp.max(scores, axis=-1, keepdims=True)
        weights = jnp.exp(scores - top)
        weights = (weights / jnp.sum(weights, axis=-1, keepdims=True)).astype(BF)
        AP[0, b] = weights
        O[0, block_rows(b), :] = unstack(mm(weights, v)).astype(BF)

    def diag_backward(b, grad_o):
        q, k, v = qkv_block(0, b)
        low = stack(grad_o.astype(BF))
        weights = AP[0, b]
        wide = weights.astype(F32)
        grad_v = mm(weights, low, TN)
        grad_w = mm(low, v, NT)
        grad_s = wide * (grad_w - jnp.sum(grad_w * wide, axis=-1, keepdims=True))
        grad_s = (grad_s * (1.0 / math.sqrt(DH))).astype(BF)
        grad_q = unstack(mm(grad_s, k))
        grad_k = mm(grad_s, stack(q), TN)
        rows = block_rows(b)
        GQKV[rows, 0:C] = grad_q.astype(BF)
        GQKV[rows, C : 2 * C] = grad_k.astype(BF)
        GQKV[rows, 2 * C : 3 * C] = grad_v.astype(BF)

    def fold(square):
        out = square[0:DH] * head_f[0]
        for h in range(1, NH):
            out = out + square[h * DH : (h + 1) * DH] * head_f[h]
        return out

    def unfold(flat):
        return stack(flat.astype(BF))

    def wide_lanes(column):
        return jnp.concatenate([column] * (C // 128), axis=1)

    def norm_state(b, state):
        q, k, v = qkv_block(1, b)
        ST[b] = state
        key = features(k)
        term = mm(key, (v.astype(F32) * wide_lanes(TAIL[b])).astype(BF), TN)
        return wide_lanes(KEEP[b, 0:1, :]) * state + fold(term)

    def norm_forward(b, passed):
        q, k, v = qkv_block(1, b)
        query, key = features(q), features(k)
        local = jnp.where(tall(MSK[b]) > 0.5, mm(stack(query), key, NT), 0.0).astype(BF)
        AP[1, b] = local
        state = ST[b] + passed * SIN[0].astype(F32)
        ST[b] = state
        mixed = unstack(mm(local, v)) + wide_lanes(CAR[b]) * mm(query, unfold(state))
        rows = block_rows(b)
        UU[rows, :] = mixed
        O[1, rows, :] = (mixed * lax.rsqrt(head_mean(mixed * mixed) + EPS)).astype(BF)
        return passed * wide_lanes(KEEP[b, 0:1, :])

    def norm_back_first(b, grad_o, state):
        rows = block_rows(b)
        mixed = UU[rows, :]
        scale = lax.rsqrt(head_mean(mixed * mixed) + EPS)
        grad = scale * grad_o - mixed * (scale * scale * scale) * head_mean(grad_o * mixed)
        low = grad.astype(BF)
        DU[rows, :] = low
        ST2_store(b, state)
        query = features(QKV[1, rows, 0:C])
        term = mm(query, (low.astype(F32) * wide_lanes(CAR[b])).astype(BF), TN)
        return wide_lanes(KEEP[b, 0:1, :]) * state + fold(term)

    def ST2_store(b, state):
        ST[NBH + b] = state

    def norm_back_second(b, passed):
        rows = block_rows(b)
        q, k, v = qkv_block(1, b)
        query, key = features(q), features(k)
        low = DU[rows, :]
        stacked = stack(low)
        grad_state = ST[NBH + b] + passed * SIN[1].astype(F32)
        grad_wide = unfold(grad_state)
        grad_a = jnp.where(tall(MSK[b]) > 0.5, mm(stacked, v, NT), 0.0).astype(BF)
        tail, carry = wide_lanes(TAIL[b]), wide_lanes(CAR[b])
        grad_q = unstack(mm(grad_a, key)) + carry * mm(low, unfold(ST[b]), NT)
        grad_k = mm(grad_a, stack(query), TN) + tail * mm(v, grad_wide, NT)
        grad_v = mm(AP[1, b], stacked, TN) + tail * mm(key, grad_wide)
        sig_q = 1.0 / (1.0 + jnp.exp(-q.astype(F32)))
        sig_k = 1.0 / (1.0 + jnp.exp(-k.astype(F32)))
        GQKV[rows, 0:C] = (grad_q * sig_q).astype(BF)
        GQKV[rows, C : 2 * C] = (grad_k * sig_k).astype(BF)
        GQKV[rows, 2 * C : 3 * C] = grad_v.astype(BF)
        return passed * wide_lanes(KEEP[b, 0:1, :])

    @scoped
    def masks():
        row = lax.broadcasted_iota(jnp.int32, (BLOCK, BLOCK), 0)
        col = lax.broadcasted_iota(jnp.int32, (BLOCK, BLOCK), 1)
        upper = (row <= col).astype(F32).astype(BF)
        start = marks[...].astype(BF)
        count_row = mm(start, upper)
        count_col = mm(upper, start, (((0,), (1,)), ((), ())))
        lane = lax.broadcasted_iota(jnp.int32, count_col.shape, 1)
        for b in range(NBH):
            c_row = count_row[b : b + 1, :]
            c_col = jnp.sum(jnp.where(lane == b, count_col, 0.0), axis=1, keepdims=True)
            last = jnp.sum(
                jnp.where(col[0:1] == BLOCK - 1, c_row, 0.0), axis=1, keepdims=True
            )
            MSK[b] = jnp.where((c_row == c_col) & (row >= col), 1.0, 0.0)
            CAR[b] = jnp.broadcast_to(jnp.where(c_col == 0.0, 1.0, 0.0), (BLOCK, 128))
            TAIL[b] = jnp.broadcast_to(jnp.where(c_col == last, 1.0, 0.0), (BLOCK, 128))
            KEEP[b] = jnp.broadcast_to(jnp.where(last == 0.0, 1.0, 0.0), (8, 128))

    place = d * nt + z

    def gain_copy(i):
        return remote(GL.at[place], GL.at[place], gl_ss.at[i], gl_rs.at[i], section_dev(i))

    def gains_out():
        GL[place] = gain_in[...]

        def one(i, carry):
            gain_copy(i).start()
            return carry

        lax.fori_loop(1, nd * nt, one, 0)

    @scoped
    def gains_in():
        def one(i, carry):
            gain_copy(i).wait_send()
            source = (d + nd - i // nt) % nd * nt + (z + nt - i % nt) % nt
            got(GL.at[source], gl_rs.at[i])
            return carry

        lax.fori_loop(1, nd * nt, one, 0)
        each = nd * nt * 128 // D
        for t in range(D // 128):
            total = GL[t * each]
            for i in range(1, each):
                total = total + GL[t * each + i]
            GV[s, :, t * 128 : (t + 1) * 128] = total
        gain_swap().start()

    def gain_swap():
        return remote(GV.at[s], GV.at[s], g_ss.at[2, 0], g_rs.at[2, 0], core_dev)

    def gains_other():
        gain_swap().wait_send()
        got(GV.at[1 - s], g_rs.at[2, 0])

    def dp_gain(step):
        return remote(
            GOWN, DL2.at[step - 1], g_ss.at[5, step - 1], g_rs.at[5, step - 1], dp_dev(step)
        )

    def core_gain():
        return remote(DG.at[1 - s], DL0, g_ss.at[3, 0], g_rs.at[3, 0], core_dev)

    def z_gain(step):
        return remote(
            DG.at[s], DL1.at[step - 1], g_ss.at[4, step - 1], g_rs.at[4, step - 1], z_dev(step)
        )

    @scoped
    def gain_second():
        core_gain().wait()
        DG[s] = DG[s] + DL0[...]
        for step in range(1, nt):
            z_gain(step).start()

    @scoped
    def gain_third():
        total = DG[s]
        for step in range(1, nt):
            z_gain(step).wait()
            total = total + DL1[step - 1]
        GOWN[...] = total
        for step in range(1, nd):
            dp_gain(step).start()

    @scoped
    def gain_final():
        total = GOWN[...]
        for step in range(1, nd):
            dp_gain(step).wait()
            total = total + DL2[step - 1]
        out_gain[...] = total

    def loop(count, fn):
        def step(i, carry):
            fn(i)
            return carry

        with jax.named_scope(fn.__name__):
            lax.fori_loop(0, count, step, 0)

    def chunk(m):
        return pl.ds(pl.multiple_of(m * MB, BLOCK), MB)

    def w_cols(l, p):
        col, width = pieces[p]
        return W[l, :, col : col + width]

    @scoped
    def state_copy(slot):
        return remote(
            SEND_STATE.at[slot],
            SIN.at[slot],
            st_ss.at[slot],
            st_rs.at[slot],
            (s, d, (z + Hn) % nt),
        )

    @scoped
    def pass_state(slot, value, sender):
        SEND_STATE[slot] = value.astype(BF)

        @pl.when(zh == sender)
        def _():
            SIN[slot] = jnp.zeros((DH, C), BF)
            state_copy(slot).start()

        @pl.when(zh != sender)
        def _():
            state_copy(slot).wait_recv()

    outer = zh == zl
    inner, far = jnp.logical_not(outer), jnp.logical_not(near)

    def only(cond, fn):
        pl.when(cond)(fn)

    def hand_far(l, cond, ps):
        def go():
            for p in ps:
                w_hand_far(l, p)

        pl.when((s == l) & cond)(go)

    gains_out()
    hand_far(0, s == 0, [5])
    for l in range(2):

        @pl.when(s == l)
        def _():
            for p in gathered:
                w_hand_near(l, p)

    own_tokens(xin, XF, 0)
    own_tokens(cot, GF.at[1], 1)

    def x_out():
        spread_tokens(xin, XF, 0)

    def x_and_feed():
        x_out()
        for p in (2, 3, 4):
            w_hand_far(0, p)

    only((s == 0) & inner, x_and_feed)
    masks()
    for l in range(2):
        DG[l] = jnp.zeros((2, D), F32)
    pump_near([("s", 0, 5), ("s", 0, 2)])
    gains_in()
    pump_far([("s", 0, 5)])
    only((s == 0) & outer & far, x_out)
    pump([("f", 0, 5)])
    hand_far(0, outer & far, [2, 3, 4])
    pump_near([("f", 0, 2), ("s", 0, 3)])
    only((s == 0) & outer & near, x_out)
    pump_near([("f", 0, 3), ("s", 0, 4)])
    hand_far(0, outer & near, [2, 3, 4])
    only(s == 1, gains_other)

    def cot_out():
        spread_tokens(cot, GF.at[1], 1)

    stage = {
        (0, "attended"): lambda: (
            pump_near([("f", 0, 4), ("s", 1, 5)]),
            pump_far([("s", 0, 2), ("s", 0, 3), ("f", 0, 2), ("s", 0, 4)]),
        ),
        (0, "hidden"): lambda: (
            hand_far(1, inner, gathered),
            hand_far(1, outer, [5]),
            pump_near([("f", 1, 5)]),
            pump_far([("f", 0, 3), ("f", 0, 4)]),
        ),
        (0, "ready"): lambda: (
            hand_far(1, outer, [2, 3]),
            pump_near([("s", 1, 2)]),
        ),
        (0, "fed"): lambda: (
            hand_far(1, outer, [4]),
            pump_near([("f", 1, 2), ("s", 1, 3)]),
            pump_far([("s", 1, 5)]),
            only(s == 0, gains_other),
        ),
        (0, "result"): lambda: (
            pump_near([("f", 1, 3), ("s", 1, 4)]),
            pump_far([("f", 1, 5), ("s", 1, 2)]),
        ),
        (1, "states"): lambda: (
            only(s == 1, cot_out),
            pump_near([("f", 1, 4)]),
            pump_far([("f", 1, 2), ("s", 1, 3)]),
        ),
        (1, "attended"): lambda: (pump_far([("f", 1, 3), ("s", 1, 4)]),),
        (1, "hidden"): lambda: (pump_far([("f", 1, 4)]),),
        (1, "ready"): lambda: (),
        (1, "fed"): lambda: (),
        (1, "result"): lambda: (),
        "b1 second": lambda: (),
        "b1 middle": lambda: (),
        "b1 feed": lambda: (d_mid(1, 4),),
        "b1 third": lambda: (d_mid(1, 2),),
        "b1 end": lambda: (d_mid(1, 3),),
        "b0 second": lambda: (d_mid(1, 0), d_mid(1, 1), d_sum(1, 4)),
        "b0 middle": lambda: (d_sum(1, 2),),
        "b0 feed": lambda: (d_sum(1, 3), d_mid(0, 4)),
        "b0 third": lambda: (d_sum(1, 0), d_sum(1, 1)),
        "b0 end": lambda: (
            core_gain().start(),
            d_mid(0, 2),
            d_sum(0, 4),
            gain_second(),
            d_mid(0, 3),
            d_sum(0, 2),
            d_mid(0, 0),
            d_sum(0, 3),
            gain_third(),
            d_mid(0, 1),
            d_sum(0, 0),
            d_sum(0, 1),
        ),
    }

    def input_rows(l, m):
        if l == 0:
            return XF[chunk_rows(m, own), :].astype(F32)
        return Y[0, own_rows(m), :].astype(F32)

    def finish_layer(l, rs2, ag3):
        def result(m):
            rows = (H[l, own_rows(m), :] + rs_third(rs2, m)).astype(BF)
            Y[l, own_rows(m), :] = rows
            send_out(Y, l, out_y, 0, m)
            if l == 0:
                wide = rows.astype(F32)
                N1[1, chunk_rows(m, own), :] = (wide * rms(wide) * gain(1, 0)).astype(BF)
                ag_send(ag3, N1.at[1], m)

        loop(MH, result)

    def forward(l, ag1, rs1, ag2, rs2, ag3):
        w_ready(l, 5)

        def qkv_chunk(m):
            if l == 0:
                await_tokens(XF, 0, m)
                rows = XF[chunk(m), :].astype(F32)
                N1[0, chunk(m), :] = (rows * rms(rows) * gain(0, 0)).astype(BF)
            else:
                ag_forward(ag1, N1.at[1], m)
                ag_wait(ag1, N1.at[1], m)
            QKV[l, chunk(m), :] = mm(N1[l, chunk(m), :], w_cols(l, 0)).astype(BF)

        def out_chunk(m):
            rs_first(rs1, m, mm(O[l, chunk(m), :], w_cols(l, 1), NT))

        if l == 0:

            def attend(m):
                qkv_chunk(m)
                for i in range(NB):
                    diag_forward(m * NB + i)
                out_chunk(m)
                after(rs1, m, m - 1)

            loop(MH, attend)
            rs_second(rs1, MH - 1)
            stage[l, "attended"]()
        else:

            def states(m, state):
                qkv_chunk(m)
                for i in range(NB):
                    state = norm_state(m * NB + i, state)
                return state

            with jax.named_scope('states'):
                last = lax.fori_loop(0, MH, states, jnp.zeros((DH, C), F32))
            pass_state(0, last, 0)
            stage[l, "states"]()

            def attend(m, passed):
                for i in range(NB):
                    passed = norm_forward(m * NB + i, passed)
                out_chunk(m)
                after(rs1, m, m - 1)
                return passed

            with jax.named_scope('attend'):
                lax.fori_loop(0, MH, attend, jnp.ones((1, C), F32))
            rs_second(rs1, MH - 1)
            stage[l, "attended"]()

        def hidden_rows(m):
            rows = input_rows(l, m) + rs_third(rs1, m)
            H[l, own_rows(m), :] = rows
            N2[l, chunk_rows(m, own), :] = (rows * rms(rows) * gain(l, 1)).astype(BF)
            ag_send(ag2, N2.at[l], m)

        loop(MH, hidden_rows)
        stage[l, "hidden"]()
        w_ready(l, 2)
        w_ready(l, 3)
        w_ready(l, 4)
        stage[l, "ready"]()

        def feed(m):
            ag_forward(ag2, N2.at[l], m)
            ag_wait(ag2, N2.at[l], m)
            rows = N2[l, chunk(m), :]
            gate = mm(rows, w_cols(l, 2))
            up = mm(rows, w_cols(l, 3))
            GATE[l, chunk(m), :] = gate.astype(BF)
            UP[l, chunk(m), :] = up.astype(BF)
            hidden = (gate * up).astype(BF)
            HID[l, chunk(m), :] = hidden
            rs_first(rs2, m, mm(hidden, w_cols(l, 4), NT))
            after(rs2, m, m - 1)

        loop(MH, feed)
        rs_second(rs2, MH - 1)
        stage[l, "fed"]()

        if l == 0:
            finish_layer(l, rs2, ag3)
            stage[l, "result"]()

    forward(0, None, 0, 0, 1, 1)
    forward(1, 1, 2, 2, 3, None)

    RB = min(D, 256)

    @scoped
    def grad_weight(l, p, left, right):
        col, width = pieces[p]
        for r in range(D // RB):
            W[l, r * RB : (r + 1) * RB, col : col + width] = mm(
                left[:, r * RB : (r + 1) * RB], right, TN
            ).astype(BF)
        d_send(l, p)

    def backward(l, ag_in, rs1, ag2, rs2, ag_out):
        for p in gathered:
            w_shared(l, p)

        def feed_back(i):
            m = MH - 1 - i
            if l == 0:
                ag_forward(ag_in, GF.at[0], m)
                ag_wait(ag_in, GF.at[0], m)
            else:
                await_tokens(GF.at[1], 1, m)
            grad = mm(GF[l, chunk(m), :], w_cols(l, 4))
            GGU[chunk(m), 0:FP] = (grad * UP[l, chunk(m), :].astype(F32)).astype(BF)
            GGU[chunk(m), FP : 2 * FP] = (grad * GATE[l, chunk(m), :].astype(F32)).astype(BF)
            rs_first(
                rs1,
                m,
                mm(GGU[chunk(m), :], W[l, :, z_.oG : z_.oG + 2 * FP], NT),
            )
            after(rs1, i, m + 1)

        loop(MH, feed_back)
        rs_second(rs1, 0)
        grad_weight(l, 4, GF[l], HID[l])
        if l == 1:
            finish_layer(1, 3, None)
        stage[f"b{l} second"]()

        def middle(i):
            m = MH - 1 - i
            rows = H[l, own_rows(m), :]
            grad = GF[l, chunk_rows(m, own), :].astype(F32) + rms_back(
                l, 1, rows, rs_third(rs1, m)
            )
            GH[own_rows(m), :] = grad
            GA[l, chunk_rows(m, own), :] = grad.astype(BF)
            ag_send(ag2, GA.at[l], m)

        loop(MH, middle)
        stage[f"b{l} middle"]()
        grad_weight(l, 2, N2[l], GGU[:, 0:FP])
        grad_weight(l, 3, N2[l], GGU[:, FP : 2 * FP])
        stage[f"b{l} feed"]()

        def grad_o(m):
            ag_forward(ag2, GA.at[l], m)
            ag_wait(ag2, GA.at[l], m)
            return mm(GA[l, chunk(m), :], w_cols(l, 1))

        def qkv_back(i, m):
            rs_first(rs2, m, mm(GQKV[chunk(m), :], w_cols(l, 0), NT))
            after(rs2, i, m + 1)

        if l == 0:

            def attend(i):
                m = MH - 1 - i
                grad = grad_o(m)
                for j in range(NB):
                    diag_backward(m * NB + j, grad[j * BLOCK : (j + 1) * BLOCK])
                qkv_back(i, m)

            loop(MH, attend)
        else:

            def states(i, state):
                m = MH - 1 - i
                grad = grad_o(m)
                for j in reversed(range(NB)):
                    state = norm_back_first(m * NB + j, grad[j * BLOCK : (j + 1) * BLOCK], state)
                return state

            with jax.named_scope("states"):
                last = lax.fori_loop(0, MH, states, jnp.zeros((DH, C), F32))
            pass_state(1, last, 1)

            def attend(i, passed):
                m = MH - 1 - i
                for j in reversed(range(NB)):
                    passed = norm_back_second(m * NB + j, passed)
                qkv_back(i, m)
                return passed

            with jax.named_scope("attend"):
                lax.fori_loop(0, MH, attend, jnp.ones((1, C), F32))

        rs_second(rs2, 0)
        stage[f"b{l} third"]()
        grad_weight(l, 0, N1[l], GQKV[...])
        grad_weight(l, 1, GA[l], O[l])

        def result(i):
            m = MH - 1 - i
            grad = GH[own_rows(m), :] + rms_back(l, 0, input_rows(l, m), rs_third(rs2, m))
            low = grad.astype(BF)
            GX[l, own_rows(m), :] = low
            send_out(GX, l, out_g, 1, m)
            if l == 1:
                GF[0, chunk_rows(m, own), :] = low
                ag_send(ag_out, GF.at[0], m)

        loop(MH, result)
        stage[f"b{l} end"]()

    backward(1, None, 4, 3, 5, 4)
    backward(0, 4, 6, 5, 7, None)

    for p in (4, 2, 3, 0, 1):
        d_final(p)
    gain_final()
    for l in range(2):
        for p in range(5):
            d_sent(l, p)
        for p in gathered:

            @pl.when(s == l)
            def _():
                w_handed_out(l, p)

    ags = ((0, N2.at[0]), (1, N1.at[1]), (2, N2.at[1]), (3, GA.at[1]), (4, GF.at[0]), (5, GA.at[0]))

    for slot in range(2):

        @pl.when(zh == slot)
        def _():
            state_copy(slot).wait_send()

    def finish(m):
        for k, buf in ags:
            ag_sent(k, buf, m)
        for l in range(2):
            sent_out(Y, l, out_y, 0, m)
            sent_out(GX, l, out_g, 1, m)
        for half in range(2):
            got(out_y.at[half * MH + m], o_rs.at[0, half, m])
            got(out_g.at[half * MH + m], o_rs.at[1, half, m])

    loop(MH, finish)
    for array, src, dst in ((0, xin, XF), (1, cot, GF.at[1])):

        @pl.when(s == array)
        def _():
            for m in range(MH):
                mine = dst.at[pl.ds(m * MB + z * R, R)]
                for step in range(1, nt):
                    copy = remote(
                        src.at[m], mine, x_ss.at[m, step - 1], x_rs.at[array, m, step - 1], core_dev
                    )
                    copy.wait_send()
                    remote(
                        mine, mine, x_fs.at[m, step - 1], x_rs.at[array, m, step - 1], core_dev
                    ).wait_send()


def solution(mesh):
    nd, nt = mesh.shape["dp"], mesh.shape["tensor"]

    def on_device(inputs, starts, cotangent, qkv_m, out_m, gateup_m, down_m, gain_m):
        z_ = Sizes(
            mesh,
            inputs.shape[3],
            inputs.shape[1],
            inputs.shape[2],
            qkv_m.shape[3],
            gateup_m.shape[3],
        )
        D, R, C, F, FP, Dr, M, MH, Hn, MB, T, NBH, N, NH = (
            z_.D,
            z_.R,
            z_.C,
            z_.F,
            z_.FP,
            z_.Dr,
            z_.M,
            z_.MH,
            z_.Hn,
            z_.MB,
            z_.T,
            z_.NBH,
            z_.N,
            z_.NH,
        )
        pad = ((0, 0), (0, FP - F))
        shard = jnp.concatenate(
            [
                qkv_m[0].reshape(Dr, 3 * C).astype(BF),
                out_m[0].T.astype(BF),
                jnp.pad(gateup_m[0, :, 0].astype(BF), pad),
                jnp.pad(gateup_m[0, :, 1].astype(BF), pad),
                jnp.pad(down_m[0].T.astype(BF), pad),
            ],
            axis=1,
        )
        half = lax.axis_index("tensor") // Hn
        marks = (
            lax.dynamic_slice_in_dim(starts[0], half * MH, MH, 0)
            .reshape(NBH, BLOCK)
            .astype(F32)
        )
        width = gain_m.shape[2]
        place = lax.axis_index("dp") * nt + lax.axis_index("tensor")
        low = gain_m[0].astype(BF).astype(F32)
        each = 128 // width
        gain_in = jnp.where(
            jnp.arange(128)[None] // width == place % each, jnp.tile(low, (1, each)), 0.0
        )
        anywhere = pl.BlockSpec(memory_space=pl.ANY)
        vmem = pl.BlockSpec(memory_space=pltpu.VMEM)
        DMA = pltpu.SemaphoreType.DMA
        V = pltpu.VMEM
        scratch = [
            V((2, D, N), BF),
            V((2, nd - 1, Dr, N), BF),
            V((2, Dr, N), BF),
            V((T, D), BF),
            V((2, T, D), BF),
            V((2, T, D), BF),
            V((2, T, D), BF),
            V((2, T, 3 * C), BF),
            V((2, T, C), BF),
            V((2, T, FP), BF),
            V((2, T, FP), BF),
            V((2, T, FP), BF),
            V((2, MH * R, D), F32),
            V((2, MH * R, D), BF),
            V((2, T, D), BF),
            V((T, 2 * FP), BF),
            V((T, 3 * C), BF),
            V((MH * R, D), F32),
            V((2, MH * R, D), BF),
            V((2, T, D), BF),
            V((2, MH, Hn * R, D), BF),
            V((2, MH, Hn - 1, R, D), BF),
            V((2, MH, Hn - 1, R, D), BF),
            V((2, NBH, NH * BLOCK, BLOCK), BF),
            V((T, C), F32),
            V((T, C), BF),
            V((2 * NBH, DH, C), F32),
            V((2, DH, C), BF),
            V((2, DH, C), BF),
            V((NBH, BLOCK, BLOCK), F32),
            V((NBH, BLOCK, 128), F32),
            V((NBH, BLOCK, 128), F32),
            V((NBH, 8, 128), F32),
            V((nd * nt, 2, 128), F32),
            V((2, 2, D), F32),
            V((2, D), F32),
            V((2, 2, D), F32),
            V((2, D), F32),
            V((nt - 1, 2, D), F32),
            V((nd - 1, 2, D), F32),
            DMA((2, MH)),
            DMA((MH, nt - 1)),
            DMA((2, MH, nt - 1)),
            DMA((MH, nt - 1)),
            DMA((6, 2)),
            DMA((2, 6)),
            DMA((2, 6, max(4, nd - 1))),
            DMA((2, 6, max(4, nd - 1))),
            DMA((6, MH, Hn)),
            DMA((6, MH, Hn - 1)),
            DMA((6, MH, nt)),
            DMA((8, MH)),
            DMA((8, MH)),
            DMA((8, MH, Hn - 1)),
            DMA((8, MH, Hn - 1)),
            DMA((2,)),
            DMA((2,)),
            DMA((2, 2, MH)),
            DMA((2, 2, MH)),
            DMA((2, 5, max(6, nd - 1))),
            DMA((2, 5, max(6, nd - 1))),
            DMA((2, 5)),
            DMA((5, 2)),
            DMA((6, max(nd, nt) - 1)),
            DMA((6, max(nd, nt) - 1)),
            DMA((nd * nt,)),
            DMA((nd * nt,)),
        ]
        out_y, out_g, out_w, out_gain = pl.pallas_call(
            functools.partial(body, z_),
            out_shape=(
                jax.ShapeDtypeStruct((M, R, D), BF),
                jax.ShapeDtypeStruct((M, R, D), BF),
                jax.ShapeDtypeStruct((Dr, N), F32),
                jax.ShapeDtypeStruct((2, D), F32),
            ),
            in_specs=[anywhere, anywhere, anywhere, vmem, vmem],
            out_specs=(anywhere, anywhere, vmem, vmem),
            scratch_shapes=scratch,
            compiler_params=pltpu.CompilerParams(
                collective_id=0, has_side_effects=True, vmem_limit_bytes=63 * 1024 * 1024
            ),
        )(shard, inputs[0], cotangent[0], marks, gain_in)
        gateup = jnp.stack(
            [out_w[:, z_.oG : z_.oG + F], out_w[:, z_.oU : z_.oU + F]], axis=1
        )
        gain_share = lax.dynamic_slice_in_dim(out_gain, place * width, width, 1)
        return (
            out_y[None, None],
            out_g[None, None],
            out_w[:, : 3 * C].reshape(1, Dr, 3, C),
            out_w[:, z_.oO : z_.oO + C].T[None],
            gateup[None],
            out_w[:, z_.oD : z_.oD + F].T[None],
            gain_share[None],
        )

    return jax.shard_map(
        on_device,
        mesh=mesh,
        in_specs=(
            P("dp", None, "tensor", None),
            P("dp", None, None),
            P("dp", None, "tensor", None),
            P("section", "dp", None, "tensor"),
            P("section", "tensor", "dp"),
            P("section", "dp", None, "tensor"),
            P("section", "tensor", "dp"),
            P("section", None, ("dp", "tensor")),
        ),
        out_specs=(
            P("section", "dp", None, "tensor", None),
            P("section", "dp", None, "tensor", None),
            P("section", "dp", None, "tensor"),
            P("section", "tensor", "dp"),
            P("section", "dp", None, "tensor"),
            P("section", "tensor", "dp"),
            P("section", None, ("dp", "tensor")),
        ),
        check_vma=False,
    )
```

```python
import functools
import math

import jax
import jax.numpy as jnp
from jax import lax
from jax.experimental import pallas as pl
from jax.experimental.pallas import tpu as pltpu
from jax.sharding import PartitionSpec as P

DH = 64
BLOCK = 64
EPS = 1e-6
BF = jnp.bfloat16
F32 = jnp.float32
MESH = pl.DeviceIdType.MESH
NN = (((1,), (0,)), ((), ()))
NT = (((1,), (1,)), ((), ()))
TN = (((0,), (0,)), ((), ()))


def mm(a, b, dims=NN):
    return lax.dot_general(a, b, dims, preferred_element_type=F32)


def ceil_to(value, unit):
    return (value + unit - 1) // unit * unit


def scoped(fn):
    @functools.wraps(fn)
    def inner(*args):
        with jax.named_scope(fn.__name__):
            return fn(*args)

    return inner


class Sizes:
    def __init__(self, mesh, model, micro, rows, cols, hidden):
        self.nd, self.nt = mesh.shape["dp"], mesh.shape["tensor"]
        self.D, self.M, self.R, self.C, self.F = model, micro, rows, cols, hidden
        self.GUw, self.Dw = ceil_to(2 * hidden, 128), ceil_to(hidden, 128)
        self.Dr = model // self.nd
        self.MH, self.Hn = micro // 2, self.nt // 2
        self.MB = rows * self.nt
        self.T = self.MH * self.MB
        self.NH = cols // DH
        self.NB = self.MB // BLOCK
        self.NBH = self.MH * self.NB
        self.oO, self.oG = 3 * cols, 4 * cols
        self.oD = self.oG + self.GUw
        self.N = self.oD + self.Dw
        first = ceil_to(self.GUw // 2, 128)
        self.pieces = (
            (0, 3 * cols),
            (self.oO, cols),
            (self.oG, first),
            (self.oG + first, self.GUw - first),
            (self.oD, self.Dw),
            (0, 4 * cols),
        )


def body(
    z_,
    qkv_in,
    o_in,
    gu_in,
    d_in,
    xin,
    cot,
    starts_in,
    gain_in,
    out_y,
    out_g,
    out_qkv,
    out_o,
    out_gu,
    out_d,
    out_gain,
    MQ,
    MO,
    MGU,
    MD,
    W,
    LW,
    L2,
    XF,
    GF,
    N1,
    N2,
    QKV,
    O,
    GU,
    HID,
    H,
    Y,
    GA,
    GGU,
    GQKV,
    GH,
    GX,
    PT,
    RL1,
    RL2,
    RSB,
    AP,
    UU,
    DU,
    ST,
    SIN,
    SEND_STATE,
    MSK,
    CAR,
    TAIL,
    KEEP,
    GL,
    GV,
    GOWN,
    DG,
    DL0,
    DL1,
    DL2,
    in_sem,
    x_ss,
    x_rs,
    x_fs,
    w1_ss,
    w1_rs,
    w2_ss,
    w2_rs,
    ag_ss,
    ag_fs,
    ag_rs,
    r1_ss,
    r1_rs,
    r2_ss,
    r2_rs,
    st_ss,
    st_rs,
    o_ss,
    o_rs,
    d1_ss,
    d1_rs,
    d2_ss,
    d2_rs,
    g_ss,
    g_rs,
    gl_ss,
    gl_rs,
    m_sem,
):
    D, R, C, F, Dr, MH, Hn, MB, T, NH, NB, NBH = (
        z_.D,
        z_.R,
        z_.C,
        z_.F,
        z_.Dr,
        z_.MH,
        z_.Hn,
        z_.MB,
        z_.T,
        z_.NH,
        z_.NB,
        z_.NBH,
    )
    nd, nt = z_.nd, z_.nt
    pieces = z_.pieces
    s, d, z = lax.axis_index("section"), lax.axis_index("dp"), lax.axis_index("tensor")
    zh, zl = z // Hn, z % Hn
    own = s * Hn + zl
    core_dev = (1 - s, d, z)

    def remote(src, dst, ssem, rsem, dev):
        return pltpu.make_async_remote_copy(
            src_ref=src, dst_ref=dst, send_sem=ssem, recv_sem=rsem, device_id=dev, device_id_type=MESH
        )

    def got(dst, sem):
        pltpu.make_async_copy(dst, dst, sem).wait()

    def dp_dev(step):
        return (s, (d + step) % nd, z)

    def z_dev(step):
        return (s, d, (z + step) % nt)

    def peer_zl(step):
        return (zl + step) % Hn

    masters = (
        pltpu.make_async_copy(qkv_in, MQ, m_sem.at[0]),
        pltpu.make_async_copy(o_in, MO, m_sem.at[1]),
        pltpu.make_async_copy(gu_in, MGU, m_sem.at[2]),
        pltpu.make_async_copy(d_in, MD, m_sem.at[3]),
    )
    for copy in masters:
        copy.start()

    barrier = pltpu.get_barrier_semaphore()

    def section_dev(i):
        return (s, (d + i // nt) % nd, (z + i % nt) % nt)

    def greet(i, carry):
        pl.semaphore_signal(barrier, inc=1, device_id=section_dev(i), device_id_type=MESH)
        return carry

    lax.fori_loop(1, nd * nt, greet, 0)
    pl.semaphore_signal(barrier, inc=1, device_id=core_dev, device_id_type=MESH)
    far_dev = (1 - s, d, (z + Hn) % nt)
    pl.semaphore_signal(barrier, inc=1, device_id=far_dev, device_id_type=MESH)
    pl.semaphore_wait(barrier, nd * nt + 1)

    def own_tokens(src, dst, array):
        for m in range(MH):
            mine = dst.at[pl.ds(m * MB + z * R, R)]
            pltpu.make_async_copy(src.at[zh * MH + m], mine, in_sem.at[array, m]).start()

    def spread_tokens(src, dst, array):
        for m in range(MH):
            mine = dst.at[pl.ds(m * MB + z * R, R)]
            for step in range(1, nt):
                other = (z + step) % nt
                remote(
                    src.at[(other // Hn) * MH + m],
                    mine,
                    x_ss.at[m, step - 1],
                    x_rs.at[array, m, step - 1],
                    z_dev(step),
                ).start()

    def await_tokens(dst, array, m):
        got(dst.at[pl.ds(m * MB + z * R, R)], in_sem.at[array, m])
        for step in range(1, nt):
            rows = dst.at[pl.ds(m * MB + (z + nt - step) % nt * R, R)]
            got(rows, x_rs.at[array, m, step - 1])

            @pl.when(s == array)
            def _():
                remote(
                    rows, rows, x_fs.at[m, step - 1], x_rs.at[array, m, step - 1], core_dev
                ).start()

    def w_rows(l, block, p):
        col, width = pieces[p]
        return W.at[l, pl.ds(block * Dr, Dr), pl.ds(col, width)]

    def shard_cols(p):
        col, width = pieces[p]
        return L2.at[0, :, pl.ds(col, width)]

    def w_hand_near(l, p):
        @pl.when(zh == s)
        def _():
            pltpu.make_async_copy(shard_cols(p), w_rows(l, d, p), w1_rs.at[l, p]).start()

        @pl.when(zh != s)
        def _():
            w_hand(l, p, 0, core_dev).start()

    def w_hand(l, p, which, dev):
        return remote(
            shard_cols(p), w_rows(l, d, p), w1_ss.at[p, which], w1_rs.at[l, p], dev
        )

    def w_hand_far(l, p):
        w_hand(l, p, 1, (zh, d, (z + Hn) % nt)).start()

    def w_handed_out(l, p):
        @pl.when(zh != s)
        def _():
            w_hand(l, p, 0, core_dev).wait_send()

        w_hand(l, p, 1, core_dev).wait_send()

    square = nd == 4
    half_rows = Dr // 2
    dp_x, dp_y = d + 1 - 2 * (d % 2), (d + 2) % nd

    def w_half(l, block, half, p):
        col, width = pieces[p]
        return W.at[l, pl.ds(block * Dr + half * half_rows, half_rows), pl.ds(col, width)]

    def w_copy(l, p, k):
        if not square:
            rows, dev = w_rows(l, d, p), dp_dev(k + 1)
        elif k < 2:
            rows, dev = w_rows(l, d, p), (s, (dp_x, dp_y)[k], z)
        elif k == 2:
            rows, dev = w_half(l, dp_x, 0, p), (s, dp_y, z)
        else:
            rows, dev = w_half(l, dp_y, 1, p), (s, dp_x, z)
        return remote(rows, rows, w2_ss.at[l, p, k], w2_rs.at[l, p, k], dev)

    def w_share(l, p):
        got(w_rows(l, d, p), w1_rs.at[l, p])
        for k in range(2 if square else nd - 1):
            w_copy(l, p, k).start()

    def w_forward(l, p):
        if square:
            got(w_rows(l, dp_x, p), w2_rs.at[l, p, 0])
            w_copy(l, p, 2).start()
            got(w_rows(l, dp_y, p), w2_rs.at[l, p, 1])
            w_copy(l, p, 3).start()

    def w_ready(l, p):
        if square:
            got(w_half(l, 3 - d, 0, p), w2_rs.at[l, p, 2])
            got(w_half(l, 3 - d, 1, p), w2_rs.at[l, p, 3])
        else:
            for step in range(1, nd):
                got(w_rows(l, (d + nd - step) % nd, p), w2_rs.at[l, p, step - 1])

    def w_shared(l, p):
        for k in range(4 if square else nd - 1):
            w_copy(l, p, k).wait_send()

    def pump(ops):
        for what, l, p in ops:
            with jax.named_scope(what + str(l) + str(p)):
                {"s": w_share, "f": w_forward}[what](l, p)

    near = s == zh
    gathered = (5, 2, 3, 4)

    def pump_near(ops):
        pl.when(near)(lambda: pump(ops))

    def pump_far(ops):
        pl.when(jnp.logical_not(near))(lambda: pump(ops))

    def d_copy(l, p, k):
        col, width = pieces[p]
        cols = pl.ds(col, width)
        if not square:
            src, dst, dev = w_rows(l, (d + k + 1) % nd, p), LW.at[l, k, :, cols], dp_dev(k + 1)
        else:
            first, second = pl.ds(0, half_rows), pl.ds(half_rows, half_rows)
            block, half, slot, rows, to = (
                (3 - d, 0, 2, first, dp_x),
                (3 - d, 1, 2, second, dp_y),
                (dp_x, 0, 0, first, dp_x),
                (dp_y, 1, 1, second, dp_y),
                (dp_y, 0, 1, first, dp_y),
                (dp_x, 1, 0, second, dp_x),
            )[k]
            src, dst, dev = w_half(l, block, half, p), LW.at[l, slot, rows, cols], (s, to, z)
        return remote(src, dst, d1_ss.at[l, p, k], d1_rs.at[l, p, k], dev)

    def d_send(l, p):
        for k in range(4 if square else nd - 1):
            d_copy(l, p, k).start()

    @scoped
    def d_mid(l, p):
        if square:
            col, width = pieces[p]
            cols = pl.ds(col, width)
            for k, block, half in ((0, dp_y, 0), (1, dp_x, 1)):
                copy = d_copy(l, p, k)
                copy.wait_recv()
                rows = pl.ds(block * Dr + half * half_rows, half_rows)
                arrived = LW[l, 2, half * half_rows : (half + 1) * half_rows, cols]
                W[l, rows, cols] = (W[l, rows, cols].astype(F32) + arrived.astype(F32)).astype(BF)
                d_copy(l, p, 4 + k).start()

    part_rows = Dr // 4

    def d_hop(l, p, q):
        col, width = pieces[p]
        cols = pl.ds(col, width)
        return (
            W.at[l, pl.ds(d * Dr + q * part_rows, part_rows), cols],
            L2.at[zh, pl.ds(q * part_rows, part_rows), cols],
            d2_ss.at[l, p, q],
            d2_rs.at[p, zh, q],
        )

    def d_pass(l, p, q):
        src, dst, ssem, rsem = d_hop(l, p, q)
        to_self = (s == l) & (zh == s)

        @pl.when(to_self)
        def _():
            pltpu.make_async_copy(src, dst, rsem).start()

        @pl.when(jnp.logical_not(to_self))
        def _():
            remote(src, dst, ssem, rsem, (l, d, s * Hn + zl)).start()

    @scoped
    def d_total_rows(l, p):
        col, width = pieces[p]
        for k in (2, 3, 4, 5) if square else range(nd - 1):
            d_copy(l, p, k).wait_recv()
        rows = pl.ds(d * Dr, Dr)
        cols = pl.ds(col, width)
        total = W[l, rows, cols].astype(F32)
        for slot in range(2 if square else nd - 1):
            total = total + LW[l, slot, :, cols].astype(F32)
        W[l, rows, cols] = total.astype(BF)

    def d_sum(l, p):
        d_total_rows(l, p)
        for q in range(4):
            d_pass(l, p, q)

    def d_sent(l, p):
        for k in range(6 if square else nd - 1):
            d_copy(l, p, k).wait_send()
        to_self = (s == l) & (zh == s)

        @pl.when(jnp.logical_not(to_self))
        def _():
            for q in range(4):
                remote(*d_hop(l, p, q), core_dev).wait_send()

    outs = (
        pltpu.make_async_copy(MQ, out_qkv, m_sem.at[0]),
        pltpu.make_async_copy(MO, out_o, m_sem.at[1]),
        pltpu.make_async_copy(MGU, out_gu, m_sem.at[2]),
        pltpu.make_async_copy(MD, out_d, m_sem.at[3]),
    )

    def d_arrived(p):
        col, width = pieces[p]
        for half in range(2):
            for q in range(4):
                rows = pl.ds(q * part_rows, part_rows)
                got(L2.at[half, rows, pl.ds(col, width)], d2_rs.at[p, half, q])

    def d_total(col, width):
        return L2[0, :, col : col + width].astype(F32) + L2[1, :, col : col + width].astype(F32)

    @scoped
    def d_final(p):
        d_arrived(p)
        if p == 0:
            for j in range(3):
                MQ[j] = d_total(j * C, C)
            outs[0].start()
        elif p == 1:
            MO[...] = d_total(z_.oO, C).T
            outs[1].start()
        elif p == 3:
            MGU[...] = d_total(z_.oG, z_.GUw).T[: 2 * F]
            outs[2].start()
        elif p == 4:
            MD[...] = d_total(z_.oD, z_.Dw).T[:F]
            outs[3].start()

    def shard_attention():
        masters[0].wait()
        masters[1].wait()
        for j in range(3):
            L2[0, :, j * C : (j + 1) * C] = MQ[j].astype(BF)
        L2[0, :, z_.oO : z_.oG] = MO[...].T.astype(BF)

    def shard_feed():
        masters[2].wait()
        masters[3].wait()
        for ref, col, width, rows in ((MGU, z_.oG, z_.GUw, 2 * F), (MD, z_.oD, z_.Dw, F)):
            value = ref[...]
            if width > rows:
                value = jnp.concatenate([value, jnp.zeros((width - rows, Dr), F32)], axis=0)
            L2[0, :, col : col + width] = value.T.astype(BF)

    def chunk_rows(m, c):
        return pl.ds(m * MB + c * R, R)

    def ag_send(k, buf, m):
        rows = buf.at[chunk_rows(m, own)]
        for step in range(1, Hn):
            remote(
                rows,
                rows,
                ag_ss.at[k, m, step],
                ag_rs.at[k, m, own],
                (s, d, zh * Hn + peer_zl(step)),
            ).start()
        remote(rows, rows, ag_ss.at[k, m, 0], ag_rs.at[k, m, own], core_dev).start()

    def ag_forward(k, buf, m):
        for step in range(1, Hn):
            c = s * Hn + peer_zl(step)
            rows = buf.at[chunk_rows(m, c)]
            got(rows, ag_rs.at[k, m, c])
            remote(rows, rows, ag_fs.at[k, m, step - 1], ag_rs.at[k, m, c], core_dev).start()

    def ag_wait(k, buf, m):
        for step in range(Hn):
            c = (1 - s) * Hn + step
            got(buf.at[chunk_rows(m, c)], ag_rs.at[k, m, c])

    def ag_sent(k, buf, m):
        rows = buf.at[chunk_rows(m, own)]
        for step in range(Hn):
            remote(rows, rows, ag_ss.at[k, m, step], ag_rs.at[k, m, own], core_dev).wait_send()
        for step in range(1, Hn):
            rows = buf.at[chunk_rows(m, s * Hn + peer_zl(step))]
            remote(rows, rows, ag_fs.at[k, m, step - 1], ag_rs.at[k, m, own], core_dev).wait_send()

    def rs_copy1(k, m):
        par = k % 2
        return remote(
            PT.at[par, pl.ds(m * MB + (1 - s) * Hn * R, Hn * R)],
            RL1.at[par, m],
            r1_ss.at[k, m],
            r1_rs.at[k, m],
            core_dev,
        )

    def rs_copy2(k, m, step):
        par = k % 2
        return remote(
            RSB.at[par, m, step - 1],
            RL2.at[par, m, step - 1],
            r2_ss.at[k, m, step - 1],
            r2_rs.at[k, m, step - 1],
            (s, d, zh * Hn + peer_zl(step)),
        )

    def rs_first(k, m, value):
        PT[k % 2, pl.ds(m * MB, MB), :] = value.astype(BF)
        rs_copy1(k, m).start()

    def rs_second(k, m):
        par = k % 2
        copy = rs_copy1(k, m)
        copy.wait_send()
        copy.wait_recv()
        for step in range(1, Hn):
            there = peer_zl(step)
            part = PT[par, chunk_rows(m, s * Hn + there), :].astype(F32) + RL1[
                par, m, pl.ds(there * R, R), :
            ].astype(F32)
            RSB[par, m, step - 1] = part.astype(BF)
            rs_copy2(k, m, step).start()

    def after(k, i, m):
        @pl.when(i > 0)
        def _():
            rs_second(k, m)

    def rs_third(k, m):
        par = k % 2
        total = PT[par, chunk_rows(m, own), :].astype(F32) + RL1[
            par, m, pl.ds(zl * R, R), :
        ].astype(F32)
        for step in range(1, Hn):
            copy = rs_copy2(k, m, step)
            copy.wait_send()
            copy.wait_recv()
            total = total + RL2[par, m, step - 1].astype(F32)
        return total

    def own_rows(m):
        return pl.ds(m * R, R)

    def rms(rows):
        return lax.rsqrt(jnp.mean(rows * rows, axis=-1, keepdims=True) + EPS)

    def gain(l, which):
        return GV[l, which : which + 1, :]

    def rms_back(l, which, rows, grad):
        inverse = rms(rows)
        scaled = grad * gain(l, which)
        back = inverse * scaled - rows * (inverse * inverse * inverse) * jnp.mean(
            scaled * rows, axis=-1, keepdims=True
        )
        DG[l, which : which + 1, :] += jnp.sum(grad * rows * inverse, axis=0, keepdims=True)
        return back

    def send_out(buf, l, out, which, m):
        src = buf.at[l, own_rows(m)]
        dst = out.at[zh * MH + m]
        to_self = (s == l) & (zh == s)

        @pl.when(to_self)
        def _():
            pltpu.make_async_copy(src, dst, o_rs.at[which, zh, m]).start()

        @pl.when(jnp.logical_not(to_self))
        def _():
            remote(
                src, dst, o_ss.at[which, l, m], o_rs.at[which, zh, m], (l, d, s * Hn + zl)
            ).start()

    def sent_out(buf, l, out, which, m):
        to_self = (s == l) & (zh == s)

        @pl.when(jnp.logical_not(to_self))
        def _():
            remote(
                buf.at[l, own_rows(m)],
                out.at[zh * MH + m],
                o_ss.at[which, l, m],
                o_rs.at[which, zh, m],
                core_dev,
            ).wait_send()

    lane_head = lax.broadcasted_iota(jnp.int32, (1, C), 1) // DH
    head_bf = [(lane_head == h).astype(F32).astype(BF) for h in range(NH)]
    head_f = [(lane_head == h).astype(F32) for h in range(NH)]

    def stack(rows):
        return jnp.concatenate([rows * head_bf[h] for h in range(NH)], axis=0)

    def unstack(wide):
        out = wide[0:DH] * head_f[0]
        for h in range(1, NH):
            out = out + wide[h * DH : (h + 1) * DH] * head_f[h]
        return out

    def tall(mask):
        return jnp.concatenate([mask] * NH, axis=0)

    def head_mean(values):
        row = lax.broadcasted_iota(jnp.int32, (C, C), 0) // DH
        col = lax.broadcasted_iota(jnp.int32, (C, C), 1) // DH
        same = jnp.where(row == col, 1.0 / DH, 0.0).astype(BF)
        high = values.astype(BF)
        low = (values - high.astype(F32)).astype(BF)
        return mm(high, same) + mm(low, same)

    def block_rows(b):
        return pl.ds(pl.multiple_of(b * BLOCK, BLOCK), BLOCK)

    def qkv_block(l, b):
        rows = block_rows(b)
        return (QKV[l, rows, 0:C], QKV[l, rows, C : 2 * C], QKV[l, rows, 2 * C : 3 * C])

    def softplus(values):
        return jnp.maximum(values, 0.0) + jnp.log(1.0 + jnp.exp(-jnp.abs(values)))

    def features(values):
        return softplus(values.astype(F32)).astype(BF)

    def diag_forward(b):
        q, k, v = qkv_block(0, b)
        scores = mm(stack(q), k, NT) * (1.0 / math.sqrt(DH))
        scores = jnp.where(tall(MSK[b]) > 0.5, scores, -1e9)
        top = jnp.max(scores, axis=-1, keepdims=True)
        weights = jnp.exp(scores - top)
        weights = (weights / jnp.sum(weights, axis=-1, keepdims=True)).astype(BF)
        AP[0, b] = weights
        O[0, block_rows(b), :] = unstack(mm(weights, v)).astype(BF)

    def diag_backward(b, grad_o):
        q, k, v = qkv_block(0, b)
        low = stack(grad_o.astype(BF))
        weights = AP[0, b]
        wide = weights.astype(F32)
        grad_v = mm(weights, low, TN)
        grad_w = mm(low, v, NT)
        grad_s = wide * (grad_w - jnp.sum(grad_w * wide, axis=-1, keepdims=True))
        grad_s = (grad_s * (1.0 / math.sqrt(DH))).astype(BF)
        grad_q = unstack(mm(grad_s, k))
        grad_k = mm(grad_s, stack(q), TN)
        rows = block_rows(b)
        GQKV[rows, 0:C] = grad_q.astype(BF)
        GQKV[rows, C : 2 * C] = grad_k.astype(BF)
        GQKV[rows, 2 * C : 3 * C] = grad_v.astype(BF)

    def fold(square):
        out = square[0:DH] * head_f[0]
        for h in range(1, NH):
            out = out + square[h * DH : (h + 1) * DH] * head_f[h]
        return out

    def unfold(flat):
        return stack(flat.astype(BF))

    def wide_lanes(column):
        return jnp.concatenate([column] * (C // 128), axis=1)

    def norm_state(b, state):
        q, k, v = qkv_block(1, b)
        ST[b] = state
        key = features(k)
        term = mm(key, (v.astype(F32) * wide_lanes(TAIL[b])).astype(BF), TN)
        return wide_lanes(KEEP[b, 0:1, :]) * state + fold(term)

    def norm_forward(b, passed):
        q, k, v = qkv_block(1, b)
        query, key = features(q), features(k)
        local = jnp.where(tall(MSK[b]) > 0.5, mm(stack(query), key, NT), 0.0).astype(BF)
        AP[1, b] = local
        state = ST[b] + passed * SIN[0].astype(F32)
        ST[b] = state
        mixed = unstack(mm(local, v)) + wide_lanes(CAR[b]) * mm(query, unfold(state))
        rows = block_rows(b)
        UU[rows, :] = mixed
        O[1, rows, :] = (mixed * lax.rsqrt(head_mean(mixed * mixed) + EPS)).astype(BF)
        return passed * wide_lanes(KEEP[b, 0:1, :])

    def norm_back_first(b, grad_o, state):
        rows = block_rows(b)
        mixed = UU[rows, :]
        scale = lax.rsqrt(head_mean(mixed * mixed) + EPS)
        grad = scale * grad_o - mixed * (scale * scale * scale) * head_mean(grad_o * mixed)
        low = grad.astype(BF)
        DU[rows, :] = low
        ST2_store(b, state)
        query = features(QKV[1, rows, 0:C])
        term = mm(query, (low.astype(F32) * wide_lanes(CAR[b])).astype(BF), TN)
        return wide_lanes(KEEP[b, 0:1, :]) * state + fold(term)

    def ST2_store(b, state):
        ST[NBH + b] = state

    def norm_back_second(b, passed):
        rows = block_rows(b)
        q, k, v = qkv_block(1, b)
        query, key = features(q), features(k)
        low = DU[rows, :]
        stacked = stack(low)
        grad_state = ST[NBH + b] + passed * SIN[1].astype(F32)
        grad_wide = unfold(grad_state)
        grad_a = jnp.where(tall(MSK[b]) > 0.5, mm(stacked, v, NT), 0.0).astype(BF)
        tail, carry = wide_lanes(TAIL[b]), wide_lanes(CAR[b])
        grad_q = unstack(mm(grad_a, key)) + carry * mm(low, unfold(ST[b]), NT)
        grad_k = mm(grad_a, stack(query), TN) + tail * mm(v, grad_wide, NT)
        grad_v = mm(AP[1, b], stacked, TN) + tail * mm(key, grad_wide)
        sig_q = 1.0 / (1.0 + jnp.exp(-q.astype(F32)))
        sig_k = 1.0 / (1.0 + jnp.exp(-k.astype(F32)))
        GQKV[rows, 0:C] = (grad_q * sig_q).astype(BF)
        GQKV[rows, C : 2 * C] = (grad_k * sig_k).astype(BF)
        GQKV[rows, 2 * C : 3 * C] = grad_v.astype(BF)
        return passed * wide_lanes(KEEP[b, 0:1, :])

    @scoped
    def masks():
        row = lax.broadcasted_iota(jnp.int32, (BLOCK, BLOCK), 0)
        col = lax.broadcasted_iota(jnp.int32, (BLOCK, BLOCK), 1)
        token = lax.broadcasted_iota(jnp.int32, (MB, BLOCK), 0)
        lane = lax.broadcasted_iota(jnp.int32, (MB, BLOCK), 1)
        start = jnp.concatenate([starts_in[zh * MH + m] for m in range(MH)], axis=0)
        start = start.astype(F32).astype(BF)
        chunk_lane = lax.broadcasted_iota(jnp.int32, (BLOCK, MH), 1)
        for j in range(NB):
            upper = ((token // BLOCK == j) & (token % BLOCK <= lane)).astype(F32).astype(BF)
            count_row = mm(start, upper)
            count_col = mm(upper, start, (((0,), (1,)), ((), ())))
            for m in range(MH):
                b = m * NB + j
                c_row = count_row[m : m + 1, :]
                c_col = jnp.sum(
                    jnp.where(chunk_lane == m, count_col, 0.0), axis=1, keepdims=True
                )
                last = jnp.sum(
                    jnp.where(col[0:1] == BLOCK - 1, c_row, 0.0), axis=1, keepdims=True
                )
                MSK[b] = jnp.where((c_row == c_col) & (row >= col), 1.0, 0.0)
                CAR[b] = jnp.broadcast_to(jnp.where(c_col == 0.0, 1.0, 0.0), (BLOCK, 128))
                TAIL[b] = jnp.broadcast_to(jnp.where(c_col == last, 1.0, 0.0), (BLOCK, 128))
                KEEP[b] = jnp.broadcast_to(jnp.where(last == 0.0, 1.0, 0.0), (8, 128))

    place = d * nt + z

    def gain_copy(i):
        return remote(GL.at[place], GL.at[place], gl_ss.at[i], gl_rs.at[i], section_dev(i))

    def gains_out():
        width = gain_in.shape[1]
        row = lax.broadcasted_iota(jnp.int32, (width, 128), 0)
        col = lax.broadcasted_iota(jnp.int32, (width, 128), 1)
        spot = (col % width == row) & (col // width == place % (128 // width))
        GL[place] = mm(gain_in[...].astype(BF), spot.astype(F32).astype(BF))

        def one(i, carry):
            gain_copy(i).start()
            return carry

        lax.fori_loop(1, nd * nt, one, 0)

    @scoped
    def gains_in():
        def one(i, carry):
            gain_copy(i).wait_send()
            source = (d + nd - i // nt) % nd * nt + (z + nt - i % nt) % nt
            got(GL.at[source], gl_rs.at[i])
            return carry

        lax.fori_loop(1, nd * nt, one, 0)
        each = nd * nt * 128 // D
        for t in range(D // 128):
            total = GL[t * each]
            for i in range(1, each):
                total = total + GL[t * each + i]
            GV[s, :, t * 128 : (t + 1) * 128] = total
        gain_swap().start()

    def gain_swap():
        return remote(GV.at[s], GV.at[s], g_ss.at[2, 0], g_rs.at[2, 0], core_dev)

    def gains_other():
        gain_swap().wait_send()
        got(GV.at[1 - s], g_rs.at[2, 0])

    def dp_gain(step):
        return remote(
            GOWN, DL2.at[step - 1], g_ss.at[5, step - 1], g_rs.at[5, step - 1], dp_dev(step)
        )

    def core_gain():
        return remote(DG.at[1 - s], DL0, g_ss.at[3, 0], g_rs.at[3, 0], core_dev)

    def z_gain(step):
        return remote(
            DG.at[s], DL1.at[step - 1], g_ss.at[4, step - 1], g_rs.at[4, step - 1], z_dev(step)
        )

    @scoped
    def gain_second():
        core_gain().wait()
        DG[s] = DG[s] + DL0[...]
        for step in range(1, nt):
            z_gain(step).start()

    @scoped
    def gain_third():
        total = DG[s]
        for step in range(1, nt):
            z_gain(step).wait()
            total = total + DL1[step - 1]
        GOWN[...] = total
        for step in range(1, nd):
            dp_gain(step).start()

    @scoped
    def gain_final():
        total = GOWN[...]
        for step in range(1, nd):
            dp_gain(step).wait()
            total = total + DL2[step - 1]
        GOWN[...] = total
        width = out_gain.shape[1]
        each = 128 // width
        tile = GOWN[:, pl.ds(pl.multiple_of(place // each * 128, 128), 128)]
        mine = jnp.zeros((2, width), F32)
        for i in range(each):
            piece = tile[:, i * width : (i + 1) * width]
            mine = jnp.where(place % each == i, piece, mine)
        out_gain[...] = mine

    def loop(count, fn):
        def step(i, carry):
            fn(i)
            return carry

        with jax.named_scope(fn.__name__):
            lax.fori_loop(0, count, step, 0)

    def chunk(m):
        return pl.ds(pl.multiple_of(m * MB, BLOCK), MB)

    def w_cols(l, p):
        col, width = pieces[p]
        return W[l, :, col : col + width]

    def w_gate_up(l):
        return W[l, :, z_.oG : z_.oD]

    @scoped
    def state_copy(slot):
        return remote(
            SEND_STATE.at[slot],
            SIN.at[slot],
            st_ss.at[slot],
            st_rs.at[slot],
            (s, d, (z + Hn) % nt),
        )

    def state_out(slot, value, sender):
        SEND_STATE[slot] = value.astype(BF)

        @pl.when(zh == sender)
        def _():
            SIN[slot] = jnp.zeros((DH, C), BF)
            state_copy(slot).start()

    @scoped
    def state_in(slot, sender):
        @pl.when(zh != sender)
        def _():
            state_copy(slot).wait_recv()

    outer = zh == zl
    inner, far = jnp.logical_not(outer), jnp.logical_not(near)

    def only(cond, fn):
        pl.when(cond)(fn)

    def hand_far(l, cond, ps):
        def go():
            for p in ps:
                w_hand_far(l, p)

        pl.when((s == l) & cond)(go)

    def hand_near(ps):
        for l in range(2):

            @pl.when(s == l)
            def _():
                for p in ps:
                    w_hand_near(l, p)

    def x_out():
        spread_tokens(xin, XF, 0)

    gains_out()
    shard_attention()
    hand_far(0, s == 0, [5])
    hand_near([5])
    only((s == 0) & inner, x_out)
    pump_near([("s", 0, 5)])
    own_tokens(xin, XF, 0)
    own_tokens(cot, GF.at[1], 1)
    shard_feed()
    hand_far(0, inner, [2, 3, 4])
    hand_near([2, 3, 4])
    masks()
    for l in range(2):
        DG[l] = jnp.zeros((2, D), F32)
    pump_near([("s", 0, 2)])
    gains_in()
    pump_far([("s", 0, 5)])
    only((s == 0) & outer & far, x_out)
    pump([("f", 0, 5)])
    hand_far(0, outer & far, [2, 3, 4])
    pump_near([("f", 0, 2)])
    only((s == 0) & outer & near, x_out)
    only(s == 1, gains_other)
    await_tokens(XF, 0, 0)
    hand_far(0, outer & near, [2, 3, 4])

    def cot_out():
        spread_tokens(cot, GF.at[1], 1)

    stage = {
        (0, "attended"): lambda: (
            pump_near([("f", 0, 3), ("f", 0, 4)]),
            pump_far([("s", 0, 2), ("s", 0, 3), ("f", 0, 2), ("s", 0, 4)]),
        ),
        (0, "hidden"): lambda: (
            hand_far(1, inner, [5, 4, 2, 3]),
            hand_far(1, outer, [5]),
            pump_near([("s", 1, 5)]),
            pump_far([("f", 0, 3), ("f", 0, 4)]),
        ),
        (0, "ready"): lambda: (
            pump_near([("f", 1, 5)]),
            pump_far([("s", 1, 5)]),
        ),
        (0, "feeding"): lambda: (
            hand_far(1, outer, [4]),
            pump_near([("s", 1, 4)]),
        ),
        (0, "fed"): lambda: (
            hand_far(1, outer, [2, 3]),
            pump_near([("s", 1, 2), ("f", 1, 4)]),
            pump_far([("f", 1, 5), ("s", 1, 4)]),
            only(s == 0, gains_other),
        ),
        (0, "result"): lambda: (
            pump_near([("s", 1, 3)]),
            pump_far([("s", 1, 2), ("f", 1, 4)]),
        ),
        (1, "states"): lambda: (
            only(s == 1, cot_out),
            pump_near([("f", 1, 2), ("f", 1, 3)]),
            pump_far([("s", 1, 3), ("f", 1, 2)]),
        ),
        (1, "attended"): lambda: (pump_far([("f", 1, 3)]),),
        (1, "hidden"): lambda: (),
        (1, "ready"): lambda: (),
        (1, "fed"): lambda: (),
        "b1 second": lambda: (),
        "b1 middle": lambda: (d_mid(1, 4),),
        "b1 feed": lambda: (),
        "b1 third": lambda: (d_mid(1, 3), d_total_rows(1, 2)),
        "b1 end": lambda: (d_mid(1, 1), d_mid(1, 0), d_total_rows(1, 3)),
        "b0 second": lambda: (d_total_rows(1, 0),),
        "b0 middle": lambda: (),
        "b0 feed": lambda: (d_total_rows(1, 1), d_mid(0, 4)),
        "b0 third": lambda: (d_mid(0, 2),),
        "b0 end": lambda: (
            core_gain().start(),
            d_sum(0, 4),
            gain_second(),
            d_sum(0, 2),
            d_mid(0, 0),
            d_sum(0, 3),
            d_mid(0, 1),
            d_sum(0, 0),
            d_sum(0, 1),
            gain_third(),
        ),
    }

    def input_rows(l, m):
        if l == 0:
            return XF[chunk_rows(m, own), :].astype(F32)
        return Y[0, own_rows(m), :].astype(F32)

    def gate_up_grad(grad, both):
        parts = [grad * both[:, F : 2 * F], grad * both[:, :F]]
        if z_.GUw > 2 * F:
            parts.append(jnp.zeros((MB, z_.GUw - 2 * F), F32))
        return jnp.concatenate(parts, axis=1).astype(BF)

    def finish_layer(l, rs2, ag3):
        def result(m):
            rows = (H[l, own_rows(m), :] + rs_third(rs2, m)).astype(BF)
            Y[l, own_rows(m), :] = rows
            send_out(Y, l, out_y, 0, m)
            if l == 0:
                wide = rows.astype(F32)
                N1[1, chunk_rows(m, own), :] = (wide * rms(wide) * gain(1, 0)).astype(BF)
                ag_send(ag3, N1.at[1], m)

        loop(MH, result)

    def forward(l, ag1, rs1, ag2, rs2, ag3):
        w_ready(l, 5)

        def qkv_chunk(m):
            if l == 0:
                pl.when(m > 0)(lambda: await_tokens(XF, 0, m))
                pl.when((m == 1) & near)(lambda: pump([("s", 0, 3), ("s", 0, 4)]))
                rows = XF[chunk(m), :].astype(F32)
                N1[0, chunk(m), :] = (rows * rms(rows) * gain(0, 0)).astype(BF)
            else:
                ag_forward(ag1, N1.at[1], m)
                ag_wait(ag1, N1.at[1], m)
            QKV[l, chunk(m), :] = mm(N1[l, chunk(m), :], w_cols(l, 0)).astype(BF)

        def out_chunk(m):
            rs_first(rs1, m, mm(O[l, chunk(m), :], w_cols(l, 1), NT))

        if l == 0:

            def attend(m):
                qkv_chunk(m)
                for i in range(NB):
                    diag_forward(m * NB + i)
                out_chunk(m)
                after(rs1, m, m - 1)

            loop(MH, attend)
            rs_second(rs1, MH - 1)
            stage[l, "attended"]()
        else:

            def states(m, state):
                qkv_chunk(m)
                for i in range(NB):
                    state = norm_state(m * NB + i, state)
                return state

            with jax.named_scope('states'):
                last = lax.fori_loop(0, MH, states, jnp.zeros((DH, C), F32))
            for p in gathered:
                for k in range(2):

                    @pl.when(s == k)
                    def _():
                        w_handed_out(k, p)

            state_out(0, last, 0)
            state_in(0, 0)
            stage[l, "states"]()

            def attend(m, passed):
                for i in range(NB):
                    passed = norm_forward(m * NB + i, passed)
                out_chunk(m)
                after(rs1, m, m - 1)
                return passed

            with jax.named_scope('attend'):
                lax.fori_loop(0, MH, attend, jnp.ones((1, C), F32))
            rs_second(rs1, MH - 1)
            stage[l, "attended"]()

        def hidden_rows(m):
            rows = input_rows(l, m) + rs_third(rs1, m)
            H[l, own_rows(m), :] = rows
            N2[l, chunk_rows(m, own), :] = (rows * rms(rows) * gain(l, 1)).astype(BF)
            ag_send(ag2, N2.at[l], m)

        loop(MH, hidden_rows)
        stage[l, "hidden"]()
        w_ready(l, 4)
        if l == 1:

            def hidden_grad(m):
                await_tokens(GF.at[1], 1, m)
                GGU[chunk(m), 0 : z_.Dw] = mm(GF[1, chunk(m), :], w_cols(1, 4)).astype(BF)

            loop(MH, hidden_grad)
        w_ready(l, 2)
        w_ready(l, 3)
        stage[l, "ready"]()

        def feed(m):
            ag_forward(ag2, N2.at[l], m)
            ag_wait(ag2, N2.at[l], m)
            rows = N2[l, chunk(m), :]
            both = mm(rows, w_gate_up(l))
            if l == 0:
                GU[l, chunk(m), :] = both.astype(BF)
            else:
                grad = GGU[chunk(m), 0 : z_.Dw].astype(F32)[:, :F]
                GGU[chunk(m), :] = gate_up_grad(grad, both)
            hidden = both[:, :F] * both[:, F : 2 * F]
            if z_.Dw > F:
                hidden = jnp.concatenate([hidden, jnp.zeros((MB, z_.Dw - F), F32)], axis=1)
            hidden = hidden.astype(BF)
            HID[l, chunk(m), :] = hidden
            rs_first(rs2, m, mm(hidden, w_cols(l, 4), NT))
            if l == 0:


                @pl.when(m == 1)
                def _():
                    stage[0, "feeding"]()

            after(rs2, m, m - 1)

        loop(MH, feed)
        rs_second(rs2, MH - 1)
        stage[l, "fed"]()

        if l == 0:
            finish_layer(l, rs2, ag3)
            stage[l, "result"]()

    forward(0, None, 0, 0, 1, 1)
    forward(1, 1, 2, 2, 3, None)

    RB = min(D, 256)

    @scoped
    def grad_weight(l, p, left, right, send=True):
        col, width = pieces[p]
        for r in range(D // RB):
            W[l, r * RB : (r + 1) * RB, col : col + width] = mm(
                left[:, r * RB : (r + 1) * RB], right, TN
            ).astype(BF)
        if send:
            d_send(l, p)

    def rest(l, p):
        for q in range(MH, 4):
            d_pass(l, p, q)

    def grad_part(l, p):
        col, width = pieces[p]
        grad_weight(l, p, N2[l], GGU[:, col - z_.oG : col - z_.oG + width])

    def backward(l, ag_in, rs1, ag2, rs2, ag_out):
        for p in gathered:
            w_shared(l, p)

        def feed_back(i):
            m = MH - 1 - i
            if l == 0:
                ag_forward(ag_in, GF.at[0], m)
                ag_wait(ag_in, GF.at[0], m)
                grad = mm(GF[l, chunk(m), :], w_cols(l, 4))[:, :F]
                GGU[chunk(m), :] = gate_up_grad(grad, GU[l, chunk(m), :].astype(F32))
            rs_first(rs1, m, mm(GGU[chunk(m), :], w_gate_up(l), NT))
            after(rs1, i, m + 1)
            if l == 0:
                d_pass(1, 3, i)

        if l == 1:
            grad_weight(l, 4, GF[l], HID[l])
        loop(MH, feed_back)
        rs_second(rs1, 0)
        if l == 0:
            rest(1, 3)
            grad_weight(l, 4, GF[l], HID[l])
        else:
            grad_part(l, 2)
            finish_layer(1, 3, None)
        stage[f"b{l} second"]()

        def middle(i):
            m = MH - 1 - i
            rows = H[l, own_rows(m), :]
            grad = GF[l, chunk_rows(m, own), :].astype(F32) + rms_back(
                l, 1, rows, rs_third(rs1, m)
            )
            GH[own_rows(m), :] = grad
            GA[l, chunk_rows(m, own), :] = grad.astype(BF)
            ag_send(ag2, GA.at[l], m)
            if l == 0:
                d_pass(1, 0, i)

        loop(MH, middle)
        if l == 0:
            rest(1, 0)
        stage[f"b{l} middle"]()
        if l == 0:
            grad_part(l, 2)
        grad_part(l, 3)
        stage[f"b{l} feed"]()

        def grad_o(m):
            ag_forward(ag2, GA.at[l], m)
            ag_wait(ag2, GA.at[l], m)
            return mm(GA[l, chunk(m), :], w_cols(l, 1))

        def qkv_back(i, m):
            rs_first(rs2, m, mm(GQKV[chunk(m), :], w_cols(l, 0), NT))
            after(rs2, i, m + 1)

        if l == 0:

            def attend(i):
                m = MH - 1 - i
                grad = grad_o(m)
                for j in range(NB):
                    diag_backward(m * NB + j, grad[j * BLOCK : (j + 1) * BLOCK])
                qkv_back(i, m)
                d_pass(1, 1, i)

            loop(MH, attend)
        else:

            def states(i, state):
                m = MH - 1 - i
                grad = grad_o(m)
                for j in reversed(range(NB)):
                    state = norm_back_first(m * NB + j, grad[j * BLOCK : (j + 1) * BLOCK], state)
                return state

            with jax.named_scope("states"):
                last = lax.fori_loop(0, MH, states, jnp.zeros((DH, C), F32))
            state_out(1, last, 1)
            d_mid(1, 2)
            grad_weight(l, 1, GA[l], O[l])
            state_in(1, 1)
            d_total_rows(1, 4)

            def attend(i, passed):
                m = MH - 1 - i
                for j in reversed(range(NB)):
                    passed = norm_back_second(m * NB + j, passed)
                qkv_back(i, m)
                d_pass(1, 4, i)
                return passed

            with jax.named_scope("attend"):
                lax.fori_loop(0, MH, attend, jnp.ones((1, C), F32))

        rs_second(rs2, 0)
        rest(1, 4 if l == 1 else 1)
        stage[f"b{l} third"]()
        grad_weight(l, 0, N1[l], GQKV[...], l == 1)
        if l == 0:
            grad_weight(l, 1, GA[l], O[l], False)
            d_mid(0, 3)
            d_send(0, 0)
            d_send(0, 1)

        def result(i):
            m = MH - 1 - i
            grad = GH[own_rows(m), :] + rms_back(l, 0, input_rows(l, m), rs_third(rs2, m))
            low = grad.astype(BF)
            GX[l, own_rows(m), :] = low
            send_out(GX, l, out_g, 1, m)
            if l == 1:
                GF[0, chunk_rows(m, own), :] = low
                ag_send(ag_out, GF.at[0], m)
                d_pass(1, 2, i)

        loop(MH, result)
        if l == 1:
            rest(1, 2)
        stage[f"b{l} end"]()

    backward(1, None, 4, 3, 5, 4)
    backward(0, 4, 6, 5, 7, None)

    for p in (4, 2, 3, 0, 1):
        d_final(p)
    gain_final()
    for copy in outs:
        copy.wait()
    for l in range(2):
        for p in range(5):
            d_sent(l, p)

    ags = ((0, N2.at[0]), (1, N1.at[1]), (2, N2.at[1]), (3, GA.at[1]), (4, GF.at[0]), (5, GA.at[0]))

    for slot in range(2):

        @pl.when(zh == slot)
        def _():
            state_copy(slot).wait_send()

    def finish(m):
        for k, buf in ags:
            ag_sent(k, buf, m)
        for l in range(2):
            sent_out(Y, l, out_y, 0, m)
            sent_out(GX, l, out_g, 1, m)
        for half in range(2):
            got(out_y.at[half * MH + m], o_rs.at[0, half, m])
            got(out_g.at[half * MH + m], o_rs.at[1, half, m])

    loop(MH, finish)
    for array, src, dst in ((0, xin, XF), (1, cot, GF.at[1])):

        @pl.when(s == array)
        def _():
            for m in range(MH):
                mine = dst.at[pl.ds(m * MB + z * R, R)]
                for step in range(1, nt):
                    copy = remote(
                        src.at[m], mine, x_ss.at[m, step - 1], x_rs.at[array, m, step - 1], core_dev
                    )
                    copy.wait_send()
                    remote(
                        mine, mine, x_fs.at[m, step - 1], x_rs.at[array, m, step - 1], core_dev
                    ).wait_send()


def place_results(*refs):
    count = (len(refs) - 2) // 3
    sources, targets, held = refs[:count], refs[count : 2 * count], refs[2 * count : 3 * count]
    in_sem, out_sem = refs[-2:]
    reads = [pltpu.make_async_copy(sources[i], held[i], in_sem.at[i]) for i in range(count)]
    writes = [pltpu.make_async_copy(held[i], targets[i], out_sem.at[i]) for i in range(count)]
    for copy in reads:
        copy.start()
    for read, write in zip(reads, writes):
        read.wait()
        write.start()
    for copy in writes:
        copy.wait()


def solution(mesh):
    nd, nt = mesh.shape["dp"], mesh.shape["tensor"]

    def on_device(inputs, starts, cotangent, qkv_m, out_m, gateup_m, down_m, gain_m):
        z_ = Sizes(
            mesh,
            inputs.shape[3],
            inputs.shape[1],
            inputs.shape[2],
            qkv_m.shape[3],
            gateup_m.shape[3],
        )
        D, R, C, F, Dr, M, MH, Hn, MB, T, NBH, N, NH = (
            z_.D,
            z_.R,
            z_.C,
            z_.F,
            z_.Dr,
            z_.M,
            z_.MH,
            z_.Hn,
            z_.MB,
            z_.T,
            z_.NBH,
            z_.N,
            z_.NH,
        )
        width = gain_m.shape[2]
        qkv_rows = jnp.transpose(qkv_m[0], (1, 0, 2))
        gateup_rows = jnp.transpose(gateup_m[0], (1, 2, 0)).reshape(2 * F, Dr)
        anywhere = pl.BlockSpec(memory_space=pl.ANY)
        vmem = pl.BlockSpec(memory_space=pltpu.VMEM)
        DMA = pltpu.SemaphoreType.DMA
        V = pltpu.VMEM
        scratch = [
            V((3, Dr, C), F32),
            V((C, Dr), F32),
            V((2 * F, Dr), F32),
            V((F, Dr), F32),
            V((2, D, N), BF),
            V((2, nd - 1, Dr, N), BF),
            V((2, Dr, N), BF),
            V((T, D), BF),
            V((2, T, D), BF),
            V((2, T, D), BF),
            V((2, T, D), BF),
            V((2, T, 3 * C), BF),
            V((2, T, C), BF),
            V((1, T, z_.GUw), BF),
            V((2, T, z_.Dw), BF),
            V((2, MH * R, D), F32),
            V((2, MH * R, D), BF),
            V((2, T, D), BF),
            V((T, z_.GUw), BF),
            V((T, 3 * C), BF),
            V((MH * R, D), F32),
            V((2, MH * R, D), BF),
            V((2, T, D), BF),
            V((2, MH, Hn * R, D), BF),
            V((2, MH, Hn - 1, R, D), BF),
            V((2, MH, Hn - 1, R, D), BF),
            V((2, NBH, NH * BLOCK, BLOCK), BF),
            V((T, C), F32),
            V((T, C), BF),
            V((2 * NBH, DH, C), F32),
            V((2, DH, C), BF),
            V((2, DH, C), BF),
            V((NBH, BLOCK, BLOCK), F32),
            V((NBH, BLOCK, 128), F32),
            V((NBH, BLOCK, 128), F32),
            V((NBH, 8, 128), F32),
            V((nd * nt, 2, 128), F32),
            V((2, 2, D), F32),
            V((2, D), F32),
            V((2, 2, D), F32),
            V((2, D), F32),
            V((nt - 1, 2, D), F32),
            V((nd - 1, 2, D), F32),
            DMA((2, MH)),
            DMA((MH, nt - 1)),
            DMA((2, MH, nt - 1)),
            DMA((MH, nt - 1)),
            DMA((6, 2)),
            DMA((2, 6)),
            DMA((2, 6, max(4, nd - 1))),
            DMA((2, 6, max(4, nd - 1))),
            DMA((6, MH, Hn)),
            DMA((6, MH, Hn - 1)),
            DMA((6, MH, nt)),
            DMA((8, MH)),
            DMA((8, MH)),
            DMA((8, MH, Hn - 1)),
            DMA((8, MH, Hn - 1)),
            DMA((2,)),
            DMA((2,)),
            DMA((2, 2, MH)),
            DMA((2, 2, MH)),
            DMA((2, 5, max(6, nd - 1))),
            DMA((2, 5, max(6, nd - 1))),
            DMA((2, 5, 4)),
            DMA((5, 2, 4)),
            DMA((6, max(nd, nt) - 1)),
            DMA((6, max(nd, nt) - 1)),
            DMA((nd * nt,)),
            DMA((nd * nt,)),
            DMA((4,)),
        ]
        out_y, out_g, grad_qkv, grad_o, grad_gu, grad_d, grad_gain = pl.pallas_call(
            functools.partial(body, z_),
            out_shape=(
                jax.ShapeDtypeStruct((M, R, D), BF),
                jax.ShapeDtypeStruct((M, R, D), BF),
                jax.ShapeDtypeStruct((3, Dr, C), F32),
                jax.ShapeDtypeStruct((C, Dr), F32),
                jax.ShapeDtypeStruct((2 * F, Dr), F32),
                jax.ShapeDtypeStruct((F, Dr), F32),
                jax.ShapeDtypeStruct((2, width), F32),
            ),
            in_specs=[anywhere] * 6 + [vmem, vmem],
            out_specs=(anywhere,) * 6 + (vmem,),
            scratch_shapes=scratch,
            compiler_params=pltpu.CompilerParams(
                collective_id=0, has_side_effects=True, vmem_limit_bytes=63 * 1024 * 1024
            ),
        )(
            qkv_rows,
            out_m[0],
            gateup_rows,
            down_m[0],
            inputs[0],
            cotangent[0],
            jnp.transpose(starts, (1, 0, 2)),
            gain_m[0],
        )
        results = (out_y, out_g, grad_qkv, grad_o, grad_gu, grad_d, grad_gain)
        out_y, out_g, grad_qkv, grad_o, grad_gu, grad_d, grad_gain = pl.pallas_call(
            place_results,
            out_shape=tuple(jax.ShapeDtypeStruct(r.shape, r.dtype) for r in results),
            in_specs=[anywhere] * len(results),
            out_specs=(anywhere,) * len(results),
            scratch_shapes=[V(r.shape, r.dtype) for r in results]
            + [DMA((len(results),)), DMA((len(results),))],
        )(*results)
        return (
            out_y[None, None],
            out_g[None, None],
            jnp.transpose(grad_qkv, (1, 0, 2))[None],
            grad_o[None],
            jnp.transpose(grad_gu.reshape(2, F, Dr), (2, 0, 1))[None],
            grad_d[None],
            grad_gain[None],
        )

    return jax.shard_map(
        on_device,
        mesh=mesh,
        in_specs=(
            P("dp", None, "tensor", None),
            P("dp", None, None),
            P("dp", None, "tensor", None),
            P("section", "dp", None, "tensor"),
            P("section", "tensor", "dp"),
            P("section", "dp", None, "tensor"),
            P("section", "tensor", "dp"),
            P("section", None, ("dp", "tensor")),
        ),
        out_specs=(
            P("section", "dp", None, "tensor", None),
            P("section", "dp", None, "tensor", None),
            P("section", "dp", None, "tensor"),
            P("section", "tensor", "dp"),
            P("section", "dp", None, "tensor"),
            P("section", "tensor", "dp"),
            P("section", None, ("dp", "tensor")),
        ),
        check_vma=False,
    )
```

```python
import functools
import math

import jax
import jax.numpy as jnp
from jax import lax
from jax.experimental import pallas as pl
from jax.experimental.pallas import tpu as pltpu
from jax.sharding import PartitionSpec as P

DH = 64
BLOCK = 64
EPS = 1e-6
BF = jnp.bfloat16
F32 = jnp.float32
MESH = pl.DeviceIdType.MESH
NN = (((1,), (0,)), ((), ()))
NT = (((1,), (1,)), ((), ()))
TN = (((0,), (0,)), ((), ()))


def mm(a, b, dims=NN):
    return lax.dot_general(a, b, dims, preferred_element_type=F32)


def ceil_to(value, unit):
    return (value + unit - 1) // unit * unit


def scoped(fn):
    @functools.wraps(fn)
    def inner(*args):
        with jax.named_scope(fn.__name__):
            return fn(*args)

    return inner


class Sizes:
    def __init__(self, mesh, model, micro, rows, cols, hidden):
        self.nd, self.nt = mesh.shape["dp"], mesh.shape["tensor"]
        self.D, self.M, self.R, self.C, self.F = model, micro, rows, cols, hidden
        self.GUw, self.Dw = ceil_to(2 * hidden, 128), ceil_to(hidden, 128)
        self.Dr = model // self.nd
        self.MH, self.Hn = micro // 2, self.nt // 2
        self.MB = rows * self.nt
        self.T = self.MH * self.MB
        self.NH = cols // DH
        self.NB = self.MB // BLOCK
        self.NBH = self.MH * self.NB
        self.oO, self.oG = 3 * cols, 4 * cols
        self.oD = self.oG + self.GUw
        self.N = self.oD + self.Dw
        first = ceil_to(self.GUw // 2, 128)
        self.pieces = (
            (0, 3 * cols),
            (self.oO, cols),
            (self.oG, first),
            (self.oG + first, self.GUw - first),
            (self.oD, self.Dw),
            (0, 4 * cols),
            (0, cols),
            (cols, cols),
            (2 * cols, cols),
        )


def body(
    z_,
    qkv_in,
    o_in,
    gu_in,
    d_in,
    xin,
    cot,
    starts_in,
    gain_in,
    out_y,
    out_g,
    out_qkv,
    out_o,
    out_gu,
    out_d,
    out_gain,
    MQ,
    MO,
    MGU,
    MD,
    W,
    LW,
    L2,
    XF,
    GF,
    N1,
    N2,
    QKV,
    O,
    GU,
    HID,
    H,
    Y,
    GA,
    GGU,
    GQKV,
    GH,
    GX,
    PT,
    RL1,
    RL2,
    RSB,
    AP,
    UU,
    DU,
    ST,
    SIN,
    SEND_STATE,
    MSK,
    CAR,
    TAIL,
    KEEP,
    GL,
    GV,
    GOWN,
    DG,
    DL0,
    DL1,
    DL2,
    in_sem,
    x_sem,
    x_rs,
    w1_ss,
    w1_rs,
    w2_ss,
    w2_rs,
    ag_ss,
    ag_rs,
    r1_ss,
    r1_rs,
    r2_ss,
    r2_rs,
    st_ss,
    st_rs,
    o_ss,
    o_rs,
    d1_ss,
    d1_rs,
    d2_ss,
    d2_rs,
    g1_sem,
    g_ss,
    g_rs,
    gl_sem,
    m_sem,
):
    D, R, C, F, Dr, MH, Hn, MB, T, NH, NB, NBH = (
        z_.D,
        z_.R,
        z_.C,
        z_.F,
        z_.Dr,
        z_.MH,
        z_.Hn,
        z_.MB,
        z_.T,
        z_.NH,
        z_.NB,
        z_.NBH,
    )
    nd, nt = z_.nd, z_.nt
    pieces = z_.pieces
    s, d, z = lax.axis_index("section"), lax.axis_index("dp"), lax.axis_index("tensor")
    zh, zl = z // Hn, z % Hn
    own = s * Hn + zl
    core_dev = (1 - s, d, z)

    def remote(src, dst, ssem, rsem, dev):
        return pltpu.make_async_remote_copy(
            src_ref=src, dst_ref=dst, send_sem=ssem, recv_sem=rsem, device_id=dev, device_id_type=MESH
        )

    def got(dst, sem):
        pltpu.make_async_copy(dst, dst, sem).wait()

    def dp_dev(step):
        return (s, (d + step) % nd, z)

    def z_dev(step):
        return (s, d, (z + step) % nt)

    def peer_zl(step):
        return (zl + step) % Hn

    masters = (
        pltpu.make_async_copy(qkv_in, MQ, m_sem.at[0]),
        pltpu.make_async_copy(o_in, MO, m_sem.at[1]),
        pltpu.make_async_copy(gu_in, MGU, m_sem.at[2]),
        pltpu.make_async_copy(d_in, MD, m_sem.at[3]),
    )
    for copy in masters:
        copy.start()

    barrier = pltpu.get_barrier_semaphore()

    def section_dev(i):
        return (s, (d + i // nt) % nd, (z + i % nt) % nt)

    def greet(i, carry):
        pl.semaphore_signal(barrier, inc=1, device_id=section_dev(i), device_id_type=MESH)
        return carry

    lax.fori_loop(1, nd * nt, greet, 0)
    pl.semaphore_signal(barrier, inc=1, device_id=core_dev, device_id_type=MESH)
    far_dev = (1 - s, d, (z + Hn) % nt)
    pl.semaphore_signal(barrier, inc=1, device_id=far_dev, device_id_type=MESH)
    pl.semaphore_wait(barrier, nd * nt + 1)

    def own_tokens(src, dst, array):
        for m in range(MH):
            mine = dst.at[pl.ds(m * MB + z * R, R)]
            pltpu.make_async_copy(src.at[zh * MH + m], mine, in_sem.at[array, m]).start()

    def spread_tokens(src, dst, array):
        for m in range(MH):
            mine = dst.at[pl.ds(m * MB + z * R, R)]
            for step in range(1, nt):
                other = (z + step) % nt
                remote(
                    src.at[(other // Hn) * MH + m],
                    mine,
                    x_sem.at[0],
                    x_rs.at[array, m, step - 1],
                    z_dev(step),
                ).start()

    def await_tokens(dst, array, m):
        got(dst.at[pl.ds(m * MB + z * R, R)], in_sem.at[array, m])
        for step in range(1, nt):
            rows = dst.at[pl.ds(m * MB + (z + nt - step) % nt * R, R)]
            got(rows, x_rs.at[array, m, step - 1])

            @pl.when(s == array)
            def _():
                remote(
                    rows, rows, x_sem.at[1], x_rs.at[array, m, step - 1], core_dev
                ).start()

    spot = {5: 0, 2: 1, 3: 2, 4: 3}

    def w_rows(l, block, p):
        col, width = pieces[p]
        return W.at[l, pl.ds(block * Dr, Dr), pl.ds(col, width)]

    def shard_cols(p):
        col, width = pieces[p]
        return L2.at[0, :, pl.ds(col, width)]

    def w_hand_near(l, p):
        @pl.when(zh == s)
        def _():
            pltpu.make_async_copy(shard_cols(p), w_rows(l, d, p), w1_rs.at[l, spot[p]]).start()

        @pl.when(zh != s)
        def _():
            w_hand(l, p, 0, core_dev).start()

    def w_hand(l, p, which, dev):
        return remote(
            shard_cols(p), w_rows(l, d, p), w1_ss.at[which], w1_rs.at[l, spot[p]], dev
        )

    def w_hand_far(l, p):
        w_hand(l, p, 1, (zh, d, (z + Hn) % nt)).start()

    def w_handed_out():
        @pl.when(zh != s)
        def _():
            got(L2.at[0], w1_ss.at[0])

        got(L2.at[0], w1_ss.at[1])

    square = nd == 4
    half_rows = Dr // 2
    dp_x, dp_y = d + 1 - 2 * (d % 2), (d + 2) % nd

    def w_half(l, block, half, p):
        col, width = pieces[p]
        return W.at[l, pl.ds(block * Dr + half * half_rows, half_rows), pl.ds(col, width)]

    def w_copy(l, p, k):
        if not square:
            rows, dev = w_rows(l, d, p), dp_dev(k + 1)
        elif k < 2:
            rows, dev = w_rows(l, d, p), (s, (dp_x, dp_y)[k], z)
        elif k == 2:
            rows, dev = w_half(l, dp_x, 0, p), (s, dp_y, z)
        else:
            rows, dev = w_half(l, dp_y, 1, p), (s, dp_x, z)
        return remote(rows, rows, w2_ss.at[l], w2_rs.at[l, spot[p], k], dev)

    def w_share(l, p):
        got(w_rows(l, d, p), w1_rs.at[l, spot[p]])
        for k in range(2 if square else nd - 1):
            w_copy(l, p, k).start()

    def w_forward(l, p):
        if square:
            got(w_rows(l, dp_x, p), w2_rs.at[l, spot[p], 0])
            w_copy(l, p, 2).start()
            got(w_rows(l, dp_y, p), w2_rs.at[l, spot[p], 1])
            w_copy(l, p, 3).start()

    def w_ready(l, p):
        if square:
            got(w_half(l, 3 - d, 0, p), w2_rs.at[l, spot[p], 2])
            got(w_half(l, 3 - d, 1, p), w2_rs.at[l, spot[p], 3])
        else:
            for step in range(1, nd):
                got(w_rows(l, (d + nd - step) % nd, p), w2_rs.at[l, spot[p], step - 1])

    def w_shared(l):
        got(W.at[l, pl.ds(0, (nd - 1) * Dr)], w2_ss.at[l])

    def pump(ops):
        for what, l, p in ops:
            with jax.named_scope(what + str(l) + str(p)):
                {"s": w_share, "f": w_forward}[what](l, p)

    near = s == zh
    gathered = (5, 2, 3, 4)

    def pump_near(ops):
        pl.when(near)(lambda: pump(ops))

    def pump_far(ops):
        pl.when(jnp.logical_not(near))(lambda: pump(ops))

    where = {4: 0, 2: 1, 3: 2, 1: 3, 6: 4, 7: 5, 8: 6}

    def split(p):
        return (6, 7, 8) if p == 0 else (p,)

    def d_copy(l, p, k):
        col, width = pieces[p]
        cols = pl.ds(col, width)
        if not square:
            src, dst, dev = w_rows(l, (d + k + 1) % nd, p), LW.at[l, k, :, cols], dp_dev(k + 1)
        else:
            first, second = pl.ds(0, half_rows), pl.ds(half_rows, half_rows)
            block, half, slot, rows, to = (
                (3 - d, 0, 2, first, dp_x),
                (3 - d, 1, 2, second, dp_y),
                (dp_x, 0, 0, first, dp_x),
                (dp_y, 1, 1, second, dp_y),
                (dp_y, 0, 1, first, dp_y),
                (dp_x, 1, 0, second, dp_x),
            )[k]
            src, dst, dev = w_half(l, block, half, p), LW.at[l, slot, rows, cols], (s, to, z)
        group = k if square and k < 2 else 2
        return remote(src, dst, d1_ss.at[l], d1_rs.at[l, where[p], group], dev)

    def d_send(l, p):
        for part in split(p):
            for k in range(4 if square else nd - 1):
                d_copy(l, part, k).start()

    @scoped
    def d_mid(l, p):
        if p == 0:
            for part in split(p):
                d_mid(l, part)
        elif square:
            col, width = pieces[p]
            cols = pl.ds(col, width)
            for k, block, half in ((0, dp_y, 0), (1, dp_x, 1)):
                copy = d_copy(l, p, k)
                copy.wait_recv()
                rows = pl.ds(block * Dr + half * half_rows, half_rows)
                arrived = LW[l, 2, half * half_rows : (half + 1) * half_rows, cols]
                W[l, rows, cols] = (W[l, rows, cols].astype(F32) + arrived.astype(F32)).astype(BF)
                d_copy(l, p, 4 + k).start()

    part_rows = Dr // 4

    def d_pass(l, p, q, rows=part_rows):
        for part in split(p):
            col, width = pieces[part]
            cols = pl.ds(col, width)
            src = W.at[l, pl.ds(d * Dr + q * rows, rows), cols]
            dst = L2.at[zh, pl.ds(q * rows, rows), cols]
            arrival = d2_rs.at[where[part], zh]
            to_self = (s == l) & (zh == s)

            @pl.when(to_self)
            def _():
                pltpu.make_async_copy(src, dst, arrival).start()

            @pl.when(jnp.logical_not(to_self))
            def _():
                remote(src, dst, d2_ss.at[l], arrival, (l, d, s * Hn + zl)).start()

    @scoped
    def d_total_rows(l, p):
        for part in split(p):
            col, width = pieces[part]
            cols = pl.ds(col, width)
            slots = 2 if square else nd - 1
            got(LW.at[l, pl.ds(0, slots), :, cols], d1_rs.at[l, where[part], 2])
            rows = pl.ds(d * Dr, Dr)
            total = W[l, rows, cols].astype(F32)
            for slot in range(slots):
                total = total + LW[l, slot, :, cols].astype(F32)
            W[l, rows, cols] = total.astype(BF)

    def d_sum(l, p):
        d_total_rows(l, p)
        d_pass(l, p, 0, Dr)

    def d_sent(l):
        got(W.at[l, pl.ds(0, (nd - 1) * Dr)], d1_ss.at[l])

        @pl.when(jnp.logical_not((s == l) & (zh == s)))
        def _():
            got(W.at[l, pl.ds(0, Dr)], d2_ss.at[l])

    outs = (
        pltpu.make_async_copy(MQ, out_qkv, m_sem.at[0]),
        pltpu.make_async_copy(MO, out_o, m_sem.at[1]),
        pltpu.make_async_copy(MGU, out_gu, m_sem.at[2]),
        pltpu.make_async_copy(MD, out_d, m_sem.at[3]),
    )

    def d_arrived(p):
        col, width = pieces[p]
        for half in range(2):
            got(L2.at[half, :, pl.ds(col, width)], d2_rs.at[where[p], half])

    def d_total(col, width):
        return L2[0, :, col : col + width].astype(F32) + L2[1, :, col : col + width].astype(F32)

    @scoped
    def d_final(p):
        d_arrived(p)
        if p >= 6:
            j = p - 6
            MQ[j] = d_total(j * C, C)
            pltpu.make_async_copy(MQ.at[j], out_qkv.at[j], m_sem.at[0]).start()
        elif p == 1:
            MO[...] = d_total(z_.oO, C).T
            outs[1].start()
        elif p == 3:
            MGU[...] = d_total(z_.oG, z_.GUw).T[: 2 * F]
            outs[2].start()
        elif p == 4:
            MD[...] = d_total(z_.oD, z_.Dw).T[:F]
            outs[3].start()

    @scoped
    def shard_attention():
        masters[0].wait()
        masters[1].wait()
        for j in range(3):
            L2[0, :, j * C : (j + 1) * C] = MQ[j].astype(BF)
        L2[0, :, z_.oO : z_.oG] = MO[...].T.astype(BF)

    @scoped
    def shard_feed():
        masters[2].wait()
        masters[3].wait()
        for ref, col, width, rows in ((MGU, z_.oG, z_.GUw, 2 * F), (MD, z_.oD, z_.Dw, F)):
            value = ref[...]
            if width > rows:
                value = jnp.concatenate([value, jnp.zeros((width - rows, Dr), F32)], axis=0)
            L2[0, :, col : col + width] = value.T.astype(BF)

    def chunk_rows(m, c):
        return pl.ds(m * MB + c * R, R)

    def ag_send(k, buf, m):
        rows = buf.at[chunk_rows(m, own)]
        for step in range(1, Hn):
            dev = (s, d, zh * Hn + peer_zl(step))
            remote(rows, rows, ag_ss.at[k], ag_rs.at[k, m, Hn - step], dev).start()
        remote(rows, rows, ag_ss.at[k], ag_rs.at[k, m, 0], core_dev).start()

    def ag_forward(k, buf, m):
        for step in range(1, Hn):
            rows = buf.at[chunk_rows(m, s * Hn + peer_zl(step))]
            got(rows, ag_rs.at[k, m, step])
            remote(rows, rows, ag_ss.at[k], ag_rs.at[k, m, 0], core_dev).start()

    def ag_wait(k, buf, m):
        got(buf.at[pl.ds(m * MB + (1 - s) * Hn * R, Hn * R)], ag_rs.at[k, m, 0])

    def ag_sent(k, buf):
        got(buf.at[pl.ds(0, MH * (2 * Hn - 1) * R)], ag_ss.at[k])

    def rs_copy1(k, m):
        par = k % 2
        return remote(
            PT.at[par, pl.ds(m * MB + (1 - s) * Hn * R, Hn * R)],
            RL1.at[par, m],
            r1_ss.at[par, m],
            r1_rs.at[par, m],
            core_dev,
        )

    def rs_copy2(k, m, step):
        par = k % 2
        return remote(
            RSB.at[par, m, step - 1],
            RL2.at[par, m, step - 1],
            r2_ss.at[par, m, step - 1],
            r2_rs.at[par, m, step - 1],
            (s, d, zh * Hn + peer_zl(step)),
        )

    def rs_first(k, m, value):
        PT[k % 2, pl.ds(m * MB, MB), :] = value.astype(BF)
        rs_copy1(k, m).start()

    def rs_second(k, m):
        par = k % 2
        copy = rs_copy1(k, m)
        copy.wait_send()
        copy.wait_recv()
        for step in range(1, Hn):
            there = peer_zl(step)
            part = PT[par, chunk_rows(m, s * Hn + there), :].astype(F32) + RL1[
                par, m, pl.ds(there * R, R), :
            ].astype(F32)
            RSB[par, m, step - 1] = part.astype(BF)
            rs_copy2(k, m, step).start()

    def after(k, i, m):
        @pl.when(i > 0)
        def _():
            rs_second(k, m)

    def rs_third(k, m):
        par = k % 2
        total = PT[par, chunk_rows(m, own), :].astype(F32) + RL1[
            par, m, pl.ds(zl * R, R), :
        ].astype(F32)
        for step in range(1, Hn):
            copy = rs_copy2(k, m, step)
            copy.wait_send()
            copy.wait_recv()
            total = total + RL2[par, m, step - 1].astype(F32)
        return total

    def own_rows(m):
        return pl.ds(m * R, R)

    def rms(rows):
        return lax.rsqrt(jnp.mean(rows * rows, axis=-1, keepdims=True) + EPS)

    def gain(l, which):
        return GV[l, which : which + 1, :]

    def rms_back(l, which, rows, grad):
        inverse = rms(rows)
        scaled = grad * gain(l, which)
        back = inverse * scaled - rows * (inverse * inverse * inverse) * jnp.mean(
            scaled * rows, axis=-1, keepdims=True
        )
        DG[l, which : which + 1, :] += jnp.sum(grad * rows * inverse, axis=0, keepdims=True)
        return back

    def send_out(buf, l, out, which, m):
        src = buf.at[l, own_rows(m)]
        dst = out.at[zh * MH + m]
        to_self = (s == l) & (zh == s)

        @pl.when(to_self)
        def _():
            pltpu.make_async_copy(src, dst, o_rs.at[which, zh]).start()

        @pl.when(jnp.logical_not(to_self))
        def _():
            remote(
                src, dst, o_ss.at[l], o_rs.at[which, zh], (l, d, s * Hn + zl)
            ).start()

    lane_head = lax.broadcasted_iota(jnp.int32, (1, C), 1) // DH
    head_bf = [(lane_head == h).astype(F32).astype(BF) for h in range(NH)]
    head_f = [(lane_head == h).astype(F32) for h in range(NH)]

    def stack(rows):
        return jnp.concatenate([rows * head_bf[h] for h in range(NH)], axis=0)

    def unstack(wide):
        out = wide[0:DH] * head_f[0]
        for h in range(1, NH):
            out = out + wide[h * DH : (h + 1) * DH] * head_f[h]
        return out

    def tall(mask):
        return jnp.concatenate([mask] * NH, axis=0)

    def head_mean(values):
        row = lax.broadcasted_iota(jnp.int32, (C, C), 0) // DH
        col = lax.broadcasted_iota(jnp.int32, (C, C), 1) // DH
        same = jnp.where(row == col, 1.0 / DH, 0.0).astype(BF)
        high = values.astype(BF)
        low = (values - high.astype(F32)).astype(BF)
        return mm(high, same) + mm(low, same)

    def block_rows(b):
        return pl.ds(pl.multiple_of(b * BLOCK, BLOCK), BLOCK)

    def qkv_block(l, b):
        rows = block_rows(b)
        return (QKV[l, rows, 0:C], QKV[l, rows, C : 2 * C], QKV[l, rows, 2 * C : 3 * C])

    def softplus(values):
        return jnp.maximum(values, 0.0) + jnp.log(1.0 + jnp.exp(-jnp.abs(values)))

    def features(values):
        return softplus(values.astype(F32)).astype(BF)

    def diag_forward(b):
        q, k, v = qkv_block(0, b)
        scores = mm(stack(q), k, NT) * (1.0 / math.sqrt(DH))
        scores = jnp.where(tall(MSK[b]) > 0.5, scores, -1e9)
        top = jnp.max(scores, axis=-1, keepdims=True)
        weights = jnp.exp(scores - top)
        weights = (weights / jnp.sum(weights, axis=-1, keepdims=True)).astype(BF)
        AP[0, b] = weights
        O[0, block_rows(b), :] = unstack(mm(weights, v)).astype(BF)

    def diag_backward(b, grad_o):
        q, k, v = qkv_block(0, b)
        low = stack(grad_o.astype(BF))
        weights = AP[0, b]
        wide = weights.astype(F32)
        grad_v = mm(weights, low, TN)
        grad_w = mm(low, v, NT)
        grad_s = wide * (grad_w - jnp.sum(grad_w * wide, axis=-1, keepdims=True))
        grad_s = (grad_s * (1.0 / math.sqrt(DH))).astype(BF)
        grad_q = unstack(mm(grad_s, k))
        grad_k = mm(grad_s, stack(q), TN)
        rows = block_rows(b)
        GQKV[rows, 0:C] = grad_q.astype(BF)
        GQKV[rows, C : 2 * C] = grad_k.astype(BF)
        GQKV[rows, 2 * C : 3 * C] = grad_v.astype(BF)

    def fold(square):
        out = square[0:DH] * head_f[0]
        for h in range(1, NH):
            out = out + square[h * DH : (h + 1) * DH] * head_f[h]
        return out

    def unfold(flat):
        return stack(flat.astype(BF))

    def wide_lanes(column):
        return jnp.concatenate([column] * (C // 128), axis=1)

    def norm_state(b, state):
        q, k, v = qkv_block(1, b)
        ST[b] = state
        key = features(k)
        term = mm(key, (v.astype(F32) * wide_lanes(TAIL[b])).astype(BF), TN)
        return wide_lanes(KEEP[b, 0:1, :]) * state + fold(term)

    def norm_forward(b, passed):
        q, k, v = qkv_block(1, b)
        query, key = features(q), features(k)
        local = jnp.where(tall(MSK[b]) > 0.5, mm(stack(query), key, NT), 0.0).astype(BF)
        AP[1, b] = local
        state = ST[b] + passed * SIN[0].astype(F32)
        ST[b] = state
        mixed = unstack(mm(local, v)) + wide_lanes(CAR[b]) * mm(query, unfold(state))
        rows = block_rows(b)
        UU[rows, :] = mixed
        O[1, rows, :] = (mixed * lax.rsqrt(head_mean(mixed * mixed) + EPS)).astype(BF)
        return passed * wide_lanes(KEEP[b, 0:1, :])

    def norm_back_first(b, grad_o, state):
        rows = block_rows(b)
        mixed = UU[rows, :]
        scale = lax.rsqrt(head_mean(mixed * mixed) + EPS)
        grad = scale * grad_o - mixed * (scale * scale * scale) * head_mean(grad_o * mixed)
        low = grad.astype(BF)
        DU[rows, :] = low
        ST2_store(b, state)
        query = features(QKV[1, rows, 0:C])
        term = mm(query, (low.astype(F32) * wide_lanes(CAR[b])).astype(BF), TN)
        return wide_lanes(KEEP[b, 0:1, :]) * state + fold(term)

    def ST2_store(b, state):
        ST[NBH + b] = state

    def sigmoid(values):
        return 1.0 / (1.0 + jnp.exp(-values.astype(F32)))

    def norm_back_local(b):
        rows = block_rows(b)
        q, k, v = qkv_block(1, b)
        query, key = features(q), features(k)
        low = DU[rows, :]
        stacked = stack(low)
        grad_a = jnp.where(tall(MSK[b]) > 0.5, mm(stacked, v, NT), 0.0).astype(BF)
        grad_q = unstack(mm(grad_a, key)) + wide_lanes(CAR[b]) * mm(low, unfold(ST[b]), NT)
        GQKV[rows, 0:C] = (grad_q * sigmoid(q)).astype(BF)
        GQKV[rows, C : 2 * C] = (mm(grad_a, stack(query), TN) * sigmoid(k)).astype(BF)
        GQKV[rows, 2 * C : 3 * C] = mm(AP[1, b], stacked, TN).astype(BF)

    def norm_back_state(b, passed):
        rows = block_rows(b)
        q, k, v = qkv_block(1, b)
        grad_wide = unfold(ST[NBH + b] + passed * SIN[1].astype(F32))
        tail = wide_lanes(TAIL[b])
        grad_k = tail * mm(v, grad_wide, NT) * sigmoid(k)
        grad_v = tail * mm(features(k), grad_wide)
        GQKV[rows, C : 2 * C] = (GQKV[rows, C : 2 * C].astype(F32) + grad_k).astype(BF)
        GQKV[rows, 2 * C : 3 * C] = (GQKV[rows, 2 * C : 3 * C].astype(F32) + grad_v).astype(BF)
        return passed * wide_lanes(KEEP[b, 0:1, :])

    @scoped
    def masks():
        row = lax.broadcasted_iota(jnp.int32, (BLOCK, BLOCK), 0)
        col = lax.broadcasted_iota(jnp.int32, (BLOCK, BLOCK), 1)
        token = lax.broadcasted_iota(jnp.int32, (MB, BLOCK), 0)
        lane = lax.broadcasted_iota(jnp.int32, (MB, BLOCK), 1)
        start = jnp.concatenate([starts_in[zh * MH + m] for m in range(MH)], axis=0)
        start = start.astype(F32).astype(BF)
        chunk_lane = lax.broadcasted_iota(jnp.int32, (BLOCK, MH), 1)
        for j in range(NB):
            upper = ((token // BLOCK == j) & (token % BLOCK <= lane)).astype(F32).astype(BF)
            count_row = mm(start, upper)
            count_col = mm(upper, start, (((0,), (1,)), ((), ())))
            for m in range(MH):
                b = m * NB + j
                c_row = count_row[m : m + 1, :]
                c_col = jnp.sum(
                    jnp.where(chunk_lane == m, count_col, 0.0), axis=1, keepdims=True
                )
                last = jnp.sum(
                    jnp.where(col[0:1] == BLOCK - 1, c_row, 0.0), axis=1, keepdims=True
                )
                MSK[b] = jnp.where((c_row == c_col) & (row >= col), 1.0, 0.0)
                CAR[b] = jnp.broadcast_to(jnp.where(c_col == 0.0, 1.0, 0.0), (BLOCK, 128))
                TAIL[b] = jnp.broadcast_to(jnp.where(c_col == last, 1.0, 0.0), (BLOCK, 128))
                KEEP[b] = jnp.broadcast_to(jnp.where(last == 0.0, 1.0, 0.0), (8, 128))

    place = d * nt + z

    def gain_copy(i):
        return remote(GL.at[place], GL.at[place], gl_sem.at[0], gl_sem.at[1], section_dev(i))

    @scoped
    def gains_out():
        width = gain_in.shape[1]
        row = lax.broadcasted_iota(jnp.int32, (width, 128), 0)
        col = lax.broadcasted_iota(jnp.int32, (width, 128), 1)
        spot = (col % width == row) & (col // width == place % (128 // width))
        GL[place] = mm(gain_in[...].astype(BF), spot.astype(F32).astype(BF))

        def one(i, carry):
            gain_copy(i).start()
            return carry

        lax.fori_loop(1, nd * nt, one, 0)

    @scoped
    def gains_in():
        for k in (1, 0):
            got(GL.at[pl.ds(0, nd * nt - 1)], gl_sem.at[k])
        each = nd * nt * 128 // D
        for t in range(D // 128):
            total = GL[t * each]
            for i in range(1, each):
                total = total + GL[t * each + i]
            GV[s, :, t * 128 : (t + 1) * 128] = total
        gain_swap().start()

    def gain_swap():
        return remote(GV.at[s], GV.at[s], g1_sem.at[0], g1_sem.at[1], core_dev)

    def gains_other():
        gain_swap().wait_send()
        got(GV.at[1 - s], g1_sem.at[1])

    def dp_gain(step):
        return remote(
            GOWN, DL2.at[step - 1], g_ss.at[1, step - 1], g_rs.at[1, step - 1], dp_dev(step)
        )

    def core_gain():
        return remote(DG.at[1 - s], DL0, g1_sem.at[2], g1_sem.at[3], core_dev)

    def z_gain(step):
        return remote(
            DG.at[s], DL1.at[step - 1], g_ss.at[0, step - 1], g_rs.at[0, step - 1], z_dev(step)
        )

    @scoped
    def gain_second():
        core_gain().wait()
        DG[s] = DG[s] + DL0[...]
        for step in range(1, nt):
            z_gain(step).start()

    @scoped
    def gain_third():
        total = DG[s]
        for step in range(1, nt):
            z_gain(step).wait()
            total = total + DL1[step - 1]
        GOWN[...] = total
        for step in range(1, nd):
            dp_gain(step).start()

    @scoped
    def gain_final():
        total = GOWN[...]
        for step in range(1, nd):
            dp_gain(step).wait()
            total = total + DL2[step - 1]
        GOWN[...] = total
        width = out_gain.shape[1]
        each = 128 // width
        tile = GOWN[:, pl.ds(pl.multiple_of(place // each * 128, 128), 128)]
        mine = jnp.zeros((2, width), F32)
        for i in range(each):
            piece = tile[:, i * width : (i + 1) * width]
            mine = jnp.where(place % each == i, piece, mine)
        out_gain[...] = mine

    def loop(count, fn):
        def step(i, carry):
            fn(i)
            return carry

        with jax.named_scope(fn.__name__):
            lax.fori_loop(0, count, step, 0)

    def chunk(m):
        return pl.ds(pl.multiple_of(m * MB, BLOCK), MB)

    def w_cols(l, p):
        col, width = pieces[p]
        return W[l, :, col : col + width]

    def w_gate_up(l):
        return W[l, :, z_.oG : z_.oD]

    @scoped
    def state_copy(slot):
        return remote(
            SEND_STATE.at[slot],
            SIN.at[slot],
            st_ss.at[slot],
            st_rs.at[slot],
            (s, d, (z + Hn) % nt),
        )

    def state_out(slot, value, sender):
        SEND_STATE[slot] = value.astype(BF)

        @pl.when(zh == sender)
        def _():
            SIN[slot] = jnp.zeros((DH, C), BF)
            state_copy(slot).start()

    @scoped
    def state_in(slot, sender):
        @pl.when(zh != sender)
        def _():
            state_copy(slot).wait_recv()

    outer = zh == zl
    inner, far = jnp.logical_not(outer), jnp.logical_not(near)

    def only(cond, fn):
        pl.when(cond)(fn)

    def hand_far(l, cond, ps):
        def go():
            for p in ps:
                w_hand_far(l, p)

        pl.when((s == l) & cond)(go)

    def hand_near(ps):
        for l in range(2):

            @pl.when(s == l)
            def _():
                for p in ps:
                    w_hand_near(l, p)

    def x_out():
        spread_tokens(xin, XF, 0)

    gains_out()
    shard_attention()
    hand_far(0, s == 0, [5])
    hand_near([5])
    only((s == 0) & inner, x_out)
    pump_near([("s", 0, 5)])
    own_tokens(xin, XF, 0)
    own_tokens(cot, GF.at[1], 1)
    shard_feed()
    hand_far(0, inner, [2, 3, 4])
    hand_near([2, 3, 4])
    masks()
    for l in range(2):
        DG[l] = jnp.zeros((2, D), F32)
    pump_near([("s", 0, 2)])
    gains_in()
    pump_far([("s", 0, 5)])
    only((s == 0) & outer & far, x_out)
    pump([("f", 0, 5)])
    hand_far(0, outer & far, [2, 3, 4])
    pump_near([("f", 0, 2)])
    only((s == 0) & outer & near, x_out)
    only(s == 1, gains_other)
    await_tokens(XF, 0, 0)
    hand_far(0, outer & near, [2, 3, 4])

    def cot_out():
        spread_tokens(cot, GF.at[1], 1)

    stage = {
        (0, "attended"): lambda: (
            pump_near([("f", 0, 3), ("f", 0, 4)]),
            pump_far([("s", 0, 2), ("s", 0, 3), ("f", 0, 2), ("s", 0, 4)]),
        ),
        (0, "hidden"): lambda: (
            hand_far(1, inner, [5, 4, 2, 3]),
            hand_far(1, outer, [5]),
            pump_near([("s", 1, 5)]),
            pump_far([("f", 0, 3), ("f", 0, 4)]),
        ),
        (0, "ready"): lambda: (
            pump_near([("f", 1, 5)]),
            pump_far([("s", 1, 5)]),
        ),
        (0, "feeding"): lambda: (
            hand_far(1, outer, [4]),
            pump_near([("s", 1, 4)]),
        ),
        (0, "fed"): lambda: (
            hand_far(1, outer, [2, 3]),
            pump_near([("s", 1, 2), ("f", 1, 4)]),
            pump_far([("f", 1, 5), ("s", 1, 4)]),
            only(s == 0, gains_other),
        ),
        (0, "result"): lambda: (
            only(s == 1, cot_out),
            pump_near([("s", 1, 3)]),
            pump_far([("s", 1, 2), ("f", 1, 4)]),
        ),
        (1, "states"): lambda: (
            pump_near([("f", 1, 2), ("f", 1, 3)]),
            pump_far([("s", 1, 3), ("f", 1, 2)]),
        ),
        (1, "attended"): lambda: (pump_far([("f", 1, 3)]),),
        (1, "hidden"): lambda: (),
        (1, "ready"): lambda: (),
        (1, "fed"): lambda: (),
        "b1 second": lambda: (),
        "b1 middle": lambda: (d_mid(1, 4),),
        "b1 feed": lambda: (),
        "b1 third": lambda: (d_mid(1, 3), d_total_rows(1, 2)),
        "b1 end": lambda: (d_total_rows(1, 3),),
        "b0 second": lambda: (d_total_rows(1, 0),),
        "b0 middle": lambda: (),
        "b0 feed": lambda: (d_total_rows(1, 1),),
        "b0 third": lambda: (
            only(far, lambda: run(d_mid, 2)),
            only(near, lambda: run(d_mid, 4) or run(d_send, 2, 3)),
        ),
        "b0 end": lambda: (
            core_gain().start(),
            only(near, lambda: run(d_send, 0, 1)),
            gain_second(),
            only(far, lambda: far_tail()),
            only(near, lambda: near_tail()),
            gain_third(),
        ),
    }

    def run(step, *parts):
        for p in parts:
            step(0, p)

    def far_tail():
        run(d_sum, 2)
        run(d_mid, 6)
        run(d_sum, 3)
        run(d_mid, 7, 8)
        run(d_sum, 6)
        run(d_mid, 1)
        run(d_sum, 7, 8, 1)

    def near_tail():
        run(d_sum, 4)
        run(d_mid, 2, 3, 6, 7, 8, 1)
        run(d_sum, 2, 3, 6, 7, 8, 1)

    def input_rows(l, m):
        if l == 0:
            return XF[chunk_rows(m, own), :].astype(F32)
        return Y[0, own_rows(m), :].astype(F32)

    def gate_up_grad(grad, both):
        parts = [grad * both[:, F : 2 * F], grad * both[:, :F]]
        if z_.GUw > 2 * F:
            parts.append(jnp.zeros((MB, z_.GUw - 2 * F), F32))
        return jnp.concatenate(parts, axis=1).astype(BF)

    def finish_layer(l, rs2, ag3):
        def result(m):
            rows = (H[l, own_rows(m), :] + rs_third(rs2, m)).astype(BF)
            Y[l, own_rows(m), :] = rows
            send_out(Y, l, out_y, 0, m)
            if l == 0:
                wide = rows.astype(F32)
                N1[1, chunk_rows(m, own), :] = (wide * rms(wide) * gain(1, 0)).astype(BF)
                ag_send(ag3, N1.at[1], m)

        loop(MH, result)

    def forward(l, ag1, rs1, ag2, rs2, ag3):
        w_ready(l, 5)

        def qkv_chunk(m):
            if l == 0:
                pl.when(m > 0)(lambda: await_tokens(XF, 0, m))
                pl.when((m == 1) & near)(lambda: pump([("s", 0, 3), ("s", 0, 4)]))
                rows = XF[chunk(m), :].astype(F32)
                N1[0, chunk(m), :] = (rows * rms(rows) * gain(0, 0)).astype(BF)
            else:
                ag_forward(ag1, N1.at[1], m)
                ag_wait(ag1, N1.at[1], m)
            QKV[l, chunk(m), :] = mm(N1[l, chunk(m), :], w_cols(l, 0)).astype(BF)

        def out_chunk(m):
            rs_first(rs1, m, mm(O[l, chunk(m), :], w_cols(l, 1), NT))

        if l == 0:

            def attend(m):
                qkv_chunk(m)
                for i in range(NB):
                    diag_forward(m * NB + i)
                out_chunk(m)
                after(rs1, m, m - 1)

            loop(MH, attend)
            rs_second(rs1, MH - 1)
            stage[l, "attended"]()
        else:

            def states(m, state):
                qkv_chunk(m)
                for i in range(NB):
                    state = norm_state(m * NB + i, state)
                return state

            with jax.named_scope('states'):
                last = lax.fori_loop(0, MH, states, jnp.zeros((DH, C), F32))
            w_handed_out()
            state_out(0, last, 0)
            state_in(0, 0)
            stage[l, "states"]()

            def attend(m, passed):
                for i in range(NB):
                    passed = norm_forward(m * NB + i, passed)
                out_chunk(m)
                after(rs1, m, m - 1)
                return passed

            with jax.named_scope('attend'):
                lax.fori_loop(0, MH, attend, jnp.ones((1, C), F32))
            rs_second(rs1, MH - 1)
            stage[l, "attended"]()

        def hidden_rows(m):
            rows = input_rows(l, m) + rs_third(rs1, m)
            H[l, own_rows(m), :] = rows
            N2[l, chunk_rows(m, own), :] = (rows * rms(rows) * gain(l, 1)).astype(BF)
            ag_send(ag2, N2.at[l], m)

        loop(MH, hidden_rows)
        stage[l, "hidden"]()
        w_ready(l, 4)
        if l == 1:

            def hidden_grad(m):
                await_tokens(GF.at[1], 1, m)
                GGU[chunk(m), 0 : z_.Dw] = mm(GF[1, chunk(m), :], w_cols(1, 4)).astype(BF)

            loop(MH, hidden_grad)
        w_ready(l, 2)
        w_ready(l, 3)
        stage[l, "ready"]()

        def feed(m):
            ag_forward(ag2, N2.at[l], m)
            ag_wait(ag2, N2.at[l], m)
            rows = N2[l, chunk(m), :]
            both = mm(rows, w_gate_up(l))
            if l == 0:
                GU[l, chunk(m), :] = both.astype(BF)
            else:
                grad = GGU[chunk(m), 0 : z_.Dw].astype(F32)[:, :F]
                GGU[chunk(m), :] = gate_up_grad(grad, both)
            hidden = both[:, :F] * both[:, F : 2 * F]
            if z_.Dw > F:
                hidden = jnp.concatenate([hidden, jnp.zeros((MB, z_.Dw - F), F32)], axis=1)
            hidden = hidden.astype(BF)
            HID[l, chunk(m), :] = hidden
            rs_first(rs2, m, mm(hidden, w_cols(l, 4), NT))
            if l == 0:


                @pl.when(m == 1)
                def _():
                    stage[0, "feeding"]()

            after(rs2, m, m - 1)

        loop(MH, feed)
        rs_second(rs2, MH - 1)
        stage[l, "fed"]()

        if l == 0:
            finish_layer(l, rs2, ag3)
            stage[l, "result"]()

    forward(0, None, 0, 0, 1, 1)
    forward(1, 1, 2, 2, 3, None)

    RB = min(D, 256)

    @scoped
    def grad_weight(l, p, left, right, send=True):
        col, width = pieces[p]
        for r in range(D // RB):
            W[l, r * RB : (r + 1) * RB, col : col + width] = mm(
                left[:, r * RB : (r + 1) * RB], right, TN
            ).astype(BF)
        if send:
            d_send(l, p)

    def rest(l, p):
        for q in range(MH, 4):
            d_pass(l, p, q)

    def grad_part(l, p, send=True):
        col, width = pieces[p]
        grad_weight(l, p, N2[l], GGU[:, col - z_.oG : col - z_.oG + width], send)

    def backward(l, ag_in, rs1, ag2, rs2, ag_out):
        w_shared(l)

        def feed_back(i):
            m = MH - 1 - i
            if l == 0:
                ag_forward(ag_in, GF.at[0], m)
                ag_wait(ag_in, GF.at[0], m)
                grad = mm(GF[l, chunk(m), :], w_cols(l, 4))[:, :F]
                GGU[chunk(m), :] = gate_up_grad(grad, GU[l, chunk(m), :].astype(F32))
            rs_first(rs1, m, mm(GGU[chunk(m), :], w_gate_up(l), NT))
            after(rs1, i, m + 1)
            if l == 0:

                @pl.when(i == 0)
                def _():
                    d_mid(1, 1)
                    d_mid(1, 0)

                d_pass(1, 3, i)
        if l == 1:
            grad_weight(l, 4, GF[l], HID[l])
        loop(MH, feed_back)
        rs_second(rs1, 0)
        if l == 0:
            rest(1, 3)
            grad_weight(l, 4, GF[l], HID[l], False)
            only(far, lambda: d_send(0, 4))
        else:
            grad_part(l, 2)
            finish_layer(1, 3, None)
        stage[f"b{l} second"]()

        def middle(i):
            m = MH - 1 - i
            rows = H[l, own_rows(m), :]
            grad = GF[l, chunk_rows(m, own), :].astype(F32) + rms_back(
                l, 1, rows, rs_third(rs1, m)
            )
            GH[own_rows(m), :] = grad
            GA[l, chunk_rows(m, own), :] = grad.astype(BF)
            ag_send(ag2, GA.at[l], m)
            if l == 0:
                only((i == 1) & near, lambda: d_send(0, 4))
                d_pass(1, 0, i)

        loop(MH, middle)
        if l == 0:
            rest(1, 0)
        stage[f"b{l} middle"]()
        if l == 0:
            grad_part(l, 2, False)

            @pl.when(far)
            def _():
                d_mid(0, 4)
                d_send(0, 2)

            grad_part(l, 3, False)
            only(far, lambda: d_send(0, 3))
        else:
            grad_part(l, 3)
        stage[f"b{l} feed"]()

        def grad_o(m):
            ag_forward(ag2, GA.at[l], m)
            ag_wait(ag2, GA.at[l], m)
            return mm(GA[l, chunk(m), :], w_cols(l, 1))

        def qkv_back(i, m):
            rs_first(rs2, m, mm(GQKV[chunk(m), :], w_cols(l, 0), NT))
            after(rs2, i, m + 1)

        if l == 0:

            def attend(i):
                m = MH - 1 - i
                grad = grad_o(m)
                for j in range(NB):
                    diag_backward(m * NB + j, grad[j * BLOCK : (j + 1) * BLOCK])
                qkv_back(i, m)
                d_pass(1, 1, i)
                only((i == 0) & far, lambda: d_sum(0, 4))

            loop(MH, attend)
        else:

            def states(i, state):
                m = MH - 1 - i
                grad = grad_o(m)
                for j in reversed(range(NB)):
                    state = norm_back_first(m * NB + j, grad[j * BLOCK : (j + 1) * BLOCK], state)
                return state

            with jax.named_scope("states"):
                last = lax.fori_loop(0, MH, states, jnp.zeros((DH, C), F32))
            state_out(1, last, 1)
            d_mid(1, 2)
            grad_weight(l, 1, GA[l], O[l])
            d_total_rows(1, 4)

            def attend_local(m):
                for j in range(NB):
                    norm_back_local(m * NB + j)

            loop(MH, attend_local)
            state_in(1, 1)
            pl.when(zh == 0)(lambda: d_pass(1, 4, 0, Dr))

            def attend(i, passed):
                m = MH - 1 - i
                for j in reversed(range(NB)):
                    passed = norm_back_state(m * NB + j, passed)
                qkv_back(i, m)

                @pl.when(zh == 1)
                def _():
                    d_pass(1, 4, i)

                return passed

            with jax.named_scope("attend"):
                lax.fori_loop(0, MH, attend, jnp.ones((1, C), F32))

        rs_second(rs2, 0)
        if l == 0:
            rest(1, 1)
        else:
            pl.when(zh == 1)(lambda: rest(1, 4))
        stage[f"b{l} third"]()
        grad_weight(l, 0, N1[l], GQKV[...], l == 1)
        if l == 0:
            grad_weight(l, 1, GA[l], O[l], False)

            @pl.when(far)
            def _():
                d_mid(0, 3)
                d_send(0, 0)
                d_send(0, 1)


        def result(i):
            m = MH - 1 - i
            grad = GH[own_rows(m), :] + rms_back(l, 0, input_rows(l, m), rs_third(rs2, m))
            low = grad.astype(BF)
            GX[l, own_rows(m), :] = low
            send_out(GX, l, out_g, 1, m)
            if l == 1:
                GF[0, chunk_rows(m, own), :] = low
                ag_send(ag_out, GF.at[0], m)
                d_pass(1, 2, i)

        loop(MH, result)
        if l == 1:
            rest(1, 2)
        stage[f"b{l} end"]()

    backward(1, None, 4, 3, 5, 4)
    backward(0, 4, 6, 5, 7, None)

    for p in (4, 2, 3, 6, 7, 8, 1):
        d_final(p)
    gain_final()
    for copy in outs:
        copy.wait()
    for l in range(2):
        d_sent(l)

    ags = ((0, N2.at[0]), (1, N1.at[1]), (2, N2.at[1]), (3, GA.at[1]), (4, GF.at[0]), (5, GA.at[0]))

    for slot in range(2):

        @pl.when(zh == slot)
        def _():
            state_copy(slot).wait_send()

    for k, buf in ags:
        ag_sent(k, buf)
    for l in range(2):

        @pl.when(jnp.logical_not((s == l) & (zh == s)))
        def _():
            got(XF.at[pl.ds(0, 2 * MH * R)], o_ss.at[l])

    for half in range(2):
        got(out_y.at[pl.ds(half * MH, MH)], o_rs.at[0, half])
        got(out_g.at[pl.ds(half * MH, MH)], o_rs.at[1, half])
    for k in range(2):
        got(XF.at[pl.ds(0, MH * (nt - 1) * R)], x_sem.at[k])


def place_results(*refs):
    count = (len(refs) - 2) // 3
    sources, targets, held = refs[:count], refs[count : 2 * count], refs[2 * count : 3 * count]
    in_sem, out_sem = refs[-2:]
    reads = [pltpu.make_async_copy(sources[i], held[i], in_sem.at[i]) for i in range(count)]
    writes = [pltpu.make_async_copy(held[i], targets[i], out_sem.at[i]) for i in range(count)]
    for copy in reads:
        copy.start()
    for read, write in zip(reads, writes):
        read.wait()
        write.start()
    for copy in writes:
        copy.wait()


def solution(mesh):
    nd, nt = mesh.shape["dp"], mesh.shape["tensor"]

    def on_device(inputs, starts, cotangent, qkv_m, out_m, gateup_m, down_m, gain_m):
        z_ = Sizes(
            mesh,
            inputs.shape[3],
            inputs.shape[1],
            inputs.shape[2],
            qkv_m.shape[3],
            gateup_m.shape[3],
        )
        D, R, C, F, Dr, M, MH, Hn, MB, T, NBH, N, NH = (
            z_.D,
            z_.R,
            z_.C,
            z_.F,
            z_.Dr,
            z_.M,
            z_.MH,
            z_.Hn,
            z_.MB,
            z_.T,
            z_.NBH,
            z_.N,
            z_.NH,
        )
        width = gain_m.shape[2]
        qkv_rows = jnp.transpose(qkv_m[0], (1, 0, 2))
        gateup_rows = jnp.transpose(gateup_m[0], (1, 2, 0)).reshape(2 * F, Dr)
        anywhere = pl.BlockSpec(memory_space=pl.ANY)
        vmem = pl.BlockSpec(memory_space=pltpu.VMEM)
        DMA = pltpu.SemaphoreType.DMA
        V = pltpu.VMEM
        scratch = [
            V((3, Dr, C), F32),
            V((C, Dr), F32),
            V((2 * F, Dr), F32),
            V((F, Dr), F32),
            V((2, D, N), BF),
            V((2, nd - 1, Dr, N), BF),
            V((2, Dr, N), BF),
            V((T, D), BF),
            V((2, T, D), BF),
            V((2, T, D), BF),
            V((2, T, D), BF),
            V((2, T, 3 * C), BF),
            V((2, T, C), BF),
            V((1, T, z_.GUw), BF),
            V((2, T, z_.Dw), BF),
            V((2, MH * R, D), F32),
            V((2, MH * R, D), BF),
            V((2, T, D), BF),
            V((T, z_.GUw), BF),
            V((T, 3 * C), BF),
            V((MH * R, D), F32),
            V((2, MH * R, D), BF),
            V((2, T, D), BF),
            V((2, MH, Hn * R, D), BF),
            V((2, MH, Hn - 1, R, D), BF),
            V((2, MH, Hn - 1, R, D), BF),
            V((2, NBH, NH * BLOCK, BLOCK), BF),
            V((T, C), F32),
            V((T, C), BF),
            V((2 * NBH, DH, C), F32),
            V((2, DH, C), BF),
            V((2, DH, C), BF),
            V((NBH, BLOCK, BLOCK), F32),
            V((NBH, BLOCK, 128), F32),
            V((NBH, BLOCK, 128), F32),
            V((NBH, 8, 128), F32),
            V((nd * nt, 2, 128), F32),
            V((2, 2, D), F32),
            V((2, D), F32),
            V((2, 2, D), F32),
            V((2, D), F32),
            V((nt - 1, 2, D), F32),
            V((nd - 1, 2, D), F32),
            DMA((2, MH)),
            DMA((2,)),
            DMA((2, MH, nt - 1)),
            DMA((2,)),
            DMA((2, 4)),
            DMA((2,)),
            DMA((2, 4, max(4, nd - 1))),
            DMA((6,)),
            DMA((6, MH, Hn)),
            DMA((2, MH)),
            DMA((2, MH)),
            DMA((2, MH, Hn - 1)),
            DMA((2, MH, Hn - 1)),
            DMA((2,)),
            DMA((2,)),
            DMA((2,)),
            DMA((2, 2)),
            DMA((2,)),
            DMA((2, 7, 3)),
            DMA((2,)),
            DMA((7, 2)),
            DMA((4,)),
            DMA((2, max(nd, nt) - 1)),
            DMA((2, max(nd, nt) - 1)),
            DMA((2,)),
            DMA((4,)),
        ]
        out_y, out_g, grad_qkv, grad_o, grad_gu, grad_d, grad_gain = pl.pallas_call(
            functools.partial(body, z_),
            out_shape=(
                jax.ShapeDtypeStruct((M, R, D), BF),
                jax.ShapeDtypeStruct((M, R, D), BF),
                jax.ShapeDtypeStruct((3, Dr, C), F32),
                jax.ShapeDtypeStruct((C, Dr), F32),
                jax.ShapeDtypeStruct((2 * F, Dr), F32),
                jax.ShapeDtypeStruct((F, Dr), F32),
                jax.ShapeDtypeStruct((2, width), F32),
            ),
            in_specs=[anywhere] * 6 + [vmem, vmem],
            out_specs=(anywhere,) * 6 + (vmem,),
            scratch_shapes=scratch,
            compiler_params=pltpu.CompilerParams(
                collective_id=0, has_side_effects=True, vmem_limit_bytes=63 * 1024 * 1024
            ),
        )(
            qkv_rows,
            out_m[0],
            gateup_rows,
            down_m[0],
            inputs[0],
            cotangent[0],
            jnp.transpose(starts, (1, 0, 2)),
            gain_m[0],
        )
        results = (out_y, out_g, grad_qkv, grad_o, grad_gu, grad_d, grad_gain)
        out_y, out_g, grad_qkv, grad_o, grad_gu, grad_d, grad_gain = pl.pallas_call(
            place_results,
            out_shape=tuple(jax.ShapeDtypeStruct(r.shape, r.dtype) for r in results),
            in_specs=[anywhere] * len(results),
            out_specs=(anywhere,) * len(results),
            scratch_shapes=[V(r.shape, r.dtype) for r in results]
            + [DMA((len(results),)), DMA((len(results),))],
        )(*results)
        return (
            out_y[None, None],
            out_g[None, None],
            jnp.transpose(grad_qkv, (1, 0, 2))[None],
            grad_o[None],
            jnp.transpose(grad_gu.reshape(2, F, Dr), (2, 0, 1))[None],
            grad_d[None],
            grad_gain[None],
        )

    return jax.shard_map(
        on_device,
        mesh=mesh,
        in_specs=(
            P("dp", None, "tensor", None),
            P("dp", None, None),
            P("dp", None, "tensor", None),
            P("section", "dp", None, "tensor"),
            P("section", "tensor", "dp"),
            P("section", "dp", None, "tensor"),
            P("section", "tensor", "dp"),
            P("section", None, ("dp", "tensor")),
        ),
        out_specs=(
            P("section", "dp", None, "tensor", None),
            P("section", "dp", None, "tensor", None),
            P("section", "dp", None, "tensor"),
            P("section", "tensor", "dp"),
            P("section", "dp", None, "tensor"),
            P("section", "tensor", "dp"),
            P("section", None, ("dp", "tensor")),
        ),
        check_vma=False,
    )
```

```python
import functools
import math

import jax
import jax.numpy as jnp
from jax import lax
from jax.experimental import pallas as pl
from jax.experimental.pallas import tpu as pltpu
from jax.sharding import PartitionSpec as P

DH = 64
BLOCK = 64
EPS = 1e-6
BF = jnp.bfloat16
F32 = jnp.float32
MESH = pl.DeviceIdType.MESH
NN = (((1,), (0,)), ((), ()))
NT = (((1,), (1,)), ((), ()))
TN = (((0,), (0,)), ((), ()))


def mm(a, b, dims=NN):
    return lax.dot_general(a, b, dims, preferred_element_type=F32)


def ceil_to(value, unit):
    return (value + unit - 1) // unit * unit


def scoped(fn):
    @functools.wraps(fn)
    def inner(*args):
        with jax.named_scope(fn.__name__):
            return fn(*args)

    return inner


class Sizes:
    def __init__(self, mesh, model, micro, rows, cols, hidden):
        self.nd, self.nt = mesh.shape["dp"], mesh.shape["tensor"]
        self.D, self.M, self.R, self.C, self.F = model, micro, rows, cols, hidden
        self.GUw, self.Dw = ceil_to(2 * hidden, 128), ceil_to(hidden, 128)
        self.Dr = model // self.nd
        self.MH, self.Hn = micro // 2, self.nt // 2
        self.MB = rows * self.nt
        self.T = self.MH * self.MB
        self.NH = cols // DH
        self.NB = self.MB // BLOCK
        self.NBH = self.MH * self.NB
        self.oO, self.oG = 3 * cols, 4 * cols
        self.oD = self.oG + self.GUw
        self.N = self.oD + self.Dw
        first = ceil_to(self.GUw // 2, 128)
        self.pieces = (
            (0, 3 * cols),
            (self.oO, cols),
            (self.oG, first),
            (self.oG + first, self.GUw - first),
            (self.oD, self.Dw),
            (0, 4 * cols),
            (0, cols),
            (cols, cols),
            (2 * cols, cols),
        )


def body(
    z_,
    qkv_in,
    o_in,
    gu_in,
    d_in,
    xin,
    cot,
    starts_in,
    gain_in,
    out_y,
    out_g,
    out_qkv,
    out_o,
    out_gu,
    out_d,
    out_gain,
    MQ,
    MO,
    MGU,
    MD,
    W,
    LW,
    L2,
    XF,
    GF,
    N1,
    N2,
    QKV,
    O,
    GU,
    HID,
    H,
    Y,
    GA,
    GGU,
    GQKV,
    GH,
    GX,
    PT,
    RL1,
    RL2,
    RSB,
    AP,
    UU,
    DU,
    ST,
    SIN,
    SEND_STATE,
    MSK,
    CAR,
    TAIL,
    KEEP,
    GL,
    GV,
    GOWN,
    DG,
    DL0,
    DL1,
    DL2,
    in_sem,
    x_sem,
    x_rs,
    w1_ss,
    w1_rs,
    w2_ss,
    w2_rs,
    ag_ss,
    ag_rs,
    r1_ss,
    r1_rs,
    r2_ss,
    r2_rs,
    st_ss,
    st_rs,
    o_ss,
    o_rs,
    d1_ss,
    d1_rs,
    d2_ss,
    d2_rs,
    g1_sem,
    g_ss,
    g_rs,
    gl_sem,
    m_sem,
):
    D, R, C, F, Dr, MH, Hn, MB, T, NH, NB, NBH = (
        z_.D,
        z_.R,
        z_.C,
        z_.F,
        z_.Dr,
        z_.MH,
        z_.Hn,
        z_.MB,
        z_.T,
        z_.NH,
        z_.NB,
        z_.NBH,
    )
    nd, nt = z_.nd, z_.nt
    pieces = z_.pieces
    s, d, z = lax.axis_index("section"), lax.axis_index("dp"), lax.axis_index("tensor")
    zh, zl = z // Hn, z % Hn
    own = s * Hn + zl
    core_dev = (1 - s, d, z)

    def remote(src, dst, ssem, rsem, dev):
        return pltpu.make_async_remote_copy(
            src_ref=src, dst_ref=dst, send_sem=ssem, recv_sem=rsem, device_id=dev, device_id_type=MESH
        )

    def got(dst, sem):
        pltpu.make_async_copy(dst, dst, sem).wait()

    def dp_dev(step):
        return (s, (d + step) % nd, z)

    def z_dev(step):
        return (s, d, (z + step) % nt)

    def peer_zl(step):
        return (zl + step) % Hn

    masters = (
        pltpu.make_async_copy(qkv_in, MQ, m_sem.at[0]),
        pltpu.make_async_copy(o_in, MO, m_sem.at[1]),
        pltpu.make_async_copy(gu_in, MGU, m_sem.at[2]),
        pltpu.make_async_copy(d_in, MD, m_sem.at[3]),
    )
    for copy in masters:
        copy.start()

    barrier = pltpu.get_barrier_semaphore()

    def section_dev(i):
        return (s, (d + i // nt) % nd, (z + i % nt) % nt)

    def greet(i, carry):
        pl.semaphore_signal(barrier, inc=1, device_id=section_dev(i), device_id_type=MESH)
        return carry

    lax.fori_loop(1, nd * nt, greet, 0)
    pl.semaphore_signal(barrier, inc=1, device_id=core_dev, device_id_type=MESH)
    far_dev = (1 - s, d, (z + Hn) % nt)
    pl.semaphore_signal(barrier, inc=1, device_id=far_dev, device_id_type=MESH)
    pl.semaphore_wait(barrier, nd * nt + 1)

    def own_tokens(src, dst, array):
        for m in range(MH):
            mine = dst.at[pl.ds(m * MB + z * R, R)]
            pltpu.make_async_copy(src.at[zh * MH + m], mine, in_sem.at[array, m]).start()

    def spread_tokens(src, dst, array):
        for m in range(MH):
            mine = dst.at[pl.ds(m * MB + z * R, R)]
            for step in range(1, nt):
                other = (z + step) % nt

                @pl.when((other // Hn == zh) | (step == Hn))
                def _():
                    remote(
                        src.at[(other // Hn) * MH + m],
                        mine,
                        x_sem.at[0],
                        x_rs.at[array, m, step - 1],
                        z_dev(step),
                    ).start()

    def relay_tokens(dst, array, m):
        @pl.when(s == array)
        def _():
            chip = (z + Hn) % nt
            rows = dst.at[pl.ds(m * MB + chip * R, R)]
            got(rows, x_rs.at[array, m, Hn - 1])
            for step in range(1, Hn):
                peer = zh * Hn + peer_zl(step)
                remote(
                    rows,
                    rows,
                    x_sem.at[0],
                    x_rs.at[array, m, (peer + nt - chip) % nt - 1],
                    (s, d, peer),
                ).start()

    def await_tokens(dst, array, m):
        got(dst.at[pl.ds(m * MB + z * R, R)], in_sem.at[array, m])
        for step in range(1, nt):
            rows = dst.at[pl.ds(m * MB + (z + nt - step) % nt * R, R)]
            if step == Hn:
                pl.when(s != array)(lambda: got(rows, x_rs.at[array, m, step - 1]))
            else:
                got(rows, x_rs.at[array, m, step - 1])

            @pl.when(s == array)
            def _():
                remote(
                    rows, rows, x_sem.at[1], x_rs.at[array, m, step - 1], core_dev
                ).start()

    spot = {5: 0, 2: 1, 3: 2, 4: 3}

    def w_rows(l, block, p):
        col, width = pieces[p]
        return W.at[l, pl.ds(block * Dr, Dr), pl.ds(col, width)]

    def shard_cols(p):
        col, width = pieces[p]
        return L2.at[0, :, pl.ds(col, width)]

    def w_hand_near(l, p):
        @pl.when(zh == s)
        def _():
            pltpu.make_async_copy(shard_cols(p), w_rows(l, d, p), w1_rs.at[l, spot[p]]).start()

        @pl.when(zh != s)
        def _():
            w_hand(l, p, 0, core_dev).start()

    def w_hand(l, p, which, dev):
        return remote(
            shard_cols(p), w_rows(l, d, p), w1_ss.at[which], w1_rs.at[l, spot[p]], dev
        )

    def w_hand_far(l, p):
        w_hand(l, p, 1, (zh, d, (z + Hn) % nt)).start()

    def w_handed_out():
        @pl.when(zh != s)
        def _():
            got(L2.at[0], w1_ss.at[0])

        got(L2.at[0], w1_ss.at[1])

    square = nd == 4
    half_rows = Dr // 2
    dp_x, dp_y = d + 1 - 2 * (d % 2), (d + 2) % nd

    def w_half(l, block, half, p):
        col, width = pieces[p]
        return W.at[l, pl.ds(block * Dr + half * half_rows, half_rows), pl.ds(col, width)]

    def w_copy(l, p, k):
        if not square:
            rows, dev = w_rows(l, d, p), dp_dev(k + 1)
        elif k < 2:
            rows, dev = w_rows(l, d, p), (s, (dp_x, dp_y)[k], z)
        elif k == 2:
            rows, dev = w_half(l, dp_x, 0, p), (s, dp_y, z)
        else:
            rows, dev = w_half(l, dp_y, 1, p), (s, dp_x, z)
        return remote(rows, rows, w2_ss.at[l], w2_rs.at[l, spot[p], k], dev)

    def w_share(l, p):
        got(w_rows(l, d, p), w1_rs.at[l, spot[p]])
        for k in range(2 if square else nd - 1):
            w_copy(l, p, k).start()

    def w_forward(l, p):
        if square:
            got(w_rows(l, dp_x, p), w2_rs.at[l, spot[p], 0])
            w_copy(l, p, 2).start()
            got(w_rows(l, dp_y, p), w2_rs.at[l, spot[p], 1])
            w_copy(l, p, 3).start()

    def w_ready(l, p):
        if square:
            got(w_half(l, 3 - d, 0, p), w2_rs.at[l, spot[p], 2])
            got(w_half(l, 3 - d, 1, p), w2_rs.at[l, spot[p], 3])
        else:
            for step in range(1, nd):
                got(w_rows(l, (d + nd - step) % nd, p), w2_rs.at[l, spot[p], step - 1])

    def w_shared(l):
        got(W.at[l, pl.ds(0, (nd - 1) * Dr)], w2_ss.at[l])

    def pump(ops):
        for what, l, p in ops:
            with jax.named_scope(what + str(l) + str(p)):
                {"s": w_share, "f": w_forward}[what](l, p)

    near = s == zh
    gathered = (5, 2, 3, 4)

    def pump_near(ops):
        pl.when(near)(lambda: pump(ops))

    def pump_far(ops):
        pl.when(jnp.logical_not(near))(lambda: pump(ops))

    where = {4: 0, 2: 1, 3: 2, 1: 3, 6: 4, 7: 5, 8: 6}

    def split(p):
        return (6, 7, 8) if p == 0 else (p,)

    def d_copy(l, p, k):
        col, width = pieces[p]
        cols = pl.ds(col, width)
        if not square:
            src, dst, dev = w_rows(l, (d + k + 1) % nd, p), LW.at[l, k, :, cols], dp_dev(k + 1)
        else:
            first, second = pl.ds(0, half_rows), pl.ds(half_rows, half_rows)
            block, half, slot, rows, to = (
                (3 - d, 0, 2, first, dp_x),
                (3 - d, 1, 2, second, dp_y),
                (dp_x, 0, 0, first, dp_x),
                (dp_y, 1, 1, second, dp_y),
                (dp_y, 0, 1, first, dp_y),
                (dp_x, 1, 0, second, dp_x),
            )[k]
            src, dst, dev = w_half(l, block, half, p), LW.at[l, slot, rows, cols], (s, to, z)
        group = k if square and k < 2 else 2
        return remote(src, dst, d1_ss.at[l], d1_rs.at[l, where[p], group], dev)

    def d_send(l, p):
        for part in split(p):
            for k in range(4 if square else nd - 1):
                d_copy(l, part, k).start()

    @scoped
    def d_mid(l, p):
        if p == 0:
            for part in split(p):
                d_mid(l, part)
        elif square:
            col, width = pieces[p]
            cols = pl.ds(col, width)
            for k, block, half in ((0, dp_y, 0), (1, dp_x, 1)):
                copy = d_copy(l, p, k)
                copy.wait_recv()
                rows = pl.ds(block * Dr + half * half_rows, half_rows)
                arrived = LW[l, 2, half * half_rows : (half + 1) * half_rows, cols]
                W[l, rows, cols] = (W[l, rows, cols].astype(F32) + arrived.astype(F32)).astype(BF)
                d_copy(l, p, 4 + k).start()

    part_rows = Dr // 4

    def d_pass(l, p, q, rows=part_rows):
        for part in split(p):
            col, width = pieces[part]
            cols = pl.ds(col, width)
            src = W.at[l, pl.ds(d * Dr + q * rows, rows), cols]
            dst = L2.at[zh, pl.ds(q * rows, rows), cols]
            arrival = d2_rs.at[where[part], zh]
            to_self = (s == l) & (zh == s)

            @pl.when(to_self)
            def _():
                pltpu.make_async_copy(src, dst, arrival).start()

            @pl.when(jnp.logical_not(to_self))
            def _():
                remote(src, dst, d2_ss.at[l], arrival, (l, d, s * Hn + zl)).start()

    @scoped
    def d_total_rows(l, p):
        for part in split(p):
            col, width = pieces[part]
            cols = pl.ds(col, width)
            slots = 2 if square else nd - 1
            got(LW.at[l, pl.ds(0, slots), :, cols], d1_rs.at[l, where[part], 2])
            rows = pl.ds(d * Dr, Dr)
            total = W[l, rows, cols].astype(F32)
            for slot in range(slots):
                total = total + LW[l, slot, :, cols].astype(F32)
            W[l, rows, cols] = total.astype(BF)

    def d_sum(l, p):
        d_total_rows(l, p)
        d_pass(l, p, 0, Dr)

    def d_sent(l):
        got(W.at[l, pl.ds(0, (nd - 1) * Dr)], d1_ss.at[l])

        @pl.when(jnp.logical_not((s == l) & (zh == s)))
        def _():
            got(W.at[l, pl.ds(0, Dr)], d2_ss.at[l])

    outs = (
        pltpu.make_async_copy(MQ, out_qkv, m_sem.at[0]),
        pltpu.make_async_copy(MO, out_o, m_sem.at[1]),
        pltpu.make_async_copy(MGU, out_gu, m_sem.at[2]),
        pltpu.make_async_copy(MD, out_d, m_sem.at[3]),
    )

    def d_arrived(p):
        col, width = pieces[p]
        for half in range(2):
            got(L2.at[half, :, pl.ds(col, width)], d2_rs.at[where[p], half])

    def d_total(col, width):
        return L2[0, :, col : col + width].astype(F32) + L2[1, :, col : col + width].astype(F32)

    @scoped
    def d_final(p):
        d_arrived(p)
        if p >= 6:
            j = p - 6
            MQ[j] = d_total(j * C, C)
            pltpu.make_async_copy(MQ.at[j], out_qkv.at[j], m_sem.at[0]).start()
        elif p == 1:
            MO[...] = d_total(z_.oO, C).T
            outs[1].start()
        elif p == 3:
            MGU[...] = d_total(z_.oG, z_.GUw).T[: 2 * F]
            outs[2].start()
        elif p == 4:
            MD[...] = d_total(z_.oD, z_.Dw).T[:F]
            outs[3].start()

    @scoped
    def shard_attention():
        masters[0].wait()
        masters[1].wait()
        for j in range(3):
            L2[0, :, j * C : (j + 1) * C] = MQ[j].astype(BF)
        L2[0, :, z_.oO : z_.oG] = MO[...].T.astype(BF)

    @scoped
    def shard_feed():
        masters[2].wait()
        masters[3].wait()
        for ref, col, width, rows in ((MGU, z_.oG, z_.GUw, 2 * F), (MD, z_.oD, z_.Dw, F)):
            value = ref[...]
            if width > rows:
                value = jnp.concatenate([value, jnp.zeros((width - rows, Dr), F32)], axis=0)
            L2[0, :, col : col + width] = value.T.astype(BF)

    def chunk_rows(m, c):
        return pl.ds(m * MB + c * R, R)

    def ag_send(k, buf, m):
        rows = buf.at[chunk_rows(m, own)]
        for step in range(1, Hn):
            dev = (s, d, zh * Hn + peer_zl(step))
            remote(rows, rows, ag_ss.at[k], ag_rs.at[k, m, Hn - step], dev).start()
        remote(rows, rows, ag_ss.at[k], ag_rs.at[k, m, 0], core_dev).start()

    def ag_forward(k, buf, m):
        for step in range(1, Hn):
            rows = buf.at[chunk_rows(m, s * Hn + peer_zl(step))]
            got(rows, ag_rs.at[k, m, step])
            remote(rows, rows, ag_ss.at[k], ag_rs.at[k, m, 0], core_dev).start()

    def ag_wait(k, buf, m):
        got(buf.at[pl.ds(m * MB + (1 - s) * Hn * R, Hn * R)], ag_rs.at[k, m, 0])

    def ag_sent(k, buf):
        got(buf.at[pl.ds(0, MH * (2 * Hn - 1) * R)], ag_ss.at[k])

    def rs_copy1(k, m):
        par = k % 2
        return remote(
            PT.at[par, pl.ds(m * MB + (1 - s) * Hn * R, Hn * R)],
            RL1.at[par, m],
            r1_ss.at[par, m],
            r1_rs.at[par, m],
            core_dev,
        )

    def rs_copy2(k, m, step):
        par = k % 2
        return remote(
            RSB.at[par, m, step - 1],
            RL2.at[par, m, step - 1],
            r2_ss.at[par, m, step - 1],
            r2_rs.at[par, m, step - 1],
            (s, d, zh * Hn + peer_zl(step)),
        )

    def rs_first(k, m, value):
        PT[k % 2, pl.ds(m * MB, MB), :] = value.astype(BF)
        rs_copy1(k, m).start()

    def rs_second(k, m):
        par = k % 2
        copy = rs_copy1(k, m)
        copy.wait_send()
        copy.wait_recv()
        for step in range(1, Hn):
            there = peer_zl(step)
            part = PT[par, chunk_rows(m, s * Hn + there), :].astype(F32) + RL1[
                par, m, pl.ds(there * R, R), :
            ].astype(F32)
            RSB[par, m, step - 1] = part.astype(BF)
            rs_copy2(k, m, step).start()

    def after(k, i, m):
        @pl.when(i > 0)
        def _():
            rs_second(k, m)

    def rs_third(k, m):
        par = k % 2
        total = PT[par, chunk_rows(m, own), :].astype(F32) + RL1[
            par, m, pl.ds(zl * R, R), :
        ].astype(F32)
        for step in range(1, Hn):
            copy = rs_copy2(k, m, step)
            copy.wait_send()
            copy.wait_recv()
            total = total + RL2[par, m, step - 1].astype(F32)
        return total

    def own_rows(m):
        return pl.ds(m * R, R)

    def rms(rows):
        return lax.rsqrt(jnp.mean(rows * rows, axis=-1, keepdims=True) + EPS)

    def gain(l, which):
        return GV[l, which : which + 1, :]

    def rms_back(l, which, rows, grad):
        inverse = rms(rows)
        scaled = grad * gain(l, which)
        back = inverse * scaled - rows * (inverse * inverse * inverse) * jnp.mean(
            scaled * rows, axis=-1, keepdims=True
        )
        DG[l, which : which + 1, :] += jnp.sum(grad * rows * inverse, axis=0, keepdims=True)
        return back

    def send_out(buf, l, out, which, m):
        src = buf.at[l, own_rows(m)]
        dst = out.at[zh * MH + m]
        to_self = (s == l) & (zh == s)

        @pl.when(to_self)
        def _():
            pltpu.make_async_copy(src, dst, o_rs.at[which, zh]).start()

        @pl.when(jnp.logical_not(to_self))
        def _():
            remote(
                src, dst, o_ss.at[l], o_rs.at[which, zh], (l, d, s * Hn + zl)
            ).start()

    lane_head = lax.broadcasted_iota(jnp.int32, (1, C), 1) // DH
    head_bf = [(lane_head == h).astype(F32).astype(BF) for h in range(NH)]
    head_f = [(lane_head == h).astype(F32) for h in range(NH)]

    def stack(rows):
        return jnp.concatenate([rows * head_bf[h] for h in range(NH)], axis=0)

    def unstack(wide):
        out = wide[0:DH] * head_f[0]
        for h in range(1, NH):
            out = out + wide[h * DH : (h + 1) * DH] * head_f[h]
        return out

    def tall(mask):
        return jnp.concatenate([mask] * NH, axis=0)

    def head_mean(values):
        row = lax.broadcasted_iota(jnp.int32, (C, C), 0) // DH
        col = lax.broadcasted_iota(jnp.int32, (C, C), 1) // DH
        same = jnp.where(row == col, 1.0 / DH, 0.0).astype(BF)
        high = values.astype(BF)
        low = (values - high.astype(F32)).astype(BF)
        return mm(high, same) + mm(low, same)

    def block_rows(b):
        return pl.ds(pl.multiple_of(b * BLOCK, BLOCK), BLOCK)

    def qkv_block(l, b):
        rows = block_rows(b)
        return (QKV[l, rows, 0:C], QKV[l, rows, C : 2 * C], QKV[l, rows, 2 * C : 3 * C])

    def softplus(values):
        return jnp.maximum(values, 0.0) + jnp.log(1.0 + jnp.exp(-jnp.abs(values)))

    def features(values):
        return softplus(values.astype(F32)).astype(BF)

    def diag_forward(b):
        q, k, v = qkv_block(0, b)
        scores = mm(stack(q), k, NT) * (1.0 / math.sqrt(DH))
        scores = jnp.where(tall(MSK[b]) > 0.5, scores, -1e9)
        top = jnp.max(scores, axis=-1, keepdims=True)
        weights = jnp.exp(scores - top)
        weights = (weights / jnp.sum(weights, axis=-1, keepdims=True)).astype(BF)
        AP[0, b] = weights
        O[0, block_rows(b), :] = unstack(mm(weights, v)).astype(BF)

    def diag_backward(b, grad_o):
        q, k, v = qkv_block(0, b)
        low = stack(grad_o.astype(BF))
        weights = AP[0, b]
        wide = weights.astype(F32)
        grad_v = mm(weights, low, TN)
        grad_w = mm(low, v, NT)
        grad_s = wide * (grad_w - jnp.sum(grad_w * wide, axis=-1, keepdims=True))
        grad_s = (grad_s * (1.0 / math.sqrt(DH))).astype(BF)
        grad_q = unstack(mm(grad_s, k))
        grad_k = mm(grad_s, stack(q), TN)
        rows = block_rows(b)
        GQKV[rows, 0:C] = grad_q.astype(BF)
        GQKV[rows, C : 2 * C] = grad_k.astype(BF)
        GQKV[rows, 2 * C : 3 * C] = grad_v.astype(BF)

    def fold(square):
        out = square[0:DH] * head_f[0]
        for h in range(1, NH):
            out = out + square[h * DH : (h + 1) * DH] * head_f[h]
        return out

    def unfold(flat):
        return stack(flat.astype(BF))

    def wide_lanes(column):
        return jnp.concatenate([column] * (C // 128), axis=1)

    def norm_state(b, state):
        q, k, v = qkv_block(1, b)
        ST[b] = state
        key = features(k)
        term = mm(key, (v.astype(F32) * wide_lanes(TAIL[b])).astype(BF), TN)
        return wide_lanes(KEEP[b, 0:1, :]) * state + fold(term)

    def norm_forward(b, passed):
        q, k, v = qkv_block(1, b)
        query, key = features(q), features(k)
        local = jnp.where(tall(MSK[b]) > 0.5, mm(stack(query), key, NT), 0.0).astype(BF)
        AP[1, b] = local
        state = ST[b] + passed * SIN[0].astype(F32)
        ST[b] = state
        mixed = unstack(mm(local, v)) + wide_lanes(CAR[b]) * mm(query, unfold(state))
        rows = block_rows(b)
        UU[rows, :] = mixed
        O[1, rows, :] = (mixed * lax.rsqrt(head_mean(mixed * mixed) + EPS)).astype(BF)
        return passed * wide_lanes(KEEP[b, 0:1, :])

    def norm_back_first(b, grad_o, state):
        rows = block_rows(b)
        mixed = UU[rows, :]
        scale = lax.rsqrt(head_mean(mixed * mixed) + EPS)
        grad = scale * grad_o - mixed * (scale * scale * scale) * head_mean(grad_o * mixed)
        low = grad.astype(BF)
        DU[rows, :] = low
        ST2_store(b, state)
        query = features(QKV[1, rows, 0:C])
        term = mm(query, (low.astype(F32) * wide_lanes(CAR[b])).astype(BF), TN)
        return wide_lanes(KEEP[b, 0:1, :]) * state + fold(term)

    def ST2_store(b, state):
        ST[NBH + b] = state

    def sigmoid(values):
        return 1.0 / (1.0 + jnp.exp(-values.astype(F32)))

    def norm_back_local(b):
        rows = block_rows(b)
        q, k, v = qkv_block(1, b)
        query, key = features(q), features(k)
        low = DU[rows, :]
        stacked = stack(low)
        grad_a = jnp.where(tall(MSK[b]) > 0.5, mm(stacked, v, NT), 0.0).astype(BF)
        grad_q = unstack(mm(grad_a, key)) + wide_lanes(CAR[b]) * mm(low, unfold(ST[b]), NT)
        GQKV[rows, 0:C] = (grad_q * sigmoid(q)).astype(BF)
        GQKV[rows, C : 2 * C] = (mm(grad_a, stack(query), TN) * sigmoid(k)).astype(BF)
        GQKV[rows, 2 * C : 3 * C] = mm(AP[1, b], stacked, TN).astype(BF)

    def norm_back_state(b, passed):
        rows = block_rows(b)
        q, k, v = qkv_block(1, b)
        grad_wide = unfold(ST[NBH + b] + passed * SIN[1].astype(F32))
        tail = wide_lanes(TAIL[b])
        grad_k = tail * mm(v, grad_wide, NT) * sigmoid(k)
        grad_v = tail * mm(features(k), grad_wide)
        GQKV[rows, C : 2 * C] = (GQKV[rows, C : 2 * C].astype(F32) + grad_k).astype(BF)
        GQKV[rows, 2 * C : 3 * C] = (GQKV[rows, 2 * C : 3 * C].astype(F32) + grad_v).astype(BF)
        return passed * wide_lanes(KEEP[b, 0:1, :])

    @scoped
    def masks():
        row = lax.broadcasted_iota(jnp.int32, (BLOCK, BLOCK), 0)
        col = lax.broadcasted_iota(jnp.int32, (BLOCK, BLOCK), 1)
        token = lax.broadcasted_iota(jnp.int32, (MB, BLOCK), 0)
        lane = lax.broadcasted_iota(jnp.int32, (MB, BLOCK), 1)
        start = jnp.concatenate([starts_in[zh * MH + m] for m in range(MH)], axis=0)
        start = start.astype(F32).astype(BF)
        chunk_lane = lax.broadcasted_iota(jnp.int32, (BLOCK, MH), 1)
        for j in range(NB):
            upper = ((token // BLOCK == j) & (token % BLOCK <= lane)).astype(F32).astype(BF)
            count_row = mm(start, upper)
            count_col = mm(upper, start, (((0,), (1,)), ((), ())))
            for m in range(MH):
                b = m * NB + j
                c_row = count_row[m : m + 1, :]
                c_col = jnp.sum(
                    jnp.where(chunk_lane == m, count_col, 0.0), axis=1, keepdims=True
                )
                last = jnp.sum(
                    jnp.where(col[0:1] == BLOCK - 1, c_row, 0.0), axis=1, keepdims=True
                )
                MSK[b] = jnp.where((c_row == c_col) & (row >= col), 1.0, 0.0)
                CAR[b] = jnp.broadcast_to(jnp.where(c_col == 0.0, 1.0, 0.0), (BLOCK, 128))
                TAIL[b] = jnp.broadcast_to(jnp.where(c_col == last, 1.0, 0.0), (BLOCK, 128))
                KEEP[b] = jnp.broadcast_to(jnp.where(last == 0.0, 1.0, 0.0), (8, 128))

    place = d * nt + z

    def gain_copy(i):
        return remote(GL.at[place], GL.at[place], gl_sem.at[0], gl_sem.at[1], section_dev(i))

    @scoped
    def gains_out():
        width = gain_in.shape[1]
        row = lax.broadcasted_iota(jnp.int32, (width, 128), 0)
        col = lax.broadcasted_iota(jnp.int32, (width, 128), 1)
        spot = (col % width == row) & (col // width == place % (128 // width))
        GL[place] = mm(gain_in[...].astype(BF), spot.astype(F32).astype(BF))

        def one(i, carry):
            gain_copy(i).start()
            return carry

        lax.fori_loop(1, nd * nt, one, 0)

    @scoped
    def gains_in():
        for k in (1, 0):
            got(GL.at[pl.ds(0, nd * nt - 1)], gl_sem.at[k])
        each = nd * nt * 128 // D
        for t in range(D // 128):
            total = GL[t * each]
            for i in range(1, each):
                total = total + GL[t * each + i]
            GV[s, :, t * 128 : (t + 1) * 128] = total
        gain_swap().start()

    def gain_swap():
        return remote(GV.at[s], GV.at[s], g1_sem.at[0], g1_sem.at[1], core_dev)

    def gains_other():
        gain_swap().wait_send()
        got(GV.at[1 - s], g1_sem.at[1])

    def dp_gain(step):
        return remote(
            GOWN, DL2.at[step - 1], g_ss.at[1, step - 1], g_rs.at[1, step - 1], dp_dev(step)
        )

    def core_gain():
        return remote(DG.at[1 - s], DL0, g1_sem.at[2], g1_sem.at[3], core_dev)

    def z_gain(step):
        return remote(
            DG.at[s], DL1.at[step - 1], g_ss.at[0, step - 1], g_rs.at[0, step - 1], z_dev(step)
        )

    @scoped
    def gain_second():
        core_gain().wait()
        DG[s] = DG[s] + DL0[...]
        for step in range(1, nt):
            z_gain(step).start()

    @scoped
    def gain_third():
        total = DG[s]
        for step in range(1, nt):
            z_gain(step).wait()
            total = total + DL1[step - 1]
        GOWN[...] = total
        for step in range(1, nd):
            dp_gain(step).start()

    @scoped
    def gain_final():
        total = GOWN[...]
        for step in range(1, nd):
            dp_gain(step).wait()
            total = total + DL2[step - 1]
        GOWN[...] = total
        width = out_gain.shape[1]
        each = 128 // width
        tile = GOWN[:, pl.ds(pl.multiple_of(place // each * 128, 128), 128)]
        mine = jnp.zeros((2, width), F32)
        for i in range(each):
            piece = tile[:, i * width : (i + 1) * width]
            mine = jnp.where(place % each == i, piece, mine)
        out_gain[...] = mine

    def loop(count, fn):
        def step(i, carry):
            fn(i)
            return carry

        with jax.named_scope(fn.__name__):
            lax.fori_loop(0, count, step, 0)

    def chunk(m):
        return pl.ds(pl.multiple_of(m * MB, BLOCK), MB)

    def w_cols(l, p):
        col, width = pieces[p]
        return W[l, :, col : col + width]

    def w_gate_up(l):
        return W[l, :, z_.oG : z_.oD]

    @scoped
    def state_copy(slot):
        return remote(
            SEND_STATE.at[slot],
            SIN.at[slot],
            st_ss.at[slot],
            st_rs.at[slot],
            (s, d, (z + Hn) % nt),
        )

    def state_out(slot, value, sender):
        SEND_STATE[slot] = value.astype(BF)

        @pl.when(zh == sender)
        def _():
            SIN[slot] = jnp.zeros((DH, C), BF)
            state_copy(slot).start()

    @scoped
    def state_in(slot, sender):
        @pl.when(zh != sender)
        def _():
            state_copy(slot).wait_recv()

    outer = zh == zl
    inner, far = jnp.logical_not(outer), jnp.logical_not(near)

    def only(cond, fn):
        pl.when(cond)(fn)

    def hand_far(l, cond, ps):
        def go():
            for p in ps:
                w_hand_far(l, p)

        pl.when((s == l) & cond)(go)

    def hand_near(ps):
        for l in range(2):

            @pl.when(s == l)
            def _():
                for p in ps:
                    w_hand_near(l, p)

    def x_out():
        spread_tokens(xin, XF, 0)

    gains_out()
    shard_attention()
    hand_far(0, s == 0, [5])
    hand_near([5])
    only((s == 0) & inner, x_out)
    pump_near([("s", 0, 5)])
    own_tokens(xin, XF, 0)
    own_tokens(cot, GF.at[1], 1)
    shard_feed()
    hand_near([2, 3, 4])
    masks()
    for l in range(2):
        DG[l] = jnp.zeros((2, D), F32)
    pump_near([("s", 0, 2)])
    gains_in()
    pump_far([("s", 0, 5)])
    only((s == 0) & outer & far, x_out)
    pump([("f", 0, 5)])
    pump_near([("f", 0, 2)])
    only((s == 0) & outer & near, x_out)
    only(s == 1, gains_other)
    for m in range(MH):
        relay_tokens(XF, 0, m)
    hand_far(0, s == 0, [2, 3, 4])
    await_tokens(XF, 0, 0)

    def cot_out():
        spread_tokens(cot, GF.at[1], 1)

    stage = {
        (0, "attended"): lambda: (
            pump_near([("f", 0, 3), ("f", 0, 4)]),
            pump_far([("s", 0, 2), ("s", 0, 3), ("f", 0, 2), ("s", 0, 4)]),
        ),
        (0, "hidden"): lambda: (
            hand_far(1, inner, [5, 4, 2, 3]),
            hand_far(1, outer, [5]),
            pump_near([("s", 1, 5)]),
            pump_far([("f", 0, 3), ("f", 0, 4)]),
        ),
        (0, "ready"): lambda: (
            pump_near([("f", 1, 5)]),
            pump_far([("s", 1, 5)]),
        ),
        (0, "feeding"): lambda: (
            hand_far(1, outer, [4]),
            pump_near([("s", 1, 4)]),
        ),
        (0, "fed"): lambda: (
            hand_far(1, outer, [2, 3]),
            pump_near([("s", 1, 2), ("f", 1, 4)]),
            pump_far([("f", 1, 5), ("s", 1, 4)]),
            only(s == 0, gains_other),
        ),
        (0, "result"): lambda: (
            only(s == 1, cot_out),
            pump_near([("s", 1, 3)]),
            pump_far([("s", 1, 2), ("f", 1, 4)]),
        ),
        (1, "states"): lambda: (
            [relay_tokens(GF.at[1], 1, m) for m in reversed(range(MH))],
            pump_near([("f", 1, 2), ("f", 1, 3)]),
            pump_far([("s", 1, 3), ("f", 1, 2)]),
        ),
        (1, "attended"): lambda: (pump_far([("f", 1, 3)]),),
        (1, "hidden"): lambda: (),
        (1, "ready"): lambda: (),
        (1, "fed"): lambda: (),
        "b1 second": lambda: (),
        "b1 middle": lambda: (d_mid(1, 4),),
        "b1 feed": lambda: (),
        "b1 third": lambda: (d_mid(1, 3), d_total_rows(1, 2)),
        "b1 end": lambda: (d_total_rows(1, 3),),
        "b0 second": lambda: (d_total_rows(1, 0),),
        "b0 middle": lambda: (),
        "b0 feed": lambda: (d_total_rows(1, 1),),
        "b0 third": lambda: (
            only(far, lambda: run(d_mid, 2)),
            only(near, lambda: run(d_mid, 4) or run(d_send, 2, 3)),
        ),
        "b0 end": lambda: (
            core_gain().start(),
            only(near, lambda: run(d_send, 0, 1)),
            gain_second(),
            only(far, lambda: far_tail()),
            only(near, lambda: near_tail()),
            gain_third(),
        ),
    }

    def run(step, *parts):
        for p in parts:
            step(0, p)

    def far_tail():
        run(d_sum, 2)
        run(d_mid, 6)
        run(d_sum, 3)
        run(d_mid, 7, 8)
        run(d_sum, 6)
        run(d_mid, 1)
        run(d_sum, 7, 8, 1)

    def near_tail():
        run(d_sum, 4)
        run(d_mid, 2, 3, 6, 7, 8, 1)
        run(d_sum, 2, 3, 6, 7, 8, 1)

    def input_rows(l, m):
        if l == 0:
            return XF[chunk_rows(m, own), :].astype(F32)
        return Y[0, own_rows(m), :].astype(F32)

    def gate_up_grad(grad, both):
        parts = [grad * both[:, F : 2 * F], grad * both[:, :F]]
        if z_.GUw > 2 * F:
            parts.append(jnp.zeros((MB, z_.GUw - 2 * F), F32))
        return jnp.concatenate(parts, axis=1).astype(BF)

    def finish_layer(l, rs2, ag3):
        def result(m):
            rows = (H[l, own_rows(m), :] + rs_third(rs2, m)).astype(BF)
            Y[l, own_rows(m), :] = rows
            send_out(Y, l, out_y, 0, m)
            if l == 0:
                wide = rows.astype(F32)
                N1[1, chunk_rows(m, own), :] = (wide * rms(wide) * gain(1, 0)).astype(BF)
                ag_send(ag3, N1.at[1], m)

        loop(MH, result)

    def forward(l, ag1, rs1, ag2, rs2, ag3):
        w_ready(l, 5)

        def qkv_chunk(m):
            if l == 0:
                pl.when(m > 0)(lambda: await_tokens(XF, 0, m))
                pl.when((m == 1) & near)(lambda: pump([("s", 0, 3), ("s", 0, 4)]))
                rows = XF[chunk(m), :].astype(F32)
                N1[0, chunk(m), :] = (rows * rms(rows) * gain(0, 0)).astype(BF)
            else:
                ag_forward(ag1, N1.at[1], m)
                ag_wait(ag1, N1.at[1], m)
            QKV[l, chunk(m), :] = mm(N1[l, chunk(m), :], w_cols(l, 0)).astype(BF)

        def out_chunk(m):
            rs_first(rs1, m, mm(O[l, chunk(m), :], w_cols(l, 1), NT))

        if l == 0:

            def attend(m):
                qkv_chunk(m)
                for i in range(NB):
                    diag_forward(m * NB + i)
                out_chunk(m)
                after(rs1, m, m - 1)

            loop(MH, attend)
            rs_second(rs1, MH - 1)
            stage[l, "attended"]()
        else:

            def states(m, state):
                qkv_chunk(m)
                for i in range(NB):
                    state = norm_state(m * NB + i, state)
                return state

            with jax.named_scope('states'):
                last = lax.fori_loop(0, MH, states, jnp.zeros((DH, C), F32))
            w_handed_out()
            state_out(0, last, 0)
            state_in(0, 0)
            stage[l, "states"]()

            def attend(m, passed):
                for i in range(NB):
                    passed = norm_forward(m * NB + i, passed)
                out_chunk(m)
                after(rs1, m, m - 1)
                return passed

            with jax.named_scope('attend'):
                lax.fori_loop(0, MH, attend, jnp.ones((1, C), F32))
            rs_second(rs1, MH - 1)
            stage[l, "attended"]()

        def hidden_rows(m):
            rows = input_rows(l, m) + rs_third(rs1, m)
            H[l, own_rows(m), :] = rows
            N2[l, chunk_rows(m, own), :] = (rows * rms(rows) * gain(l, 1)).astype(BF)
            ag_send(ag2, N2.at[l], m)

        loop(MH, hidden_rows)
        stage[l, "hidden"]()
        w_ready(l, 4)
        if l == 1:

            def hidden_grad(m):
                await_tokens(GF.at[1], 1, m)
                GGU[chunk(m), 0 : z_.Dw] = mm(GF[1, chunk(m), :], w_cols(1, 4)).astype(BF)

            loop(MH, hidden_grad)
        w_ready(l, 2)
        w_ready(l, 3)
        stage[l, "ready"]()

        def feed(m):
            ag_forward(ag2, N2.at[l], m)
            ag_wait(ag2, N2.at[l], m)
            rows = N2[l, chunk(m), :]
            both = mm(rows, w_gate_up(l))
            if l == 0:
                GU[l, chunk(m), :] = both.astype(BF)
            else:
                grad = GGU[chunk(m), 0 : z_.Dw].astype(F32)[:, :F]
                GGU[chunk(m), :] = gate_up_grad(grad, both)
            hidden = both[:, :F] * both[:, F : 2 * F]
            if z_.Dw > F:
                hidden = jnp.concatenate([hidden, jnp.zeros((MB, z_.Dw - F), F32)], axis=1)
            hidden = hidden.astype(BF)
            HID[l, chunk(m), :] = hidden
            rs_first(rs2, m, mm(hidden, w_cols(l, 4), NT))
            if l == 0:


                @pl.when(m == 1)
                def _():
                    stage[0, "feeding"]()

            after(rs2, m, m - 1)

        loop(MH, feed)
        rs_second(rs2, MH - 1)
        stage[l, "fed"]()

        if l == 0:
            finish_layer(l, rs2, ag3)
            stage[l, "result"]()

    forward(0, None, 0, 0, 1, 1)
    forward(1, 1, 2, 2, 3, None)

    RB = min(D, 256)

    @scoped
    def grad_weight(l, p, left, right, send=True):
        col, width = pieces[p]
        for r in range(D // RB):
            W[l, r * RB : (r + 1) * RB, col : col + width] = mm(
                left[:, r * RB : (r + 1) * RB], right, TN
            ).astype(BF)
        if send:
            d_send(l, p)

    def rest(l, p):
        for q in range(MH, 4):
            d_pass(l, p, q)

    def grad_part(l, p, send=True):
        col, width = pieces[p]
        grad_weight(l, p, N2[l], GGU[:, col - z_.oG : col - z_.oG + width], send)

    def backward(l, ag_in, rs1, ag2, rs2, ag_out):
        w_shared(l)

        def feed_back(i):
            m = MH - 1 - i
            if l == 0:
                ag_forward(ag_in, GF.at[0], m)
                ag_wait(ag_in, GF.at[0], m)
                grad = mm(GF[l, chunk(m), :], w_cols(l, 4))[:, :F]
                GGU[chunk(m), :] = gate_up_grad(grad, GU[l, chunk(m), :].astype(F32))
            rs_first(rs1, m, mm(GGU[chunk(m), :], w_gate_up(l), NT))
            after(rs1, i, m + 1)
            if l == 0:

                @pl.when(i == 0)
                def _():
                    d_mid(1, 1)
                    d_mid(1, 0)

                d_pass(1, 3, i)
        if l == 1:
            grad_weight(l, 4, GF[l], HID[l])
        loop(MH, feed_back)
        rs_second(rs1, 0)
        if l == 0:
            rest(1, 3)
            grad_weight(l, 4, GF[l], HID[l], False)
            only(far, lambda: d_send(0, 4))
        else:
            grad_part(l, 2)
            finish_layer(1, 3, None)
        stage[f"b{l} second"]()

        def middle(i):
            m = MH - 1 - i
            rows = H[l, own_rows(m), :]
            grad = GF[l, chunk_rows(m, own), :].astype(F32) + rms_back(
                l, 1, rows, rs_third(rs1, m)
            )
            GH[own_rows(m), :] = grad
            GA[l, chunk_rows(m, own), :] = grad.astype(BF)
            ag_send(ag2, GA.at[l], m)
            if l == 0:
                only((i == 1) & near, lambda: d_send(0, 4))
                d_pass(1, 0, i)

        loop(MH, middle)
        if l == 0:
            rest(1, 0)
        stage[f"b{l} middle"]()
        if l == 0:
            grad_part(l, 2, False)

            @pl.when(far)
            def _():
                d_mid(0, 4)
                d_send(0, 2)

            grad_part(l, 3, False)
            only(far, lambda: d_send(0, 3))
        else:
            grad_part(l, 3)
        stage[f"b{l} feed"]()

        def grad_o(m):
            ag_forward(ag2, GA.at[l], m)
            ag_wait(ag2, GA.at[l], m)
            return mm(GA[l, chunk(m), :], w_cols(l, 1))

        def qkv_back(i, m):
            rs_first(rs2, m, mm(GQKV[chunk(m), :], w_cols(l, 0), NT))
            after(rs2, i, m + 1)

        if l == 0:

            def attend(i):
                m = MH - 1 - i
                grad = grad_o(m)
                for j in range(NB):
                    diag_backward(m * NB + j, grad[j * BLOCK : (j + 1) * BLOCK])
                qkv_back(i, m)
                d_pass(1, 1, i)
                only((i == 0) & far, lambda: d_sum(0, 4))

            loop(MH, attend)
        else:

            def states(i, state):
                m = MH - 1 - i
                grad = grad_o(m)
                for j in reversed(range(NB)):
                    state = norm_back_first(m * NB + j, grad[j * BLOCK : (j + 1) * BLOCK], state)
                return state

            with jax.named_scope("states"):
                last = lax.fori_loop(0, MH, states, jnp.zeros((DH, C), F32))
            state_out(1, last, 1)
            d_mid(1, 2)
            grad_weight(l, 1, GA[l], O[l])
            d_total_rows(1, 4)

            def attend_local(m):
                for j in range(NB):
                    norm_back_local(m * NB + j)

            loop(MH, attend_local)
            state_in(1, 1)
            pl.when(zh == 0)(lambda: d_pass(1, 4, 0, Dr))

            def attend(i, passed):
                m = MH - 1 - i
                for j in reversed(range(NB)):
                    passed = norm_back_state(m * NB + j, passed)
                qkv_back(i, m)

                @pl.when(zh == 1)
                def _():
                    d_pass(1, 4, i)

                return passed

            with jax.named_scope("attend"):
                lax.fori_loop(0, MH, attend, jnp.ones((1, C), F32))

        rs_second(rs2, 0)
        if l == 0:
            rest(1, 1)
        else:
            pl.when(zh == 1)(lambda: rest(1, 4))
        stage[f"b{l} third"]()
        grad_weight(l, 0, N1[l], GQKV[...], l == 1)
        if l == 0:
            grad_weight(l, 1, GA[l], O[l], False)

            @pl.when(far)
            def _():
                d_mid(0, 3)
                d_send(0, 0)
                d_send(0, 1)


        def result(i):
            m = MH - 1 - i
            grad = GH[own_rows(m), :] + rms_back(l, 0, input_rows(l, m), rs_third(rs2, m))
            low = grad.astype(BF)
            GX[l, own_rows(m), :] = low
            send_out(GX, l, out_g, 1, m)
            if l == 1:
                GF[0, chunk_rows(m, own), :] = low
                ag_send(ag_out, GF.at[0], m)
                d_pass(1, 2, i)

        loop(MH, result)
        if l == 1:
            rest(1, 2)
        stage[f"b{l} end"]()

    backward(1, None, 4, 3, 5, 4)
    backward(0, 4, 6, 5, 7, None)

    for p in (4, 2, 3, 6, 7, 8, 1):
        d_final(p)
    gain_final()
    for copy in outs:
        copy.wait()
    for l in range(2):
        d_sent(l)

    ags = ((0, N2.at[0]), (1, N1.at[1]), (2, N2.at[1]), (3, GA.at[1]), (4, GF.at[0]), (5, GA.at[0]))

    for slot in range(2):

        @pl.when(zh == slot)
        def _():
            state_copy(slot).wait_send()

    for k, buf in ags:
        ag_sent(k, buf)
    for l in range(2):

        @pl.when(jnp.logical_not((s == l) & (zh == s)))
        def _():
            got(XF.at[pl.ds(0, 2 * MH * R)], o_ss.at[l])

    for half in range(2):
        got(out_y.at[pl.ds(half * MH, MH)], o_rs.at[0, half])
        got(out_g.at[pl.ds(half * MH, MH)], o_rs.at[1, half])
    for k in range(2):
        got(XF.at[pl.ds(0, MH * (nt - 1) * R)], x_sem.at[k])


def place_results(*refs):
    count = (len(refs) - 2) // 3
    sources, targets, held = refs[:count], refs[count : 2 * count], refs[2 * count : 3 * count]
    in_sem, out_sem = refs[-2:]
    reads = [pltpu.make_async_copy(sources[i], held[i], in_sem.at[i]) for i in range(count)]
    writes = [pltpu.make_async_copy(held[i], targets[i], out_sem.at[i]) for i in range(count)]
    for copy in reads:
        copy.start()
    for read, write in zip(reads, writes):
        read.wait()
        write.start()
    for copy in writes:
        copy.wait()


def solution(mesh):
    nd, nt = mesh.shape["dp"], mesh.shape["tensor"]

    def on_device(inputs, starts, cotangent, qkv_m, out_m, gateup_m, down_m, gain_m):
        z_ = Sizes(
            mesh,
            inputs.shape[3],
            inputs.shape[1],
            inputs.shape[2],
            qkv_m.shape[3],
            gateup_m.shape[3],
        )
        D, R, C, F, Dr, M, MH, Hn, MB, T, NBH, N, NH = (
            z_.D,
            z_.R,
            z_.C,
            z_.F,
            z_.Dr,
            z_.M,
            z_.MH,
            z_.Hn,
            z_.MB,
            z_.T,
            z_.NBH,
            z_.N,
            z_.NH,
        )
        width = gain_m.shape[2]
        qkv_rows = jnp.transpose(qkv_m[0], (1, 0, 2))
        gateup_rows = jnp.transpose(gateup_m[0], (1, 2, 0)).reshape(2 * F, Dr)
        anywhere = pl.BlockSpec(memory_space=pl.ANY)
        vmem = pl.BlockSpec(memory_space=pltpu.VMEM)
        DMA = pltpu.SemaphoreType.DMA
        V = pltpu.VMEM
        scratch = [
            V((3, Dr, C), F32),
            V((C, Dr), F32),
            V((2 * F, Dr), F32),
            V((F, Dr), F32),
            V((2, D, N), BF),
            V((2, nd - 1, Dr, N), BF),
            V((2, Dr, N), BF),
            V((T, D), BF),
            V((2, T, D), BF),
            V((2, T, D), BF),
            V((2, T, D), BF),
            V((2, T, 3 * C), BF),
            V((2, T, C), BF),
            V((1, T, z_.GUw), BF),
            V((2, T, z_.Dw), BF),
            V((2, MH * R, D), F32),
            V((2, MH * R, D), BF),
            V((2, T, D), BF),
            V((T, z_.GUw), BF),
            V((T, 3 * C), BF),
            V((MH * R, D), F32),
            V((2, MH * R, D), BF),
            V((2, T, D), BF),
            V((2, MH, Hn * R, D), BF),
            V((2, MH, Hn - 1, R, D), BF),
            V((2, MH, Hn - 1, R, D), BF),
            V((2, NBH, NH * BLOCK, BLOCK), BF),
            V((T, C), F32),
            V((T, C), BF),
            V((2 * NBH, DH, C), F32),
            V((2, DH, C), BF),
            V((2, DH, C), BF),
            V((NBH, BLOCK, BLOCK), F32),
            V((NBH, BLOCK, 128), F32),
            V((NBH, BLOCK, 128), F32),
            V((NBH, 8, 128), F32),
            V((nd * nt, 2, 128), F32),
            V((2, 2, D), F32),
            V((2, D), F32),
            V((2, 2, D), F32),
            V((2, D), F32),
            V((nt - 1, 2, D), F32),
            V((nd - 1, 2, D), F32),
            DMA((2, MH)),
            DMA((2,)),
            DMA((2, MH, nt - 1)),
            DMA((2,)),
            DMA((2, 4)),
            DMA((2,)),
            DMA((2, 4, max(4, nd - 1))),
            DMA((6,)),
            DMA((6, MH, Hn)),
            DMA((2, MH)),
            DMA((2, MH)),
            DMA((2, MH, Hn - 1)),
            DMA((2, MH, Hn - 1)),
            DMA((2,)),
            DMA((2,)),
            DMA((2,)),
            DMA((2, 2)),
            DMA((2,)),
            DMA((2, 7, 3)),
            DMA((2,)),
            DMA((7, 2)),
            DMA((4,)),
            DMA((2, max(nd, nt) - 1)),
            DMA((2, max(nd, nt) - 1)),
            DMA((2,)),
            DMA((4,)),
        ]
        out_y, out_g, grad_qkv, grad_o, grad_gu, grad_d, grad_gain = pl.pallas_call(
            functools.partial(body, z_),
            out_shape=(
                jax.ShapeDtypeStruct((M, R, D), BF),
                jax.ShapeDtypeStruct((M, R, D), BF),
                jax.ShapeDtypeStruct((3, Dr, C), F32),
                jax.ShapeDtypeStruct((C, Dr), F32),
                jax.ShapeDtypeStruct((2 * F, Dr), F32),
                jax.ShapeDtypeStruct((F, Dr), F32),
                jax.ShapeDtypeStruct((2, width), F32),
            ),
            in_specs=[anywhere] * 6 + [vmem, vmem],
            out_specs=(anywhere,) * 6 + (vmem,),
            scratch_shapes=scratch,
            compiler_params=pltpu.CompilerParams(
                collective_id=0, has_side_effects=True, vmem_limit_bytes=63 * 1024 * 1024
            ),
        )(
            qkv_rows,
            out_m[0],
            gateup_rows,
            down_m[0],
            inputs[0],
            cotangent[0],
            jnp.transpose(starts, (1, 0, 2)),
            gain_m[0],
        )
        results = (out_y, out_g, grad_qkv, grad_o, grad_gu, grad_d, grad_gain)
        out_y, out_g, grad_qkv, grad_o, grad_gu, grad_d, grad_gain = pl.pallas_call(
            place_results,
            out_shape=tuple(jax.ShapeDtypeStruct(r.shape, r.dtype) for r in results),
            in_specs=[anywhere] * len(results),
            out_specs=(anywhere,) * len(results),
            scratch_shapes=[V(r.shape, r.dtype) for r in results]
            + [DMA((len(results),)), DMA((len(results),))],
        )(*results)
        return (
            out_y[None, None],
            out_g[None, None],
            jnp.transpose(grad_qkv, (1, 0, 2))[None],
            grad_o[None],
            jnp.transpose(grad_gu.reshape(2, F, Dr), (2, 0, 1))[None],
            grad_d[None],
            grad_gain[None],
        )

    return jax.shard_map(
        on_device,
        mesh=mesh,
        in_specs=(
            P("dp", None, "tensor", None),
            P("dp", None, None),
            P("dp", None, "tensor", None),
            P("section", "dp", None, "tensor"),
            P("section", "tensor", "dp"),
            P("section", "dp", None, "tensor"),
            P("section", "tensor", "dp"),
            P("section", None, ("dp", "tensor")),
        ),
        out_specs=(
            P("section", "dp", None, "tensor", None),
            P("section", "dp", None, "tensor", None),
            P("section", "dp", None, "tensor"),
            P("section", "tensor", "dp"),
            P("section", "dp", None, "tensor"),
            P("section", "tensor", "dp"),
            P("section", None, ("dp", "tensor")),
        ),
        check_vma=False,
    )
```

```python
import functools
import math

import jax
import jax.numpy as jnp
from jax import lax
from jax.experimental import pallas as pl
from jax.experimental.pallas import tpu as pltpu
from jax.sharding import PartitionSpec as P

DH = 64
BLOCK = 64
EPS = 1e-6
BF = jnp.bfloat16
F32 = jnp.float32
MESH = pl.DeviceIdType.MESH
NN = (((1,), (0,)), ((), ()))
NT = (((1,), (1,)), ((), ()))
TN = (((0,), (0,)), ((), ()))


def mm(a, b, dims=NN):
    return lax.dot_general(a, b, dims, preferred_element_type=F32)


def ceil_to(value, unit):
    return (value + unit - 1) // unit * unit


def scoped(fn):
    @functools.wraps(fn)
    def inner(*args):
        with jax.named_scope(fn.__name__):
            return fn(*args)

    return inner


class Sizes:
    def __init__(self, mesh, model, micro, rows, cols, hidden):
        self.nd, self.nt = mesh.shape["dp"], mesh.shape["tensor"]
        self.D, self.M, self.R, self.C, self.F = model, micro, rows, cols, hidden
        self.GUw, self.Dw = ceil_to(2 * hidden, 128), ceil_to(hidden, 128)
        self.Dr = model // self.nd
        self.MH, self.Hn = micro // 2, self.nt // 2
        self.MB = rows * self.nt
        self.T = self.MH * self.MB
        self.NH = cols // DH
        self.NB = self.MB // BLOCK
        self.NBH = self.MH * self.NB
        self.oO, self.oG = 3 * cols, 4 * cols
        self.oD = self.oG + self.GUw
        self.N = self.oD + self.Dw
        first = ceil_to(self.GUw // 2, 128)
        self.pieces = (
            (0, 3 * cols),
            (self.oO, cols),
            (self.oG, first),
            (self.oG + first, self.GUw - first),
            (self.oD, self.Dw),
            (0, 4 * cols),
            (0, cols),
            (cols, cols),
            (2 * cols, cols),
        )


def body(
    z_,
    qkv_in,
    o_in,
    gu_in,
    d_in,
    xin,
    cot,
    starts_in,
    gain_in,
    out_y,
    out_g,
    out_qkv,
    out_o,
    out_gu,
    out_d,
    out_gain,
    MQ,
    MO,
    MGU,
    MD,
    W,
    LW,
    L2,
    XF,
    GF,
    N1,
    N2,
    QKV,
    O,
    GU,
    HID,
    H,
    Y,
    GA,
    GGU,
    GQKV,
    GH,
    GX,
    PT,
    RL1,
    RL2,
    RSB,
    AP,
    UU,
    DU,
    ST,
    SIN,
    SEND_STATE,
    MSK,
    CAR,
    TAIL,
    KEEP,
    GL,
    GV,
    GOWN,
    DG,
    DL0,
    DL1,
    DL2,
    in_sem,
    x_sem,
    x_rs,
    w1_ss,
    w1_rs,
    w2_ss,
    w2_rs,
    ag_ss,
    ag_rs,
    r1_ss,
    r1_rs,
    r2_ss,
    r2_rs,
    st_ss,
    st_rs,
    o_ss,
    o_rs,
    d1_ss,
    d1_rs,
    d2_ss,
    d2_rs,
    g1_sem,
    g_ss,
    g_rs,
    gl_sem,
    m_sem,
):
    D, R, C, F, Dr, MH, Hn, MB, T, NH, NB, NBH = (
        z_.D,
        z_.R,
        z_.C,
        z_.F,
        z_.Dr,
        z_.MH,
        z_.Hn,
        z_.MB,
        z_.T,
        z_.NH,
        z_.NB,
        z_.NBH,
    )
    nd, nt = z_.nd, z_.nt
    pieces = z_.pieces
    s, d, z = lax.axis_index("section"), lax.axis_index("dp"), lax.axis_index("tensor")
    zh, zl = z // Hn, z % Hn
    own = s * Hn + zl
    core_dev = (1 - s, d, z)

    def remote(src, dst, ssem, rsem, dev):
        return pltpu.make_async_remote_copy(
            src_ref=src, dst_ref=dst, send_sem=ssem, recv_sem=rsem, device_id=dev, device_id_type=MESH
        )

    def got(dst, sem):
        pltpu.make_async_copy(dst, dst, sem).wait()

    def dp_dev(step):
        return (s, (d + step) % nd, z)

    def z_dev(step):
        return (s, d, (z + step) % nt)

    def peer_zl(step):
        return (zl + step) % Hn

    masters = (
        pltpu.make_async_copy(qkv_in, MQ, m_sem.at[0]),
        pltpu.make_async_copy(o_in, MO, m_sem.at[1]),
        pltpu.make_async_copy(gu_in, MGU, m_sem.at[2]),
        pltpu.make_async_copy(d_in, MD, m_sem.at[3]),
    )
    for copy in masters:
        copy.start()

    barrier = pltpu.get_barrier_semaphore()

    def section_dev(i):
        return (s, (d + i // nt) % nd, (z + i % nt) % nt)

    def greet(i, carry):
        pl.semaphore_signal(barrier, inc=1, device_id=section_dev(i), device_id_type=MESH)
        return carry

    lax.fori_loop(1, nd * nt, greet, 0)
    pl.semaphore_signal(barrier, inc=1, device_id=core_dev, device_id_type=MESH)
    far_dev = (1 - s, d, (z + Hn) % nt)
    pl.semaphore_signal(barrier, inc=1, device_id=far_dev, device_id_type=MESH)
    pl.semaphore_wait(barrier, nd * nt + 1)

    def own_tokens(src, dst, array):
        for m in range(MH):
            mine = dst.at[pl.ds(m * MB + z * R, R)]
            pltpu.make_async_copy(src.at[zh * MH + m], mine, in_sem.at[array, m]).start()

    def spread_tokens(src, dst, array):
        for m in range(MH):
            mine = dst.at[pl.ds(m * MB + z * R, R)]
            for step in range(1, nt):
                other = (z + step) % nt

                @pl.when((other // Hn == zh) | (step == Hn))
                def _():
                    remote(
                        src.at[(other // Hn) * MH + m],
                        mine,
                        x_sem.at[0],
                        x_rs.at[array, m, step - 1],
                        z_dev(step),
                    ).start()

    def relay_tokens(dst, array, m):
        @pl.when(s == array)
        def _():
            chip = (z + Hn) % nt
            rows = dst.at[pl.ds(m * MB + chip * R, R)]
            got(rows, x_rs.at[array, m, Hn - 1])
            for step in range(1, Hn):
                peer = zh * Hn + peer_zl(step)
                remote(
                    rows,
                    rows,
                    x_sem.at[0],
                    x_rs.at[array, m, (peer + nt - chip) % nt - 1],
                    (s, d, peer),
                ).start()

    def await_tokens(dst, array, m):
        got(dst.at[pl.ds(m * MB + z * R, R)], in_sem.at[array, m])
        for step in range(1, nt):
            rows = dst.at[pl.ds(m * MB + (z + nt - step) % nt * R, R)]
            if step == Hn:
                pl.when(s != array)(lambda: got(rows, x_rs.at[array, m, step - 1]))
            else:
                got(rows, x_rs.at[array, m, step - 1])

            @pl.when(s == array)
            def _():
                remote(
                    rows, rows, x_sem.at[1], x_rs.at[array, m, step - 1], core_dev
                ).start()

    spot = {5: 0, 2: 1, 3: 2, 4: 3}

    def w_rows(l, block, p):
        col, width = pieces[p]
        return W.at[l, pl.ds(block * Dr, Dr), pl.ds(col, width)]

    def shard_cols(p):
        col, width = pieces[p]
        return L2.at[0, :, pl.ds(col, width)]

    def w_hand_near(l, p):
        @pl.when(zh == s)
        def _():
            pltpu.make_async_copy(shard_cols(p), w_rows(l, d, p), w1_rs.at[l, spot[p]]).start()

        @pl.when(zh != s)
        def _():
            w_hand(l, p, 0, core_dev).start()

    def w_hand(l, p, which, dev):
        return remote(
            shard_cols(p), w_rows(l, d, p), w1_ss.at[which], w1_rs.at[l, spot[p]], dev
        )

    def w_hand_far(l, p):
        w_hand(l, p, 1, (zh, d, (z + Hn) % nt)).start()

    def w_handed_out():
        @pl.when(zh != s)
        def _():
            got(L2.at[0], w1_ss.at[0])

        got(L2.at[0], w1_ss.at[1])

    square = nd == 4
    half_rows = Dr // 2
    dp_x, dp_y = d + 1 - 2 * (d % 2), (d + 2) % nd

    def w_half(l, block, half, p):
        col, width = pieces[p]
        return W.at[l, pl.ds(block * Dr + half * half_rows, half_rows), pl.ds(col, width)]

    def w_copy(l, p, k):
        if not square:
            rows, dev = w_rows(l, d, p), dp_dev(k + 1)
        elif k < 2:
            rows, dev = w_rows(l, d, p), (s, (dp_x, dp_y)[k], z)
        elif k == 2:
            rows, dev = w_half(l, dp_x, 0, p), (s, dp_y, z)
        else:
            rows, dev = w_half(l, dp_y, 1, p), (s, dp_x, z)
        return remote(rows, rows, w2_ss.at[l], w2_rs.at[l, spot[p], k], dev)

    def w_share(l, p):
        got(w_rows(l, d, p), w1_rs.at[l, spot[p]])
        for k in range(2 if square else nd - 1):
            w_copy(l, p, k).start()

    def w_forward(l, p):
        if square:
            got(w_rows(l, dp_x, p), w2_rs.at[l, spot[p], 0])
            w_copy(l, p, 2).start()
            got(w_rows(l, dp_y, p), w2_rs.at[l, spot[p], 1])
            w_copy(l, p, 3).start()

    def w_ready(l, p):
        if square:
            got(w_half(l, 3 - d, 0, p), w2_rs.at[l, spot[p], 2])
            got(w_half(l, 3 - d, 1, p), w2_rs.at[l, spot[p], 3])
        else:
            for step in range(1, nd):
                got(w_rows(l, (d + nd - step) % nd, p), w2_rs.at[l, spot[p], step - 1])

    def w_shared(l):
        got(W.at[l, pl.ds(0, (nd - 1) * Dr)], w2_ss.at[l])

    def pump(ops):
        for what, l, p in ops:
            with jax.named_scope(what + str(l) + str(p)):
                {"s": w_share, "f": w_forward}[what](l, p)

    near = s == zh
    gathered = (5, 2, 3, 4)

    def pump_near(ops):
        pl.when(near)(lambda: pump(ops))

    def pump_far(ops):
        pl.when(jnp.logical_not(near))(lambda: pump(ops))

    where = {4: 0, 2: 1, 3: 2, 1: 3, 6: 4, 7: 5, 8: 6}

    def split(p):
        return (6, 7, 8) if p == 0 else (p,)

    def d_copy(l, p, k):
        col, width = pieces[p]
        cols = pl.ds(col, width)
        if not square:
            src, dst, dev = w_rows(l, (d + k + 1) % nd, p), LW.at[l, k, :, cols], dp_dev(k + 1)
        else:
            first, second = pl.ds(0, half_rows), pl.ds(half_rows, half_rows)
            block, half, slot, rows, to = (
                (3 - d, 0, 2, first, dp_x),
                (3 - d, 1, 2, second, dp_y),
                (dp_x, 0, 0, first, dp_x),
                (dp_y, 1, 1, second, dp_y),
                (dp_y, 0, 1, first, dp_y),
                (dp_x, 1, 0, second, dp_x),
            )[k]
            src, dst, dev = w_half(l, block, half, p), LW.at[l, slot, rows, cols], (s, to, z)
        group = k if square and k < 2 else 2
        return remote(src, dst, d1_ss.at[l], d1_rs.at[l, where[p], group], dev)

    def d_send(l, p):
        for part in split(p):
            for k in range(4 if square else nd - 1):
                d_copy(l, part, k).start()

    @scoped
    def d_mid(l, p):
        if p == 0:
            for part in split(p):
                d_mid(l, part)
        elif square:
            col, width = pieces[p]
            cols = pl.ds(col, width)
            for k, block, half in ((0, dp_y, 0), (1, dp_x, 1)):
                copy = d_copy(l, p, k)
                copy.wait_recv()
                rows = pl.ds(block * Dr + half * half_rows, half_rows)
                arrived = LW[l, 2, half * half_rows : (half + 1) * half_rows, cols]
                W[l, rows, cols] = (W[l, rows, cols].astype(F32) + arrived.astype(F32)).astype(BF)
                d_copy(l, p, 4 + k).start()

    part_rows = Dr // 4

    def d_pass(l, p, q, rows=part_rows):
        for part in split(p):
            col, width = pieces[part]
            cols = pl.ds(col, width)
            src = W.at[l, pl.ds(d * Dr + q * rows, rows), cols]
            dst = L2.at[zh, pl.ds(q * rows, rows), cols]
            arrival = d2_rs.at[where[part], zh]
            to_self = (s == l) & (zh == s)

            @pl.when(to_self)
            def _():
                pltpu.make_async_copy(src, dst, arrival).start()

            @pl.when(jnp.logical_not(to_self))
            def _():
                remote(src, dst, d2_ss.at[l], arrival, (l, d, s * Hn + zl)).start()

    @scoped
    def d_total_rows(l, p):
        for part in split(p):
            col, width = pieces[part]
            cols = pl.ds(col, width)
            slots = 2 if square else nd - 1
            got(LW.at[l, pl.ds(0, slots), :, cols], d1_rs.at[l, where[part], 2])
            rows = pl.ds(d * Dr, Dr)
            total = W[l, rows, cols].astype(F32)
            for slot in range(slots):
                total = total + LW[l, slot, :, cols].astype(F32)
            W[l, rows, cols] = total.astype(BF)

    def d_sum(l, p):
        d_total_rows(l, p)
        d_pass(l, p, 0, Dr)

    def d_sent(l):
        got(W.at[l, pl.ds(0, (nd - 1) * Dr)], d1_ss.at[l])

        @pl.when(jnp.logical_not((s == l) & (zh == s)))
        def _():
            got(W.at[l, pl.ds(0, Dr)], d2_ss.at[l])

    outs = (
        pltpu.make_async_copy(MQ, out_qkv, m_sem.at[0]),
        pltpu.make_async_copy(MO, out_o, m_sem.at[1]),
        pltpu.make_async_copy(MGU, out_gu, m_sem.at[2]),
        pltpu.make_async_copy(MD, out_d, m_sem.at[3]),
    )

    def d_arrived(p):
        col, width = pieces[p]
        for half in range(2):
            got(L2.at[half, :, pl.ds(col, width)], d2_rs.at[where[p], half])

    def d_total(col, width):
        return L2[0, :, col : col + width].astype(F32) + L2[1, :, col : col + width].astype(F32)

    @scoped
    def d_final(p):
        d_arrived(p)
        if p >= 6:
            j = p - 6
            MQ[j] = d_total(j * C, C)
            pltpu.make_async_copy(MQ.at[j], out_qkv.at[j], m_sem.at[0]).start()
        elif p == 1:
            MO[...] = d_total(z_.oO, C).T
            outs[1].start()
        elif p == 3:
            MGU[...] = d_total(z_.oG, z_.GUw).T[: 2 * F]
            outs[2].start()
        elif p == 4:
            MD[...] = d_total(z_.oD, z_.Dw).T[:F]
            outs[3].start()

    @scoped
    def shard_attention():
        masters[0].wait()
        masters[1].wait()
        for j in range(3):
            L2[0, :, j * C : (j + 1) * C] = MQ[j].astype(BF)
        L2[0, :, z_.oO : z_.oG] = MO[...].T.astype(BF)

    @scoped
    def shard_feed():
        masters[2].wait()
        masters[3].wait()
        for ref, col, width, rows in ((MGU, z_.oG, z_.GUw, 2 * F), (MD, z_.oD, z_.Dw, F)):
            value = ref[...]
            if width > rows:
                value = jnp.concatenate([value, jnp.zeros((width - rows, Dr), F32)], axis=0)
            L2[0, :, col : col + width] = value.T.astype(BF)

    def chunk_rows(m, c):
        return pl.ds(m * MB + c * R, R)

    def ag_send(k, buf, m):
        rows = buf.at[chunk_rows(m, own)]
        for step in range(1, Hn):
            dev = (s, d, zh * Hn + peer_zl(step))
            remote(rows, rows, ag_ss.at[k], ag_rs.at[k, m, Hn - step], dev).start()
        remote(rows, rows, ag_ss.at[k], ag_rs.at[k, m, 0], core_dev).start()

    def ag_forward(k, buf, m):
        for step in range(1, Hn):
            rows = buf.at[chunk_rows(m, s * Hn + peer_zl(step))]
            got(rows, ag_rs.at[k, m, step])
            remote(rows, rows, ag_ss.at[k], ag_rs.at[k, m, 0], core_dev).start()

    def ag_wait(k, buf, m):
        got(buf.at[pl.ds(m * MB + (1 - s) * Hn * R, Hn * R)], ag_rs.at[k, m, 0])

    def ag_sent(k, buf):
        got(buf.at[pl.ds(0, MH * (2 * Hn - 1) * R)], ag_ss.at[k])

    def rs_copy1(k, m):
        par = k % 2
        return remote(
            PT.at[par, pl.ds(m * MB + (1 - s) * Hn * R, Hn * R)],
            RL1.at[par, m],
            r1_ss.at[par, m],
            r1_rs.at[par, m],
            core_dev,
        )

    def rs_copy2(k, m, step):
        par = k % 2
        return remote(
            RSB.at[par, m, step - 1],
            RL2.at[par, m, step - 1],
            r2_ss.at[par, m, step - 1],
            r2_rs.at[par, m, step - 1],
            (s, d, zh * Hn + peer_zl(step)),
        )

    def rs_first(k, m, value):
        PT[k % 2, pl.ds(m * MB, MB), :] = value.astype(BF)
        rs_copy1(k, m).start()

    def rs_second(k, m):
        par = k % 2
        copy = rs_copy1(k, m)
        copy.wait_send()
        copy.wait_recv()
        for step in range(1, Hn):
            there = peer_zl(step)
            part = PT[par, chunk_rows(m, s * Hn + there), :].astype(F32) + RL1[
                par, m, pl.ds(there * R, R), :
            ].astype(F32)
            RSB[par, m, step - 1] = part.astype(BF)
            rs_copy2(k, m, step).start()

    def after(k, i, m):
        @pl.when(i > 0)
        def _():
            rs_second(k, m)

    def rs_third(k, m):
        par = k % 2
        total = PT[par, chunk_rows(m, own), :].astype(F32) + RL1[
            par, m, pl.ds(zl * R, R), :
        ].astype(F32)
        for step in range(1, Hn):
            copy = rs_copy2(k, m, step)
            copy.wait_send()
            copy.wait_recv()
            total = total + RL2[par, m, step - 1].astype(F32)
        return total

    def own_rows(m):
        return pl.ds(m * R, R)

    def rms(rows):
        return lax.rsqrt(jnp.mean(rows * rows, axis=-1, keepdims=True) + EPS)

    def gain(l, which):
        return GV[l, which : which + 1, :]

    def rms_back(l, which, rows, grad):
        inverse = rms(rows)
        scaled = grad * gain(l, which)
        back = inverse * scaled - rows * (inverse * inverse * inverse) * jnp.mean(
            scaled * rows, axis=-1, keepdims=True
        )
        DG[l, which : which + 1, :] += jnp.sum(grad * rows * inverse, axis=0, keepdims=True)
        return back

    def send_out(buf, l, out, which, m):
        src = buf.at[l, own_rows(m)]
        dst = out.at[zh * MH + m]
        to_self = (s == l) & (zh == s)

        @pl.when(to_self)
        def _():
            pltpu.make_async_copy(src, dst, o_rs.at[which, zh]).start()

        @pl.when(jnp.logical_not(to_self))
        def _():
            remote(
                src, dst, o_ss.at[l], o_rs.at[which, zh], (l, d, s * Hn + zl)
            ).start()

    lane_head = lax.broadcasted_iota(jnp.int32, (1, C), 1) // DH
    head_bf = [(lane_head == h).astype(F32).astype(BF) for h in range(NH)]
    head_f = [(lane_head == h).astype(F32) for h in range(NH)]

    def stack(rows):
        return jnp.concatenate([rows * head_bf[h] for h in range(NH)], axis=0)

    def unstack(wide):
        out = wide[0:DH] * head_f[0]
        for h in range(1, NH):
            out = out + wide[h * DH : (h + 1) * DH] * head_f[h]
        return out

    def tall(mask):
        return jnp.concatenate([mask] * NH, axis=0)

    def head_mean(values):
        row = lax.broadcasted_iota(jnp.int32, (C, C), 0) // DH
        col = lax.broadcasted_iota(jnp.int32, (C, C), 1) // DH
        same = jnp.where(row == col, 1.0 / DH, 0.0).astype(BF)
        high = values.astype(BF)
        low = (values - high.astype(F32)).astype(BF)
        return mm(high, same) + mm(low, same)

    def block_rows(b):
        return pl.ds(pl.multiple_of(b * BLOCK, BLOCK), BLOCK)

    def qkv_block(l, b):
        rows = block_rows(b)
        return (QKV[l, rows, 0:C], QKV[l, rows, C : 2 * C], QKV[l, rows, 2 * C : 3 * C])

    def softplus(values):
        return jnp.maximum(values, 0.0) + jnp.log(1.0 + jnp.exp(-jnp.abs(values)))

    def features(values):
        return softplus(values.astype(F32)).astype(BF)

    def diag_forward(b):
        q, k, v = qkv_block(0, b)
        scores = mm(stack(q), k, NT) * (1.0 / math.sqrt(DH))
        scores = jnp.where(tall(MSK[b]) > 0.5, scores, -1e9)
        top = jnp.max(scores, axis=-1, keepdims=True)
        weights = jnp.exp(scores - top)
        weights = (weights / jnp.sum(weights, axis=-1, keepdims=True)).astype(BF)
        AP[0, b] = weights
        O[0, block_rows(b), :] = unstack(mm(weights, v)).astype(BF)

    def diag_backward(b, grad_o):
        q, k, v = qkv_block(0, b)
        low = stack(grad_o.astype(BF))
        weights = AP[0, b]
        wide = weights.astype(F32)
        grad_v = mm(weights, low, TN)
        grad_w = mm(low, v, NT)
        grad_s = wide * (grad_w - jnp.sum(grad_w * wide, axis=-1, keepdims=True))
        grad_s = (grad_s * (1.0 / math.sqrt(DH))).astype(BF)
        grad_q = unstack(mm(grad_s, k))
        grad_k = mm(grad_s, stack(q), TN)
        rows = block_rows(b)
        GQKV[rows, 0:C] = grad_q.astype(BF)
        GQKV[rows, C : 2 * C] = grad_k.astype(BF)
        GQKV[rows, 2 * C : 3 * C] = grad_v.astype(BF)

    def fold(square):
        out = square[0:DH] * head_f[0]
        for h in range(1, NH):
            out = out + square[h * DH : (h + 1) * DH] * head_f[h]
        return out

    def unfold(flat):
        return stack(flat.astype(BF))

    def wide_lanes(column):
        return jnp.concatenate([column] * (C // 128), axis=1)

    def norm_state(b, state):
        q, k, v = qkv_block(1, b)
        ST[b] = state
        key = features(k)
        term = mm(key, (v.astype(F32) * wide_lanes(TAIL[b])).astype(BF), TN)
        return wide_lanes(KEEP[b, 0:1, :]) * state + fold(term)

    def norm_forward(b, passed):
        q, k, v = qkv_block(1, b)
        query, key = features(q), features(k)
        local = jnp.where(tall(MSK[b]) > 0.5, mm(stack(query), key, NT), 0.0).astype(BF)
        AP[1, b] = local
        state = ST[b] + passed * SIN[0].astype(F32)
        ST[b] = state
        mixed = unstack(mm(local, v)) + wide_lanes(CAR[b]) * mm(query, unfold(state))
        rows = block_rows(b)
        UU[rows, :] = mixed
        O[1, rows, :] = (mixed * lax.rsqrt(head_mean(mixed * mixed) + EPS)).astype(BF)
        return passed * wide_lanes(KEEP[b, 0:1, :])

    def norm_back_first(b, grad_o, state):
        rows = block_rows(b)
        mixed = UU[rows, :]
        scale = lax.rsqrt(head_mean(mixed * mixed) + EPS)
        grad = scale * grad_o - mixed * (scale * scale * scale) * head_mean(grad_o * mixed)
        low = grad.astype(BF)
        DU[rows, :] = low
        ST2_store(b, state)
        query = features(QKV[1, rows, 0:C])
        term = mm(query, (low.astype(F32) * wide_lanes(CAR[b])).astype(BF), TN)
        return wide_lanes(KEEP[b, 0:1, :]) * state + fold(term)

    def ST2_store(b, state):
        ST[NBH + b] = state

    def sigmoid(values):
        return 1.0 / (1.0 + jnp.exp(-values.astype(F32)))

    def norm_back_local(b):
        rows = block_rows(b)
        q, k, v = qkv_block(1, b)
        query, key = features(q), features(k)
        low = DU[rows, :]
        stacked = stack(low)
        grad_a = jnp.where(tall(MSK[b]) > 0.5, mm(stacked, v, NT), 0.0).astype(BF)
        grad_q = unstack(mm(grad_a, key)) + wide_lanes(CAR[b]) * mm(low, unfold(ST[b]), NT)
        GQKV[rows, 0:C] = (grad_q * sigmoid(q)).astype(BF)
        GQKV[rows, C : 2 * C] = (mm(grad_a, stack(query), TN) * sigmoid(k)).astype(BF)
        GQKV[rows, 2 * C : 3 * C] = mm(AP[1, b], stacked, TN).astype(BF)

    def norm_back_state(b, passed):
        rows = block_rows(b)
        q, k, v = qkv_block(1, b)
        grad_wide = unfold(ST[NBH + b] + passed * SIN[1].astype(F32))
        tail = wide_lanes(TAIL[b])
        grad_k = tail * mm(v, grad_wide, NT) * sigmoid(k)
        grad_v = tail * mm(features(k), grad_wide)
        GQKV[rows, C : 2 * C] = (GQKV[rows, C : 2 * C].astype(F32) + grad_k).astype(BF)
        GQKV[rows, 2 * C : 3 * C] = (GQKV[rows, 2 * C : 3 * C].astype(F32) + grad_v).astype(BF)
        return passed * wide_lanes(KEEP[b, 0:1, :])

    @scoped
    def masks():
        row = lax.broadcasted_iota(jnp.int32, (BLOCK, BLOCK), 0)
        col = lax.broadcasted_iota(jnp.int32, (BLOCK, BLOCK), 1)
        token = lax.broadcasted_iota(jnp.int32, (MB, BLOCK), 0)
        lane = lax.broadcasted_iota(jnp.int32, (MB, BLOCK), 1)
        start = jnp.concatenate([starts_in[zh * MH + m] for m in range(MH)], axis=0)
        start = start.astype(F32).astype(BF)
        chunk_lane = lax.broadcasted_iota(jnp.int32, (BLOCK, MH), 1)
        for j in range(NB):
            upper = ((token // BLOCK == j) & (token % BLOCK <= lane)).astype(F32).astype(BF)
            count_row = mm(start, upper)
            count_col = mm(upper, start, (((0,), (1,)), ((), ())))
            for m in range(MH):
                b = m * NB + j
                c_row = count_row[m : m + 1, :]
                c_col = jnp.sum(
                    jnp.where(chunk_lane == m, count_col, 0.0), axis=1, keepdims=True
                )
                last = jnp.sum(
                    jnp.where(col[0:1] == BLOCK - 1, c_row, 0.0), axis=1, keepdims=True
                )
                MSK[b] = jnp.where((c_row == c_col) & (row >= col), 1.0, 0.0)
                CAR[b] = jnp.broadcast_to(jnp.where(c_col == 0.0, 1.0, 0.0), (BLOCK, 128))
                TAIL[b] = jnp.broadcast_to(jnp.where(c_col == last, 1.0, 0.0), (BLOCK, 128))
                KEEP[b] = jnp.broadcast_to(jnp.where(last == 0.0, 1.0, 0.0), (8, 128))

    place = d * nt + z

    def gain_copy(i):
        return remote(GL.at[place], GL.at[place], gl_sem.at[0], gl_sem.at[1], section_dev(i))

    @scoped
    def gains_out():
        width = gain_in.shape[1]
        row = lax.broadcasted_iota(jnp.int32, (width, 128), 0)
        col = lax.broadcasted_iota(jnp.int32, (width, 128), 1)
        spot = (col % width == row) & (col // width == place % (128 // width))
        GL[place] = mm(gain_in[...].astype(BF), spot.astype(F32).astype(BF))

        def one(i, carry):
            gain_copy(i).start()
            return carry

        lax.fori_loop(1, nd * nt, one, 0)

    @scoped
    def gains_in():
        for k in (1, 0):
            got(GL.at[pl.ds(0, nd * nt - 1)], gl_sem.at[k])
        each = nd * nt * 128 // D
        for t in range(D // 128):
            total = GL[t * each]
            for i in range(1, each):
                total = total + GL[t * each + i]
            GV[s, :, t * 128 : (t + 1) * 128] = total
        gain_swap().start()

    def gain_swap():
        return remote(GV.at[s], GV.at[s], g1_sem.at[0], g1_sem.at[1], core_dev)

    def gains_other():
        gain_swap().wait_send()
        got(GV.at[1 - s], g1_sem.at[1])

    def dp_gain(step):
        return remote(
            GOWN, DL2.at[step - 1], g_ss.at[1, step - 1], g_rs.at[1, step - 1], dp_dev(step)
        )

    def core_gain():
        return remote(DG.at[1 - s], DL0, g1_sem.at[2], g1_sem.at[3], core_dev)

    def z_gain(step):
        return remote(
            DG.at[s], DL1.at[step - 1], g_ss.at[0, step - 1], g_rs.at[0, step - 1], z_dev(step)
        )

    @scoped
    def gain_second():
        core_gain().wait()
        DG[s] = DG[s] + DL0[...]
        for step in range(1, nt):
            z_gain(step).start()

    @scoped
    def gain_third():
        total = DG[s]
        for step in range(1, nt):
            z_gain(step).wait()
            total = total + DL1[step - 1]
        GOWN[...] = total
        for step in range(1, nd):
            dp_gain(step).start()

    @scoped
    def gain_final():
        total = GOWN[...]
        for step in range(1, nd):
            dp_gain(step).wait()
            total = total + DL2[step - 1]
        GOWN[...] = total
        width = out_gain.shape[1]
        each = 128 // width
        tile = GOWN[:, pl.ds(pl.multiple_of(place // each * 128, 128), 128)]
        mine = jnp.zeros((2, width), F32)
        for i in range(each):
            piece = tile[:, i * width : (i + 1) * width]
            mine = jnp.where(place % each == i, piece, mine)
        out_gain[...] = mine

    def loop(count, fn):
        def step(i, carry):
            fn(i)
            return carry

        with jax.named_scope(fn.__name__):
            lax.fori_loop(0, count, step, 0)

    def chunk(m):
        return pl.ds(pl.multiple_of(m * MB, BLOCK), MB)

    def w_cols(l, p):
        col, width = pieces[p]
        return W[l, :, col : col + width]

    def w_gate_up(l):
        return W[l, :, z_.oG : z_.oD]

    @scoped
    def state_copy(slot):
        return remote(
            SEND_STATE.at[slot],
            SIN.at[slot],
            st_ss.at[slot],
            st_rs.at[slot],
            (s, d, (z + Hn) % nt),
        )

    def state_out(slot, value, sender):
        SEND_STATE[slot] = value.astype(BF)

        @pl.when(zh == sender)
        def _():
            SIN[slot] = jnp.zeros((DH, C), BF)
            state_copy(slot).start()

    @scoped
    def state_in(slot, sender):
        @pl.when(zh != sender)
        def _():
            state_copy(slot).wait_recv()

    outer = zh == zl
    inner, far = jnp.logical_not(outer), jnp.logical_not(near)

    def only(cond, fn):
        pl.when(cond)(fn)

    def hand_far(l, cond, ps):
        def go():
            for p in ps:
                w_hand_far(l, p)

        pl.when((s == l) & cond)(go)

    def hand_near(ps):
        for l in range(2):

            @pl.when(s == l)
            def _():
                for p in ps:
                    w_hand_near(l, p)

    def x_out():
        spread_tokens(xin, XF, 0)

    gains_out()
    shard_attention()
    hand_far(0, s == 0, [5])
    hand_near([5])
    only((s == 0) & inner, x_out)
    pump_near([("s", 0, 5)])
    own_tokens(xin, XF, 0)
    own_tokens(cot, GF.at[1], 1)
    shard_feed()
    hand_near([2, 3, 4])
    masks()
    for l in range(2):
        DG[l] = jnp.zeros((2, D), F32)
    pump_near([("s", 0, 2)])
    gains_in()
    pump_far([("s", 0, 5)])
    only((s == 0) & outer & far, x_out)
    pump([("f", 0, 5)])
    pump_near([("f", 0, 2)])
    only((s == 0) & outer & near, x_out)
    only(s == 1, gains_other)
    for m in range(MH):
        relay_tokens(XF, 0, m)
    hand_far(0, s == 0, [2, 3, 4])
    await_tokens(XF, 0, 0)

    def cot_out():
        spread_tokens(cot, GF.at[1], 1)

    stage = {
        (0, "attended"): lambda: (
            pump_near([("f", 0, 3), ("f", 0, 4)]),
            pump_far([("s", 0, 2), ("s", 0, 3), ("f", 0, 2), ("s", 0, 4)]),
        ),
        (0, "hidden"): lambda: (
            hand_far(1, inner, [5, 4, 2, 3]),
            hand_far(1, outer, [5]),
            pump_near([("s", 1, 5)]),
            pump_far([("f", 0, 3), ("f", 0, 4)]),
        ),
        (0, "ready"): lambda: (
            pump_near([("f", 1, 5)]),
            pump_far([("s", 1, 5)]),
        ),
        (0, "feeding"): lambda: (
            hand_far(1, outer, [4]),
            pump_near([("s", 1, 4)]),
        ),
        (0, "fed"): lambda: (
            hand_far(1, outer, [2, 3]),
            pump_near([("s", 1, 2), ("f", 1, 4)]),
            pump_far([("f", 1, 5), ("s", 1, 4)]),
            only(s == 0, gains_other),
        ),
        (0, "result"): lambda: (
            only(s == 1, cot_out),
            pump_near([("s", 1, 3)]),
            pump_far([("s", 1, 2), ("f", 1, 4)]),
        ),
        (1, "states"): lambda: (
            [relay_tokens(GF.at[1], 1, m) for m in reversed(range(MH))],
            pump_near([("f", 1, 2), ("f", 1, 3)]),
            pump_far([("s", 1, 3), ("f", 1, 2)]),
        ),
        (1, "attended"): lambda: (pump_far([("f", 1, 3)]),),
        (1, "hidden"): lambda: (results_out(Y, 0, out_y, 0),),
        (1, "ready"): lambda: (),
        (1, "fed"): lambda: (),
        "b1 second": lambda: (),
        "b1 middle": lambda: (results_out(Y, 1, out_y, 0), d_mid(1, 4)),
        "b1 feed": lambda: (),
        "b1 third": lambda: (d_mid(1, 3),),
        "b1 end": lambda: (d_total_rows(1, 3),),
        "b0 second": lambda: (d_total_rows(1, 0),),
        "b0 middle": lambda: (),
        "b0 feed": lambda: (results_out(GX, 1, out_g, 1), d_total_rows(1, 1)),
        "b0 third": lambda: (
            only(far, lambda: run(d_mid, 2)),
            only(near, lambda: run(d_mid, 4) or run(d_send, 2, 3)),
        ),
        "b0 end": lambda: (
            core_gain().start(),
            only(near, lambda: run(d_send, 0, 1)),
            only(far, lambda: far_tail()),
            only(near, lambda: near_tail()),
            gain_third(),
        ),
    }

    def run(step, *parts):
        for p in parts:
            step(0, p)

    def far_tail():
        gain_second()
        run(d_mid, 6)
        run(d_sum, 3)
        run(d_mid, 7, 8)
        run(d_sum, 6)
        run(d_mid, 1)
        run(d_sum, 7, 8, 1)
        results_out(GX, 0, out_g, 1)

    def near_tail():
        run(d_sum, 4)
        run(d_mid, 2, 3)
        gain_second()
        run(d_mid, 6, 7, 8, 1)
        results_out(GX, 0, out_g, 1)
        run(d_sum, 2, 3, 6, 7, 8, 1)

    def results_out(buf, l, out, which):
        for m in range(MH):
            send_out(buf, l, out, which, m)

    def input_rows(l, m):
        if l == 0:
            return XF[chunk_rows(m, own), :].astype(F32)
        return Y[0, own_rows(m), :].astype(F32)

    def gate_up_grad(grad, both):
        parts = [grad * both[:, F : 2 * F], grad * both[:, :F]]
        if z_.GUw > 2 * F:
            parts.append(jnp.zeros((MB, z_.GUw - 2 * F), F32))
        return jnp.concatenate(parts, axis=1).astype(BF)

    def finish_layer(l, rs2, ag3):
        def result(m):
            rows = (H[l, own_rows(m), :] + rs_third(rs2, m)).astype(BF)
            Y[l, own_rows(m), :] = rows
            if l == 0:
                wide = rows.astype(F32)
                N1[1, chunk_rows(m, own), :] = (wide * rms(wide) * gain(1, 0)).astype(BF)
                ag_send(ag3, N1.at[1], m)

        loop(MH, result)

    def forward(l, ag1, rs1, ag2, rs2, ag3):
        w_ready(l, 5)

        def qkv_chunk(m):
            if l == 0:
                pl.when(m > 0)(lambda: await_tokens(XF, 0, m))
                pl.when((m == 1) & near)(lambda: pump([("s", 0, 3), ("s", 0, 4)]))
                rows = XF[chunk(m), :].astype(F32)
                N1[0, chunk(m), :] = (rows * rms(rows) * gain(0, 0)).astype(BF)
            else:
                ag_forward(ag1, N1.at[1], m)
                ag_wait(ag1, N1.at[1], m)
            QKV[l, chunk(m), :] = mm(N1[l, chunk(m), :], w_cols(l, 0)).astype(BF)

        def out_chunk(m):
            rs_first(rs1, m, mm(O[l, chunk(m), :], w_cols(l, 1), NT))

        if l == 0:

            def attend(m):
                qkv_chunk(m)
                for i in range(NB):
                    diag_forward(m * NB + i)
                out_chunk(m)
                after(rs1, m, m - 1)

            loop(MH, attend)
            rs_second(rs1, MH - 1)
            stage[l, "attended"]()
        else:

            def states(m, state):
                qkv_chunk(m)
                for i in range(NB):
                    state = norm_state(m * NB + i, state)
                return state

            with jax.named_scope('states'):
                last = lax.fori_loop(0, MH, states, jnp.zeros((DH, C), F32))
            w_handed_out()
            state_out(0, last, 0)
            state_in(0, 0)
            stage[l, "states"]()

            def attend(m, passed):
                for i in range(NB):
                    passed = norm_forward(m * NB + i, passed)
                out_chunk(m)
                after(rs1, m, m - 1)
                return passed

            with jax.named_scope('attend'):
                lax.fori_loop(0, MH, attend, jnp.ones((1, C), F32))
            rs_second(rs1, MH - 1)
            stage[l, "attended"]()

        def hidden_rows(m):
            rows = input_rows(l, m) + rs_third(rs1, m)
            H[l, own_rows(m), :] = rows
            N2[l, chunk_rows(m, own), :] = (rows * rms(rows) * gain(l, 1)).astype(BF)
            ag_send(ag2, N2.at[l], m)

        loop(MH, hidden_rows)
        stage[l, "hidden"]()
        w_ready(l, 4)
        if l == 1:

            def hidden_grad(m):
                await_tokens(GF.at[1], 1, m)
                GGU[chunk(m), 0 : z_.Dw] = mm(GF[1, chunk(m), :], w_cols(1, 4)).astype(BF)

            loop(MH, hidden_grad)
        w_ready(l, 2)
        w_ready(l, 3)
        stage[l, "ready"]()

        def feed(m):
            ag_forward(ag2, N2.at[l], m)
            ag_wait(ag2, N2.at[l], m)
            rows = N2[l, chunk(m), :]
            both = mm(rows, w_gate_up(l))
            if l == 0:
                GU[l, chunk(m), :] = both.astype(BF)
            else:
                grad = GGU[chunk(m), 0 : z_.Dw].astype(F32)[:, :F]
                GGU[chunk(m), :] = gate_up_grad(grad, both)
            hidden = both[:, :F] * both[:, F : 2 * F]
            if z_.Dw > F:
                hidden = jnp.concatenate([hidden, jnp.zeros((MB, z_.Dw - F), F32)], axis=1)
            hidden = hidden.astype(BF)
            HID[l, chunk(m), :] = hidden
            rs_first(rs2, m, mm(hidden, w_cols(l, 4), NT))
            if l == 0:


                @pl.when(m == 1)
                def _():
                    stage[0, "feeding"]()

            after(rs2, m, m - 1)

        loop(MH, feed)
        rs_second(rs2, MH - 1)
        stage[l, "fed"]()

        if l == 0:
            finish_layer(l, rs2, ag3)
            stage[l, "result"]()

    forward(0, None, 0, 0, 1, 1)
    forward(1, 1, 2, 2, 3, None)

    RB = min(D, 256)

    @scoped
    def grad_weight(l, p, left, right, send=True):
        col, width = pieces[p]
        for r in range(D // RB):
            W[l, r * RB : (r + 1) * RB, col : col + width] = mm(
                left[:, r * RB : (r + 1) * RB], right, TN
            ).astype(BF)
        if send:
            d_send(l, p)

    def rest(l, p):
        for q in range(MH, 4):
            d_pass(l, p, q)

    def grad_part(l, p, send=True):
        col, width = pieces[p]
        grad_weight(l, p, N2[l], GGU[:, col - z_.oG : col - z_.oG + width], send)

    def backward(l, ag_in, rs1, ag2, rs2, ag_out):
        w_shared(l)

        def feed_back(i):
            m = MH - 1 - i
            if l == 0:
                ag_forward(ag_in, GF.at[0], m)
                ag_wait(ag_in, GF.at[0], m)
                grad = mm(GF[l, chunk(m), :], w_cols(l, 4))[:, :F]
                GGU[chunk(m), :] = gate_up_grad(grad, GU[l, chunk(m), :].astype(F32))
            rs_first(rs1, m, mm(GGU[chunk(m), :], w_gate_up(l), NT))
            after(rs1, i, m + 1)
            if l == 0:

                @pl.when(i == 0)
                def _():
                    d_mid(1, 1)
                    d_mid(1, 0)

                d_pass(1, 3, i)
        if l == 1:
            grad_weight(l, 4, GF[l], HID[l])
        loop(MH, feed_back)
        rs_second(rs1, 0)
        if l == 0:
            rest(1, 3)
            grad_weight(l, 4, GF[l], HID[l], False)
            only(far, lambda: d_send(0, 4))
        else:
            grad_part(l, 2)
            finish_layer(1, 3, None)
        stage[f"b{l} second"]()

        def middle(i):
            m = MH - 1 - i
            rows = H[l, own_rows(m), :]
            grad = GF[l, chunk_rows(m, own), :].astype(F32) + rms_back(
                l, 1, rows, rs_third(rs1, m)
            )
            GH[own_rows(m), :] = grad
            GA[l, chunk_rows(m, own), :] = grad.astype(BF)
            ag_send(ag2, GA.at[l], m)
            if l == 0:
                only((i == 1) & near, lambda: d_send(0, 4))
                d_pass(1, 0, i)

        loop(MH, middle)
        if l == 0:
            rest(1, 0)
        stage[f"b{l} middle"]()
        if l == 0:
            grad_part(l, 2, False)

            @pl.when(far)
            def _():
                d_mid(0, 4)
                d_send(0, 2)

            grad_part(l, 3, False)
            only(far, lambda: d_send(0, 3))
        else:
            grad_part(l, 3)
        stage[f"b{l} feed"]()

        def grad_o(m):
            ag_forward(ag2, GA.at[l], m)
            ag_wait(ag2, GA.at[l], m)
            return mm(GA[l, chunk(m), :], w_cols(l, 1))

        def qkv_back(i, m):
            rs_first(rs2, m, mm(GQKV[chunk(m), :], w_cols(l, 0), NT))
            after(rs2, i, m + 1)

        if l == 0:

            def attend(i):
                m = MH - 1 - i
                grad = grad_o(m)
                for j in range(NB):
                    diag_backward(m * NB + j, grad[j * BLOCK : (j + 1) * BLOCK])
                qkv_back(i, m)
                d_pass(1, 1, i)
                only((i == 0) & far, lambda: d_sum(0, 4))

            loop(MH, attend)
        else:

            def states(i, state):
                m = MH - 1 - i
                grad = grad_o(m)
                for j in reversed(range(NB)):
                    state = norm_back_first(m * NB + j, grad[j * BLOCK : (j + 1) * BLOCK], state)
                return state

            with jax.named_scope("states"):
                last = lax.fori_loop(0, MH, states, jnp.zeros((DH, C), F32))
            state_out(1, last, 1)
            d_mid(1, 2)
            grad_weight(l, 1, GA[l], O[l])

            def attend_local(m):
                for j in range(NB):
                    norm_back_local(m * NB + j)

            loop(MH, attend_local)
            d_total_rows(1, 4)
            state_in(1, 1)
            pl.when(zh == 0)(lambda: d_pass(1, 4, 0, Dr))

            def attend(i, passed):
                m = MH - 1 - i
                for j in reversed(range(NB)):
                    passed = norm_back_state(m * NB + j, passed)
                qkv_back(i, m)

                @pl.when(zh == 1)
                def _():
                    d_pass(1, 4, i)

                return passed

            with jax.named_scope("attend"):
                lax.fori_loop(0, MH, attend, jnp.ones((1, C), F32))

        rs_second(rs2, 0)
        if l == 0:
            rest(1, 1)
        else:
            pl.when(zh == 1)(lambda: rest(1, 4))
        stage[f"b{l} third"]()
        grad_weight(l, 0, N1[l], GQKV[...], l == 1)
        if l == 0:
            grad_weight(l, 1, GA[l], O[l], False)

            @pl.when(far)
            def _():
                d_mid(0, 3)
                d_send(0, 0)
                d_send(0, 1)
                d_sum(0, 2)


        def result(i):
            m = MH - 1 - i
            grad = GH[own_rows(m), :] + rms_back(l, 0, input_rows(l, m), rs_third(rs2, m))
            low = grad.astype(BF)
            GX[l, own_rows(m), :] = low
            if l == 1:
                GF[0, chunk_rows(m, own), :] = low
                ag_send(ag_out, GF.at[0], m)
                pl.when(i == 0)(lambda: d_total_rows(1, 2))
                d_pass(1, 2, i)

        loop(MH, result)
        if l == 1:
            rest(1, 2)
        stage[f"b{l} end"]()

    backward(1, None, 4, 3, 5, 4)
    backward(0, 4, 6, 5, 7, None)

    for p in (4, 2, 3, 6, 7, 8, 1):
        d_final(p)
    gain_final()
    for copy in outs:
        copy.wait()
    for l in range(2):
        d_sent(l)

    ags = ((0, N2.at[0]), (1, N1.at[1]), (2, N2.at[1]), (3, GA.at[1]), (4, GF.at[0]), (5, GA.at[0]))

    for slot in range(2):

        @pl.when(zh == slot)
        def _():
            state_copy(slot).wait_send()

    for k, buf in ags:
        ag_sent(k, buf)
    for l in range(2):

        @pl.when(jnp.logical_not((s == l) & (zh == s)))
        def _():
            got(XF.at[pl.ds(0, 2 * MH * R)], o_ss.at[l])

    for half in range(2):
        got(out_y.at[pl.ds(half * MH, MH)], o_rs.at[0, half])
        got(out_g.at[pl.ds(half * MH, MH)], o_rs.at[1, half])
    for k in range(2):
        got(XF.at[pl.ds(0, MH * (nt - 1) * R)], x_sem.at[k])


def place_results(*refs):
    count = (len(refs) - 2) // 3
    sources, targets, held = refs[:count], refs[count : 2 * count], refs[2 * count : 3 * count]
    in_sem, out_sem = refs[-2:]
    reads = [pltpu.make_async_copy(sources[i], held[i], in_sem.at[i]) for i in range(count)]
    writes = [pltpu.make_async_copy(held[i], targets[i], out_sem.at[i]) for i in range(count)]
    for copy in reads:
        copy.start()
    for read, write in zip(reads, writes):
        read.wait()
        write.start()
    for copy in writes:
        copy.wait()


def solution(mesh):
    nd, nt = mesh.shape["dp"], mesh.shape["tensor"]

    def on_device(inputs, starts, cotangent, qkv_m, out_m, gateup_m, down_m, gain_m):
        z_ = Sizes(
            mesh,
            inputs.shape[3],
            inputs.shape[1],
            inputs.shape[2],
            qkv_m.shape[3],
            gateup_m.shape[3],
        )
        D, R, C, F, Dr, M, MH, Hn, MB, T, NBH, N, NH = (
            z_.D,
            z_.R,
            z_.C,
            z_.F,
            z_.Dr,
            z_.M,
            z_.MH,
            z_.Hn,
            z_.MB,
            z_.T,
            z_.NBH,
            z_.N,
            z_.NH,
        )
        width = gain_m.shape[2]
        qkv_rows = jnp.transpose(qkv_m[0], (1, 0, 2))
        gateup_rows = jnp.transpose(gateup_m[0], (1, 2, 0)).reshape(2 * F, Dr)
        anywhere = pl.BlockSpec(memory_space=pl.ANY)
        vmem = pl.BlockSpec(memory_space=pltpu.VMEM)
        DMA = pltpu.SemaphoreType.DMA
        V = pltpu.VMEM
        scratch = [
            V((3, Dr, C), F32),
            V((C, Dr), F32),
            V((2 * F, Dr), F32),
            V((F, Dr), F32),
            V((2, D, N), BF),
            V((2, nd - 1, Dr, N), BF),
            V((2, Dr, N), BF),
            V((T, D), BF),
            V((2, T, D), BF),
            V((2, T, D), BF),
            V((2, T, D), BF),
            V((2, T, 3 * C), BF),
            V((2, T, C), BF),
            V((1, T, z_.GUw), BF),
            V((2, T, z_.Dw), BF),
            V((2, MH * R, D), F32),
            V((2, MH * R, D), BF),
            V((2, T, D), BF),
            V((T, z_.GUw), BF),
            V((T, 3 * C), BF),
            V((MH * R, D), F32),
            V((2, MH * R, D), BF),
            V((2, T, D), BF),
            V((2, MH, Hn * R, D), BF),
            V((2, MH, Hn - 1, R, D), BF),
            V((2, MH, Hn - 1, R, D), BF),
            V((2, NBH, NH * BLOCK, BLOCK), BF),
            V((T, C), F32),
            V((T, C), BF),
            V((2 * NBH, DH, C), F32),
            V((2, DH, C), BF),
            V((2, DH, C), BF),
            V((NBH, BLOCK, BLOCK), F32),
            V((NBH, BLOCK, 128), F32),
            V((NBH, BLOCK, 128), F32),
            V((NBH, 8, 128), F32),
            V((nd * nt, 2, 128), F32),
            V((2, 2, D), F32),
            V((2, D), F32),
            V((2, 2, D), F32),
            V((2, D), F32),
            V((nt - 1, 2, D), F32),
            V((nd - 1, 2, D), F32),
            DMA((2, MH)),
            DMA((2,)),
            DMA((2, MH, nt - 1)),
            DMA((2,)),
            DMA((2, 4)),
            DMA((2,)),
            DMA((2, 4, max(4, nd - 1))),
            DMA((6,)),
            DMA((6, MH, Hn)),
            DMA((2, MH)),
            DMA((2, MH)),
            DMA((2, MH, Hn - 1)),
            DMA((2, MH, Hn - 1)),
            DMA((2,)),
            DMA((2,)),
            DMA((2,)),
            DMA((2, 2)),
            DMA((2,)),
            DMA((2, 7, 3)),
            DMA((2,)),
            DMA((7, 2)),
            DMA((4,)),
            DMA((2, max(nd, nt) - 1)),
            DMA((2, max(nd, nt) - 1)),
            DMA((2,)),
            DMA((4,)),
        ]
        out_y, out_g, grad_qkv, grad_o, grad_gu, grad_d, grad_gain = pl.pallas_call(
            functools.partial(body, z_),
            out_shape=(
                jax.ShapeDtypeStruct((M, R, D), BF),
                jax.ShapeDtypeStruct((M, R, D), BF),
                jax.ShapeDtypeStruct((3, Dr, C), F32),
                jax.ShapeDtypeStruct((C, Dr), F32),
                jax.ShapeDtypeStruct((2 * F, Dr), F32),
                jax.ShapeDtypeStruct((F, Dr), F32),
                jax.ShapeDtypeStruct((2, width), F32),
            ),
            in_specs=[anywhere] * 6 + [vmem, vmem],
            out_specs=(anywhere,) * 6 + (vmem,),
            scratch_shapes=scratch,
            compiler_params=pltpu.CompilerParams(
                collective_id=0, has_side_effects=True, vmem_limit_bytes=63 * 1024 * 1024
            ),
        )(
            qkv_rows,
            out_m[0],
            gateup_rows,
            down_m[0],
            inputs[0],
            cotangent[0],
            jnp.transpose(starts, (1, 0, 2)),
            gain_m[0],
        )
        results = (out_y, out_g, grad_qkv, grad_o, grad_gu, grad_d, grad_gain)
        out_y, out_g, grad_qkv, grad_o, grad_gu, grad_d, grad_gain = pl.pallas_call(
            place_results,
            out_shape=tuple(jax.ShapeDtypeStruct(r.shape, r.dtype) for r in results),
            in_specs=[anywhere] * len(results),
            out_specs=(anywhere,) * len(results),
            scratch_shapes=[V(r.shape, r.dtype) for r in results]
            + [DMA((len(results),)), DMA((len(results),))],
        )(*results)
        return (
            out_y[None, None],
            out_g[None, None],
            jnp.transpose(grad_qkv, (1, 0, 2))[None],
            grad_o[None],
            jnp.transpose(grad_gu.reshape(2, F, Dr), (2, 0, 1))[None],
            grad_d[None],
            grad_gain[None],
        )

    return jax.shard_map(
        on_device,
        mesh=mesh,
        in_specs=(
            P("dp", None, "tensor", None),
            P("dp", None, None),
            P("dp", None, "tensor", None),
            P("section", "dp", None, "tensor"),
            P("section", "tensor", "dp"),
            P("section", "dp", None, "tensor"),
            P("section", "tensor", "dp"),
            P("section", None, ("dp", "tensor")),
        ),
        out_specs=(
            P("section", "dp", None, "tensor", None),
            P("section", "dp", None, "tensor", None),
            P("section", "dp", None, "tensor"),
            P("section", "tensor", "dp"),
            P("section", "dp", None, "tensor"),
            P("section", "tensor", "dp"),
            P("section", None, ("dp", "tensor")),
        ),
        check_vma=False,
    )
```

```python
import functools
import math

import jax
import jax.numpy as jnp
from jax import lax
from jax.experimental import pallas as pl
from jax.experimental.pallas import tpu as pltpu
from jax.sharding import PartitionSpec as P

DH = 64
BLOCK = 64
EPS = 1e-6
BF = jnp.bfloat16
F32 = jnp.float32
MESH = pl.DeviceIdType.MESH
NN = (((1,), (0,)), ((), ()))
NT = (((1,), (1,)), ((), ()))
TN = (((0,), (0,)), ((), ()))


def mm(a, b, dims=NN):
    return lax.dot_general(a, b, dims, preferred_element_type=F32)


def ceil_to(value, unit):
    return (value + unit - 1) // unit * unit


def scoped(fn):
    @functools.wraps(fn)
    def inner(*args):
        with jax.named_scope(fn.__name__):
            return fn(*args)

    return inner


class Sizes:
    def __init__(self, mesh, model, micro, rows, cols, hidden):
        self.nd, self.nt = mesh.shape["dp"], mesh.shape["tensor"]
        self.D, self.M, self.R, self.C, self.F = model, micro, rows, cols, hidden
        self.GUw, self.Dw = ceil_to(2 * hidden, 128), ceil_to(hidden, 128)
        self.Dr = model // self.nd
        self.MH, self.Hn = micro // 2, self.nt // 2
        self.MB = rows * self.nt
        self.T = self.MH * self.MB
        self.NH = cols // DH
        self.NB = self.MB // BLOCK
        self.NBH = self.MH * self.NB
        self.oO, self.oG = 3 * cols, 4 * cols
        self.oD = self.oG + self.GUw
        self.N = self.oD + self.Dw
        first = ceil_to(self.GUw // 2, 128)
        self.pieces = (
            (0, 3 * cols),
            (self.oO, cols),
            (self.oG, first),
            (self.oG + first, self.GUw - first),
            (self.oD, self.Dw),
            (0, 4 * cols),
            (0, cols),
            (cols, cols),
            (2 * cols, cols),
        )


def body(
    z_,
    qkv_in,
    o_in,
    gu_in,
    d_in,
    xin,
    cot,
    starts_in,
    gain_in,
    out_y,
    out_g,
    out_qkv,
    out_o,
    out_gu,
    out_d,
    out_gain,
    MQ,
    MO,
    MGU,
    MD,
    W,
    LW,
    L2,
    XF,
    GF,
    N1,
    N2,
    QKV,
    O,
    GU,
    HID,
    H,
    Y,
    GA,
    GGU,
    GQKV,
    GH,
    GX,
    PT,
    RL1,
    RL2,
    RSB,
    AP,
    UU,
    DU,
    ST,
    SIN,
    SEND_STATE,
    MSK,
    CAR,
    TAIL,
    KEEP,
    GL,
    GV,
    GOWN,
    DG,
    DL0,
    DL1,
    DL2,
    in_sem,
    x_sem,
    x_rs,
    w1_ss,
    w1_rs,
    w2_ss,
    w2_rs,
    ag_ss,
    ag_rs,
    r1_ss,
    r1_rs,
    r2_ss,
    r2_rs,
    st_ss,
    st_rs,
    o_ss,
    o_rs,
    d1_ss,
    d1_rs,
    d2_ss,
    d2_rs,
    g1_sem,
    g_ss,
    g_rs,
    gl_sem,
    m_sem,
):
    D, R, C, F, Dr, MH, Hn, MB, T, NH, NB, NBH = (
        z_.D,
        z_.R,
        z_.C,
        z_.F,
        z_.Dr,
        z_.MH,
        z_.Hn,
        z_.MB,
        z_.T,
        z_.NH,
        z_.NB,
        z_.NBH,
    )
    nd, nt = z_.nd, z_.nt
    pieces = z_.pieces
    s, d, z = lax.axis_index("section"), lax.axis_index("dp"), lax.axis_index("tensor")
    zh, zl = z // Hn, z % Hn
    own = s * Hn + zl
    core_dev = (1 - s, d, z)

    def remote(src, dst, ssem, rsem, dev):
        return pltpu.make_async_remote_copy(
            src_ref=src, dst_ref=dst, send_sem=ssem, recv_sem=rsem, device_id=dev, device_id_type=MESH
        )

    def got(dst, sem):
        pltpu.make_async_copy(dst, dst, sem).wait()

    def dp_dev(step):
        return (s, (d + step) % nd, z)

    def z_dev(step):
        return (s, d, (z + step) % nt)

    def peer_zl(step):
        return (zl + step) % Hn

    masters = (
        pltpu.make_async_copy(qkv_in, MQ, m_sem.at[0]),
        pltpu.make_async_copy(o_in, MO, m_sem.at[1]),
        pltpu.make_async_copy(gu_in, MGU, m_sem.at[2]),
        pltpu.make_async_copy(d_in, MD, m_sem.at[3]),
    )
    for copy in masters:
        copy.start()

    barrier = pltpu.get_barrier_semaphore()

    def section_dev(i):
        return (s, (d + i // nt) % nd, (z + i % nt) % nt)

    def greet(i, carry):
        pl.semaphore_signal(barrier, inc=1, device_id=section_dev(i), device_id_type=MESH)
        return carry

    lax.fori_loop(1, nd * nt, greet, 0)
    pl.semaphore_signal(barrier, inc=1, device_id=core_dev, device_id_type=MESH)
    far_dev = (1 - s, d, (z + Hn) % nt)
    pl.semaphore_signal(barrier, inc=1, device_id=far_dev, device_id_type=MESH)
    pl.semaphore_wait(barrier, nd * nt + 1)

    def own_tokens(src, dst, array):
        for m in range(MH):
            mine = dst.at[pl.ds(m * MB + z * R, R)]
            pltpu.make_async_copy(src.at[zh * MH + m], mine, in_sem.at[array, m]).start()

    def spread_tokens(src, dst, array):
        for m in range(MH):
            mine = dst.at[pl.ds(m * MB + z * R, R)]
            for step in range(1, nt):
                other = (z + step) % nt

                @pl.when((other // Hn == zh) | (step == Hn))
                def _():
                    remote(
                        src.at[(other // Hn) * MH + m],
                        mine,
                        x_sem.at[0],
                        x_rs.at[array, m, step - 1],
                        z_dev(step),
                    ).start()

    def relay_tokens(dst, array, m):
        @pl.when(s == array)
        def _():
            chip = (z + Hn) % nt
            rows = dst.at[pl.ds(m * MB + chip * R, R)]
            got(rows, x_rs.at[array, m, Hn - 1])
            for step in range(1, Hn):
                peer = zh * Hn + peer_zl(step)
                remote(
                    rows,
                    rows,
                    x_sem.at[0],
                    x_rs.at[array, m, (peer + nt - chip) % nt - 1],
                    (s, d, peer),
                ).start()

    def await_tokens(dst, array, m):
        got(dst.at[pl.ds(m * MB + z * R, R)], in_sem.at[array, m])
        for step in range(1, nt):
            rows = dst.at[pl.ds(m * MB + (z + nt - step) % nt * R, R)]
            if step == Hn:
                pl.when(s != array)(lambda: got(rows, x_rs.at[array, m, step - 1]))
            else:
                got(rows, x_rs.at[array, m, step - 1])

            @pl.when(s == array)
            def _():
                remote(
                    rows, rows, x_sem.at[1], x_rs.at[array, m, step - 1], core_dev
                ).start()

    spot = {5: 0, 2: 1, 3: 2, 4: 3}

    def w_rows(l, block, p):
        col, width = pieces[p]
        return W.at[l, pl.ds(block * Dr, Dr), pl.ds(col, width)]

    def shard_cols(p):
        col, width = pieces[p]
        return L2.at[0, :, pl.ds(col, width)]

    def w_hand_near(l, p):
        @pl.when(zh == s)
        def _():
            pltpu.make_async_copy(shard_cols(p), w_rows(l, d, p), w1_rs.at[l, spot[p]]).start()

        @pl.when(zh != s)
        def _():
            w_hand(l, p, 0, core_dev).start()

    def w_hand(l, p, which, dev):
        return remote(
            shard_cols(p), w_rows(l, d, p), w1_ss.at[which], w1_rs.at[l, spot[p]], dev
        )

    def w_hand_far(l, p):
        w_hand(l, p, 1, (zh, d, (z + Hn) % nt)).start()

    def w_handed_out():
        @pl.when(zh != s)
        def _():
            got(L2.at[0], w1_ss.at[0])

        got(L2.at[0], w1_ss.at[1])

    square = nd == 4
    half_rows = Dr // 2
    dp_x, dp_y = d + 1 - 2 * (d % 2), (d + 2) % nd

    def w_half(l, block, half, p):
        col, width = pieces[p]
        return W.at[l, pl.ds(block * Dr + half * half_rows, half_rows), pl.ds(col, width)]

    def w_copy(l, p, k):
        if not square:
            rows, dev = w_rows(l, d, p), dp_dev(k + 1)
        elif k < 2:
            rows, dev = w_rows(l, d, p), (s, (dp_x, dp_y)[k], z)
        elif k == 2:
            rows, dev = w_half(l, dp_x, 0, p), (s, dp_y, z)
        else:
            rows, dev = w_half(l, dp_y, 1, p), (s, dp_x, z)
        return remote(rows, rows, w2_ss.at[l], w2_rs.at[l, spot[p], k], dev)

    def w_share(l, p):
        got(w_rows(l, d, p), w1_rs.at[l, spot[p]])
        for k in range(2 if square else nd - 1):
            w_copy(l, p, k).start()

    def w_forward(l, p):
        if square:
            got(w_rows(l, dp_x, p), w2_rs.at[l, spot[p], 0])
            w_copy(l, p, 2).start()
            got(w_rows(l, dp_y, p), w2_rs.at[l, spot[p], 1])
            w_copy(l, p, 3).start()

    def w_ready(l, p):
        if square:
            got(w_half(l, 3 - d, 0, p), w2_rs.at[l, spot[p], 2])
            got(w_half(l, 3 - d, 1, p), w2_rs.at[l, spot[p], 3])
        else:
            for step in range(1, nd):
                got(w_rows(l, (d + nd - step) % nd, p), w2_rs.at[l, spot[p], step - 1])

    def w_shared(l):
        got(W.at[l, pl.ds(0, (nd - 1) * Dr)], w2_ss.at[l])

    def pump(ops):
        for what, l, p in ops:
            with jax.named_scope(what + str(l) + str(p)):
                {"s": w_share, "f": w_forward}[what](l, p)

    near = s == zh
    gathered = (5, 2, 3, 4)

    def pump_near(ops):
        pl.when(near)(lambda: pump(ops))

    def pump_far(ops):
        pl.when(jnp.logical_not(near))(lambda: pump(ops))

    where = {4: 0, 2: 1, 3: 2, 1: 3, 6: 4, 7: 5, 8: 6}

    def split(p):
        return (6, 7, 8) if p == 0 else (p,)

    def d_copy(l, p, k):
        col, width = pieces[p]
        cols = pl.ds(col, width)
        if not square:
            src, dst, dev = w_rows(l, (d + k + 1) % nd, p), LW.at[l, k, :, cols], dp_dev(k + 1)
        else:
            first, second = pl.ds(0, half_rows), pl.ds(half_rows, half_rows)
            block, half, slot, rows, to = (
                (3 - d, 0, 2, first, dp_x),
                (3 - d, 1, 2, second, dp_y),
                (dp_x, 0, 0, first, dp_x),
                (dp_y, 1, 1, second, dp_y),
                (dp_y, 0, 1, first, dp_y),
                (dp_x, 1, 0, second, dp_x),
            )[k]
            src, dst, dev = w_half(l, block, half, p), LW.at[l, slot, rows, cols], (s, to, z)
        group = k if square and k < 2 else 2
        return remote(src, dst, d1_ss.at[l], d1_rs.at[l, where[p], group], dev)

    def d_send(l, p):
        for part in split(p):
            for k in range(4 if square else nd - 1):
                d_copy(l, part, k).start()

    @scoped
    def d_mid(l, p):
        if p == 0:
            for part in split(p):
                d_mid(l, part)
        elif square:
            col, width = pieces[p]
            cols = pl.ds(col, width)
            for k, block, half in ((0, dp_y, 0), (1, dp_x, 1)):
                copy = d_copy(l, p, k)
                copy.wait_recv()
                rows = pl.ds(block * Dr + half * half_rows, half_rows)
                arrived = LW[l, 2, half * half_rows : (half + 1) * half_rows, cols]
                W[l, rows, cols] = (W[l, rows, cols].astype(F32) + arrived.astype(F32)).astype(BF)
                d_copy(l, p, 4 + k).start()

    part_rows = Dr // 4

    def d_pass(l, p, q, rows=part_rows):
        for part in split(p):
            col, width = pieces[part]
            cols = pl.ds(col, width)
            src = W.at[l, pl.ds(d * Dr + q * rows, rows), cols]
            dst = L2.at[zh, pl.ds(q * rows, rows), cols]
            arrival = d2_rs.at[where[part], zh]
            to_self = (s == l) & (zh == s)

            @pl.when(to_self)
            def _():
                pltpu.make_async_copy(src, dst, arrival).start()

            @pl.when(jnp.logical_not(to_self))
            def _():
                remote(src, dst, d2_ss.at[l], arrival, (l, d, s * Hn + zl)).start()

    @scoped
    def d_total_rows(l, p):
        for part in split(p):
            col, width = pieces[part]
            cols = pl.ds(col, width)
            slots = 2 if square else nd - 1
            got(LW.at[l, pl.ds(0, slots), :, cols], d1_rs.at[l, where[part], 2])
            rows = pl.ds(d * Dr, Dr)
            total = W[l, rows, cols].astype(F32)
            for slot in range(slots):
                total = total + LW[l, slot, :, cols].astype(F32)
            W[l, rows, cols] = total.astype(BF)

    def d_sum(l, p):
        d_total_rows(l, p)
        d_pass(l, p, 0, Dr)

    def d_sent(l):
        got(W.at[l, pl.ds(0, (nd - 1) * Dr)], d1_ss.at[l])

        @pl.when(jnp.logical_not((s == l) & (zh == s)))
        def _():
            got(W.at[l, pl.ds(0, Dr)], d2_ss.at[l])

    outs = (
        pltpu.make_async_copy(MQ, out_qkv, m_sem.at[0]),
        pltpu.make_async_copy(MO, out_o, m_sem.at[1]),
        pltpu.make_async_copy(MGU, out_gu, m_sem.at[2]),
        pltpu.make_async_copy(MD, out_d, m_sem.at[3]),
    )

    def d_arrived(p):
        col, width = pieces[p]
        for half in range(2):
            got(L2.at[half, :, pl.ds(col, width)], d2_rs.at[where[p], half])

    def d_total(col, width):
        return L2[0, :, col : col + width].astype(F32) + L2[1, :, col : col + width].astype(F32)

    @scoped
    def d_final(p):
        d_arrived(p)
        if p >= 6:
            j = p - 6
            MQ[j] = d_total(j * C, C)
            pltpu.make_async_copy(MQ.at[j], out_qkv.at[j], m_sem.at[0]).start()
        elif p == 1:
            MO[...] = d_total(z_.oO, C).T
            outs[1].start()
        elif p == 3:
            MGU[...] = d_total(z_.oG, z_.GUw).T[: 2 * F]
            outs[2].start()
        elif p == 4:
            MD[...] = d_total(z_.oD, z_.Dw).T[:F]
            outs[3].start()

    @scoped
    def shard_attention():
        masters[0].wait()
        masters[1].wait()
        for j in range(3):
            L2[0, :, j * C : (j + 1) * C] = MQ[j].astype(BF)
        L2[0, :, z_.oO : z_.oG] = MO[...].T.astype(BF)

    @scoped
    def shard_feed():
        masters[2].wait()
        masters[3].wait()
        for ref, col, width, rows in ((MGU, z_.oG, z_.GUw, 2 * F), (MD, z_.oD, z_.Dw, F)):
            value = ref[...]
            if width > rows:
                value = jnp.concatenate([value, jnp.zeros((width - rows, Dr), F32)], axis=0)
            L2[0, :, col : col + width] = value.T.astype(BF)

    def chunk_rows(m, c):
        return pl.ds(m * MB + c * R, R)

    def ag_send(k, buf, m):
        rows = buf.at[chunk_rows(m, own)]
        for step in range(1, Hn):
            dev = (s, d, zh * Hn + peer_zl(step))
            remote(rows, rows, ag_ss.at[k], ag_rs.at[k, m, Hn - step], dev).start()
        remote(rows, rows, ag_ss.at[k], ag_rs.at[k, m, 0], core_dev).start()

    def ag_forward(k, buf, m):
        for step in range(1, Hn):
            rows = buf.at[chunk_rows(m, s * Hn + peer_zl(step))]
            got(rows, ag_rs.at[k, m, step])
            remote(rows, rows, ag_ss.at[k], ag_rs.at[k, m, 0], core_dev).start()

    def ag_wait(k, buf, m):
        got(buf.at[pl.ds(m * MB + (1 - s) * Hn * R, Hn * R)], ag_rs.at[k, m, 0])

    def ag_sent(k, buf):
        got(buf.at[pl.ds(0, MH * (2 * Hn - 1) * R)], ag_ss.at[k])

    def rs_copy1(k, m):
        par = k % 2
        return remote(
            PT.at[par, pl.ds(m * MB + (1 - s) * Hn * R, Hn * R)],
            RL1.at[par, m],
            r1_ss.at[par, m],
            r1_rs.at[par, m],
            core_dev,
        )

    def rs_copy2(k, m, step):
        par = k % 2
        return remote(
            RSB.at[par, m, step - 1],
            RL2.at[par, m, step - 1],
            r2_ss.at[par, m, step - 1],
            r2_rs.at[par, m, step - 1],
            (s, d, zh * Hn + peer_zl(step)),
        )

    def rs_first(k, m, value):
        PT[k % 2, pl.ds(m * MB, MB), :] = value.astype(BF)
        rs_copy1(k, m).start()

    def rs_second(k, m):
        par = k % 2
        copy = rs_copy1(k, m)
        copy.wait_send()
        copy.wait_recv()
        for step in range(1, Hn):
            there = peer_zl(step)
            part = PT[par, chunk_rows(m, s * Hn + there), :].astype(F32) + RL1[
                par, m, pl.ds(there * R, R), :
            ].astype(F32)
            RSB[par, m, step - 1] = part.astype(BF)
            rs_copy2(k, m, step).start()

    def after(k, i, m):
        @pl.when(i > 0)
        def _():
            rs_second(k, m)

    def rs_third(k, m):
        par = k % 2
        total = PT[par, chunk_rows(m, own), :].astype(F32) + RL1[
            par, m, pl.ds(zl * R, R), :
        ].astype(F32)
        for step in range(1, Hn):
            copy = rs_copy2(k, m, step)
            copy.wait_send()
            copy.wait_recv()
            total = total + RL2[par, m, step - 1].astype(F32)
        return total

    def own_rows(m):
        return pl.ds(m * R, R)

    def rms(rows):
        return lax.rsqrt(jnp.mean(rows * rows, axis=-1, keepdims=True) + EPS)

    def gain(l, which):
        return GV[l, which : which + 1, :]

    def rms_back(l, which, rows, grad):
        inverse = rms(rows)
        scaled = grad * gain(l, which)
        back = inverse * scaled - rows * (inverse * inverse * inverse) * jnp.mean(
            scaled * rows, axis=-1, keepdims=True
        )
        DG[l, which : which + 1, :] += jnp.sum(grad * rows * inverse, axis=0, keepdims=True)
        return back

    def send_out(buf, l, out, which, m):
        src = buf.at[l, own_rows(m)]
        dst = out.at[zh * MH + m]
        to_self = (s == l) & (zh == s)

        @pl.when(to_self)
        def _():
            pltpu.make_async_copy(src, dst, o_rs.at[which, zh]).start()

        @pl.when(jnp.logical_not(to_self))
        def _():
            remote(
                src, dst, o_ss.at[l], o_rs.at[which, zh], (l, d, s * Hn + zl)
            ).start()

    lane_head = lax.broadcasted_iota(jnp.int32, (1, C), 1) // DH
    head_bf = [(lane_head == h).astype(F32).astype(BF) for h in range(NH)]
    head_f = [(lane_head == h).astype(F32) for h in range(NH)]

    def stack(rows):
        return jnp.concatenate([rows * head_bf[h] for h in range(NH)], axis=0)

    def unstack(wide):
        out = wide[0:DH] * head_f[0]
        for h in range(1, NH):
            out = out + wide[h * DH : (h + 1) * DH] * head_f[h]
        return out

    def tall(mask):
        return jnp.concatenate([mask] * NH, axis=0)

    def head_mean(values):
        row = lax.broadcasted_iota(jnp.int32, (C, C), 0) // DH
        col = lax.broadcasted_iota(jnp.int32, (C, C), 1) // DH
        same = jnp.where(row == col, 1.0 / DH, 0.0).astype(BF)
        high = values.astype(BF)
        low = (values - high.astype(F32)).astype(BF)
        return mm(high, same) + mm(low, same)

    def block_rows(b):
        return pl.ds(pl.multiple_of(b * BLOCK, BLOCK), BLOCK)

    def qkv_block(l, b):
        rows = block_rows(b)
        return (QKV[l, rows, 0:C], QKV[l, rows, C : 2 * C], QKV[l, rows, 2 * C : 3 * C])

    def softplus(values):
        return jnp.maximum(values, 0.0) + jnp.log(1.0 + jnp.exp(-jnp.abs(values)))

    def features(values):
        return softplus(values.astype(F32)).astype(BF)

    def diag_forward(b):
        q, k, v = qkv_block(0, b)
        scores = mm(stack(q), k, NT) * (1.0 / math.sqrt(DH))
        scores = jnp.where(tall(MSK[b]) > 0.5, scores, -1e9)
        top = jnp.max(scores, axis=-1, keepdims=True)
        weights = jnp.exp(scores - top)
        weights = (weights / jnp.sum(weights, axis=-1, keepdims=True)).astype(BF)
        AP[0, b] = weights
        O[0, block_rows(b), :] = unstack(mm(weights, v)).astype(BF)

    def diag_backward(b, grad_o):
        q, k, v = qkv_block(0, b)
        low = stack(grad_o.astype(BF))
        weights = AP[0, b]
        wide = weights.astype(F32)
        grad_v = mm(weights, low, TN)
        grad_w = mm(low, v, NT)
        grad_s = wide * (grad_w - jnp.sum(grad_w * wide, axis=-1, keepdims=True))
        grad_s = (grad_s * (1.0 / math.sqrt(DH))).astype(BF)
        grad_q = unstack(mm(grad_s, k))
        grad_k = mm(grad_s, stack(q), TN)
        rows = block_rows(b)
        GQKV[rows, 0:C] = grad_q.astype(BF)
        GQKV[rows, C : 2 * C] = grad_k.astype(BF)
        GQKV[rows, 2 * C : 3 * C] = grad_v.astype(BF)

    def fold(square):
        out = square[0:DH] * head_f[0]
        for h in range(1, NH):
            out = out + square[h * DH : (h + 1) * DH] * head_f[h]
        return out

    def unfold(flat):
        return stack(flat.astype(BF))

    def wide_lanes(column):
        return jnp.concatenate([column] * (C // 128), axis=1)

    def norm_state(b, state):
        q, k, v = qkv_block(1, b)
        ST[b] = state
        key = features(k)
        term = mm(key, (v.astype(F32) * wide_lanes(TAIL[b])).astype(BF), TN)
        return wide_lanes(KEEP[b, 0:1, :]) * state + fold(term)

    def norm_forward(b, passed):
        q, k, v = qkv_block(1, b)
        query, key = features(q), features(k)
        local = jnp.where(tall(MSK[b]) > 0.5, mm(stack(query), key, NT), 0.0).astype(BF)
        AP[1, b] = local
        state = ST[b] + passed * SIN[0].astype(F32)
        ST[b] = state
        mixed = unstack(mm(local, v)) + wide_lanes(CAR[b]) * mm(query, unfold(state))
        rows = block_rows(b)
        UU[rows, :] = mixed
        O[1, rows, :] = (mixed * lax.rsqrt(head_mean(mixed * mixed) + EPS)).astype(BF)
        return passed * wide_lanes(KEEP[b, 0:1, :])

    def norm_back_first(b, grad_o, state):
        rows = block_rows(b)
        mixed = UU[rows, :]
        scale = lax.rsqrt(head_mean(mixed * mixed) + EPS)
        grad = scale * grad_o - mixed * (scale * scale * scale) * head_mean(grad_o * mixed)
        low = grad.astype(BF)
        DU[rows, :] = low
        ST2_store(b, state)
        query = features(QKV[1, rows, 0:C])
        term = mm(query, (low.astype(F32) * wide_lanes(CAR[b])).astype(BF), TN)
        return wide_lanes(KEEP[b, 0:1, :]) * state + fold(term)

    def ST2_store(b, state):
        ST[NBH + b] = state

    def sigmoid(values):
        return 1.0 / (1.0 + jnp.exp(-values.astype(F32)))

    def norm_back_local(b):
        rows = block_rows(b)
        q, k, v = qkv_block(1, b)
        query, key = features(q), features(k)
        low = DU[rows, :]
        stacked = stack(low)
        grad_a = jnp.where(tall(MSK[b]) > 0.5, mm(stacked, v, NT), 0.0).astype(BF)
        grad_q = unstack(mm(grad_a, key)) + wide_lanes(CAR[b]) * mm(low, unfold(ST[b]), NT)
        GQKV[rows, 0:C] = (grad_q * sigmoid(q)).astype(BF)
        GQKV[rows, C : 2 * C] = (mm(grad_a, stack(query), TN) * sigmoid(k)).astype(BF)
        GQKV[rows, 2 * C : 3 * C] = mm(AP[1, b], stacked, TN).astype(BF)

    def norm_back_state(b, passed):
        rows = block_rows(b)
        q, k, v = qkv_block(1, b)
        grad_wide = unfold(ST[NBH + b] + passed * SIN[1].astype(F32))
        tail = wide_lanes(TAIL[b])
        grad_k = tail * mm(v, grad_wide, NT) * sigmoid(k)
        grad_v = tail * mm(features(k), grad_wide)
        GQKV[rows, C : 2 * C] = (GQKV[rows, C : 2 * C].astype(F32) + grad_k).astype(BF)
        GQKV[rows, 2 * C : 3 * C] = (GQKV[rows, 2 * C : 3 * C].astype(F32) + grad_v).astype(BF)
        return passed * wide_lanes(KEEP[b, 0:1, :])

    @scoped
    def masks():
        row = lax.broadcasted_iota(jnp.int32, (BLOCK, BLOCK), 0)
        col = lax.broadcasted_iota(jnp.int32, (BLOCK, BLOCK), 1)
        token = lax.broadcasted_iota(jnp.int32, (MB, BLOCK), 0)
        lane = lax.broadcasted_iota(jnp.int32, (MB, BLOCK), 1)
        start = jnp.concatenate([starts_in[zh * MH + m] for m in range(MH)], axis=0)
        start = start.astype(F32).astype(BF)
        chunk_lane = lax.broadcasted_iota(jnp.int32, (BLOCK, MH), 1)
        for j in range(NB):
            upper = ((token // BLOCK == j) & (token % BLOCK <= lane)).astype(F32).astype(BF)
            count_row = mm(start, upper)
            count_col = mm(upper, start, (((0,), (1,)), ((), ())))
            for m in range(MH):
                b = m * NB + j
                c_row = count_row[m : m + 1, :]
                c_col = jnp.sum(
                    jnp.where(chunk_lane == m, count_col, 0.0), axis=1, keepdims=True
                )
                last = jnp.sum(
                    jnp.where(col[0:1] == BLOCK - 1, c_row, 0.0), axis=1, keepdims=True
                )
                MSK[b] = jnp.where((c_row == c_col) & (row >= col), 1.0, 0.0)
                CAR[b] = jnp.broadcast_to(jnp.where(c_col == 0.0, 1.0, 0.0), (BLOCK, 128))
                TAIL[b] = jnp.broadcast_to(jnp.where(c_col == last, 1.0, 0.0), (BLOCK, 128))
                KEEP[b] = jnp.broadcast_to(jnp.where(last == 0.0, 1.0, 0.0), (8, 128))

    place = d * nt + z

    def gain_copy(i):
        return remote(GL.at[place], GL.at[place], gl_sem.at[0], gl_sem.at[1], section_dev(i))

    @scoped
    def gains_out():
        width = gain_in.shape[1]
        row = lax.broadcasted_iota(jnp.int32, (width, 128), 0)
        col = lax.broadcasted_iota(jnp.int32, (width, 128), 1)
        spot = (col % width == row) & (col // width == place % (128 // width))
        GL[place] = mm(gain_in[...].astype(BF), spot.astype(F32).astype(BF))

        def one(i, carry):
            gain_copy(i).start()
            return carry

        lax.fori_loop(1, nd * nt, one, 0)

    @scoped
    def gains_in():
        for k in (1, 0):
            got(GL.at[pl.ds(0, nd * nt - 1)], gl_sem.at[k])
        each = nd * nt * 128 // D
        for t in range(D // 128):
            total = GL[t * each]
            for i in range(1, each):
                total = total + GL[t * each + i]
            GV[s, :, t * 128 : (t + 1) * 128] = total
        gain_swap().start()

    def gain_swap():
        return remote(GV.at[s], GV.at[s], g1_sem.at[0], g1_sem.at[1], core_dev)

    def gains_other():
        gain_swap().wait_send()
        got(GV.at[1 - s], g1_sem.at[1])

    def dp_gain(step):
        return remote(
            GOWN, DL2.at[step - 1], g_ss.at[1, step - 1], g_rs.at[1, step - 1], dp_dev(step)
        )

    def core_gain():
        return remote(DG.at[1 - s], DL0, g1_sem.at[2], g1_sem.at[3], core_dev)

    def z_gain(step):
        return remote(
            DG.at[s], DL1.at[step - 1], g_ss.at[0, step - 1], g_rs.at[0, step - 1], z_dev(step)
        )

    @scoped
    def gain_second():
        core_gain().wait()
        DG[s] = DG[s] + DL0[...]
        for step in range(1, nt):
            z_gain(step).start()

    @scoped
    def gain_third():
        total = DG[s]
        for step in range(1, nt):
            z_gain(step).wait()
            total = total + DL1[step - 1]
        GOWN[...] = total
        for step in range(1, nd):
            dp_gain(step).start()

    @scoped
    def gain_final():
        total = GOWN[...]
        for step in range(1, nd):
            dp_gain(step).wait()
            total = total + DL2[step - 1]
        GOWN[...] = total
        width = out_gain.shape[1]
        each = 128 // width
        tile = GOWN[:, pl.ds(pl.multiple_of(place // each * 128, 128), 128)]
        mine = jnp.zeros((2, width), F32)
        for i in range(each):
            piece = tile[:, i * width : (i + 1) * width]
            mine = jnp.where(place % each == i, piece, mine)
        out_gain[...] = mine

    def loop(count, fn):
        def step(i, carry):
            fn(i)
            return carry

        with jax.named_scope(fn.__name__):
            lax.fori_loop(0, count, step, 0)

    def chunk(m):
        return pl.ds(pl.multiple_of(m * MB, BLOCK), MB)

    def w_cols(l, p):
        col, width = pieces[p]
        return W[l, :, col : col + width]

    def w_gate_up(l):
        return W[l, :, z_.oG : z_.oD]

    @scoped
    def state_copy(slot):
        return remote(
            SEND_STATE.at[slot],
            SIN.at[slot],
            st_ss.at[slot],
            st_rs.at[slot],
            (s, d, (z + Hn) % nt),
        )

    def state_out(slot, value, sender):
        SEND_STATE[slot] = value.astype(BF)

        @pl.when(zh == sender)
        def _():
            SIN[slot] = jnp.zeros((DH, C), BF)
            state_copy(slot).start()

    @scoped
    def state_in(slot, sender):
        @pl.when(zh != sender)
        def _():
            state_copy(slot).wait_recv()

    outer = zh == zl
    inner, far = jnp.logical_not(outer), jnp.logical_not(near)

    def only(cond, fn):
        pl.when(cond)(fn)

    def hand_far(l, cond, ps):
        def go():
            for p in ps:
                w_hand_far(l, p)

        pl.when((s == l) & cond)(go)

    def hand_near(ps):
        for l in range(2):

            @pl.when(s == l)
            def _():
                for p in ps:
                    w_hand_near(l, p)

    def x_out():
        spread_tokens(xin, XF, 0)

    gains_out()
    shard_attention()
    hand_far(0, s == 0, [5])
    hand_near([5])
    only((s == 0) & inner, x_out)
    pump_near([("s", 0, 5)])
    own_tokens(xin, XF, 0)
    own_tokens(cot, GF.at[1], 1)
    shard_feed()
    hand_near([2, 3, 4])
    masks()
    for l in range(2):
        DG[l] = jnp.zeros((2, D), F32)
    pump_near([("s", 0, 2)])
    gains_in()
    pump_far([("s", 0, 5)])
    only((s == 0) & outer & far, x_out)
    pump([("f", 0, 5)])
    pump_near([("f", 0, 2)])
    only((s == 0) & outer & near, x_out)
    only(s == 1, gains_other)
    for m in range(MH):
        relay_tokens(XF, 0, m)
    hand_far(0, s == 0, [2, 3, 4])
    await_tokens(XF, 0, 0)

    def cot_out():
        spread_tokens(cot, GF.at[1], 1)

    stage = {
        (0, "attended"): lambda: (
            pump_near([("f", 0, 3), ("f", 0, 4)]),
            pump_far([("s", 0, 2), ("s", 0, 3), ("f", 0, 2), ("s", 0, 4)]),
        ),
        (0, "hidden"): lambda: (
            hand_far(1, inner, [5, 4, 2, 3]),
            hand_far(1, outer, [5]),
            pump_near([("s", 1, 5)]),
            pump_far([("f", 0, 3), ("f", 0, 4)]),
        ),
        (0, "ready"): lambda: (
            hand_far(1, outer & far, [4]),
            pump_near([("f", 1, 5)]),
            hand_far(1, outer & near, [4]),
            pump_far([("s", 1, 5)]),
        ),
        (0, "feeding"): lambda: (
            hand_far(1, outer, [2, 3]),
            pump_near([("s", 1, 4)]),
        ),
        (0, "fed"): lambda: (
            pump_near([("s", 1, 2), ("f", 1, 4)]),
            pump_far([("f", 1, 5), ("s", 1, 4)]),
            only(s == 0, gains_other),
        ),
        (0, "result"): lambda: (
            only(s == 1, cot_out),
            pump_near([("s", 1, 3)]),
            pump_far([("s", 1, 2), ("f", 1, 4)]),
        ),
        (1, "states"): lambda: (
            [relay_tokens(GF.at[1], 1, m) for m in reversed(range(MH))],
            pump_near([("f", 1, 2), ("f", 1, 3)]),
            pump_far([("s", 1, 3), ("f", 1, 2)]),
        ),
        (1, "attended"): lambda: (pump_far([("f", 1, 3)]),),
        (1, "hidden"): lambda: (results_out(Y, 0, out_y, 0),),
        (1, "ready"): lambda: (),
        (1, "fed"): lambda: (),
        "b1 second": lambda: (),
        "b1 middle": lambda: (results_out(Y, 1, out_y, 0), d_mid(1, 4)),
        "b1 feed": lambda: (),
        "b1 third": lambda: (d_mid(1, 3),),
        "b1 end": lambda: (d_total_rows(1, 3),),
        "b0 second": lambda: (d_total_rows(1, 0),),
        "b0 middle": lambda: (),
        "b0 feed": lambda: (results_out(GX, 1, out_g, 1), d_total_rows(1, 1)),
        "b0 third": lambda: (
            only(far, lambda: run(d_mid, 2)),
            only(near, lambda: run(d_mid, 4) or run(d_send, 2, 3)),
        ),
        "b0 end": lambda: (
            core_gain().start(),
            only(near, lambda: run(d_send, 0, 1)),
            only(far, lambda: far_tail()),
            only(near, lambda: near_tail()),
            gain_third(),
        ),
    }

    def run(step, *parts):
        for p in parts:
            step(0, p)

    def far_tail():
        gain_second()
        run(d_mid, 6)
        run(d_sum, 3)
        run(d_mid, 7, 8)
        run(d_sum, 6)
        run(d_mid, 1)
        run(d_sum, 7, 8, 1)
        results_out(GX, 0, out_g, 1)

    def near_tail():
        run(d_sum, 4)
        run(d_mid, 2, 3)
        gain_second()
        run(d_mid, 6, 7, 8, 1)
        results_out(GX, 0, out_g, 1)
        run(d_sum, 2, 3, 6, 7, 8, 1)

    def results_out(buf, l, out, which):
        for m in range(MH):
            send_out(buf, l, out, which, m)

    def input_rows(l, m):
        if l == 0:
            return XF[chunk_rows(m, own), :].astype(F32)
        return Y[0, own_rows(m), :].astype(F32)

    def gate_up_grad(grad, both):
        parts = [grad * both[:, F : 2 * F], grad * both[:, :F]]
        if z_.GUw > 2 * F:
            parts.append(jnp.zeros((MB, z_.GUw - 2 * F), F32))
        return jnp.concatenate(parts, axis=1).astype(BF)

    def finish_layer(l, rs2, ag3):
        def result(m):
            rows = (H[l, own_rows(m), :] + rs_third(rs2, m)).astype(BF)
            Y[l, own_rows(m), :] = rows
            if l == 0:
                wide = rows.astype(F32)
                N1[1, chunk_rows(m, own), :] = (wide * rms(wide) * gain(1, 0)).astype(BF)
                ag_send(ag3, N1.at[1], m)

        loop(MH, result)

    def forward(l, ag1, rs1, ag2, rs2, ag3):
        w_ready(l, 5)

        def qkv_chunk(m):
            if l == 0:
                pl.when(m > 0)(lambda: await_tokens(XF, 0, m))
                pl.when((m == 1) & near)(lambda: pump([("s", 0, 3), ("s", 0, 4)]))
                rows = XF[chunk(m), :].astype(F32)
                N1[0, chunk(m), :] = (rows * rms(rows) * gain(0, 0)).astype(BF)
            else:
                ag_forward(ag1, N1.at[1], m)
                ag_wait(ag1, N1.at[1], m)
            QKV[l, chunk(m), :] = mm(N1[l, chunk(m), :], w_cols(l, 0)).astype(BF)

        def out_chunk(m):
            rs_first(rs1, m, mm(O[l, chunk(m), :], w_cols(l, 1), NT))

        if l == 0:

            def attend(m):
                qkv_chunk(m)
                for i in range(NB):
                    diag_forward(m * NB + i)
                out_chunk(m)
                after(rs1, m, m - 1)

            loop(MH, attend)
            rs_second(rs1, MH - 1)
            stage[l, "attended"]()
        else:

            def states(m, state):
                qkv_chunk(m)
                for i in range(NB):
                    state = norm_state(m * NB + i, state)
                return state

            with jax.named_scope('states'):
                last = lax.fori_loop(0, MH, states, jnp.zeros((DH, C), F32))
            w_handed_out()
            state_out(0, last, 0)
            state_in(0, 0)
            stage[l, "states"]()

            def attend(m, passed):
                for i in range(NB):
                    passed = norm_forward(m * NB + i, passed)
                out_chunk(m)
                after(rs1, m, m - 1)
                return passed

            with jax.named_scope('attend'):
                lax.fori_loop(0, MH, attend, jnp.ones((1, C), F32))
            rs_second(rs1, MH - 1)
            stage[l, "attended"]()

        def hidden_rows(m):
            rows = input_rows(l, m) + rs_third(rs1, m)
            H[l, own_rows(m), :] = rows
            N2[l, chunk_rows(m, own), :] = (rows * rms(rows) * gain(l, 1)).astype(BF)
            ag_send(ag2, N2.at[l], m)

        loop(MH, hidden_rows)
        stage[l, "hidden"]()
        w_ready(l, 4)
        if l == 1:

            def hidden_grad(m):
                await_tokens(GF.at[1], 1, m)
                GGU[chunk(m), 0 : z_.Dw] = mm(GF[1, chunk(m), :], w_cols(1, 4)).astype(BF)

            loop(MH, hidden_grad)
        w_ready(l, 2)
        w_ready(l, 3)
        stage[l, "ready"]()

        def feed(m):
            ag_forward(ag2, N2.at[l], m)
            ag_wait(ag2, N2.at[l], m)
            rows = N2[l, chunk(m), :]
            both = mm(rows, w_gate_up(l))
            if l == 0:
                GU[l, chunk(m), :] = both.astype(BF)
            else:
                grad = GGU[chunk(m), 0 : z_.Dw].astype(F32)[:, :F]
                GGU[chunk(m), :] = gate_up_grad(grad, both)
            hidden = both[:, :F] * both[:, F : 2 * F]
            if z_.Dw > F:
                hidden = jnp.concatenate([hidden, jnp.zeros((MB, z_.Dw - F), F32)], axis=1)
            hidden = hidden.astype(BF)
            HID[l, chunk(m), :] = hidden
            rs_first(rs2, m, mm(hidden, w_cols(l, 4), NT))
            if l == 0:


                @pl.when(m == 1)
                def _():
                    stage[0, "feeding"]()

            after(rs2, m, m - 1)

        loop(MH, feed)
        rs_second(rs2, MH - 1)
        stage[l, "fed"]()

        if l == 0:
            finish_layer(l, rs2, ag3)
            stage[l, "result"]()

    forward(0, None, 0, 0, 1, 1)
    forward(1, 1, 2, 2, 3, None)

    RB = min(D, 256)

    @scoped
    def grad_weight(l, p, left, right, send=True):
        col, width = pieces[p]
        for r in range(D // RB):
            W[l, r * RB : (r + 1) * RB, col : col + width] = mm(
                left[:, r * RB : (r + 1) * RB], right, TN
            ).astype(BF)
        if send:
            d_send(l, p)

    def rest(l, p):
        for q in range(MH, 4):
            d_pass(l, p, q)

    def grad_part(l, p, send=True):
        col, width = pieces[p]
        grad_weight(l, p, N2[l], GGU[:, col - z_.oG : col - z_.oG + width], send)

    def backward(l, ag_in, rs1, ag2, rs2, ag_out):
        w_shared(l)

        def feed_back(i):
            m = MH - 1 - i
            if l == 0:
                ag_forward(ag_in, GF.at[0], m)
                ag_wait(ag_in, GF.at[0], m)
                grad = mm(GF[l, chunk(m), :], w_cols(l, 4))[:, :F]
                GGU[chunk(m), :] = gate_up_grad(grad, GU[l, chunk(m), :].astype(F32))
            rs_first(rs1, m, mm(GGU[chunk(m), :], w_gate_up(l), NT))
            after(rs1, i, m + 1)
            if l == 0:

                @pl.when(i == 0)
                def _():
                    d_mid(1, 1)
                    d_mid(1, 0)

                d_pass(1, 3, i)
        if l == 1:
            grad_weight(l, 4, GF[l], HID[l])
        loop(MH, feed_back)
        rs_second(rs1, 0)
        if l == 0:
            rest(1, 3)
            grad_weight(l, 4, GF[l], HID[l], False)
            only(far, lambda: d_send(0, 4))
        else:
            grad_part(l, 2)
            finish_layer(1, 3, None)
        stage[f"b{l} second"]()

        def middle(i):
            m = MH - 1 - i
            rows = H[l, own_rows(m), :]
            grad = GF[l, chunk_rows(m, own), :].astype(F32) + rms_back(
                l, 1, rows, rs_third(rs1, m)
            )
            GH[own_rows(m), :] = grad
            GA[l, chunk_rows(m, own), :] = grad.astype(BF)
            ag_send(ag2, GA.at[l], m)
            if l == 0:
                only((i == 1) & near, lambda: d_send(0, 4))
                d_pass(1, 0, i)

        loop(MH, middle)
        if l == 0:
            rest(1, 0)
        stage[f"b{l} middle"]()
        if l == 0:
            grad_part(l, 2, False)

            @pl.when(far)
            def _():
                d_mid(0, 4)
                d_send(0, 2)

            grad_part(l, 3, False)
            only(far, lambda: d_send(0, 3))
        else:
            grad_part(l, 3)
        stage[f"b{l} feed"]()

        def grad_o(m):
            ag_forward(ag2, GA.at[l], m)
            ag_wait(ag2, GA.at[l], m)
            return mm(GA[l, chunk(m), :], w_cols(l, 1))

        def qkv_back(i, m):
            rs_first(rs2, m, mm(GQKV[chunk(m), :], w_cols(l, 0), NT))
            after(rs2, i, m + 1)

        if l == 0:

            def attend(i):
                m = MH - 1 - i
                grad = grad_o(m)
                for j in range(NB):
                    diag_backward(m * NB + j, grad[j * BLOCK : (j + 1) * BLOCK])
                qkv_back(i, m)
                d_pass(1, 1, i)
                only((i == 0) & far, lambda: d_sum(0, 4))

            loop(MH, attend)
        else:

            def states(i, state):
                m = MH - 1 - i
                grad = grad_o(m)
                for j in reversed(range(NB)):
                    state = norm_back_first(m * NB + j, grad[j * BLOCK : (j + 1) * BLOCK], state)
                return state

            with jax.named_scope("states"):
                last = lax.fori_loop(0, MH, states, jnp.zeros((DH, C), F32))
            state_out(1, last, 1)
            d_mid(1, 2)
            grad_weight(l, 1, GA[l], O[l])

            def attend_local(m):
                for j in range(NB):
                    norm_back_local(m * NB + j)

            loop(MH, attend_local)
            d_total_rows(1, 4)
            state_in(1, 1)
            pl.when(zh == 0)(lambda: d_pass(1, 4, 0, Dr))

            def attend(i, passed):
                m = MH - 1 - i
                for j in reversed(range(NB)):
                    passed = norm_back_state(m * NB + j, passed)
                qkv_back(i, m)

                @pl.when(zh == 1)
                def _():
                    d_pass(1, 4, i)

                return passed

            with jax.named_scope("attend"):
                lax.fori_loop(0, MH, attend, jnp.ones((1, C), F32))

        rs_second(rs2, 0)
        if l == 0:
            rest(1, 1)
        else:
            pl.when(zh == 1)(lambda: rest(1, 4))
        stage[f"b{l} third"]()
        grad_weight(l, 0, N1[l], GQKV[...], l == 1)
        if l == 0:
            grad_weight(l, 1, GA[l], O[l], False)

            @pl.when(far)
            def _():
                d_mid(0, 3)
                d_send(0, 0)
                d_send(0, 1)
                d_sum(0, 2)


        def result(i):
            m = MH - 1 - i
            grad = GH[own_rows(m), :] + rms_back(l, 0, input_rows(l, m), rs_third(rs2, m))
            low = grad.astype(BF)
            GX[l, own_rows(m), :] = low
            if l == 1:
                GF[0, chunk_rows(m, own), :] = low
                ag_send(ag_out, GF.at[0], m)
                pl.when(i == 0)(lambda: d_total_rows(1, 2))
                d_pass(1, 2, i)

        loop(MH, result)
        if l == 1:
            rest(1, 2)
        stage[f"b{l} end"]()

    backward(1, None, 4, 3, 5, 4)
    backward(0, 4, 6, 5, 7, None)

    for p in (4, 2, 3, 6, 7, 8, 1):
        d_final(p)
    gain_final()
    for copy in outs:
        copy.wait()
    for l in range(2):
        d_sent(l)

    ags = ((0, N2.at[0]), (1, N1.at[1]), (2, N2.at[1]), (3, GA.at[1]), (4, GF.at[0]), (5, GA.at[0]))

    for slot in range(2):

        @pl.when(zh == slot)
        def _():
            state_copy(slot).wait_send()

    for k, buf in ags:
        ag_sent(k, buf)
    for l in range(2):

        @pl.when(jnp.logical_not((s == l) & (zh == s)))
        def _():
            got(XF.at[pl.ds(0, 2 * MH * R)], o_ss.at[l])

    for half in range(2):
        got(out_y.at[pl.ds(half * MH, MH)], o_rs.at[0, half])
        got(out_g.at[pl.ds(half * MH, MH)], o_rs.at[1, half])
    for k in range(2):
        got(XF.at[pl.ds(0, MH * (nt - 1) * R)], x_sem.at[k])


def place_results(*refs):
    count = (len(refs) - 2) // 3
    sources, targets, held = refs[:count], refs[count : 2 * count], refs[2 * count : 3 * count]
    in_sem, out_sem = refs[-2:]
    reads = [pltpu.make_async_copy(sources[i], held[i], in_sem.at[i]) for i in range(count)]
    writes = [pltpu.make_async_copy(held[i], targets[i], out_sem.at[i]) for i in range(count)]
    for copy in reads:
        copy.start()
    for read, write in zip(reads, writes):
        read.wait()
        write.start()
    for copy in writes:
        copy.wait()


def solution(mesh):
    nd, nt = mesh.shape["dp"], mesh.shape["tensor"]

    def on_device(inputs, starts, cotangent, qkv_m, out_m, gateup_m, down_m, gain_m):
        z_ = Sizes(
            mesh,
            inputs.shape[3],
            inputs.shape[1],
            inputs.shape[2],
            qkv_m.shape[3],
            gateup_m.shape[3],
        )
        D, R, C, F, Dr, M, MH, Hn, MB, T, NBH, N, NH = (
            z_.D,
            z_.R,
            z_.C,
            z_.F,
            z_.Dr,
            z_.M,
            z_.MH,
            z_.Hn,
            z_.MB,
            z_.T,
            z_.NBH,
            z_.N,
            z_.NH,
        )
        width = gain_m.shape[2]
        qkv_rows = jnp.transpose(qkv_m[0], (1, 0, 2))
        gateup_rows = jnp.transpose(gateup_m[0], (1, 2, 0)).reshape(2 * F, Dr)
        anywhere = pl.BlockSpec(memory_space=pl.ANY)
        vmem = pl.BlockSpec(memory_space=pltpu.VMEM)
        DMA = pltpu.SemaphoreType.DMA
        V = pltpu.VMEM
        scratch = [
            V((3, Dr, C), F32),
            V((C, Dr), F32),
            V((2 * F, Dr), F32),
            V((F, Dr), F32),
            V((2, D, N), BF),
            V((2, nd - 1, Dr, N), BF),
            V((2, Dr, N), BF),
            V((T, D), BF),
            V((2, T, D), BF),
            V((2, T, D), BF),
            V((2, T, D), BF),
            V((2, T, 3 * C), BF),
            V((2, T, C), BF),
            V((1, T, z_.GUw), BF),
            V((2, T, z_.Dw), BF),
            V((2, MH * R, D), F32),
            V((2, MH * R, D), BF),
            V((2, T, D), BF),
            V((T, z_.GUw), BF),
            V((T, 3 * C), BF),
            V((MH * R, D), F32),
            V((2, MH * R, D), BF),
            V((2, T, D), BF),
            V((2, MH, Hn * R, D), BF),
            V((2, MH, Hn - 1, R, D), BF),
            V((2, MH, Hn - 1, R, D), BF),
            V((2, NBH, NH * BLOCK, BLOCK), BF),
            V((T, C), F32),
            V((T, C), BF),
            V((2 * NBH, DH, C), F32),
            V((2, DH, C), BF),
            V((2, DH, C), BF),
            V((NBH, BLOCK, BLOCK), F32),
            V((NBH, BLOCK, 128), F32),
            V((NBH, BLOCK, 128), F32),
            V((NBH, 8, 128), F32),
            V((nd * nt, 2, 128), F32),
            V((2, 2, D), F32),
            V((2, D), F32),
            V((2, 2, D), F32),
            V((2, D), F32),
            V((nt - 1, 2, D), F32),
            V((nd - 1, 2, D), F32),
            DMA((2, MH)),
            DMA((2,)),
            DMA((2, MH, nt - 1)),
            DMA((2,)),
            DMA((2, 4)),
            DMA((2,)),
            DMA((2, 4, max(4, nd - 1))),
            DMA((6,)),
            DMA((6, MH, Hn)),
            DMA((2, MH)),
            DMA((2, MH)),
            DMA((2, MH, Hn - 1)),
            DMA((2, MH, Hn - 1)),
            DMA((2,)),
            DMA((2,)),
            DMA((2,)),
            DMA((2, 2)),
            DMA((2,)),
            DMA((2, 7, 3)),
            DMA((2,)),
            DMA((7, 2)),
            DMA((4,)),
            DMA((2, max(nd, nt) - 1)),
            DMA((2, max(nd, nt) - 1)),
            DMA((2,)),
            DMA((4,)),
        ]
        out_y, out_g, grad_qkv, grad_o, grad_gu, grad_d, grad_gain = pl.pallas_call(
            functools.partial(body, z_),
            out_shape=(
                jax.ShapeDtypeStruct((M, R, D), BF),
                jax.ShapeDtypeStruct((M, R, D), BF),
                jax.ShapeDtypeStruct((3, Dr, C), F32),
                jax.ShapeDtypeStruct((C, Dr), F32),
                jax.ShapeDtypeStruct((2 * F, Dr), F32),
                jax.ShapeDtypeStruct((F, Dr), F32),
                jax.ShapeDtypeStruct((2, width), F32),
            ),
            in_specs=[anywhere] * 6 + [vmem, vmem],
            out_specs=(anywhere,) * 6 + (vmem,),
            scratch_shapes=scratch,
            compiler_params=pltpu.CompilerParams(
                collective_id=0, has_side_effects=True, vmem_limit_bytes=63 * 1024 * 1024
            ),
        )(
            qkv_rows,
            out_m[0],
            gateup_rows,
            down_m[0],
            inputs[0],
            cotangent[0],
            jnp.transpose(starts, (1, 0, 2)),
            gain_m[0],
        )
        results = (out_y, out_g, grad_qkv, grad_o, grad_gu, grad_d, grad_gain)
        out_y, out_g, grad_qkv, grad_o, grad_gu, grad_d, grad_gain = pl.pallas_call(
            place_results,
            out_shape=tuple(jax.ShapeDtypeStruct(r.shape, r.dtype) for r in results),
            in_specs=[anywhere] * len(results),
            out_specs=(anywhere,) * len(results),
            scratch_shapes=[V(r.shape, r.dtype) for r in results]
            + [DMA((len(results),)), DMA((len(results),))],
        )(*results)
        return (
            out_y[None, None],
            out_g[None, None],
            jnp.transpose(grad_qkv, (1, 0, 2))[None],
            grad_o[None],
            jnp.transpose(grad_gu.reshape(2, F, Dr), (2, 0, 1))[None],
            grad_d[None],
            grad_gain[None],
        )

    return jax.shard_map(
        on_device,
        mesh=mesh,
        in_specs=(
            P("dp", None, "tensor", None),
            P("dp", None, None),
            P("dp", None, "tensor", None),
            P("section", "dp", None, "tensor"),
            P("section", "tensor", "dp"),
            P("section", "dp", None, "tensor"),
            P("section", "tensor", "dp"),
            P("section", None, ("dp", "tensor")),
        ),
        out_specs=(
            P("section", "dp", None, "tensor", None),
            P("section", "dp", None, "tensor", None),
            P("section", "dp", None, "tensor"),
            P("section", "tensor", "dp"),
            P("section", "dp", None, "tensor"),
            P("section", "tensor", "dp"),
            P("section", None, ("dp", "tensor")),
        ),
        check_vma=False,
    )
```

```python
import functools
import math

import jax
import jax.numpy as jnp
from jax import lax
from jax.experimental import pallas as pl
from jax.experimental.pallas import tpu as pltpu
from jax.sharding import PartitionSpec as P

DH = 64
BLOCK = 64
EPS = 1e-6
BF = jnp.bfloat16
F32 = jnp.float32
MESH = pl.DeviceIdType.MESH
NN = (((1,), (0,)), ((), ()))
NT = (((1,), (1,)), ((), ()))
TN = (((0,), (0,)), ((), ()))


def mm(a, b, dims=NN):
    return lax.dot_general(a, b, dims, preferred_element_type=F32)


def ceil_to(value, unit):
    return (value + unit - 1) // unit * unit


def scoped(fn):
    @functools.wraps(fn)
    def inner(*args):
        with jax.named_scope(fn.__name__):
            return fn(*args)

    return inner


class Sizes:
    def __init__(self, mesh, model, micro, rows, cols, hidden):
        self.nd, self.nt = mesh.shape["dp"], mesh.shape["tensor"]
        self.D, self.M, self.R, self.C, self.F = model, micro, rows, cols, hidden
        self.GUw, self.Dw = ceil_to(2 * hidden, 128), ceil_to(hidden, 128)
        self.Dr = model // self.nd
        self.MH, self.Hn = micro // 2, self.nt // 2
        self.MB = rows * self.nt
        self.T = self.MH * self.MB
        self.NH = cols // DH
        self.NB = self.MB // BLOCK
        self.NBH = self.MH * self.NB
        self.oO, self.oG = 3 * cols, 4 * cols
        self.oD = self.oG + self.GUw
        self.N = self.oD + self.Dw
        first = ceil_to(self.GUw // 2, 128)
        self.pieces = (
            (0, 3 * cols),
            (self.oO, cols),
            (self.oG, first),
            (self.oG + first, self.GUw - first),
            (self.oD, self.Dw),
            (0, 4 * cols),
            (0, cols),
            (cols, cols),
            (2 * cols, cols),
        )


def body(
    z_,
    qkv_in,
    o_in,
    gu_in,
    d_in,
    xin,
    cot,
    starts_in,
    gain_in,
    out_y,
    out_g,
    out_qkv,
    out_o,
    out_gu,
    out_d,
    out_gain,
    MQ,
    MO,
    MGU,
    MD,
    W,
    LW,
    L2,
    XF,
    GF,
    N1,
    N2,
    QKV,
    O,
    GU,
    HID,
    H,
    Y,
    GA,
    GGU,
    GQKV,
    GH,
    GX,
    PT,
    RL1,
    RL2,
    RSB,
    AP,
    UU,
    DU,
    ST,
    SIN,
    SEND_STATE,
    MSK,
    CAR,
    TAIL,
    KEEP,
    GL,
    GV,
    GOWN,
    DG,
    DL0,
    DL1,
    DL2,
    in_sem,
    x_sem,
    x_rs,
    w1_ss,
    w1_rs,
    w2_ss,
    w2_rs,
    ag_ss,
    ag_rs,
    r1_ss,
    r1_rs,
    r2_ss,
    r2_rs,
    st_ss,
    st_rs,
    o_ss,
    o_rs,
    d1_ss,
    d1_rs,
    d2_ss,
    d2_rs,
    g1_sem,
    g_ss,
    g_rs,
    gl_sem,
    m_sem,
):
    D, R, C, F, Dr, MH, Hn, MB, T, NH, NB, NBH = (
        z_.D,
        z_.R,
        z_.C,
        z_.F,
        z_.Dr,
        z_.MH,
        z_.Hn,
        z_.MB,
        z_.T,
        z_.NH,
        z_.NB,
        z_.NBH,
    )
    nd, nt = z_.nd, z_.nt
    pieces = z_.pieces
    s, d, z = lax.axis_index("section"), lax.axis_index("dp"), lax.axis_index("tensor")
    zh, zl = z // Hn, z % Hn
    own = s * Hn + zl
    core_dev = (1 - s, d, z)

    def remote(src, dst, ssem, rsem, dev):
        return pltpu.make_async_remote_copy(
            src_ref=src, dst_ref=dst, send_sem=ssem, recv_sem=rsem, device_id=dev, device_id_type=MESH
        )

    def got(dst, sem):
        pltpu.make_async_copy(dst, dst, sem).wait()

    def dp_dev(step):
        return (s, (d + step) % nd, z)

    def z_dev(step):
        return (s, d, (z + step) % nt)

    def peer_zl(step):
        return (zl + step) % Hn

    masters = (
        pltpu.make_async_copy(qkv_in, MQ, m_sem.at[0]),
        pltpu.make_async_copy(o_in, MO, m_sem.at[1]),
        pltpu.make_async_copy(gu_in, MGU, m_sem.at[2]),
        pltpu.make_async_copy(d_in, MD, m_sem.at[3]),
    )
    for copy in masters:
        copy.start()

    barrier = pltpu.get_barrier_semaphore()

    def section_dev(i):
        return (s, (d + i // nt) % nd, (z + i % nt) % nt)

    def greet(i, carry):
        pl.semaphore_signal(barrier, inc=1, device_id=section_dev(i), device_id_type=MESH)
        return carry

    lax.fori_loop(1, nd * nt, greet, 0)
    pl.semaphore_signal(barrier, inc=1, device_id=core_dev, device_id_type=MESH)
    far_dev = (1 - s, d, (z + Hn) % nt)
    pl.semaphore_signal(barrier, inc=1, device_id=far_dev, device_id_type=MESH)
    pl.semaphore_wait(barrier, nd * nt + 1)

    def own_tokens(src, dst, array):
        for m in range(MH):
            mine = dst.at[pl.ds(m * MB + z * R, R)]
            pltpu.make_async_copy(src.at[zh * MH + m], mine, in_sem.at[array, m]).start()

    def spread_tokens(src, dst, array):
        for m in range(MH):
            mine = dst.at[pl.ds(m * MB + z * R, R)]
            for step in range(1, nt):
                other = (z + step) % nt

                @pl.when((other // Hn == zh) | (step == Hn))
                def _():
                    remote(
                        src.at[(other // Hn) * MH + m],
                        mine,
                        x_sem.at[0],
                        x_rs.at[array, m, step - 1],
                        z_dev(step),
                    ).start()

    def relay_tokens(dst, array, m):
        @pl.when(s == array)
        def _():
            chip = (z + Hn) % nt
            rows = dst.at[pl.ds(m * MB + chip * R, R)]
            got(rows, x_rs.at[array, m, Hn - 1])
            for step in range(1, Hn):
                peer = zh * Hn + peer_zl(step)
                remote(
                    rows,
                    rows,
                    x_sem.at[0],
                    x_rs.at[array, m, (peer + nt - chip) % nt - 1],
                    (s, d, peer),
                ).start()

    def await_tokens(dst, array, m):
        got(dst.at[pl.ds(m * MB + z * R, R)], in_sem.at[array, m])
        for step in range(1, nt):
            rows = dst.at[pl.ds(m * MB + (z + nt - step) % nt * R, R)]
            if step == Hn:
                pl.when(s != array)(lambda: got(rows, x_rs.at[array, m, step - 1]))
            else:
                got(rows, x_rs.at[array, m, step - 1])

            @pl.when(s == array)
            def _():
                remote(
                    rows, rows, x_sem.at[1], x_rs.at[array, m, step - 1], core_dev
                ).start()

    spot = {5: 0, 2: 1, 3: 2, 4: 3}

    def w_rows(l, block, p):
        col, width = pieces[p]
        return W.at[l, pl.ds(block * Dr, Dr), pl.ds(col, width)]

    def shard_cols(p):
        col, width = pieces[p]
        return L2.at[0, :, pl.ds(col, width)]

    def w_hand_near(l, p):
        @pl.when(zh == s)
        def _():
            pltpu.make_async_copy(shard_cols(p), w_rows(l, d, p), w1_rs.at[l, spot[p]]).start()

        @pl.when(zh != s)
        def _():
            w_hand(l, p, 0, core_dev).start()

    def w_hand(l, p, which, dev):
        return remote(
            shard_cols(p), w_rows(l, d, p), w1_ss.at[which], w1_rs.at[l, spot[p]], dev
        )

    def w_hand_far(l, p):
        w_hand(l, p, 1, (zh, d, (z + Hn) % nt)).start()

    def w_handed_out():
        @pl.when(zh != s)
        def _():
            got(L2.at[0], w1_ss.at[0])

        got(L2.at[0], w1_ss.at[1])

    square = nd == 4
    half_rows = Dr // 2
    dp_x, dp_y = d + 1 - 2 * (d % 2), (d + 2) % nd

    def w_half(l, block, half, p):
        col, width = pieces[p]
        return W.at[l, pl.ds(block * Dr + half * half_rows, half_rows), pl.ds(col, width)]

    def w_copy(l, p, k):
        if not square:
            rows, dev = w_rows(l, d, p), dp_dev(k + 1)
        elif k < 2:
            rows, dev = w_rows(l, d, p), (s, (dp_x, dp_y)[k], z)
        elif k == 2:
            rows, dev = w_half(l, dp_x, 0, p), (s, dp_y, z)
        else:
            rows, dev = w_half(l, dp_y, 1, p), (s, dp_x, z)
        return remote(rows, rows, w2_ss.at[l], w2_rs.at[l, spot[p], k], dev)

    def w_share(l, p):
        got(w_rows(l, d, p), w1_rs.at[l, spot[p]])
        for k in range(2 if square else nd - 1):
            w_copy(l, p, k).start()

    def w_forward(l, p):
        if square:
            got(w_rows(l, dp_x, p), w2_rs.at[l, spot[p], 0])
            w_copy(l, p, 2).start()
            got(w_rows(l, dp_y, p), w2_rs.at[l, spot[p], 1])
            w_copy(l, p, 3).start()

    def w_ready(l, p):
        if square:
            got(w_half(l, 3 - d, 0, p), w2_rs.at[l, spot[p], 2])
            got(w_half(l, 3 - d, 1, p), w2_rs.at[l, spot[p], 3])
        else:
            for step in range(1, nd):
                got(w_rows(l, (d + nd - step) % nd, p), w2_rs.at[l, spot[p], step - 1])

    def w_shared(l):
        got(W.at[l, pl.ds(0, (nd - 1) * Dr)], w2_ss.at[l])

    def pump(ops):
        for what, l, p in ops:
            with jax.named_scope(what + str(l) + str(p)):
                {"s": w_share, "f": w_forward}[what](l, p)

    near = s == zh
    gathered = (5, 2, 3, 4)

    def pump_near(ops):
        pl.when(near)(lambda: pump(ops))

    def pump_far(ops):
        pl.when(jnp.logical_not(near))(lambda: pump(ops))

    where = {4: 0, 2: 1, 3: 2, 1: 3, 6: 4, 7: 5, 8: 6}

    def split(p):
        return (6, 7, 8) if p == 0 else (p,)

    def d_copy(l, p, k):
        col, width = pieces[p]
        cols = pl.ds(col, width)
        if not square:
            src, dst, dev = w_rows(l, (d + k + 1) % nd, p), LW.at[l, k, :, cols], dp_dev(k + 1)
        else:
            first, second = pl.ds(0, half_rows), pl.ds(half_rows, half_rows)
            block, half, slot, rows, to = (
                (3 - d, 0, 2, first, dp_x),
                (3 - d, 1, 2, second, dp_y),
                (dp_x, 0, 0, first, dp_x),
                (dp_y, 1, 1, second, dp_y),
                (dp_y, 0, 1, first, dp_y),
                (dp_x, 1, 0, second, dp_x),
            )[k]
            src, dst, dev = w_half(l, block, half, p), LW.at[l, slot, rows, cols], (s, to, z)
        group = k if square and k < 2 else 2
        return remote(src, dst, d1_ss.at[l], d1_rs.at[l, where[p], group], dev)

    def d_send(l, p):
        for part in split(p):
            for k in range(4 if square else nd - 1):
                d_copy(l, part, k).start()

    @scoped
    def d_mid(l, p):
        if p == 0:
            for part in split(p):
                d_mid(l, part)
        elif square:
            col, width = pieces[p]
            cols = pl.ds(col, width)
            for k, block, half in ((0, dp_y, 0), (1, dp_x, 1)):
                copy = d_copy(l, p, k)
                copy.wait_recv()
                rows = pl.ds(block * Dr + half * half_rows, half_rows)
                arrived = LW[l, 2, half * half_rows : (half + 1) * half_rows, cols]
                W[l, rows, cols] = (W[l, rows, cols].astype(F32) + arrived.astype(F32)).astype(BF)
                d_copy(l, p, 4 + k).start()

    part_rows = Dr // 4

    def d_pass(l, p, q, rows=part_rows):
        for part in split(p):
            col, width = pieces[part]
            cols = pl.ds(col, width)
            src = W.at[l, pl.ds(d * Dr + q * rows, rows), cols]
            dst = L2.at[zh, pl.ds(q * rows, rows), cols]
            arrival = d2_rs.at[where[part], zh]
            to_self = (s == l) & (zh == s)

            @pl.when(to_self)
            def _():
                pltpu.make_async_copy(src, dst, arrival).start()

            @pl.when(jnp.logical_not(to_self))
            def _():
                remote(src, dst, d2_ss.at[l], arrival, (l, d, s * Hn + zl)).start()

    @scoped
    def d_total_rows(l, p):
        for part in split(p):
            col, width = pieces[part]
            cols = pl.ds(col, width)
            slots = 2 if square else nd - 1
            got(LW.at[l, pl.ds(0, slots), :, cols], d1_rs.at[l, where[part], 2])
            rows = pl.ds(d * Dr, Dr)
            total = W[l, rows, cols].astype(F32)
            for slot in range(slots):
                total = total + LW[l, slot, :, cols].astype(F32)
            W[l, rows, cols] = total.astype(BF)

    def d_sum(l, p):
        d_total_rows(l, p)
        d_pass(l, p, 0, Dr)

    def d_sent(l):
        got(W.at[l, pl.ds(0, (nd - 1) * Dr)], d1_ss.at[l])

        @pl.when(jnp.logical_not((s == l) & (zh == s)))
        def _():
            got(W.at[l, pl.ds(0, Dr)], d2_ss.at[l])

    outs = (
        pltpu.make_async_copy(MQ, out_qkv, m_sem.at[0]),
        pltpu.make_async_copy(MO, out_o, m_sem.at[1]),
        pltpu.make_async_copy(MGU, out_gu, m_sem.at[2]),
        pltpu.make_async_copy(MD, out_d, m_sem.at[3]),
    )

    def d_arrived(p):
        col, width = pieces[p]
        for half in range(2):
            got(L2.at[half, :, pl.ds(col, width)], d2_rs.at[where[p], half])

    def d_total(col, width):
        return L2[0, :, col : col + width].astype(F32) + L2[1, :, col : col + width].astype(F32)

    @scoped
    def d_final(p):
        d_arrived(p)
        if p >= 6:
            j = p - 6
            MQ[j] = d_total(j * C, C)
            pltpu.make_async_copy(MQ.at[j], out_qkv.at[j], m_sem.at[0]).start()
        elif p == 1:
            MO[...] = d_total(z_.oO, C).T
            outs[1].start()
        elif p == 3:
            MGU[...] = d_total(z_.oG, z_.GUw).T[: 2 * F]
            outs[2].start()
        elif p == 4:
            MD[...] = d_total(z_.oD, z_.Dw).T[:F]
            outs[3].start()

    @scoped
    def shard_attention():
        masters[0].wait()
        masters[1].wait()
        for j in range(3):
            L2[0, :, j * C : (j + 1) * C] = MQ[j].astype(BF)
        L2[0, :, z_.oO : z_.oG] = MO[...].T.astype(BF)

    @scoped
    def shard_feed():
        masters[2].wait()
        masters[3].wait()
        for ref, col, width, rows in ((MGU, z_.oG, z_.GUw, 2 * F), (MD, z_.oD, z_.Dw, F)):
            value = ref[...]
            if width > rows:
                value = jnp.concatenate([value, jnp.zeros((width - rows, Dr), F32)], axis=0)
            L2[0, :, col : col + width] = value.T.astype(BF)

    def chunk_rows(m, c):
        return pl.ds(m * MB + c * R, R)

    def ag_send(k, buf, m):
        rows = buf.at[chunk_rows(m, own)]
        for step in range(1, Hn):
            dev = (s, d, zh * Hn + peer_zl(step))
            remote(rows, rows, ag_ss.at[k], ag_rs.at[k, m, Hn - step], dev).start()
        remote(rows, rows, ag_ss.at[k], ag_rs.at[k, m, 0], core_dev).start()

    def ag_forward(k, buf, m):
        for step in range(1, Hn):
            rows = buf.at[chunk_rows(m, s * Hn + peer_zl(step))]
            got(rows, ag_rs.at[k, m, step])
            remote(rows, rows, ag_ss.at[k], ag_rs.at[k, m, 0], core_dev).start()

    def ag_wait(k, buf, m):
        got(buf.at[pl.ds(m * MB + (1 - s) * Hn * R, Hn * R)], ag_rs.at[k, m, 0])

    def ag_sent(k, buf):
        got(buf.at[pl.ds(0, MH * (2 * Hn - 1) * R)], ag_ss.at[k])

    def rs_copy1(k, m):
        par = k % 2
        return remote(
            PT.at[par, pl.ds(m * MB + (1 - s) * Hn * R, Hn * R)],
            RL1.at[par, m],
            r1_ss.at[par, m],
            r1_rs.at[par, m],
            core_dev,
        )

    def rs_copy2(k, m, step):
        par = k % 2
        return remote(
            RSB.at[par, m, step - 1],
            RL2.at[par, m, step - 1],
            r2_ss.at[par, m, step - 1],
            r2_rs.at[par, m, step - 1],
            (s, d, zh * Hn + peer_zl(step)),
        )

    def rs_first(k, m, value):
        PT[k % 2, pl.ds(m * MB, MB), :] = value.astype(BF)
        rs_copy1(k, m).start()

    def rs_second(k, m):
        par = k % 2
        copy = rs_copy1(k, m)
        copy.wait_send()
        copy.wait_recv()
        for step in range(1, Hn):
            there = peer_zl(step)
            part = PT[par, chunk_rows(m, s * Hn + there), :].astype(F32) + RL1[
                par, m, pl.ds(there * R, R), :
            ].astype(F32)
            RSB[par, m, step - 1] = part.astype(BF)
            rs_copy2(k, m, step).start()

    def after(k, i, m):
        @pl.when(i > 0)
        def _():
            rs_second(k, m)

    def rs_third(k, m):
        par = k % 2
        total = PT[par, chunk_rows(m, own), :].astype(F32) + RL1[
            par, m, pl.ds(zl * R, R), :
        ].astype(F32)
        for step in range(1, Hn):
            copy = rs_copy2(k, m, step)
            copy.wait_send()
            copy.wait_recv()
            total = total + RL2[par, m, step - 1].astype(F32)
        return total

    def own_rows(m):
        return pl.ds(m * R, R)

    def rms(rows):
        return lax.rsqrt(jnp.mean(rows * rows, axis=-1, keepdims=True) + EPS)

    def gain(l, which):
        return GV[l, which : which + 1, :]

    def rms_back(l, which, rows, grad):
        inverse = rms(rows)
        scaled = grad * gain(l, which)
        back = inverse * scaled - rows * (inverse * inverse * inverse) * jnp.mean(
            scaled * rows, axis=-1, keepdims=True
        )
        DG[l, which : which + 1, :] += jnp.sum(grad * rows * inverse, axis=0, keepdims=True)
        return back

    def send_out(buf, l, out, which, m):
        src = buf.at[l, own_rows(m)]
        dst = out.at[zh * MH + m]
        to_self = (s == l) & (zh == s)

        @pl.when(to_self)
        def _():
            pltpu.make_async_copy(src, dst, o_rs.at[which, zh]).start()

        @pl.when(jnp.logical_not(to_self))
        def _():
            remote(
                src, dst, o_ss.at[l], o_rs.at[which, zh], (l, d, s * Hn + zl)
            ).start()

    lane_head = lax.broadcasted_iota(jnp.int32, (1, C), 1) // DH
    head_bf = [(lane_head == h).astype(F32).astype(BF) for h in range(NH)]
    head_f = [(lane_head == h).astype(F32) for h in range(NH)]

    def stack(rows):
        return jnp.concatenate([rows * head_bf[h] for h in range(NH)], axis=0)

    def unstack(wide):
        out = wide[0:DH] * head_f[0]
        for h in range(1, NH):
            out = out + wide[h * DH : (h + 1) * DH] * head_f[h]
        return out

    def tall(mask):
        return jnp.concatenate([mask] * NH, axis=0)

    def head_mean(values):
        row = lax.broadcasted_iota(jnp.int32, (C, C), 0) // DH
        col = lax.broadcasted_iota(jnp.int32, (C, C), 1) // DH
        same = jnp.where(row == col, 1.0 / DH, 0.0).astype(BF)
        high = values.astype(BF)
        low = (values - high.astype(F32)).astype(BF)
        return mm(high, same) + mm(low, same)

    def block_rows(b):
        return pl.ds(pl.multiple_of(b * BLOCK, BLOCK), BLOCK)

    def qkv_block(l, b):
        rows = block_rows(b)
        return (QKV[l, rows, 0:C], QKV[l, rows, C : 2 * C], QKV[l, rows, 2 * C : 3 * C])

    def softplus(values):
        return jnp.maximum(values, 0.0) + jnp.log(1.0 + jnp.exp(-jnp.abs(values)))

    def features(values):
        return softplus(values.astype(F32)).astype(BF)

    def diag_forward(b):
        q, k, v = qkv_block(0, b)
        scores = mm(stack(q), k, NT) * (1.0 / math.sqrt(DH))
        scores = jnp.where(tall(MSK[b]) > 0.5, scores, -1e9)
        top = jnp.max(scores, axis=-1, keepdims=True)
        weights = jnp.exp(scores - top)
        weights = (weights / jnp.sum(weights, axis=-1, keepdims=True)).astype(BF)
        AP[0, b] = weights
        O[0, block_rows(b), :] = unstack(mm(weights, v)).astype(BF)

    def diag_backward(b, grad_o):
        q, k, v = qkv_block(0, b)
        low = stack(grad_o.astype(BF))
        weights = AP[0, b]
        wide = weights.astype(F32)
        grad_v = mm(weights, low, TN)
        grad_w = mm(low, v, NT)
        grad_s = wide * (grad_w - jnp.sum(grad_w * wide, axis=-1, keepdims=True))
        grad_s = (grad_s * (1.0 / math.sqrt(DH))).astype(BF)
        grad_q = unstack(mm(grad_s, k))
        grad_k = mm(grad_s, stack(q), TN)
        rows = block_rows(b)
        GQKV[rows, 0:C] = grad_q.astype(BF)
        GQKV[rows, C : 2 * C] = grad_k.astype(BF)
        GQKV[rows, 2 * C : 3 * C] = grad_v.astype(BF)

    def fold(square):
        out = square[0:DH] * head_f[0]
        for h in range(1, NH):
            out = out + square[h * DH : (h + 1) * DH] * head_f[h]
        return out

    def unfold(flat):
        return stack(flat.astype(BF))

    def wide_lanes(column):
        return jnp.concatenate([column] * (C // 128), axis=1)

    def norm_state(b, state):
        q, k, v = qkv_block(1, b)
        ST[b] = state
        key = features(k)
        term = mm(key, (v.astype(F32) * wide_lanes(TAIL[b])).astype(BF), TN)
        return wide_lanes(KEEP[b, 0:1, :]) * state + fold(term)

    def norm_forward(b, passed):
        q, k, v = qkv_block(1, b)
        query, key = features(q), features(k)
        local = jnp.where(tall(MSK[b]) > 0.5, mm(stack(query), key, NT), 0.0).astype(BF)
        AP[1, b] = local
        state = ST[b] + passed * SIN[0].astype(F32)
        ST[b] = state
        mixed = unstack(mm(local, v)) + wide_lanes(CAR[b]) * mm(query, unfold(state))
        rows = block_rows(b)
        UU[rows, :] = mixed
        O[1, rows, :] = (mixed * lax.rsqrt(head_mean(mixed * mixed) + EPS)).astype(BF)
        return passed * wide_lanes(KEEP[b, 0:1, :])

    def norm_back_first(b, grad_o, state):
        rows = block_rows(b)
        mixed = UU[rows, :]
        scale = lax.rsqrt(head_mean(mixed * mixed) + EPS)
        grad = scale * grad_o - mixed * (scale * scale * scale) * head_mean(grad_o * mixed)
        low = grad.astype(BF)
        DU[rows, :] = low
        ST2_store(b, state)
        query = features(QKV[1, rows, 0:C])
        term = mm(query, (low.astype(F32) * wide_lanes(CAR[b])).astype(BF), TN)
        return wide_lanes(KEEP[b, 0:1, :]) * state + fold(term)

    def ST2_store(b, state):
        ST[NBH + b] = state

    def sigmoid(values):
        return 1.0 / (1.0 + jnp.exp(-values.astype(F32)))

    def norm_back_local(b):
        rows = block_rows(b)
        q, k, v = qkv_block(1, b)
        query, key = features(q), features(k)
        low = DU[rows, :]
        stacked = stack(low)
        grad_a = jnp.where(tall(MSK[b]) > 0.5, mm(stacked, v, NT), 0.0).astype(BF)
        grad_q = unstack(mm(grad_a, key)) + wide_lanes(CAR[b]) * mm(low, unfold(ST[b]), NT)
        GQKV[rows, 0:C] = (grad_q * sigmoid(q)).astype(BF)
        GQKV[rows, C : 2 * C] = (mm(grad_a, stack(query), TN) * sigmoid(k)).astype(BF)
        GQKV[rows, 2 * C : 3 * C] = mm(AP[1, b], stacked, TN).astype(BF)

    def norm_back_state(b, passed):
        rows = block_rows(b)
        q, k, v = qkv_block(1, b)
        grad_wide = unfold(ST[NBH + b] + passed * SIN[1].astype(F32))
        tail = wide_lanes(TAIL[b])
        grad_k = tail * mm(v, grad_wide, NT) * sigmoid(k)
        grad_v = tail * mm(features(k), grad_wide)
        GQKV[rows, C : 2 * C] = (GQKV[rows, C : 2 * C].astype(F32) + grad_k).astype(BF)
        GQKV[rows, 2 * C : 3 * C] = (GQKV[rows, 2 * C : 3 * C].astype(F32) + grad_v).astype(BF)
        return passed * wide_lanes(KEEP[b, 0:1, :])

    @scoped
    def masks():
        row = lax.broadcasted_iota(jnp.int32, (BLOCK, BLOCK), 0)
        col = lax.broadcasted_iota(jnp.int32, (BLOCK, BLOCK), 1)
        token = lax.broadcasted_iota(jnp.int32, (MB, BLOCK), 0)
        lane = lax.broadcasted_iota(jnp.int32, (MB, BLOCK), 1)
        start = jnp.concatenate([starts_in[zh * MH + m] for m in range(MH)], axis=0)
        start = start.astype(F32).astype(BF)
        chunk_lane = lax.broadcasted_iota(jnp.int32, (BLOCK, MH), 1)
        for j in range(NB):
            upper = ((token // BLOCK == j) & (token % BLOCK <= lane)).astype(F32).astype(BF)
            count_row = mm(start, upper)
            count_col = mm(upper, start, (((0,), (1,)), ((), ())))
            for m in range(MH):
                b = m * NB + j
                c_row = count_row[m : m + 1, :]
                c_col = jnp.sum(
                    jnp.where(chunk_lane == m, count_col, 0.0), axis=1, keepdims=True
                )
                last = jnp.sum(
                    jnp.where(col[0:1] == BLOCK - 1, c_row, 0.0), axis=1, keepdims=True
                )
                MSK[b] = jnp.where((c_row == c_col) & (row >= col), 1.0, 0.0)
                CAR[b] = jnp.broadcast_to(jnp.where(c_col == 0.0, 1.0, 0.0), (BLOCK, 128))
                TAIL[b] = jnp.broadcast_to(jnp.where(c_col == last, 1.0, 0.0), (BLOCK, 128))
                KEEP[b] = jnp.broadcast_to(jnp.where(last == 0.0, 1.0, 0.0), (8, 128))

    place = d * nt + z

    def gain_copy(i):
        return remote(GL.at[place], GL.at[place], gl_sem.at[0], gl_sem.at[1], section_dev(i))

    @scoped
    def gains_out():
        width = gain_in.shape[1]
        row = lax.broadcasted_iota(jnp.int32, (width, 128), 0)
        col = lax.broadcasted_iota(jnp.int32, (width, 128), 1)
        spot = (col % width == row) & (col // width == place % (128 // width))
        GL[place] = mm(gain_in[...].astype(BF), spot.astype(F32).astype(BF))

        def one(i, carry):
            gain_copy(i).start()
            return carry

        lax.fori_loop(1, nd * nt, one, 0)

    @scoped
    def gains_in():
        for k in (1, 0):
            got(GL.at[pl.ds(0, nd * nt - 1)], gl_sem.at[k])
        each = nd * nt * 128 // D
        for t in range(D // 128):
            total = GL[t * each]
            for i in range(1, each):
                total = total + GL[t * each + i]
            GV[s, :, t * 128 : (t + 1) * 128] = total
        gain_swap().start()

    def gain_swap():
        return remote(GV.at[s], GV.at[s], g1_sem.at[0], g1_sem.at[1], core_dev)

    def gains_other():
        gain_swap().wait_send()
        got(GV.at[1 - s], g1_sem.at[1])

    def dp_gain(step):
        return remote(
            GOWN, DL2.at[step - 1], g_ss.at[1, step - 1], g_rs.at[1, step - 1], dp_dev(step)
        )

    def core_gain():
        return remote(DG.at[1 - s], DL0, g1_sem.at[2], g1_sem.at[3], core_dev)

    def z_gain(step):
        return remote(
            DG.at[s], DL1.at[step - 1], g_ss.at[0, step - 1], g_rs.at[0, step - 1], z_dev(step)
        )

    @scoped
    def gain_second():
        core_gain().wait()
        DG[s] = DG[s] + DL0[...]
        for step in range(1, nt):
            z_gain(step).start()

    @scoped
    def gain_third():
        total = DG[s]
        for step in range(1, nt):
            z_gain(step).wait()
            total = total + DL1[step - 1]
        GOWN[...] = total
        for step in range(1, nd):
            dp_gain(step).start()

    @scoped
    def gain_final():
        total = GOWN[...]
        for step in range(1, nd):
            dp_gain(step).wait()
            total = total + DL2[step - 1]
        GOWN[...] = total
        width = out_gain.shape[1]
        each = 128 // width
        tile = GOWN[:, pl.ds(pl.multiple_of(place // each * 128, 128), 128)]
        mine = jnp.zeros((2, width), F32)
        for i in range(each):
            piece = tile[:, i * width : (i + 1) * width]
            mine = jnp.where(place % each == i, piece, mine)
        out_gain[...] = mine

    def loop(count, fn):
        def step(i, carry):
            fn(i)
            return carry

        with jax.named_scope(fn.__name__):
            lax.fori_loop(0, count, step, 0)

    def chunk(m):
        return pl.ds(pl.multiple_of(m * MB, BLOCK), MB)

    def w_cols(l, p):
        col, width = pieces[p]
        return W[l, :, col : col + width]

    def w_gate_up(l):
        return W[l, :, z_.oG : z_.oD]

    @scoped
    def state_copy(slot):
        return remote(
            SEND_STATE.at[slot],
            SIN.at[slot],
            st_ss.at[slot],
            st_rs.at[slot],
            (s, d, (z + Hn) % nt),
        )

    def state_out(slot, value, sender):
        SEND_STATE[slot] = value.astype(BF)

        @pl.when(zh == sender)
        def _():
            SIN[slot] = jnp.zeros((DH, C), BF)
            state_copy(slot).start()

    @scoped
    def state_in(slot, sender):
        @pl.when(zh != sender)
        def _():
            state_copy(slot).wait_recv()

    outer = zh == zl
    inner, far = jnp.logical_not(outer), jnp.logical_not(near)

    def only(cond, fn):
        pl.when(cond)(fn)

    def hand_far(l, cond, ps):
        def go():
            for p in ps:
                w_hand_far(l, p)

        pl.when((s == l) & cond)(go)

    def hand_near(ps):
        for l in range(2):

            @pl.when(s == l)
            def _():
                for p in ps:
                    w_hand_near(l, p)

    def x_out():
        spread_tokens(xin, XF, 0)

    gains_out()
    shard_attention()
    hand_far(0, s == 0, [5])
    hand_near([5])
    only((s == 0) & inner, x_out)
    pump_near([("s", 0, 5)])
    own_tokens(xin, XF, 0)
    own_tokens(cot, GF.at[1], 1)
    shard_feed()
    hand_near([2, 3, 4])
    masks()
    for l in range(2):
        DG[l] = jnp.zeros((2, D), F32)
    pump_near([("s", 0, 2)])
    gains_in()
    pump_far([("s", 0, 5)])
    only((s == 0) & outer & far, x_out)
    pump([("f", 0, 5)])
    pump_near([("f", 0, 2)])
    only((s == 0) & outer & near, x_out)
    only(s == 1, gains_other)
    for m in range(MH):
        relay_tokens(XF, 0, m)
    hand_far(0, s == 0, [2, 3, 4])
    await_tokens(XF, 0, 0)

    def cot_out():
        spread_tokens(cot, GF.at[1], 1)

    stage = {
        (0, "attended"): lambda: (
            pump_near([("f", 0, 3), ("f", 0, 4)]),
            pump_far([("s", 0, 2), ("s", 0, 3), ("f", 0, 2), ("s", 0, 4)]),
        ),
        (0, "hidden"): lambda: (
            hand_far(1, inner, [5, 4, 2, 3]),
            hand_far(1, outer, [5]),
            pump_near([("s", 1, 5)]),
            pump_far([("f", 0, 3), ("f", 0, 4)]),
        ),
        (0, "ready"): lambda: (
            hand_far(1, outer & far, [4]),
            pump_near([("f", 1, 5)]),
            hand_far(1, outer & near, [4]),
            pump_far([("s", 1, 5)]),
            hand_far(1, outer & far, [2, 3]),
        ),
        (0, "feeding"): lambda: (
            hand_far(1, outer & near, [2, 3]),
            pump_near([("s", 1, 4)]),
        ),
        (0, "fed"): lambda: (
            pump_near([("s", 1, 2), ("f", 1, 4)]),
            pump_far([("f", 1, 5), ("s", 1, 4)]),
            only(s == 0, gains_other),
        ),
        (0, "result"): lambda: (
            only(s == 1, cot_out),
            pump_near([("s", 1, 3)]),
            pump_far([("s", 1, 2), ("f", 1, 4)]),
        ),
        (1, "states"): lambda: (
            [relay_tokens(GF.at[1], 1, m) for m in reversed(range(MH))],
            pump_near([("f", 1, 2), ("f", 1, 3)]),
            pump_far([("s", 1, 3), ("f", 1, 2)]),
        ),
        (1, "attended"): lambda: (pump_far([("f", 1, 3)]),),
        (1, "hidden"): lambda: (results_out(Y, 0, out_y, 0),),
        (1, "ready"): lambda: (),
        (1, "fed"): lambda: (),
        "b1 second": lambda: (),
        "b1 middle": lambda: (results_out(Y, 1, out_y, 0), d_mid(1, 4)),
        "b1 feed": lambda: (),
        "b1 third": lambda: (d_mid(1, 3),),
        "b1 end": lambda: (d_total_rows(1, 3),),
        "b0 second": lambda: (d_total_rows(1, 0),),
        "b0 middle": lambda: (),
        "b0 feed": lambda: (results_out(GX, 1, out_g, 1), d_total_rows(1, 1)),
        "b0 third": lambda: (
            only(far, lambda: run(d_mid, 2)),
            only(near, lambda: run(d_mid, 4) or run(d_send, 2, 3)),
        ),
        "b0 end": lambda: (
            core_gain().start(),
            only(near, lambda: run(d_send, 0, 1)),
            only(far, lambda: far_tail()),
            only(near, lambda: near_tail()),
            gain_third(),
        ),
    }

    def run(step, *parts):
        for p in parts:
            step(0, p)

    def far_tail():
        gain_second()
        run(d_mid, 6)
        run(d_sum, 3)
        run(d_mid, 7, 8)
        run(d_sum, 6)
        run(d_mid, 1)
        run(d_sum, 7, 8, 1)
        results_out(GX, 0, out_g, 1)

    def near_tail():
        run(d_sum, 4)
        run(d_mid, 2, 3)
        gain_second()
        run(d_mid, 6, 7, 8, 1)
        results_out(GX, 0, out_g, 1)
        run(d_sum, 2, 3, 6, 7, 8, 1)

    def results_out(buf, l, out, which):
        for m in range(MH):
            send_out(buf, l, out, which, m)

    def input_rows(l, m):
        if l == 0:
            return XF[chunk_rows(m, own), :].astype(F32)
        return Y[0, own_rows(m), :].astype(F32)

    def gate_up_grad(grad, both):
        parts = [grad * both[:, F : 2 * F], grad * both[:, :F]]
        if z_.GUw > 2 * F:
            parts.append(jnp.zeros((MB, z_.GUw - 2 * F), F32))
        return jnp.concatenate(parts, axis=1).astype(BF)

    def finish_layer(l, rs2, ag3):
        def result(m):
            rows = (H[l, own_rows(m), :] + rs_third(rs2, m)).astype(BF)
            Y[l, own_rows(m), :] = rows
            if l == 0:
                wide = rows.astype(F32)
                N1[1, chunk_rows(m, own), :] = (wide * rms(wide) * gain(1, 0)).astype(BF)
                ag_send(ag3, N1.at[1], m)

        loop(MH, result)

    def forward(l, ag1, rs1, ag2, rs2, ag3):
        w_ready(l, 5)

        def qkv_chunk(m):
            if l == 0:
                pl.when(m > 0)(lambda: await_tokens(XF, 0, m))
                pl.when((m == 1) & near)(lambda: pump([("s", 0, 3), ("s", 0, 4)]))
                rows = XF[chunk(m), :].astype(F32)
                N1[0, chunk(m), :] = (rows * rms(rows) * gain(0, 0)).astype(BF)
            else:
                ag_forward(ag1, N1.at[1], m)
                ag_wait(ag1, N1.at[1], m)
            QKV[l, chunk(m), :] = mm(N1[l, chunk(m), :], w_cols(l, 0)).astype(BF)

        def out_chunk(m):
            rs_first(rs1, m, mm(O[l, chunk(m), :], w_cols(l, 1), NT))

        if l == 0:

            def attend(m):
                qkv_chunk(m)
                for i in range(NB):
                    diag_forward(m * NB + i)
                out_chunk(m)
                after(rs1, m, m - 1)

            loop(MH, attend)
            rs_second(rs1, MH - 1)
            stage[l, "attended"]()
        else:

            def states(m, state):
                qkv_chunk(m)
                for i in range(NB):
                    state = norm_state(m * NB + i, state)
                return state

            with jax.named_scope('states'):
                last = lax.fori_loop(0, MH, states, jnp.zeros((DH, C), F32))
            w_handed_out()
            state_out(0, last, 0)
            state_in(0, 0)
            stage[l, "states"]()

            def attend(m, passed):
                for i in range(NB):
                    passed = norm_forward(m * NB + i, passed)
                out_chunk(m)
                after(rs1, m, m - 1)
                return passed

            with jax.named_scope('attend'):
                lax.fori_loop(0, MH, attend, jnp.ones((1, C), F32))
            rs_second(rs1, MH - 1)
            stage[l, "attended"]()

        def hidden_rows(m):
            rows = input_rows(l, m) + rs_third(rs1, m)
            H[l, own_rows(m), :] = rows
            N2[l, chunk_rows(m, own), :] = (rows * rms(rows) * gain(l, 1)).astype(BF)
            ag_send(ag2, N2.at[l], m)

        loop(MH, hidden_rows)
        stage[l, "hidden"]()
        w_ready(l, 4)
        if l == 1:

            def hidden_grad(m):
                await_tokens(GF.at[1], 1, m)
                GGU[chunk(m), 0 : z_.Dw] = mm(GF[1, chunk(m), :], w_cols(1, 4)).astype(BF)

            loop(MH, hidden_grad)
        w_ready(l, 2)
        w_ready(l, 3)
        stage[l, "ready"]()

        def feed(m):
            ag_forward(ag2, N2.at[l], m)
            ag_wait(ag2, N2.at[l], m)
            rows = N2[l, chunk(m), :]
            both = mm(rows, w_gate_up(l))
            if l == 0:
                GU[l, chunk(m), :] = both.astype(BF)
            else:
                grad = GGU[chunk(m), 0 : z_.Dw].astype(F32)[:, :F]
                GGU[chunk(m), :] = gate_up_grad(grad, both)
            hidden = both[:, :F] * both[:, F : 2 * F]
            if z_.Dw > F:
                hidden = jnp.concatenate([hidden, jnp.zeros((MB, z_.Dw - F), F32)], axis=1)
            hidden = hidden.astype(BF)
            HID[l, chunk(m), :] = hidden
            rs_first(rs2, m, mm(hidden, w_cols(l, 4), NT))
            if l == 0:


                @pl.when(m == 1)
                def _():
                    stage[0, "feeding"]()

            after(rs2, m, m - 1)

        loop(MH, feed)
        rs_second(rs2, MH - 1)
        stage[l, "fed"]()

        if l == 0:
            finish_layer(l, rs2, ag3)
            stage[l, "result"]()

    forward(0, None, 0, 0, 1, 1)
    forward(1, 1, 2, 2, 3, None)

    RB = min(D, 256)

    @scoped
    def grad_weight(l, p, left, right, send=True):
        col, width = pieces[p]
        for r in range(D // RB):
            W[l, r * RB : (r + 1) * RB, col : col + width] = mm(
                left[:, r * RB : (r + 1) * RB], right, TN
            ).astype(BF)
        if send:
            d_send(l, p)

    def rest(l, p):
        for q in range(MH, 4):
            d_pass(l, p, q)

    def grad_part(l, p, send=True):
        col, width = pieces[p]
        grad_weight(l, p, N2[l], GGU[:, col - z_.oG : col - z_.oG + width], send)

    def backward(l, ag_in, rs1, ag2, rs2, ag_out):
        w_shared(l)

        def feed_back(i):
            m = MH - 1 - i
            if l == 0:
                ag_forward(ag_in, GF.at[0], m)
                ag_wait(ag_in, GF.at[0], m)
                grad = mm(GF[l, chunk(m), :], w_cols(l, 4))[:, :F]
                GGU[chunk(m), :] = gate_up_grad(grad, GU[l, chunk(m), :].astype(F32))
            rs_first(rs1, m, mm(GGU[chunk(m), :], w_gate_up(l), NT))
            after(rs1, i, m + 1)
            if l == 0:

                @pl.when(i == 0)
                def _():
                    d_mid(1, 1)
                    d_mid(1, 0)

                d_pass(1, 3, i)
        if l == 1:
            grad_weight(l, 4, GF[l], HID[l])
        loop(MH, feed_back)
        rs_second(rs1, 0)
        if l == 0:
            rest(1, 3)
            grad_weight(l, 4, GF[l], HID[l], False)
            only(far, lambda: d_send(0, 4))
        else:
            grad_part(l, 2)
            finish_layer(1, 3, None)
        stage[f"b{l} second"]()

        def middle(i):
            m = MH - 1 - i
            rows = H[l, own_rows(m), :]
            grad = GF[l, chunk_rows(m, own), :].astype(F32) + rms_back(
                l, 1, rows, rs_third(rs1, m)
            )
            GH[own_rows(m), :] = grad
            GA[l, chunk_rows(m, own), :] = grad.astype(BF)
            ag_send(ag2, GA.at[l], m)
            if l == 0:
                only((i == 1) & near, lambda: d_send(0, 4))
                d_pass(1, 0, i)

        loop(MH, middle)
        if l == 0:
            rest(1, 0)
        stage[f"b{l} middle"]()
        if l == 0:
            grad_part(l, 2, False)

            @pl.when(far)
            def _():
                d_mid(0, 4)
                d_send(0, 2)

            grad_part(l, 3, False)
            only(far, lambda: d_send(0, 3))
        else:
            grad_part(l, 3)
        stage[f"b{l} feed"]()

        def grad_o(m):
            ag_forward(ag2, GA.at[l], m)
            ag_wait(ag2, GA.at[l], m)
            return mm(GA[l, chunk(m), :], w_cols(l, 1))

        def qkv_back(i, m):
            rs_first(rs2, m, mm(GQKV[chunk(m), :], w_cols(l, 0), NT))
            after(rs2, i, m + 1)

        if l == 0:

            def attend(i):
                m = MH - 1 - i
                grad = grad_o(m)
                for j in range(NB):
                    diag_backward(m * NB + j, grad[j * BLOCK : (j + 1) * BLOCK])
                qkv_back(i, m)
                d_pass(1, 1, i)
                only((i == 0) & far, lambda: d_sum(0, 4))

            loop(MH, attend)
        else:

            def states(i, state):
                m = MH - 1 - i
                grad = grad_o(m)
                for j in reversed(range(NB)):
                    state = norm_back_first(m * NB + j, grad[j * BLOCK : (j + 1) * BLOCK], state)
                return state

            with jax.named_scope("states"):
                last = lax.fori_loop(0, MH, states, jnp.zeros((DH, C), F32))
            state_out(1, last, 1)
            d_mid(1, 2)
            grad_weight(l, 1, GA[l], O[l])

            def attend_local(m):
                for j in range(NB):
                    norm_back_local(m * NB + j)

            loop(MH, attend_local)
            d_total_rows(1, 4)
            state_in(1, 1)
            pl.when(zh == 0)(lambda: d_pass(1, 4, 0, Dr))

            def attend(i, passed):
                m = MH - 1 - i
                for j in reversed(range(NB)):
                    passed = norm_back_state(m * NB + j, passed)
                qkv_back(i, m)

                @pl.when(zh == 1)
                def _():
                    d_pass(1, 4, i)

                return passed

            with jax.named_scope("attend"):
                lax.fori_loop(0, MH, attend, jnp.ones((1, C), F32))

        rs_second(rs2, 0)
        if l == 0:
            rest(1, 1)
        else:
            pl.when(zh == 1)(lambda: rest(1, 4))
        stage[f"b{l} third"]()
        grad_weight(l, 0, N1[l], GQKV[...], l == 1)
        if l == 0:
            grad_weight(l, 1, GA[l], O[l], False)

            @pl.when(far)
            def _():
                d_mid(0, 3)
                d_send(0, 0)
                d_send(0, 1)
                d_sum(0, 2)


        def result(i):
            m = MH - 1 - i
            grad = GH[own_rows(m), :] + rms_back(l, 0, input_rows(l, m), rs_third(rs2, m))
            low = grad.astype(BF)
            GX[l, own_rows(m), :] = low
            if l == 1:
                GF[0, chunk_rows(m, own), :] = low
                ag_send(ag_out, GF.at[0], m)
                pl.when(i == 0)(lambda: d_total_rows(1, 2))
                d_pass(1, 2, i)

        loop(MH, result)
        if l == 1:
            rest(1, 2)
        stage[f"b{l} end"]()

    backward(1, None, 4, 3, 5, 4)
    backward(0, 4, 6, 5, 7, None)

    for p in (4, 2, 3, 6, 7, 8, 1):
        d_final(p)
    gain_final()
    for copy in outs:
        copy.wait()
    for l in range(2):
        d_sent(l)

    ags = ((0, N2.at[0]), (1, N1.at[1]), (2, N2.at[1]), (3, GA.at[1]), (4, GF.at[0]), (5, GA.at[0]))

    for slot in range(2):

        @pl.when(zh == slot)
        def _():
            state_copy(slot).wait_send()

    for k, buf in ags:
        ag_sent(k, buf)
    for l in range(2):

        @pl.when(jnp.logical_not((s == l) & (zh == s)))
        def _():
            got(XF.at[pl.ds(0, 2 * MH * R)], o_ss.at[l])

    for half in range(2):
        got(out_y.at[pl.ds(half * MH, MH)], o_rs.at[0, half])
        got(out_g.at[pl.ds(half * MH, MH)], o_rs.at[1, half])
    for k in range(2):
        got(XF.at[pl.ds(0, MH * (nt - 1) * R)], x_sem.at[k])


def place_results(*refs):
    count = (len(refs) - 2) // 3
    sources, targets, held = refs[:count], refs[count : 2 * count], refs[2 * count : 3 * count]
    in_sem, out_sem = refs[-2:]
    reads = [pltpu.make_async_copy(sources[i], held[i], in_sem.at[i]) for i in range(count)]
    writes = [pltpu.make_async_copy(held[i], targets[i], out_sem.at[i]) for i in range(count)]
    for copy in reads:
        copy.start()
    for read, write in zip(reads, writes):
        read.wait()
        write.start()
    for copy in writes:
        copy.wait()


def solution(mesh):
    nd, nt = mesh.shape["dp"], mesh.shape["tensor"]

    def on_device(inputs, starts, cotangent, qkv_m, out_m, gateup_m, down_m, gain_m):
        z_ = Sizes(
            mesh,
            inputs.shape[3],
            inputs.shape[1],
            inputs.shape[2],
            qkv_m.shape[3],
            gateup_m.shape[3],
        )
        D, R, C, F, Dr, M, MH, Hn, MB, T, NBH, N, NH = (
            z_.D,
            z_.R,
            z_.C,
            z_.F,
            z_.Dr,
            z_.M,
            z_.MH,
            z_.Hn,
            z_.MB,
            z_.T,
            z_.NBH,
            z_.N,
            z_.NH,
        )
        width = gain_m.shape[2]
        qkv_rows = jnp.transpose(qkv_m[0], (1, 0, 2))
        gateup_rows = jnp.transpose(gateup_m[0], (1, 2, 0)).reshape(2 * F, Dr)
        anywhere = pl.BlockSpec(memory_space=pl.ANY)
        vmem = pl.BlockSpec(memory_space=pltpu.VMEM)
        DMA = pltpu.SemaphoreType.DMA
        V = pltpu.VMEM
        scratch = [
            V((3, Dr, C), F32),
            V((C, Dr), F32),
            V((2 * F, Dr), F32),
            V((F, Dr), F32),
            V((2, D, N), BF),
            V((2, nd - 1, Dr, N), BF),
            V((2, Dr, N), BF),
            V((T, D), BF),
            V((2, T, D), BF),
            V((2, T, D), BF),
            V((2, T, D), BF),
            V((2, T, 3 * C), BF),
            V((2, T, C), BF),
            V((1, T, z_.GUw), BF),
            V((2, T, z_.Dw), BF),
            V((2, MH * R, D), F32),
            V((2, MH * R, D), BF),
            V((2, T, D), BF),
            V((T, z_.GUw), BF),
            V((T, 3 * C), BF),
            V((MH * R, D), F32),
            V((2, MH * R, D), BF),
            V((2, T, D), BF),
            V((2, MH, Hn * R, D), BF),
            V((2, MH, Hn - 1, R, D), BF),
            V((2, MH, Hn - 1, R, D), BF),
            V((2, NBH, NH * BLOCK, BLOCK), BF),
            V((T, C), F32),
            V((T, C), BF),
            V((2 * NBH, DH, C), F32),
            V((2, DH, C), BF),
            V((2, DH, C), BF),
            V((NBH, BLOCK, BLOCK), F32),
            V((NBH, BLOCK, 128), F32),
            V((NBH, BLOCK, 128), F32),
            V((NBH, 8, 128), F32),
            V((nd * nt, 2, 128), F32),
            V((2, 2, D), F32),
            V((2, D), F32),
            V((2, 2, D), F32),
            V((2, D), F32),
            V((nt - 1, 2, D), F32),
            V((nd - 1, 2, D), F32),
            DMA((2, MH)),
            DMA((2,)),
            DMA((2, MH, nt - 1)),
            DMA((2,)),
            DMA((2, 4)),
            DMA((2,)),
            DMA((2, 4, max(4, nd - 1))),
            DMA((6,)),
            DMA((6, MH, Hn)),
            DMA((2, MH)),
            DMA((2, MH)),
            DMA((2, MH, Hn - 1)),
            DMA((2, MH, Hn - 1)),
            DMA((2,)),
            DMA((2,)),
            DMA((2,)),
            DMA((2, 2)),
            DMA((2,)),
            DMA((2, 7, 3)),
            DMA((2,)),
            DMA((7, 2)),
            DMA((4,)),
            DMA((2, max(nd, nt) - 1)),
            DMA((2, max(nd, nt) - 1)),
            DMA((2,)),
            DMA((4,)),
        ]
        out_y, out_g, grad_qkv, grad_o, grad_gu, grad_d, grad_gain = pl.pallas_call(
            functools.partial(body, z_),
            out_shape=(
                jax.ShapeDtypeStruct((M, R, D), BF),
                jax.ShapeDtypeStruct((M, R, D), BF),
                jax.ShapeDtypeStruct((3, Dr, C), F32),
                jax.ShapeDtypeStruct((C, Dr), F32),
                jax.ShapeDtypeStruct((2 * F, Dr), F32),
                jax.ShapeDtypeStruct((F, Dr), F32),
                jax.ShapeDtypeStruct((2, width), F32),
            ),
            in_specs=[anywhere] * 6 + [vmem, vmem],
            out_specs=(anywhere,) * 6 + (vmem,),
            scratch_shapes=scratch,
            compiler_params=pltpu.CompilerParams(
                collective_id=0, has_side_effects=True, vmem_limit_bytes=63 * 1024 * 1024
            ),
        )(
            qkv_rows,
            out_m[0],
            gateup_rows,
            down_m[0],
            inputs[0],
            cotangent[0],
            jnp.transpose(starts, (1, 0, 2)),
            gain_m[0],
        )
        results = (out_y, out_g, grad_qkv, grad_o, grad_gu, grad_d, grad_gain)
        out_y, out_g, grad_qkv, grad_o, grad_gu, grad_d, grad_gain = pl.pallas_call(
            place_results,
            out_shape=tuple(jax.ShapeDtypeStruct(r.shape, r.dtype) for r in results),
            in_specs=[anywhere] * len(results),
            out_specs=(anywhere,) * len(results),
            scratch_shapes=[V(r.shape, r.dtype) for r in results]
            + [DMA((len(results),)), DMA((len(results),))],
        )(*results)
        return (
            out_y[None, None],
            out_g[None, None],
            jnp.transpose(grad_qkv, (1, 0, 2))[None],
            grad_o[None],
            jnp.transpose(grad_gu.reshape(2, F, Dr), (2, 0, 1))[None],
            grad_d[None],
            grad_gain[None],
        )

    return jax.shard_map(
        on_device,
        mesh=mesh,
        in_specs=(
            P("dp", None, "tensor", None),
            P("dp", None, None),
            P("dp", None, "tensor", None),
            P("section", "dp", None, "tensor"),
            P("section", "tensor", "dp"),
            P("section", "dp", None, "tensor"),
            P("section", "tensor", "dp"),
            P("section", None, ("dp", "tensor")),
        ),
        out_specs=(
            P("section", "dp", None, "tensor", None),
            P("section", "dp", None, "tensor", None),
            P("section", "dp", None, "tensor"),
            P("section", "tensor", "dp"),
            P("section", "dp", None, "tensor"),
            P("section", "tensor", "dp"),
            P("section", None, ("dp", "tensor")),
        ),
        check_vma=False,
    )
```

```python
import functools
import math

import jax
import jax.numpy as jnp
from jax import lax
from jax.experimental import pallas as pl
from jax.experimental.pallas import tpu as pltpu
from jax.sharding import PartitionSpec as P

DH = 64
BLOCK = 64
EPS = 1e-6
BF = jnp.bfloat16
F32 = jnp.float32
MESH = pl.DeviceIdType.MESH
NN = (((1,), (0,)), ((), ()))
NT = (((1,), (1,)), ((), ()))
TN = (((0,), (0,)), ((), ()))


def mm(a, b, dims=NN):
    return lax.dot_general(a, b, dims, preferred_element_type=F32)


def ceil_to(value, unit):
    return (value + unit - 1) // unit * unit


def scoped(fn):
    @functools.wraps(fn)
    def inner(*args):
        with jax.named_scope(fn.__name__):
            return fn(*args)

    return inner


class Sizes:
    def __init__(self, mesh, model, micro, rows, cols, hidden):
        self.nd, self.nt = mesh.shape["dp"], mesh.shape["tensor"]
        self.D, self.M, self.R, self.C, self.F = model, micro, rows, cols, hidden
        self.GUw, self.Dw = ceil_to(2 * hidden, 128), ceil_to(hidden, 128)
        self.Dr = model // self.nd
        self.MH, self.Hn = micro // 2, self.nt // 2
        self.MB = rows * self.nt
        self.T = self.MH * self.MB
        self.NH = cols // DH
        self.NB = self.MB // BLOCK
        self.NBH = self.MH * self.NB
        self.oO, self.oG = 3 * cols, 4 * cols
        self.oD = self.oG + self.GUw
        self.N = self.oD + self.Dw
        first = ceil_to(self.GUw // 2, 128)
        self.pieces = (
            (0, 3 * cols),
            (self.oO, cols),
            (self.oG, first),
            (self.oG + first, self.GUw - first),
            (self.oD, self.Dw),
            (0, 4 * cols),
            (0, cols),
            (cols, cols),
            (2 * cols, cols),
        )


def body(
    z_,
    qkv_in,
    o_in,
    gu_in,
    d_in,
    xin,
    cot,
    starts_in,
    gain_in,
    out_y,
    out_g,
    out_qkv,
    out_o,
    out_gu,
    out_d,
    out_gain,
    MQ,
    MO,
    MGU,
    MD,
    W,
    LW,
    L2,
    XF,
    GF,
    N1,
    N2,
    QKV,
    O,
    GU,
    HID,
    H,
    Y,
    GA,
    GGU,
    GQKV,
    GH,
    GX,
    PT,
    RL1,
    RL2,
    RSB,
    AP,
    UU,
    DU,
    ST,
    SIN,
    SEND_STATE,
    MSK,
    CAR,
    TAIL,
    KEEP,
    GL,
    GV,
    GOWN,
    DG,
    DL0,
    DL1,
    DL2,
    in_sem,
    x_sem,
    x_rs,
    w1_ss,
    w1_rs,
    w2_ss,
    w2_rs,
    ag_ss,
    ag_rs,
    r1_ss,
    r1_rs,
    r2_ss,
    r2_rs,
    st_ss,
    st_rs,
    o_ss,
    o_rs,
    d1_ss,
    d1_rs,
    d2_ss,
    d2_rs,
    g1_sem,
    g_ss,
    g_rs,
    gl_sem,
    m_sem,
):
    D, R, C, F, Dr, MH, Hn, MB, T, NH, NB, NBH = (
        z_.D,
        z_.R,
        z_.C,
        z_.F,
        z_.Dr,
        z_.MH,
        z_.Hn,
        z_.MB,
        z_.T,
        z_.NH,
        z_.NB,
        z_.NBH,
    )
    nd, nt = z_.nd, z_.nt
    pieces = z_.pieces
    s, d, z = lax.axis_index("section"), lax.axis_index("dp"), lax.axis_index("tensor")
    zh, zl = z // Hn, z % Hn
    own = s * Hn + zl
    core_dev = (1 - s, d, z)

    def remote(src, dst, ssem, rsem, dev):
        return pltpu.make_async_remote_copy(
            src_ref=src, dst_ref=dst, send_sem=ssem, recv_sem=rsem, device_id=dev, device_id_type=MESH
        )

    def got(dst, sem):
        pltpu.make_async_copy(dst, dst, sem).wait()

    def dp_dev(step):
        return (s, (d + step) % nd, z)

    def z_dev(step):
        return (s, d, (z + step) % nt)

    def peer_zl(step):
        return (zl + step) % Hn

    masters = (
        pltpu.make_async_copy(qkv_in, MQ, m_sem.at[0]),
        pltpu.make_async_copy(o_in, MO, m_sem.at[1]),
        pltpu.make_async_copy(gu_in, MGU, m_sem.at[2]),
        pltpu.make_async_copy(d_in, MD, m_sem.at[3]),
    )
    for copy in masters:
        copy.start()

    barrier = pltpu.get_barrier_semaphore()

    def section_dev(i):
        return (s, (d + i // nt) % nd, (z + i % nt) % nt)

    def greet(i, carry):
        pl.semaphore_signal(barrier, inc=1, device_id=section_dev(i), device_id_type=MESH)
        return carry

    lax.fori_loop(1, nd * nt, greet, 0)
    pl.semaphore_signal(barrier, inc=1, device_id=core_dev, device_id_type=MESH)
    far_dev = (1 - s, d, (z + Hn) % nt)
    pl.semaphore_signal(barrier, inc=1, device_id=far_dev, device_id_type=MESH)
    pl.semaphore_wait(barrier, nd * nt + 1)

    def own_tokens(src, dst, array):
        for m in range(MH):
            mine = dst.at[pl.ds(m * MB + z * R, R)]
            pltpu.make_async_copy(src.at[zh * MH + m], mine, in_sem.at[array, m]).start()

    def spread_tokens(src, dst, array):
        for m in range(MH):
            mine = dst.at[pl.ds(m * MB + z * R, R)]
            for step in range(1, nt):
                other = (z + step) % nt

                @pl.when((other // Hn == zh) | (step == Hn))
                def _():
                    remote(
                        src.at[(other // Hn) * MH + m],
                        mine,
                        x_sem.at[0],
                        x_rs.at[array, m, step - 1],
                        z_dev(step),
                    ).start()

    def relay_tokens(dst, array, m):
        @pl.when(s == array)
        def _():
            chip = (z + Hn) % nt
            rows = dst.at[pl.ds(m * MB + chip * R, R)]
            got(rows, x_rs.at[array, m, Hn - 1])
            for step in range(1, Hn):
                peer = zh * Hn + peer_zl(step)
                remote(
                    rows,
                    rows,
                    x_sem.at[0],
                    x_rs.at[array, m, (peer + nt - chip) % nt - 1],
                    (s, d, peer),
                ).start()

    def await_tokens(dst, array, m):
        got(dst.at[pl.ds(m * MB + z * R, R)], in_sem.at[array, m])
        for step in range(1, nt):
            rows = dst.at[pl.ds(m * MB + (z + nt - step) % nt * R, R)]
            if step == Hn:
                pl.when(s != array)(lambda: got(rows, x_rs.at[array, m, step - 1]))
            else:
                got(rows, x_rs.at[array, m, step - 1])

            @pl.when(s == array)
            def _():
                remote(
                    rows, rows, x_sem.at[1], x_rs.at[array, m, step - 1], core_dev
                ).start()

    spot = {5: 0, 2: 1, 3: 2, 4: 3}

    def w_rows(l, block, p):
        col, width = pieces[p]
        return W.at[l, pl.ds(block * Dr, Dr), pl.ds(col, width)]

    def shard_cols(p):
        col, width = pieces[p]
        return L2.at[0, :, pl.ds(col, width)]

    def w_hand_near(l, p):
        @pl.when(zh == s)
        def _():
            pltpu.make_async_copy(shard_cols(p), w_rows(l, d, p), w1_rs.at[l, spot[p]]).start()

        @pl.when(zh != s)
        def _():
            w_hand(l, p, 0, core_dev).start()

    def w_hand(l, p, which, dev):
        return remote(
            shard_cols(p), w_rows(l, d, p), w1_ss.at[which], w1_rs.at[l, spot[p]], dev
        )

    def w_hand_far(l, p):
        w_hand(l, p, 1, (zh, d, (z + Hn) % nt)).start()

    def w_handed_out():
        @pl.when(zh != s)
        def _():
            got(L2.at[0], w1_ss.at[0])

        got(L2.at[0], w1_ss.at[1])

    square = nd == 4
    half_rows = Dr // 2
    dp_x, dp_y = d + 1 - 2 * (d % 2), (d + 2) % nd

    def w_half(l, block, half, p):
        col, width = pieces[p]
        return W.at[l, pl.ds(block * Dr + half * half_rows, half_rows), pl.ds(col, width)]

    def w_copy(l, p, k):
        if not square:
            rows, dev = w_rows(l, d, p), dp_dev(k + 1)
        elif k < 2:
            rows, dev = w_rows(l, d, p), (s, (dp_x, dp_y)[k], z)
        elif k == 2:
            rows, dev = w_half(l, dp_x, 0, p), (s, dp_y, z)
        else:
            rows, dev = w_half(l, dp_y, 1, p), (s, dp_x, z)
        return remote(rows, rows, w2_ss.at[l], w2_rs.at[l, spot[p], k], dev)

    def w_share(l, p):
        got(w_rows(l, d, p), w1_rs.at[l, spot[p]])
        for k in range(2 if square else nd - 1):
            w_copy(l, p, k).start()

    def w_forward(l, p):
        if square:
            got(w_rows(l, dp_x, p), w2_rs.at[l, spot[p], 0])
            w_copy(l, p, 2).start()
            got(w_rows(l, dp_y, p), w2_rs.at[l, spot[p], 1])
            w_copy(l, p, 3).start()

    def w_ready(l, p):
        if square:
            got(w_half(l, 3 - d, 0, p), w2_rs.at[l, spot[p], 2])
            got(w_half(l, 3 - d, 1, p), w2_rs.at[l, spot[p], 3])
        else:
            for step in range(1, nd):
                got(w_rows(l, (d + nd - step) % nd, p), w2_rs.at[l, spot[p], step - 1])

    def w_shared(l):
        got(W.at[l, pl.ds(0, (nd - 1) * Dr)], w2_ss.at[l])

    def pump(ops):
        for what, l, p in ops:
            with jax.named_scope(what + str(l) + str(p)):
                {"s": w_share, "f": w_forward}[what](l, p)

    near = s == zh
    gathered = (5, 2, 3, 4)

    def pump_near(ops):
        pl.when(near)(lambda: pump(ops))

    def pump_far(ops):
        pl.when(jnp.logical_not(near))(lambda: pump(ops))

    where = {4: 0, 2: 1, 3: 2, 1: 3, 6: 4, 7: 5, 8: 6}

    def split(p):
        return (6, 7, 8) if p == 0 else (p,)

    def d_copy(l, p, k):
        col, width = pieces[p]
        cols = pl.ds(col, width)
        if not square:
            src, dst, dev = w_rows(l, (d + k + 1) % nd, p), LW.at[l, k, :, cols], dp_dev(k + 1)
        else:
            first, second = pl.ds(0, half_rows), pl.ds(half_rows, half_rows)
            block, half, slot, rows, to = (
                (3 - d, 0, 2, first, dp_x),
                (3 - d, 1, 2, second, dp_y),
                (dp_x, 0, 0, first, dp_x),
                (dp_y, 1, 1, second, dp_y),
                (dp_y, 0, 1, first, dp_y),
                (dp_x, 1, 0, second, dp_x),
            )[k]
            src, dst, dev = w_half(l, block, half, p), LW.at[l, slot, rows, cols], (s, to, z)
        group = k if square and k < 2 else 2
        return remote(src, dst, d1_ss.at[l], d1_rs.at[l, where[p], group], dev)

    def d_send(l, p):
        for part in split(p):
            for k in range(4 if square else nd - 1):
                d_copy(l, part, k).start()

    @scoped
    def d_mid(l, p):
        if p == 0:
            for part in split(p):
                d_mid(l, part)
        elif square:
            col, width = pieces[p]
            cols = pl.ds(col, width)
            for k, block, half in ((0, dp_y, 0), (1, dp_x, 1)):
                copy = d_copy(l, p, k)
                copy.wait_recv()
                rows = pl.ds(block * Dr + half * half_rows, half_rows)
                arrived = LW[l, 2, half * half_rows : (half + 1) * half_rows, cols]
                W[l, rows, cols] = (W[l, rows, cols].astype(F32) + arrived.astype(F32)).astype(BF)
                d_copy(l, p, 4 + k).start()

    part_rows = Dr // 4

    def d_pass(l, p, q, rows=part_rows):
        for part in split(p):
            col, width = pieces[part]
            cols = pl.ds(col, width)
            src = W.at[l, pl.ds(d * Dr + q * rows, rows), cols]
            dst = L2.at[zh, pl.ds(q * rows, rows), cols]
            arrival = d2_rs.at[where[part], zh]
            to_self = (s == l) & (zh == s)

            @pl.when(to_self)
            def _():
                pltpu.make_async_copy(src, dst, arrival).start()

            @pl.when(jnp.logical_not(to_self))
            def _():
                remote(src, dst, d2_ss.at[l], arrival, (l, d, s * Hn + zl)).start()

    @scoped
    def d_total_rows(l, p):
        for part in split(p):
            col, width = pieces[part]
            cols = pl.ds(col, width)
            slots = 2 if square else nd - 1
            got(LW.at[l, pl.ds(0, slots), :, cols], d1_rs.at[l, where[part], 2])
            rows = pl.ds(d * Dr, Dr)
            total = W[l, rows, cols].astype(F32)
            for slot in range(slots):
                total = total + LW[l, slot, :, cols].astype(F32)
            W[l, rows, cols] = total.astype(BF)

    def d_sum(l, p):
        d_total_rows(l, p)
        d_pass(l, p, 0, Dr)

    def d_sent(l):
        got(W.at[l, pl.ds(0, (nd - 1) * Dr)], d1_ss.at[l])

        @pl.when(jnp.logical_not((s == l) & (zh == s)))
        def _():
            got(W.at[l, pl.ds(0, Dr)], d2_ss.at[l])

    outs = (
        pltpu.make_async_copy(MQ, out_qkv, m_sem.at[0]),
        pltpu.make_async_copy(MO, out_o, m_sem.at[1]),
        pltpu.make_async_copy(MGU, out_gu, m_sem.at[2]),
        pltpu.make_async_copy(MD, out_d, m_sem.at[3]),
    )

    def d_arrived(p):
        col, width = pieces[p]
        for half in range(2):
            got(L2.at[half, :, pl.ds(col, width)], d2_rs.at[where[p], half])

    def d_total(col, width):
        return L2[0, :, col : col + width].astype(F32) + L2[1, :, col : col + width].astype(F32)

    @scoped
    def d_final(p):
        d_arrived(p)
        if p >= 6:
            j = p - 6
            MQ[j] = d_total(j * C, C)
            pltpu.make_async_copy(MQ.at[j], out_qkv.at[j], m_sem.at[0]).start()
        elif p == 1:
            MO[...] = d_total(z_.oO, C).T
            outs[1].start()
        elif p == 3:
            MGU[...] = d_total(z_.oG, z_.GUw).T[: 2 * F]
            outs[2].start()
        elif p == 4:
            MD[...] = d_total(z_.oD, z_.Dw).T[:F]
            outs[3].start()

    @scoped
    def shard_attention():
        masters[0].wait()
        masters[1].wait()
        for j in range(3):
            L2[0, :, j * C : (j + 1) * C] = MQ[j].astype(BF)
        L2[0, :, z_.oO : z_.oG] = MO[...].T.astype(BF)

    @scoped
    def shard_feed():
        masters[2].wait()
        masters[3].wait()
        for ref, col, width, rows in ((MGU, z_.oG, z_.GUw, 2 * F), (MD, z_.oD, z_.Dw, F)):
            value = ref[...]
            if width > rows:
                value = jnp.concatenate([value, jnp.zeros((width - rows, Dr), F32)], axis=0)
            L2[0, :, col : col + width] = value.T.astype(BF)

    def chunk_rows(m, c):
        return pl.ds(m * MB + c * R, R)

    def ag_send(k, buf, m):
        rows = buf.at[chunk_rows(m, own)]
        for step in range(1, Hn):
            dev = (s, d, zh * Hn + peer_zl(step))
            remote(rows, rows, ag_ss.at[k], ag_rs.at[k, m, Hn - step], dev).start()
        remote(rows, rows, ag_ss.at[k], ag_rs.at[k, m, 0], core_dev).start()

    def ag_forward(k, buf, m):
        for step in range(1, Hn):
            rows = buf.at[chunk_rows(m, s * Hn + peer_zl(step))]
            got(rows, ag_rs.at[k, m, step])
            remote(rows, rows, ag_ss.at[k], ag_rs.at[k, m, 0], core_dev).start()

    def ag_wait(k, buf, m):
        got(buf.at[pl.ds(m * MB + (1 - s) * Hn * R, Hn * R)], ag_rs.at[k, m, 0])

    def ag_sent(k, buf):
        got(buf.at[pl.ds(0, MH * (2 * Hn - 1) * R)], ag_ss.at[k])

    def rs_copy1(k, m):
        par = k % 2
        return remote(
            PT.at[par, pl.ds(m * MB + (1 - s) * Hn * R, Hn * R)],
            RL1.at[par, m],
            r1_ss.at[par, m],
            r1_rs.at[par, m],
            core_dev,
        )

    def rs_copy2(k, m, step):
        par = k % 2
        return remote(
            RSB.at[par, m, step - 1],
            RL2.at[par, m, step - 1],
            r2_ss.at[par, m, step - 1],
            r2_rs.at[par, m, step - 1],
            (s, d, zh * Hn + peer_zl(step)),
        )

    def rs_first(k, m, value):
        PT[k % 2, pl.ds(m * MB, MB), :] = value.astype(BF)
        rs_copy1(k, m).start()

    def rs_second(k, m):
        par = k % 2
        copy = rs_copy1(k, m)
        copy.wait_send()
        copy.wait_recv()
        for step in range(1, Hn):
            there = peer_zl(step)
            part = PT[par, chunk_rows(m, s * Hn + there), :].astype(F32) + RL1[
                par, m, pl.ds(there * R, R), :
            ].astype(F32)
            RSB[par, m, step - 1] = part.astype(BF)
            rs_copy2(k, m, step).start()

    def after(k, i, m):
        @pl.when(i > 0)
        def _():
            rs_second(k, m)

    def rs_third(k, m):
        par = k % 2
        total = PT[par, chunk_rows(m, own), :].astype(F32) + RL1[
            par, m, pl.ds(zl * R, R), :
        ].astype(F32)
        for step in range(1, Hn):
            copy = rs_copy2(k, m, step)
            copy.wait_send()
            copy.wait_recv()
            total = total + RL2[par, m, step - 1].astype(F32)
        return total

    def own_rows(m):
        return pl.ds(m * R, R)

    def rms(rows):
        return lax.rsqrt(jnp.mean(rows * rows, axis=-1, keepdims=True) + EPS)

    def gain(l, which):
        return GV[l, which : which + 1, :]

    def rms_back(l, which, rows, grad):
        inverse = rms(rows)
        scaled = grad * gain(l, which)
        back = inverse * scaled - rows * (inverse * inverse * inverse) * jnp.mean(
            scaled * rows, axis=-1, keepdims=True
        )
        DG[l, which : which + 1, :] += jnp.sum(grad * rows * inverse, axis=0, keepdims=True)
        return back

    def send_out(buf, l, out, which, m):
        src = buf.at[l, own_rows(m)]
        dst = out.at[zh * MH + m]
        to_self = (s == l) & (zh == s)

        @pl.when(to_self)
        def _():
            pltpu.make_async_copy(src, dst, o_rs.at[which, zh]).start()

        @pl.when(jnp.logical_not(to_self))
        def _():
            remote(
                src, dst, o_ss.at[l], o_rs.at[which, zh], (l, d, s * Hn + zl)
            ).start()

    lane_head = lax.broadcasted_iota(jnp.int32, (1, C), 1) // DH
    head_bf = [(lane_head == h).astype(F32).astype(BF) for h in range(NH)]
    head_f = [(lane_head == h).astype(F32) for h in range(NH)]

    def stack(rows):
        return jnp.concatenate([rows * head_bf[h] for h in range(NH)], axis=0)

    def unstack(wide):
        out = wide[0:DH] * head_f[0]
        for h in range(1, NH):
            out = out + wide[h * DH : (h + 1) * DH] * head_f[h]
        return out

    def tall(mask):
        return jnp.concatenate([mask] * NH, axis=0)

    def head_mean(values):
        row = lax.broadcasted_iota(jnp.int32, (C, C), 0) // DH
        col = lax.broadcasted_iota(jnp.int32, (C, C), 1) // DH
        same = jnp.where(row == col, 1.0 / DH, 0.0).astype(BF)
        high = values.astype(BF)
        low = (values - high.astype(F32)).astype(BF)
        return mm(high, same) + mm(low, same)

    def block_rows(b):
        return pl.ds(pl.multiple_of(b * BLOCK, BLOCK), BLOCK)

    def qkv_block(l, b):
        rows = block_rows(b)
        return (QKV[l, rows, 0:C], QKV[l, rows, C : 2 * C], QKV[l, rows, 2 * C : 3 * C])

    def softplus(values):
        return jnp.maximum(values, 0.0) + jnp.log(1.0 + jnp.exp(-jnp.abs(values)))

    def features(values):
        return softplus(values.astype(F32)).astype(BF)

    def diag_forward(b):
        q, k, v = qkv_block(0, b)
        scores = mm(stack(q), k, NT) * (1.0 / math.sqrt(DH))
        scores = jnp.where(tall(MSK[b]) > 0.5, scores, -1e9)
        top = jnp.max(scores, axis=-1, keepdims=True)
        weights = jnp.exp(scores - top)
        weights = (weights / jnp.sum(weights, axis=-1, keepdims=True)).astype(BF)
        AP[0, b] = weights
        O[0, block_rows(b), :] = unstack(mm(weights, v)).astype(BF)

    def diag_backward(b, grad_o):
        q, k, v = qkv_block(0, b)
        low = stack(grad_o.astype(BF))
        weights = AP[0, b]
        wide = weights.astype(F32)
        grad_v = mm(weights, low, TN)
        grad_w = mm(low, v, NT)
        grad_s = wide * (grad_w - jnp.sum(grad_w * wide, axis=-1, keepdims=True))
        grad_s = (grad_s * (1.0 / math.sqrt(DH))).astype(BF)
        grad_q = unstack(mm(grad_s, k))
        grad_k = mm(grad_s, stack(q), TN)
        rows = block_rows(b)
        GQKV[rows, 0:C] = grad_q.astype(BF)
        GQKV[rows, C : 2 * C] = grad_k.astype(BF)
        GQKV[rows, 2 * C : 3 * C] = grad_v.astype(BF)

    def fold(square):
        out = square[0:DH] * head_f[0]
        for h in range(1, NH):
            out = out + square[h * DH : (h + 1) * DH] * head_f[h]
        return out

    def unfold(flat):
        return stack(flat.astype(BF))

    def wide_lanes(column):
        return jnp.concatenate([column] * (C // 128), axis=1)

    def norm_state(b, state):
        q, k, v = qkv_block(1, b)
        ST[b] = state
        key = features(k)
        term = mm(key, (v.astype(F32) * wide_lanes(TAIL[b])).astype(BF), TN)
        return wide_lanes(KEEP[b, 0:1, :]) * state + fold(term)

    def norm_forward(b, passed):
        q, k, v = qkv_block(1, b)
        query, key = features(q), features(k)
        local = jnp.where(tall(MSK[b]) > 0.5, mm(stack(query), key, NT), 0.0).astype(BF)
        AP[1, b] = local
        state = ST[b] + passed * SIN[0].astype(F32)
        ST[b] = state
        mixed = unstack(mm(local, v)) + wide_lanes(CAR[b]) * mm(query, unfold(state))
        rows = block_rows(b)
        UU[rows, :] = mixed
        O[1, rows, :] = (mixed * lax.rsqrt(head_mean(mixed * mixed) + EPS)).astype(BF)
        return passed * wide_lanes(KEEP[b, 0:1, :])

    def norm_back_first(b, grad_o, state):
        rows = block_rows(b)
        mixed = UU[rows, :]
        scale = lax.rsqrt(head_mean(mixed * mixed) + EPS)
        grad = scale * grad_o - mixed * (scale * scale * scale) * head_mean(grad_o * mixed)
        low = grad.astype(BF)
        DU[rows, :] = low
        ST2_store(b, state)
        query = features(QKV[1, rows, 0:C])
        term = mm(query, (low.astype(F32) * wide_lanes(CAR[b])).astype(BF), TN)
        return wide_lanes(KEEP[b, 0:1, :]) * state + fold(term)

    def ST2_store(b, state):
        ST[NBH + b] = state

    def sigmoid(values):
        return 1.0 / (1.0 + jnp.exp(-values.astype(F32)))

    def norm_back_local(b):
        rows = block_rows(b)
        q, k, v = qkv_block(1, b)
        query, key = features(q), features(k)
        low = DU[rows, :]
        stacked = stack(low)
        grad_a = jnp.where(tall(MSK[b]) > 0.5, mm(stacked, v, NT), 0.0).astype(BF)
        grad_q = unstack(mm(grad_a, key)) + wide_lanes(CAR[b]) * mm(low, unfold(ST[b]), NT)
        GQKV[rows, 0:C] = (grad_q * sigmoid(q)).astype(BF)
        GQKV[rows, C : 2 * C] = (mm(grad_a, stack(query), TN) * sigmoid(k)).astype(BF)
        GQKV[rows, 2 * C : 3 * C] = mm(AP[1, b], stacked, TN).astype(BF)

    def norm_back_state(b, passed):
        rows = block_rows(b)
        q, k, v = qkv_block(1, b)
        grad_wide = unfold(ST[NBH + b] + passed * SIN[1].astype(F32))
        tail = wide_lanes(TAIL[b])
        grad_k = tail * mm(v, grad_wide, NT) * sigmoid(k)
        grad_v = tail * mm(features(k), grad_wide)
        GQKV[rows, C : 2 * C] = (GQKV[rows, C : 2 * C].astype(F32) + grad_k).astype(BF)
        GQKV[rows, 2 * C : 3 * C] = (GQKV[rows, 2 * C : 3 * C].astype(F32) + grad_v).astype(BF)
        return passed * wide_lanes(KEEP[b, 0:1, :])

    @scoped
    def masks():
        row = lax.broadcasted_iota(jnp.int32, (BLOCK, BLOCK), 0)
        col = lax.broadcasted_iota(jnp.int32, (BLOCK, BLOCK), 1)
        token = lax.broadcasted_iota(jnp.int32, (MB, BLOCK), 0)
        lane = lax.broadcasted_iota(jnp.int32, (MB, BLOCK), 1)
        start = jnp.concatenate([starts_in[zh * MH + m] for m in range(MH)], axis=0)
        start = start.astype(F32).astype(BF)
        chunk_lane = lax.broadcasted_iota(jnp.int32, (BLOCK, MH), 1)
        for j in range(NB):
            upper = ((token // BLOCK == j) & (token % BLOCK <= lane)).astype(F32).astype(BF)
            count_row = mm(start, upper)
            count_col = mm(upper, start, (((0,), (1,)), ((), ())))
            for m in range(MH):
                b = m * NB + j
                c_row = count_row[m : m + 1, :]
                c_col = jnp.sum(
                    jnp.where(chunk_lane == m, count_col, 0.0), axis=1, keepdims=True
                )
                last = jnp.sum(
                    jnp.where(col[0:1] == BLOCK - 1, c_row, 0.0), axis=1, keepdims=True
                )
                MSK[b] = jnp.where((c_row == c_col) & (row >= col), 1.0, 0.0)
                CAR[b] = jnp.broadcast_to(jnp.where(c_col == 0.0, 1.0, 0.0), (BLOCK, 128))
                TAIL[b] = jnp.broadcast_to(jnp.where(c_col == last, 1.0, 0.0), (BLOCK, 128))
                KEEP[b] = jnp.broadcast_to(jnp.where(last == 0.0, 1.0, 0.0), (8, 128))

    place = d * nt + z

    def gain_copy(i):
        return remote(GL.at[place], GL.at[place], gl_sem.at[0], gl_sem.at[1], section_dev(i))

    @scoped
    def gains_out():
        width = gain_in.shape[1]
        row = lax.broadcasted_iota(jnp.int32, (width, 128), 0)
        col = lax.broadcasted_iota(jnp.int32, (width, 128), 1)
        spot = (col % width == row) & (col // width == place % (128 // width))
        GL[place] = mm(gain_in[...].astype(BF), spot.astype(F32).astype(BF))

        def one(i, carry):
            gain_copy(i).start()
            return carry

        lax.fori_loop(1, nd * nt, one, 0)

    @scoped
    def gains_in():
        for k in (1, 0):
            got(GL.at[pl.ds(0, nd * nt - 1)], gl_sem.at[k])
        each = nd * nt * 128 // D
        for t in range(D // 128):
            total = GL[t * each]
            for i in range(1, each):
                total = total + GL[t * each + i]
            GV[s, :, t * 128 : (t + 1) * 128] = total
        gain_swap().start()

    def gain_swap():
        return remote(GV.at[s], GV.at[s], g1_sem.at[0], g1_sem.at[1], core_dev)

    def gains_other():
        gain_swap().wait_send()
        got(GV.at[1 - s], g1_sem.at[1])

    def dp_gain(step):
        return remote(
            GOWN, DL2.at[step - 1], g_ss.at[1, step - 1], g_rs.at[1, step - 1], dp_dev(step)
        )

    def core_gain():
        return remote(DG.at[1 - s], DL0, g1_sem.at[2], g1_sem.at[3], core_dev)

    def z_gain(step):
        return remote(
            DG.at[s], DL1.at[step - 1], g_ss.at[0, step - 1], g_rs.at[0, step - 1], z_dev(step)
        )

    @scoped
    def gain_second():
        core_gain().wait()
        DG[s] = DG[s] + DL0[...]
        for step in range(1, nt):
            z_gain(step).start()

    @scoped
    def gain_third():
        total = DG[s]
        for step in range(1, nt):
            z_gain(step).wait()
            total = total + DL1[step - 1]
        GOWN[...] = total
        for step in range(1, nd):
            dp_gain(step).start()

    @scoped
    def gain_final():
        total = GOWN[...]
        for step in range(1, nd):
            dp_gain(step).wait()
            total = total + DL2[step - 1]
        GOWN[...] = total
        width = out_gain.shape[1]
        each = 128 // width
        tile = GOWN[:, pl.ds(pl.multiple_of(place // each * 128, 128), 128)]
        mine = jnp.zeros((2, width), F32)
        for i in range(each):
            piece = tile[:, i * width : (i + 1) * width]
            mine = jnp.where(place % each == i, piece, mine)
        out_gain[...] = mine

    def loop(count, fn):
        def step(i, carry):
            fn(i)
            return carry

        with jax.named_scope(fn.__name__):
            lax.fori_loop(0, count, step, 0)

    def chunk(m):
        return pl.ds(pl.multiple_of(m * MB, BLOCK), MB)

    def w_cols(l, p):
        col, width = pieces[p]
        return W[l, :, col : col + width]

    def w_gate_up(l):
        return W[l, :, z_.oG : z_.oD]

    @scoped
    def state_copy(slot):
        return remote(
            SEND_STATE.at[slot],
            SIN.at[slot],
            st_ss.at[slot],
            st_rs.at[slot],
            (s, d, (z + Hn) % nt),
        )

    def state_out(slot, value, sender):
        SEND_STATE[slot] = value.astype(BF)

        @pl.when(zh == sender)
        def _():
            SIN[slot] = jnp.zeros((DH, C), BF)
            state_copy(slot).start()

    @scoped
    def state_in(slot, sender):
        @pl.when(zh != sender)
        def _():
            state_copy(slot).wait_recv()

    outer = zh == zl
    inner, far = jnp.logical_not(outer), jnp.logical_not(near)

    def only(cond, fn):
        pl.when(cond)(fn)

    def hand_far(l, cond, ps):
        def go():
            for p in ps:
                w_hand_far(l, p)

        pl.when((s == l) & cond)(go)

    def hand_near(ps):
        for l in range(2):

            @pl.when(s == l)
            def _():
                for p in ps:
                    w_hand_near(l, p)

    def x_out():
        spread_tokens(xin, XF, 0)

    gains_out()
    shard_attention()
    hand_far(0, s == 0, [5])
    hand_near([5])
    only((s == 0) & inner, x_out)
    pump_near([("s", 0, 5)])
    own_tokens(xin, XF, 0)
    own_tokens(cot, GF.at[1], 1)
    shard_feed()
    hand_near([2, 3, 4])
    masks()
    for l in range(2):
        DG[l] = jnp.zeros((2, D), F32)
    pump_near([("s", 0, 2)])
    gains_in()
    pump_far([("s", 0, 5)])
    only((s == 0) & outer & far, x_out)
    pump([("f", 0, 5)])
    pump_near([("f", 0, 2)])
    only((s == 0) & outer & near, x_out)
    only(s == 1, gains_other)
    for m in range(MH):
        relay_tokens(XF, 0, m)
    hand_far(0, s == 0, [2, 3, 4])
    await_tokens(XF, 0, 0)

    def cot_out():
        spread_tokens(cot, GF.at[1], 1)

    stage = {
        (0, "attended"): lambda: (
            pump_near([("f", 0, 3), ("f", 0, 4)]),
            pump_far([("s", 0, 2), ("s", 0, 3), ("f", 0, 2), ("s", 0, 4)]),
        ),
        (0, "hidden"): lambda: (
            hand_far(1, inner, [5, 4, 2, 3]),
            hand_far(1, outer, [5]),
            pump_near([("s", 1, 5)]),
            pump_far([("f", 0, 3), ("f", 0, 4)]),
        ),
        (0, "ready"): lambda: (
            hand_far(1, outer & far, [4]),
            pump_near([("f", 1, 5)]),
            hand_far(1, outer & near, [4]),
            pump_far([("s", 1, 5)]),
            hand_far(1, outer & far, [2, 3]),
        ),
        (0, "feeding"): lambda: (
            hand_far(1, outer & near, [2, 3]),
            pump_near([("s", 1, 4)]),
        ),
        (0, "fed"): lambda: (
            pump_near([("f", 1, 4), ("s", 1, 2)]),
            pump_far([("f", 1, 5), ("s", 1, 4)]),
            only(s == 0, gains_other),
        ),
        (0, "result"): lambda: (
            only(s == 1, cot_out),
            pump_near([("s", 1, 3)]),
            pump_far([("s", 1, 2), ("f", 1, 4)]),
        ),
        (1, "states"): lambda: (
            [relay_tokens(GF.at[1], 1, m) for m in reversed(range(MH))],
            pump_near([("f", 1, 2), ("f", 1, 3)]),
            pump_far([("s", 1, 3), ("f", 1, 2)]),
        ),
        (1, "attended"): lambda: (pump_far([("f", 1, 3)]),),
        (1, "hidden"): lambda: (results_out(Y, 0, out_y, 0),),
        (1, "ready"): lambda: (),
        (1, "fed"): lambda: (),
        "b1 second": lambda: (),
        "b1 middle": lambda: (results_out(Y, 1, out_y, 0), d_mid(1, 4)),
        "b1 feed": lambda: (),
        "b1 third": lambda: (d_mid(1, 3),),
        "b1 end": lambda: (d_total_rows(1, 3),),
        "b0 second": lambda: (d_total_rows(1, 0),),
        "b0 middle": lambda: (),
        "b0 feed": lambda: (results_out(GX, 1, out_g, 1), d_total_rows(1, 1)),
        "b0 third": lambda: (
            only(far, lambda: run(d_mid, 2)),
            only(near, lambda: run(d_mid, 4) or run(d_send, 2, 3)),
        ),
        "b0 end": lambda: (
            core_gain().start(),
            only(near, lambda: run(d_send, 0, 1)),
            only(far, lambda: far_tail()),
            only(near, lambda: near_tail()),
            gain_third(),
        ),
    }

    def run(step, *parts):
        for p in parts:
            step(0, p)

    def far_tail():
        gain_second()
        run(d_mid, 6)
        run(d_sum, 3)
        run(d_mid, 7, 8)
        run(d_sum, 6)
        run(d_mid, 1)
        run(d_sum, 7, 8, 1)
        results_out(GX, 0, out_g, 1)

    def near_tail():
        run(d_sum, 4)
        run(d_mid, 2, 3)
        gain_second()
        run(d_mid, 6, 7, 8, 1)
        results_out(GX, 0, out_g, 1)
        run(d_sum, 2, 3, 6, 7, 8, 1)

    def results_out(buf, l, out, which):
        for m in range(MH):
            send_out(buf, l, out, which, m)

    def input_rows(l, m):
        if l == 0:
            return XF[chunk_rows(m, own), :].astype(F32)
        return Y[0, own_rows(m), :].astype(F32)

    def gate_up_grad(grad, both):
        parts = [grad * both[:, F : 2 * F], grad * both[:, :F]]
        if z_.GUw > 2 * F:
            parts.append(jnp.zeros((MB, z_.GUw - 2 * F), F32))
        return jnp.concatenate(parts, axis=1).astype(BF)

    def finish_layer(l, rs2, ag3):
        def result(m):
            rows = (H[l, own_rows(m), :] + rs_third(rs2, m)).astype(BF)
            Y[l, own_rows(m), :] = rows
            if l == 0:
                wide = rows.astype(F32)
                N1[1, chunk_rows(m, own), :] = (wide * rms(wide) * gain(1, 0)).astype(BF)
                ag_send(ag3, N1.at[1], m)

        loop(MH, result)

    def forward(l, ag1, rs1, ag2, rs2, ag3):
        w_ready(l, 5)

        def qkv_chunk(m):
            if l == 0:
                pl.when(m > 0)(lambda: await_tokens(XF, 0, m))
                pl.when((m == 1) & near)(lambda: pump([("s", 0, 3), ("s", 0, 4)]))
                rows = XF[chunk(m), :].astype(F32)
                N1[0, chunk(m), :] = (rows * rms(rows) * gain(0, 0)).astype(BF)
            else:
                ag_forward(ag1, N1.at[1], m)
                ag_wait(ag1, N1.at[1], m)
            QKV[l, chunk(m), :] = mm(N1[l, chunk(m), :], w_cols(l, 0)).astype(BF)

        def out_chunk(m):
            rs_first(rs1, m, mm(O[l, chunk(m), :], w_cols(l, 1), NT))

        if l == 0:

            def attend(m):
                qkv_chunk(m)
                for i in range(NB):
                    diag_forward(m * NB + i)
                out_chunk(m)
                after(rs1, m, m - 1)

            loop(MH, attend)
            rs_second(rs1, MH - 1)
            stage[l, "attended"]()
        else:

            def states(m, state):
                qkv_chunk(m)
                for i in range(NB):
                    state = norm_state(m * NB + i, state)
                return state

            with jax.named_scope('states'):
                last = lax.fori_loop(0, MH, states, jnp.zeros((DH, C), F32))
            w_handed_out()
            state_out(0, last, 0)
            state_in(0, 0)
            stage[l, "states"]()

            def attend(m, passed):
                for i in range(NB):
                    passed = norm_forward(m * NB + i, passed)
                out_chunk(m)
                after(rs1, m, m - 1)
                return passed

            with jax.named_scope('attend'):
                lax.fori_loop(0, MH, attend, jnp.ones((1, C), F32))
            rs_second(rs1, MH - 1)
            stage[l, "attended"]()

        def hidden_rows(m):
            rows = input_rows(l, m) + rs_third(rs1, m)
            H[l, own_rows(m), :] = rows
            N2[l, chunk_rows(m, own), :] = (rows * rms(rows) * gain(l, 1)).astype(BF)
            ag_send(ag2, N2.at[l], m)

        loop(MH, hidden_rows)
        stage[l, "hidden"]()
        w_ready(l, 4)
        if l == 1:

            def hidden_grad(m):
                await_tokens(GF.at[1], 1, m)
                GGU[chunk(m), 0 : z_.Dw] = mm(GF[1, chunk(m), :], w_cols(1, 4)).astype(BF)

            loop(MH, hidden_grad)
        w_ready(l, 2)
        w_ready(l, 3)
        stage[l, "ready"]()

        def feed(m):
            ag_forward(ag2, N2.at[l], m)
            ag_wait(ag2, N2.at[l], m)
            rows = N2[l, chunk(m), :]
            both = mm(rows, w_gate_up(l))
            if l == 0:
                GU[l, chunk(m), :] = both.astype(BF)
            else:
                grad = GGU[chunk(m), 0 : z_.Dw].astype(F32)[:, :F]
                GGU[chunk(m), :] = gate_up_grad(grad, both)
            hidden = both[:, :F] * both[:, F : 2 * F]
            if z_.Dw > F:
                hidden = jnp.concatenate([hidden, jnp.zeros((MB, z_.Dw - F), F32)], axis=1)
            hidden = hidden.astype(BF)
            HID[l, chunk(m), :] = hidden
            rs_first(rs2, m, mm(hidden, w_cols(l, 4), NT))
            if l == 0:


                @pl.when(m == 1)
                def _():
                    stage[0, "feeding"]()

            after(rs2, m, m - 1)

        loop(MH, feed)
        rs_second(rs2, MH - 1)
        stage[l, "fed"]()

        if l == 0:
            finish_layer(l, rs2, ag3)
            stage[l, "result"]()

    forward(0, None, 0, 0, 1, 1)
    forward(1, 1, 2, 2, 3, None)

    RB = min(D, 256)

    @scoped
    def grad_weight(l, p, left, right, send=True):
        col, width = pieces[p]
        for r in range(D // RB):
            W[l, r * RB : (r + 1) * RB, col : col + width] = mm(
                left[:, r * RB : (r + 1) * RB], right, TN
            ).astype(BF)
        if send:
            d_send(l, p)

    def rest(l, p):
        for q in range(MH, 4):
            d_pass(l, p, q)

    def grad_part(l, p, send=True):
        col, width = pieces[p]
        grad_weight(l, p, N2[l], GGU[:, col - z_.oG : col - z_.oG + width], send)

    def backward(l, ag_in, rs1, ag2, rs2, ag_out):
        w_shared(l)

        def feed_back(i):
            m = MH - 1 - i
            if l == 0:
                ag_forward(ag_in, GF.at[0], m)
                ag_wait(ag_in, GF.at[0], m)
                grad = mm(GF[l, chunk(m), :], w_cols(l, 4))[:, :F]
                GGU[chunk(m), :] = gate_up_grad(grad, GU[l, chunk(m), :].astype(F32))
            rs_first(rs1, m, mm(GGU[chunk(m), :], w_gate_up(l), NT))
            after(rs1, i, m + 1)
            if l == 0:

                @pl.when(i == 0)
                def _():
                    d_mid(1, 1)
                    d_mid(1, 0)

                d_pass(1, 3, i)
        if l == 1:
            grad_weight(l, 4, GF[l], HID[l])
        loop(MH, feed_back)
        rs_second(rs1, 0)
        if l == 0:
            rest(1, 3)
            grad_weight(l, 4, GF[l], HID[l], False)
            only(far, lambda: d_send(0, 4))
        else:
            grad_part(l, 2)
            finish_layer(1, 3, None)
        stage[f"b{l} second"]()

        def middle(i):
            m = MH - 1 - i
            rows = H[l, own_rows(m), :]
            grad = GF[l, chunk_rows(m, own), :].astype(F32) + rms_back(
                l, 1, rows, rs_third(rs1, m)
            )
            GH[own_rows(m), :] = grad
            GA[l, chunk_rows(m, own), :] = grad.astype(BF)
            ag_send(ag2, GA.at[l], m)
            if l == 0:
                only((i == 1) & near, lambda: d_send(0, 4))
                d_pass(1, 0, i)

        loop(MH, middle)
        if l == 0:
            rest(1, 0)
        stage[f"b{l} middle"]()
        if l == 0:
            grad_part(l, 2, False)

            @pl.when(far)
            def _():
                d_mid(0, 4)
                d_send(0, 2)

            grad_part(l, 3, False)
            only(far, lambda: d_send(0, 3))
        else:
            grad_part(l, 3)
        stage[f"b{l} feed"]()

        def grad_o(m):
            ag_forward(ag2, GA.at[l], m)
            ag_wait(ag2, GA.at[l], m)
            return mm(GA[l, chunk(m), :], w_cols(l, 1))

        def qkv_back(i, m):
            rs_first(rs2, m, mm(GQKV[chunk(m), :], w_cols(l, 0), NT))
            after(rs2, i, m + 1)

        if l == 0:

            def attend(i):
                m = MH - 1 - i
                grad = grad_o(m)
                for j in range(NB):
                    diag_backward(m * NB + j, grad[j * BLOCK : (j + 1) * BLOCK])
                qkv_back(i, m)
                d_pass(1, 1, i)
                only((i == 0) & far, lambda: d_sum(0, 4))

            loop(MH, attend)
        else:

            def states(i, state):
                m = MH - 1 - i
                grad = grad_o(m)
                for j in reversed(range(NB)):
                    state = norm_back_first(m * NB + j, grad[j * BLOCK : (j + 1) * BLOCK], state)
                return state

            with jax.named_scope("states"):
                last = lax.fori_loop(0, MH, states, jnp.zeros((DH, C), F32))
            state_out(1, last, 1)
            d_mid(1, 2)
            grad_weight(l, 1, GA[l], O[l])

            def attend_local(m):
                for j in range(NB):
                    norm_back_local(m * NB + j)

            loop(MH, attend_local)
            d_total_rows(1, 4)
            state_in(1, 1)
            pl.when(zh == 0)(lambda: d_pass(1, 4, 0, Dr))

            def attend(i, passed):
                m = MH - 1 - i
                for j in reversed(range(NB)):
                    passed = norm_back_state(m * NB + j, passed)
                qkv_back(i, m)

                @pl.when(zh == 1)
                def _():
                    d_pass(1, 4, i)

                return passed

            with jax.named_scope("attend"):
                lax.fori_loop(0, MH, attend, jnp.ones((1, C), F32))

        rs_second(rs2, 0)
        if l == 0:
            rest(1, 1)
        else:
            pl.when(zh == 1)(lambda: rest(1, 4))
        stage[f"b{l} third"]()
        grad_weight(l, 0, N1[l], GQKV[...], l == 1)
        if l == 0:
            grad_weight(l, 1, GA[l], O[l], False)

            @pl.when(far)
            def _():
                d_mid(0, 3)
                d_send(0, 0)
                d_send(0, 1)
                d_sum(0, 2)


        def result(i):
            m = MH - 1 - i
            grad = GH[own_rows(m), :] + rms_back(l, 0, input_rows(l, m), rs_third(rs2, m))
            low = grad.astype(BF)
            GX[l, own_rows(m), :] = low
            if l == 1:
                GF[0, chunk_rows(m, own), :] = low
                ag_send(ag_out, GF.at[0], m)
                pl.when(i == 0)(lambda: d_total_rows(1, 2))
                d_pass(1, 2, i)

        loop(MH, result)
        if l == 1:
            rest(1, 2)
        stage[f"b{l} end"]()

    backward(1, None, 4, 3, 5, 4)
    backward(0, 4, 6, 5, 7, None)

    for p in (4, 2, 3, 6, 7, 8, 1):
        d_final(p)
    gain_final()
    for copy in outs:
        copy.wait()
    for l in range(2):
        d_sent(l)

    ags = ((0, N2.at[0]), (1, N1.at[1]), (2, N2.at[1]), (3, GA.at[1]), (4, GF.at[0]), (5, GA.at[0]))

    for slot in range(2):

        @pl.when(zh == slot)
        def _():
            state_copy(slot).wait_send()

    for k, buf in ags:
        ag_sent(k, buf)
    for l in range(2):

        @pl.when(jnp.logical_not((s == l) & (zh == s)))
        def _():
            got(XF.at[pl.ds(0, 2 * MH * R)], o_ss.at[l])

    for half in range(2):
        got(out_y.at[pl.ds(half * MH, MH)], o_rs.at[0, half])
        got(out_g.at[pl.ds(half * MH, MH)], o_rs.at[1, half])
    for k in range(2):
        got(XF.at[pl.ds(0, MH * (nt - 1) * R)], x_sem.at[k])


def place_results(*refs):
    count = (len(refs) - 2) // 3
    sources, targets, held = refs[:count], refs[count : 2 * count], refs[2 * count : 3 * count]
    in_sem, out_sem = refs[-2:]
    reads = [pltpu.make_async_copy(sources[i], held[i], in_sem.at[i]) for i in range(count)]
    writes = [pltpu.make_async_copy(held[i], targets[i], out_sem.at[i]) for i in range(count)]
    for copy in reads:
        copy.start()
    for read, write in zip(reads, writes):
        read.wait()
        write.start()
    for copy in writes:
        copy.wait()


def solution(mesh):
    nd, nt = mesh.shape["dp"], mesh.shape["tensor"]

    def on_device(inputs, starts, cotangent, qkv_m, out_m, gateup_m, down_m, gain_m):
        z_ = Sizes(
            mesh,
            inputs.shape[3],
            inputs.shape[1],
            inputs.shape[2],
            qkv_m.shape[3],
            gateup_m.shape[3],
        )
        D, R, C, F, Dr, M, MH, Hn, MB, T, NBH, N, NH = (
            z_.D,
            z_.R,
            z_.C,
            z_.F,
            z_.Dr,
            z_.M,
            z_.MH,
            z_.Hn,
            z_.MB,
            z_.T,
            z_.NBH,
            z_.N,
            z_.NH,
        )
        width = gain_m.shape[2]
        qkv_rows = jnp.transpose(qkv_m[0], (1, 0, 2))
        gateup_rows = jnp.transpose(gateup_m[0], (1, 2, 0)).reshape(2 * F, Dr)
        anywhere = pl.BlockSpec(memory_space=pl.ANY)
        vmem = pl.BlockSpec(memory_space=pltpu.VMEM)
        DMA = pltpu.SemaphoreType.DMA
        V = pltpu.VMEM
        scratch = [
            V((3, Dr, C), F32),
            V((C, Dr), F32),
            V((2 * F, Dr), F32),
            V((F, Dr), F32),
            V((2, D, N), BF),
            V((2, nd - 1, Dr, N), BF),
            V((2, Dr, N), BF),
            V((T, D), BF),
            V((2, T, D), BF),
            V((2, T, D), BF),
            V((2, T, D), BF),
            V((2, T, 3 * C), BF),
            V((2, T, C), BF),
            V((1, T, z_.GUw), BF),
            V((2, T, z_.Dw), BF),
            V((2, MH * R, D), F32),
            V((2, MH * R, D), BF),
            V((2, T, D), BF),
            V((T, z_.GUw), BF),
            V((T, 3 * C), BF),
            V((MH * R, D), F32),
            V((2, MH * R, D), BF),
            V((2, T, D), BF),
            V((2, MH, Hn * R, D), BF),
            V((2, MH, Hn - 1, R, D), BF),
            V((2, MH, Hn - 1, R, D), BF),
            V((2, NBH, NH * BLOCK, BLOCK), BF),
            V((T, C), F32),
            V((T, C), BF),
            V((2 * NBH, DH, C), F32),
            V((2, DH, C), BF),
            V((2, DH, C), BF),
            V((NBH, BLOCK, BLOCK), F32),
            V((NBH, BLOCK, 128), F32),
            V((NBH, BLOCK, 128), F32),
            V((NBH, 8, 128), F32),
            V((nd * nt, 2, 128), F32),
            V((2, 2, D), F32),
            V((2, D), F32),
            V((2, 2, D), F32),
            V((2, D), F32),
            V((nt - 1, 2, D), F32),
            V((nd - 1, 2, D), F32),
            DMA((2, MH)),
            DMA((2,)),
            DMA((2, MH, nt - 1)),
            DMA((2,)),
            DMA((2, 4)),
            DMA((2,)),
            DMA((2, 4, max(4, nd - 1))),
            DMA((6,)),
            DMA((6, MH, Hn)),
            DMA((2, MH)),
            DMA((2, MH)),
            DMA((2, MH, Hn - 1)),
            DMA((2, MH, Hn - 1)),
            DMA((2,)),
            DMA((2,)),
            DMA((2,)),
            DMA((2, 2)),
            DMA((2,)),
            DMA((2, 7, 3)),
            DMA((2,)),
            DMA((7, 2)),
            DMA((4,)),
            DMA((2, max(nd, nt) - 1)),
            DMA((2, max(nd, nt) - 1)),
            DMA((2,)),
            DMA((4,)),
        ]
        out_y, out_g, grad_qkv, grad_o, grad_gu, grad_d, grad_gain = pl.pallas_call(
            functools.partial(body, z_),
            out_shape=(
                jax.ShapeDtypeStruct((M, R, D), BF),
                jax.ShapeDtypeStruct((M, R, D), BF),
                jax.ShapeDtypeStruct((3, Dr, C), F32),
                jax.ShapeDtypeStruct((C, Dr), F32),
                jax.ShapeDtypeStruct((2 * F, Dr), F32),
                jax.ShapeDtypeStruct((F, Dr), F32),
                jax.ShapeDtypeStruct((2, width), F32),
            ),
            in_specs=[anywhere] * 6 + [vmem, vmem],
            out_specs=(anywhere,) * 6 + (vmem,),
            scratch_shapes=scratch,
            compiler_params=pltpu.CompilerParams(
                collective_id=0, has_side_effects=True, vmem_limit_bytes=63 * 1024 * 1024
            ),
        )(
            qkv_rows,
            out_m[0],
            gateup_rows,
            down_m[0],
            inputs[0],
            cotangent[0],
            jnp.transpose(starts, (1, 0, 2)),
            gain_m[0],
        )
        results = (out_y, out_g, grad_qkv, grad_o, grad_gu, grad_d, grad_gain)
        out_y, out_g, grad_qkv, grad_o, grad_gu, grad_d, grad_gain = pl.pallas_call(
            place_results,
            out_shape=tuple(jax.ShapeDtypeStruct(r.shape, r.dtype) for r in results),
            in_specs=[anywhere] * len(results),
            out_specs=(anywhere,) * len(results),
            scratch_shapes=[V(r.shape, r.dtype) for r in results]
            + [DMA((len(results),)), DMA((len(results),))],
        )(*results)
        return (
            out_y[None, None],
            out_g[None, None],
            jnp.transpose(grad_qkv, (1, 0, 2))[None],
            grad_o[None],
            jnp.transpose(grad_gu.reshape(2, F, Dr), (2, 0, 1))[None],
            grad_d[None],
            grad_gain[None],
        )

    return jax.shard_map(
        on_device,
        mesh=mesh,
        in_specs=(
            P("dp", None, "tensor", None),
            P("dp", None, None),
            P("dp", None, "tensor", None),
            P("section", "dp", None, "tensor"),
            P("section", "tensor", "dp"),
            P("section", "dp", None, "tensor"),
            P("section", "tensor", "dp"),
            P("section", None, ("dp", "tensor")),
        ),
        out_specs=(
            P("section", "dp", None, "tensor", None),
            P("section", "dp", None, "tensor", None),
            P("section", "dp", None, "tensor"),
            P("section", "tensor", "dp"),
            P("section", "dp", None, "tensor"),
            P("section", "tensor", "dp"),
            P("section", None, ("dp", "tensor")),
        ),
        check_vma=False,
    )
```
